32 devices in a mesh: ctx: 8 (over y, x, core), fsdp: 4 (over z).
Axes of the slice: x: 2, y: 2, z: 4, core: 2. Of those that a mesh axis runs over, the one named last changes fastest.
Arguments:
- hidden_in: bfloat16 [4, 1024, 2048], P('fsdp', 'ctx'), may hold values from -6 to 6
- out_grad: bfloat16 [4, 1024, 2048], P('fsdp', 'ctx'), may hold values from -6 to 6
- doc_ids: int32 [4, 1024], P('fsdp', 'ctx'), may hold values from 0 to 2, as said below
- norm_gain: bfloat16 [2048], P(('ctx', 'fsdp')), may hold values from 0.5 to 1.5
- query_weight: bfloat16 [2048, 1024], P(('ctx', 'fsdp')), may hold values from -0.125 to 0.125
- key_matrix: bfloat16 [2048, 256], P(('ctx', 'fsdp')), may hold values from -0.125 to 0.125
- value_matrix: bfloat16 [2048, 256], P(('ctx', 'fsdp')), may hold values from -0.125 to 0.125
- attn_out_weight: bfloat16 [1024, 2048], P(('ctx', 'fsdp')), may hold values from -2 to 2
- mixer_gate_weight: bfloat16 [2048, 3072], P(('ctx', 'fsdp')), may hold values from -0.125 to 0.125
- conv_in_weight: bfloat16 [2048, 3584], P(('ctx', 'fsdp')), may hold values from -0.125 to 0.125
- step_weight: bfloat16 [2048, 48], P(('ctx', 'fsdp')), may hold values from -0.125 to 0.125
- conv_weight: bfloat16 [4, 3584], P(None, ('ctx', 'fsdp')), may hold values from -3 to 3
- conv_bias: bfloat16 [3584], P(('ctx', 'fsdp')), may hold values from -3 to 3
- step_bias: float32 [48], replicated, may hold values from -5 to -1
- log_decay: float32 [48], replicated, may hold values from -7 to 1
- skip_gain: float32 [48], replicated, may hold values from 0.5 to 1.5
- mixer_gain: bfloat16 [3072], P(('ctx', 'fsdp')), may hold values from 0.5 to 1.5
- mamba_out_weight: bfloat16 [3072, 2048], P(('ctx', 'fsdp')), may hold values from -0.109375 to 0.109375
- ffn_gain: bfloat16 [2048], P(('ctx', 'fsdp')), may hold values from 0.5 to 1.5
- gate_weight: bfloat16 [2048, 4096], P(('ctx', 'fsdp')), may hold values from -0.125 to 0.125
- up_weight: bfloat16 [2048, 4096], P(('ctx', 'fsdp')), may hold values from -0.125 to 0.125
- down_weight: bfloat16 [4096, 2048], P(('ctx', 'fsdp')), may hold values from -0.09375 to 0.09375
Outputs:
- block_out: bfloat16 [4, 1024, 2048], P('fsdp', 'ctx')
- input_grad: bfloat16 [4, 1024, 2048], P('fsdp', 'ctx')
- norm_gain_grad: float32 [2048], P(('ctx', 'fsdp'))
- query_weight_grad: float32 [2048, 1024], P(('ctx', 'fsdp'))
- key_weight_grad: float32 [2048, 256], P(('ctx', 'fsdp'))
- value_weight_grad: float32 [2048, 256], P(('ctx', 'fsdp'))
- attn_out_weight_grad: float32 [1024, 2048], P(('ctx', 'fsdp'))
- mixer_gate_weight_grad: float32 [2048, 3072], P(('ctx', 'fsdp'))
- conv_in_weight_grad: float32 [2048, 3584], P(('ctx', 'fsdp'))
- step_weight_grad: float32 [2048, 48], P(('ctx', 'fsdp'))
- conv_weight_grad: float32 [4, 3584], P(None, ('ctx', 'fsdp'))
- conv_bias_grad: float32 [3584], P(('ctx', 'fsdp'))
- step_bias_grad: float32 [48], replicated
- log_decay_grad: float32 [48], replicated
- skip_gain_grad: float32 [48], replicated
- mixer_gain_grad: float32 [3072], P(('ctx', 'fsdp'))
- mamba_out_weight_grad: float32 [3072, 2048], P(('ctx', 'fsdp'))
- ffn_gain_grad: float32 [2048], P(('ctx', 'fsdp'))
- gate_weight_grad: float32 [2048, 4096], P(('ctx', 'fsdp'))
- up_weight_grad: float32 [2048, 4096], P(('ctx', 'fsdp'))
- down_weight_grad: float32 [4096, 2048], P(('ctx', 'fsdp'))
The draws below stay inside these ranges and needn't reach their ends.
Inputs may be any that keep to these rules, and one draw needn't show every extreme that they name: `doc_ids`: each row never falls and holds three documents: the first starts the sequence and ends within its first 64 places, the last begins within its last 64 places.
All inputs are finite; a program needn't handle non-finite values.
Results may differ from the reference program's by a relative error of at most 0.023.
Values may be sent and summed in bfloat16 or wider, within the bound.
A program may use at most 448 MiB of HBM per device.

```python
import math
import jax
import jax.numpy as jnp
from jax import lax

MODEL_WIDTH = 2048
QUERY_HEADS = 8
KEY_VALUE_HEADS = 2
HEAD_SIZE = 128
HS = 48
HP = 64
STATE = 256
CONV = 4
FF = 4096
TOK_DEV = 128
DSSM = 3072
XBC = 3584
LENGTH = 1024
SEQS = 4


def draw_doc_ids(key, part):
    key = jax.random.fold_in(key, 7)
    first_key, second_key = jax.random.split(key)
    starts = jax.random.randint(first_key, (SEQS, 1), 1, TOK_DEV // 2)
    finish = LENGTH - jax.random.randint(second_key, (SEQS, 1), 1, TOK_DEV // 2)
    places = jnp.arange(LENGTH)[None, :]
    return (places >= starts).astype(jnp.int32) + (places >= finish).astype(jnp.int32)


def block_scale(stream_key, dims, cuts, least, largest):
    level, own = 1.0, jax.random.fold_in(stream_key, 6)
    for position, shards_of in cuts:
        heights = jnp.exp(jax.random.uniform(jax.random.fold_in(own, position), (shards_of,), jnp.float32, least / len(cuts), largest / len(cuts)))
        level = level * jnp.repeat(heights, dims[position] // shards_of).reshape([-1 if axis == position else 1 for axis in range(len(dims))])
    return level


def scatter_about(stream_key, extent, width, bound, cuts=(), kind=jnp.bfloat16):
    values = jax.random.normal(stream_key, extent, jnp.float32) * width
    if len(cuts) > 0:
        values = block_scale(stream_key, extent, cuts, -0.22, 0.18) * values
    return jnp.clip(values, min=-bound, max=bound).astype(kind)


def setup_inputs(seed: int = 0) -> dict:
    streams_of = jax.random.split(jax.random.key(seed), 23)
    hidden_in = scatter_about(streams_of[0], (SEQS, LENGTH, MODEL_WIDTH), 1.0, 6.0, ((0, 4), (1, 8)))
    out_grad = scatter_about(streams_of[1], (SEQS, LENGTH, MODEL_WIDTH), 1.0, 6.0, ((0, 4), (1, 8)))
    doc_ids = draw_doc_ids(jax.random.fold_in(streams_of[22], 71), 0)
    norm_gain = jnp.clip(1.0 + 0.1 * jax.random.normal(streams_of[3], (MODEL_WIDTH,), jnp.float32), 0.5, 1.5).astype(jnp.bfloat16)
    query_weight = scatter_about(streams_of[4], (MODEL_WIDTH, QUERY_HEADS * HEAD_SIZE), MODEL_WIDTH ** -0.5, 0.125, ((0, 32),))
    key_matrix = scatter_about(streams_of[5], (MODEL_WIDTH, KEY_VALUE_HEADS * HEAD_SIZE), MODEL_WIDTH ** -0.5, 0.125, ((0, 32),))
    value_matrix = scatter_about(streams_of[6], (MODEL_WIDTH, KEY_VALUE_HEADS * HEAD_SIZE), MODEL_WIDTH ** -0.5, 0.125, ((0, 32),))
    attn_out_weight = scatter_about(streams_of[7], (QUERY_HEADS * HEAD_SIZE, MODEL_WIDTH), (QUERY_HEADS * HEAD_SIZE // 128) ** -0.5, 2.0, ((0, 32),))
    mixer_gate_weight = scatter_about(streams_of[8], (MODEL_WIDTH, DSSM), MODEL_WIDTH ** -0.5, 0.125, ((0, 32),))
    conv_in_weight = scatter_about(streams_of[9], (MODEL_WIDTH, XBC), MODEL_WIDTH ** -0.5, 0.125, ((0, 32),))
    step_weight = scatter_about(streams_of[10], (MODEL_WIDTH, HS), MODEL_WIDTH ** -0.5, 0.125, ((0, 32),))
    conv_weight = scatter_about(streams_of[11], (CONV, XBC), CONV ** -0.5, 3.0, ((1, 32),))
    conv_bias = scatter_about(streams_of[12], (XBC,), 0.5, 3.0, ((0, 32),))
    step_bias = jnp.clip(jax.random.uniform(streams_of[13], (HS,), jnp.float32, -5.0, -1.0), -5.0, -1.0)
    log_decay = jnp.clip(jax.random.uniform(streams_of[14], (HS,), jnp.float32, -7.0, 1.0), -7.0, 1.0)
    skip_gain = jnp.clip(jax.random.uniform(streams_of[15], (HS,), jnp.float32, 0.5, 1.5), 0.5, 1.5)
    mixer_gain = jnp.clip(1.0 + 0.1 * jax.random.normal(streams_of[16], (DSSM,), jnp.float32), 0.5, 1.5).astype(jnp.bfloat16)
    mamba_out_weight = scatter_about(streams_of[17], (DSSM, MODEL_WIDTH), DSSM ** -0.5, 0.109375, ((0, 32),))
    ffn_gain = jnp.clip(1.0 + 0.1 * jax.random.normal(streams_of[18], (MODEL_WIDTH,), jnp.float32), 0.5, 1.5).astype(jnp.bfloat16)
    gate_weight = scatter_about(streams_of[19], (MODEL_WIDTH, FF), MODEL_WIDTH ** -0.5, 0.125, ((0, 32),))
    up_weight = scatter_about(streams_of[20], (MODEL_WIDTH, FF), MODEL_WIDTH ** -0.5, 0.125, ((0, 32),))
    down_weight = scatter_about(streams_of[21], (FF, MODEL_WIDTH), FF ** -0.5, 0.09375, ((0, 32),))
    return dict(hidden_in=hidden_in, out_grad=out_grad, doc_ids=doc_ids, norm_gain=norm_gain, query_weight=query_weight, key_matrix=key_matrix, value_matrix=value_matrix, attn_out_weight=attn_out_weight, mixer_gate_weight=mixer_gate_weight, conv_in_weight=conv_in_weight, step_weight=step_weight, conv_weight=conv_weight, conv_bias=conv_bias, step_bias=step_bias, log_decay=log_decay, skip_gain=skip_gain, mixer_gain=mixer_gain, mamba_out_weight=mamba_out_weight, ffn_gain=ffn_gain, gate_weight=gate_weight, up_weight=up_weight, down_weight=down_weight)


EPSILON = 1e-05
ROPE_BASE = 100000000000.0
NEGATIVE_FLOOR = -1e+30
HIGHEST = lax.Precision.HIGHEST

@jax.custom_vjp
def lowered_output(v):
    return lax.optimization_barrier(v.astype(jnp.bfloat16)).astype(jnp.float32)

@jax.custom_vjp
def lowered_backward(v):
    return v

def low_keep(v):
    return (lowered_output(v), None)

def low_pass(kept, grad):
    return (grad,)

def back_keep(v):
    return (v, None)

def back_low(kept, grad):
    return (lowered_output(grad),)
lowered_output.defvjp(low_keep, low_pass)
lowered_backward.defvjp(back_keep, back_low)

def matrix_product(left, right):
    return jnp.dot(left, right, precision=HIGHEST)

def rms_scale(values, gain):
    return values * lax.rsqrt(lax.optimization_barrier(jnp.mean(values * values, axis=-1, keepdims=True)) + EPSILON) * gain

def rotate(values, places):
    half_size = values.shape[-1] // 2
    freqs = ROPE_BASE ** (-jnp.arange(half_size).astype(jnp.float32) / half_size)
    angles = places[:, None] * freqs[None, :]
    cosine = jnp.cos(angles)[:, None, :]
    sine = jnp.sin(angles)[:, None, :]
    first = values[..., :half_size]
    second = values[..., half_size:]
    return jnp.concatenate([first * cosine - second * sine, second * cosine + first * sine], axis=-1)

def conv_part(widened, taps_weight, bias, widened_docs, documents):
    row_length_total = documents.shape[0]
    total = bias[None, :]
    for tap_index in range(taps_weight.shape[0]):
        same_doc = (widened_docs[tap_index:tap_index + row_length_total] == documents)[:, None]
        total = total + jnp.where(same_doc, widened[tap_index:tap_index + row_length_total] * taps_weight[tap_index][None, :], 0.0)
    return jax.nn.silu(total)

def step_part(step_lin, step_bias, log_decay):
    return (jax.nn.softplus(step_lin + step_bias), -jnp.exp(log_decay))

def block_stats(mixer_in, write_proj, step_size, decay_rate, documents, prior_doc):
    decay_log = jnp.cumsum(step_size * decay_rate[None, :], axis=0)
    last_doc = documents[-1]
    tail_weight = jnp.where((documents == last_doc)[:, None], jnp.exp(decay_log[-1][None, :] - decay_log), 0.0) * step_size
    state_loc = jnp.einsum('thp,tn->hpn', mixer_in * tail_weight[:, :, None], write_proj, precision=HIGHEST)
    carry_decay = jnp.exp(decay_log[-1]) * (last_doc == prior_doc).astype(jnp.float32)
    return (state_loc, carry_decay)

def block_mix(mixer_in, write_proj, read_proj, step_size, decay_rate, skip_gain, state_in, documents, prior_doc):
    decay_log = jnp.cumsum(step_size * decay_rate[None, :], axis=0)
    positions = jnp.arange(documents.shape[0])
    visible = (documents[:, None] == documents[None, :]) & (positions[:, None] >= positions[None, :])
    spread = decay_log.T[:, :, None] - decay_log.T[:, None, :]
    decay_pair = jnp.where(visible[None], jnp.exp(jnp.where(visible[None], spread, 0.0)), 0.0)
    gram = jnp.dot(read_proj, write_proj.T, precision=HIGHEST)
    mixing = decay_pair * gram[None] * step_size.T[:, None, :]
    inner = jnp.einsum('htu,uhp->thp', mixing, mixer_in, precision=HIGHEST)
    entry = jnp.where((documents == prior_doc)[:, None], jnp.exp(decay_log), 0.0)
    carried = jnp.einsum('tn,hpn->thp', read_proj, state_in, precision=HIGHEST) * entry[:, :, None]
    return inner + carried + skip_gain[None, :, None] * mixer_in

def gated_norm(flat_mixed, mixer_gate, gain):
    return rms_scale(flat_mixed * jax.nn.silu(mixer_gate), gain)

def attention(rotated_query, key_rot, value_lowered, documents, places):
    row_length_total = rotated_query.shape[0]
    head_cluster = QUERY_HEADS // KEY_VALUE_HEADS
    tile_block = math.gcd(row_length_total, 512)
    block_tally = row_length_total // tile_block
    blocks_of_query = rotated_query.reshape(block_tally, tile_block, KEY_VALUE_HEADS, head_cluster, HEAD_SIZE)
    doc_blocks = documents.reshape(block_tally, tile_block)
    place_blocks = places.reshape(block_tally, tile_block)

    def one_block(item):
        query_block, doc_block, place_block = item
        scores = jnp.einsum('qgrd,kgd->grqk', query_block, key_rot, precision=HIGHEST) * HEAD_SIZE ** (-0.5)
        scores = lowered_backward(scores)
        visible = (doc_block[:, None] == documents[None, :]) & (place_block[:, None] >= places[None, :])
        masked = jnp.where(visible, scores, NEGATIVE_FLOOR)
        peak = lax.optimization_barrier(jnp.max(masked, axis=-1, keepdims=True))
        weights = jnp.where(visible, jnp.exp(masked - peak), 0.0)
        probs = weights / lax.optimization_barrier(jnp.sum(weights, axis=-1, keepdims=True))
        return jnp.einsum('grqk,kgd->qgrd', lowered_output(probs), value_lowered, precision=HIGHEST)
    mixed = lax.map(jax.checkpoint(one_block), (blocks_of_query, doc_blocks, place_blocks))
    return mixed.reshape(row_length_total, QUERY_HEADS * HEAD_SIZE)

def layer(params, resid, documents):
    norm_gain, query_weight, key_matrix, value_matrix, attn_out_weight, mixer_gate_weight, conv_in_weight, step_weight, conv_weight, conv_bias, step_bias, log_decay, skip_gain, mixer_gain, mamba_out_weight, ffn_gain, gate_weight, up_weight, down_weight = params
    row_length_total = resid.shape[0]
    places = jnp.arange(row_length_total).astype(jnp.float32)
    normalized_input = lowered_output(rms_scale(resid, norm_gain))
    query_lin = lowered_backward(matrix_product(normalized_input, query_weight)).reshape(row_length_total, QUERY_HEADS, HEAD_SIZE)
    key_linear = lowered_backward(matrix_product(normalized_input, key_matrix)).reshape(row_length_total, KEY_VALUE_HEADS, HEAD_SIZE)
    rotated_query = lowered_output(rotate(query_lin, places))
    key_rot = lowered_output(rotate(key_linear, places))
    value_lowered = lowered_output(lowered_backward(matrix_product(normalized_input, value_matrix))).reshape(row_length_total, KEY_VALUE_HEADS, HEAD_SIZE)
    attn_mix = attention(rotated_query, key_rot, value_lowered, documents, places)
    attn_out = lowered_backward(matrix_product(lowered_output(lowered_backward(attn_mix)), attn_out_weight))
    mixer_gate = lowered_backward(matrix_product(normalized_input, mixer_gate_weight))
    conv_lin = lowered_output(lowered_backward(matrix_product(normalized_input, conv_in_weight)))
    step_lin = lowered_backward(matrix_product(normalized_input, step_weight))
    widened = jnp.concatenate([jnp.zeros((CONV - 1, conv_lin.shape[1]), jnp.float32), conv_lin], axis=0)
    widened_docs = jnp.concatenate([jnp.full((CONV - 1,), -1, jnp.int32), documents.astype(jnp.int32)])
    conv_act = lowered_output(conv_part(widened, conv_weight, conv_bias, widened_docs, documents))
    dssm = HS * HP
    block_tally = row_length_total // TOK_DEV
    mixer_in = conv_act[:, :dssm].reshape(block_tally, TOK_DEV, HS, HP)
    write_proj = conv_act[:, dssm:dssm + STATE].reshape(block_tally, TOK_DEV, STATE)
    read_proj = conv_act[:, dssm + STATE:].reshape(block_tally, TOK_DEV, STATE)
    step_size, decay_rate = step_part(step_lin, step_bias, log_decay)
    step_blocks = step_size.reshape(block_tally, TOK_DEV, HS)
    doc_blocks = documents.reshape(block_tally, TOK_DEV)

    def one_step(carry, item):
        state_in, prior_doc = carry
        in_block, write_block, read_block, step_block, docs_block = item
        state_loc, carry_decay = block_stats(in_block, write_block, step_block, decay_rate, docs_block, prior_doc)
        mixed = block_mix(in_block, write_block, read_block, step_block, decay_rate, skip_gain, state_in, docs_block, prior_doc)
        state_out = carry_decay[:, None, None] * state_in + state_loc
        return ((state_out, docs_block[-1]), mixed)
    start_carry = (jnp.zeros((HS, HP, STATE), jnp.float32), jnp.int32(-1))
    _, mixed_blocks = lax.scan(jax.checkpoint(one_step), start_carry, (mixer_in, write_proj, read_proj, step_blocks, doc_blocks))
    ymix = lowered_output(gated_norm(mixed_blocks.reshape(row_length_total, dssm), mixer_gate, mixer_gain))
    mamba_out = lowered_backward(matrix_product(ymix, mamba_out_weight))
    mid = resid + attn_out + mamba_out
    normed_two = lowered_output(rms_scale(mid, ffn_gain))
    gate_lin = lowered_backward(matrix_product(normed_two, gate_weight))
    up_lin = lowered_backward(matrix_product(normed_two, up_weight))
    hidden = lowered_output(jax.nn.silu(gate_lin) * up_lin)
    return mid + lowered_backward(matrix_product(hidden, down_weight))

def reference(hidden_in, out_grad, doc_ids, norm_gain, query_weight, key_matrix, value_matrix, attn_out_weight, mixer_gate_weight, conv_in_weight, step_weight, conv_weight, conv_bias, step_bias, log_decay, skip_gain, mixer_gain, mamba_out_weight, ffn_gain, gate_weight, up_weight, down_weight):
    params = tuple((weight.astype(jnp.float32) for weight in (norm_gain, query_weight, key_matrix, value_matrix, attn_out_weight, mixer_gate_weight, conv_in_weight, step_weight, conv_weight, conv_bias, step_bias, log_decay, skip_gain, mixer_gain, mamba_out_weight, ffn_gain, gate_weight, up_weight, down_weight)))

    def one_sequence(totals, item):
        sequence_in, sequence_grad, sequence_docs = item

        def forward(weights, resid):
            return layer(weights, resid, sequence_docs)
        outcome, pullback = jax.vjp(forward, params, sequence_in.astype(jnp.float32))
        weight_grads, resid_grad = pullback(sequence_grad.astype(jnp.float32))
        totals = jax.tree.map(jnp.add, totals, weight_grads)
        return (totals, (outcome.astype(jnp.bfloat16), resid_grad.astype(jnp.bfloat16)))
    zero_grads = tuple((jnp.zeros_like(weight) for weight in params))
    totals, (block_out, input_grad) = lax.scan(one_sequence, zero_grads, (hidden_in, out_grad, doc_ids))
    return (block_out, input_grad, totals[0], totals[1], totals[2], totals[3], totals[4], totals[5], totals[6], totals[7], totals[8], totals[9], totals[10], totals[11], totals[12], totals[13], totals[14], totals[15], totals[16], totals[17], totals[18])
```

```python
from functools import partial
import math

import jax
import jax.numpy as jnp
from jax import lax
from jax.sharding import PartitionSpec as P

CTX = "ctx"
FSDP = "fsdp"
QUERY_HEADS = 8
KEY_VALUE_HEADS = 2
HEAD_SIZE = 128
HS = 48
HP = 64
STATE = 256
CONV = 4


EPSILON = 1e-05
ROPE_BASE = 100000000000.0
NEGATIVE_FLOOR = -1e30
HIGHEST = lax.Precision.HIGHEST


def shifted(value, axis, steps):
    count = lax.axis_size(axis)
    leading, last = (max(0, -steps), min(count, count - steps))
    return lax.ppermute(value, axis, [(source, source + steps) for source in range(leading, last)])


def prefix(shard, axis, combine, identity):
    devices, position = (lax.axis_size(axis), lax.axis_index(axis))
    everything = jax.tree.map(
        lambda part, kind: lax.all_gather(part.astype(kind), axis),
        shard,
        (jnp.bfloat16, jnp.bfloat16),
    )
    start = jax.tree.map(
        lambda part, zero: jnp.broadcast_to(jnp.asarray(zero, part.dtype), part.shape),
        shard,
        identity,
    )

    def step(k, before):
        reached = k < position
        new = combine(
            before, jax.tree.map(lambda part, own: part[k].astype(own.dtype), everything, shard)
        )
        return jax.tree.map(lambda a, b: jnp.where(reached, a, b), new, before)

    return lax.fori_loop(0, devices, step, start)


def carried_in(shard, axis, join, neutral):
    count = lax.axis_size(axis)
    place = lax.axis_index(axis)
    ahead = count - 1 - place
    gathered = jax.tree.map(
        lambda a, kind: lax.all_gather(a.astype(kind), axis),
        shard,
        jax.tree.map(lambda a: jnp.bfloat16 if a.dtype == jnp.float32 else a.dtype, shard),
    )
    state = jax.tree.map(lambda a, e: jnp.zeros_like(a) + jnp.asarray(e, a.dtype), shard, neutral)

    def one(step, state):
        source = count - 1 - step
        return join(
            state,
            jax.tree.map(
                lambda a, own: lax.dynamic_index_in_dim(a, source, 0, False).astype(own.dtype),
                gathered,
                shard,
            ),
        )

    return lax.fori_loop(0, ahead, one, state)


def rms_scale(values, gain):
    return values * lax.rsqrt(jnp.mean(values * values, axis=-1, keepdims=True) + EPSILON) * gain


def rotate(values, places):
    half_size = values.shape[-1] // 2
    freqs = ROPE_BASE ** (-jnp.arange(half_size).astype(jnp.float32) / half_size)
    angles = places[:, None] * freqs[None, :]
    cosine = jnp.cos(angles)[:, None, :]
    sine = jnp.sin(angles)[:, None, :]
    first = values[..., :half_size]
    second = values[..., half_size:]
    return jnp.concatenate(
        [first * cosine - second * sine, second * cosine + first * sine], axis=-1
    )


def conv_part(widened, taps_weight, bias, widened_docs, documents):
    row_length_total = documents.shape[0]
    total = bias[None, :]
    for tap_index in range(taps_weight.shape[0]):
        same_doc = (widened_docs[tap_index : tap_index + row_length_total] == documents)[:, None]
        total = total + jnp.where(
            same_doc,
            widened[tap_index : tap_index + row_length_total] * taps_weight[tap_index][None, :],
            0.0,
        )
    return jax.nn.silu(total)


def step_part(step_lin, step_bias, log_decay):
    return (jax.nn.softplus(step_lin + step_bias), -jnp.exp(log_decay))


def block_stats(mixer_in, write_proj, step_size, decay_rate, documents, prior_doc):
    decay_log = jnp.cumsum(step_size * decay_rate[None, :], axis=0)
    last_doc = documents[-1]
    tail_weight = (
        jnp.where(
            (documents == last_doc)[:, None], jnp.exp(decay_log[-1][None, :] - decay_log), 0.0
        )
        * step_size
    )
    state_loc = jnp.einsum(
        "thp,tn->hpn", mixer_in * tail_weight[:, :, None], write_proj, precision=HIGHEST
    )
    carry_decay = jnp.exp(decay_log[-1]) * (last_doc == prior_doc).astype(jnp.float32)
    return (state_loc, carry_decay)


def block_mix(
    mixer_in,
    write_proj,
    read_proj,
    step_size,
    decay_rate,
    skip_gain,
    state_in,
    documents,
    prior_doc,
):
    decay_log = jnp.cumsum(step_size * decay_rate[None, :], axis=0)
    positions = jnp.arange(documents.shape[0])
    visible = (documents[:, None] == documents[None, :]) & (
        positions[:, None] >= positions[None, :]
    )
    spread = decay_log.T[:, :, None] - decay_log.T[:, None, :]
    decay_pair = jnp.where(visible[None], jnp.exp(jnp.where(visible[None], spread, 0.0)), 0.0)
    gram = jnp.dot(read_proj, write_proj.T, precision=HIGHEST)
    mixing = decay_pair * gram[None] * step_size.T[:, None, :]
    inner = jnp.einsum("htu,uhp->thp", mixing, mixer_in, precision=HIGHEST)
    entry = jnp.where((documents == prior_doc)[:, None], jnp.exp(decay_log), 0.0)
    carried = jnp.einsum("tn,hpn->thp", read_proj, state_in, precision=HIGHEST) * entry[:, :, None]
    return inner + carried + skip_gain[None, :, None] * mixer_in


def gated_norm(flat_mixed, mixer_gate, gain):
    return rms_scale(flat_mixed * jax.nn.silu(mixer_gate), gain)


def chain_combine(earlier, later):
    decay_early, state_early = earlier
    decay_late, state_late = later
    return (decay_early * decay_late, decay_late[:, None, None] * state_early + state_late)


def piece_scores(piece, start, query_group, query_docs, query_places):
    key_segment, value_segment, docs_piece = piece
    segment_rows = key_segment.shape[0]
    heads_of_key = key_segment.reshape(segment_rows, KEY_VALUE_HEADS, HEAD_SIZE).transpose(1, 0, 2)
    heads_of_value = value_segment.reshape(segment_rows, KEY_VALUE_HEADS, HEAD_SIZE).transpose(
        1, 0, 2
    )
    key_places = (start + jnp.arange(segment_rows)).astype(jnp.float32)
    visible = (docs_piece.astype(jnp.float32)[None, :] == query_docs[:, None]) & (
        key_places[None, :] <= query_places[:, None]
    )
    scores = jnp.einsum(
        "gqd,gkd->gqk", query_group, heads_of_key, preferred_element_type=jnp.float32
    ) * HEAD_SIZE ** (-0.5)
    return (heads_of_key, heads_of_value, visible, jnp.where(visible[None], scores, NEGATIVE_FLOOR))


def fold_local(step_fn, whole, start_carry):
    row_length_total = whole[0].shape[0]
    tile_block = math.gcd(row_length_total, 512)

    def advance(block_index, carry):
        start = block_index * tile_block
        piece = tuple((lax.dynamic_slice_in_dim(member, start, tile_block, 0) for member in whole))
        return step_fn(carry, piece, start)

    return lax.fori_loop(0, row_length_total // tile_block, advance, start_carry)


def on_device(
    hidden_in,
    out_grad,
    doc_ids,
    norm_gain,
    query_weight,
    key_matrix,
    value_matrix,
    attn_out_weight,
    mixer_gate_weight,
    conv_in_weight,
    step_weight,
    conv_weight,
    conv_bias,
    step_bias,
    log_decay,
    skip_gain,
    mixer_gain,
    mamba_out_weight,
    ffn_gain,
    gate_weight,
    up_weight,
    down_weight,
):
    single_float = jnp.float32
    brain_float_half = jnp.bfloat16
    (
        norm_full,
        query_full,
        complete_key,
        value_full,
        attn_out_full,
        mixer_gate_full,
        conv_in_full,
        step_full,
        conv_full,
        conv_bias_full,
        mixer_gain_full,
        mamba_out_full,
    ) = (
        lax.all_gather(norm_gain, (CTX, FSDP), axis=0, tiled=True),
        lax.all_gather(query_weight, (CTX, FSDP), axis=0, tiled=True),
        lax.all_gather(key_matrix, (CTX, FSDP), axis=0, tiled=True),
        lax.all_gather(value_matrix, (CTX, FSDP), axis=0, tiled=True),
        lax.all_gather(attn_out_weight, (CTX, FSDP), axis=0, tiled=True),
        lax.all_gather(mixer_gate_weight, (CTX, FSDP), axis=0, tiled=True),
        lax.all_gather(conv_in_weight, (CTX, FSDP), axis=0, tiled=True),
        lax.all_gather(step_weight, (CTX, FSDP), axis=0, tiled=True),
        lax.all_gather(conv_weight, (CTX, FSDP), axis=1, tiled=True),
        lax.all_gather(conv_bias, (CTX, FSDP), axis=0, tiled=True),
        lax.all_gather(mixer_gain, (CTX, FSDP), axis=0, tiled=True),
        lax.all_gather(mamba_out_weight, (CTX, FSDP), axis=0, tiled=True),
    )
    tokens_per_worker = hidden_in.shape[1]
    head_cluster = QUERY_HEADS // KEY_VALUE_HEADS
    dssm = HS * HP
    taps = CONV - 1
    resid = hidden_in[0].astype(single_float)
    documents = doc_ids[0]
    places = (lax.axis_index(CTX) * tokens_per_worker + jnp.arange(tokens_per_worker)).astype(
        single_float
    )
    norm_one, norm_one_back = jax.vjp(rms_scale, resid, norm_full.astype(single_float))
    normalized_input = norm_one.astype(brain_float_half)
    query_lin = jnp.dot(normalized_input, query_full, preferred_element_type=single_float).reshape(
        tokens_per_worker, QUERY_HEADS, HEAD_SIZE
    )
    key_linear = jnp.dot(
        normalized_input, complete_key, preferred_element_type=single_float
    ).reshape(tokens_per_worker, KEY_VALUE_HEADS, HEAD_SIZE)
    query_turned, unturn_query = jax.vjp(partial(rotate, places=places), query_lin)
    rotated_key, unrotate_key = jax.vjp(partial(rotate, places=places), key_linear)
    rotated_query = query_turned.astype(brain_float_half)
    flattened_key = rotated_key.astype(brain_float_half).reshape(
        tokens_per_worker, KEY_VALUE_HEADS * HEAD_SIZE
    )
    value_lowered = jnp.dot(
        normalized_input, value_full, preferred_element_type=single_float
    ).astype(brain_float_half)
    docs_low = documents.astype(brain_float_half)
    query_group = (
        rotated_query.reshape(tokens_per_worker, KEY_VALUE_HEADS, head_cluster, HEAD_SIZE)
        .transpose(1, 2, 0, 3)
        .reshape(KEY_VALUE_HEADS, head_cluster * tokens_per_worker, HEAD_SIZE)
    )
    query_places = jnp.tile(places, head_cluster)
    query_docs = jnp.tile(documents.astype(single_float), head_cluster)

    def attend_piece(carry, piece, start):
        previous_maximum, total_old, summed_old = carry
        heads_of_key, heads_of_value, visible, scores = piece_scores(
            piece, start, query_group, query_docs, query_places
        )
        peak_new = jnp.maximum(previous_maximum, jnp.max(scores, axis=-1))
        weights = jnp.where(visible[None], jnp.exp(scores - peak_new[:, :, None]), 0.0)
        factor = jnp.exp(previous_maximum - peak_new)
        total_new = total_old * factor + jnp.sum(weights, axis=-1)
        summed_new = summed_old * factor[:, :, None] + jnp.einsum(
            "gqk,gkd->gqd",
            weights.astype(brain_float_half),
            heads_of_value,
            preferred_element_type=single_float,
        )
        return (peak_new, total_new, summed_new)

    rows_of_query = head_cluster * tokens_per_worker
    start_forward = (
        jnp.full((KEY_VALUE_HEADS, rows_of_query), NEGATIVE_FLOOR, single_float),
        jnp.zeros((KEY_VALUE_HEADS, rows_of_query), single_float),
        jnp.zeros((KEY_VALUE_HEADS, rows_of_query, HEAD_SIZE), single_float),
    )
    kv_whole = (
        lax.all_gather(flattened_key, CTX, axis=0, tiled=True),
        lax.all_gather(value_lowered, CTX, axis=0, tiled=True),
        lax.all_gather(docs_low, CTX, axis=0, tiled=True),
    )
    peak, total, summed = fold_local(attend_piece, kv_whole, start_forward)
    attention_cluster = summed / total[:, :, None]
    log_total = peak + jnp.log(total)
    attn_low = (
        attention_cluster.reshape(KEY_VALUE_HEADS, head_cluster, tokens_per_worker, HEAD_SIZE)
        .transpose(2, 0, 1, 3)
        .reshape(tokens_per_worker, QUERY_HEADS * HEAD_SIZE)
        .astype(brain_float_half)
    )
    attn_out = jnp.dot(attn_low, attn_out_full, preferred_element_type=single_float)
    mixer_gate = jnp.dot(normalized_input, mixer_gate_full, preferred_element_type=single_float)
    conv_lin = jnp.dot(normalized_input, conv_in_full, preferred_element_type=single_float).astype(
        brain_float_half
    )
    step_lin = jnp.dot(normalized_input, step_full, preferred_element_type=single_float)
    rim_rows, rim_docs = shifted(
        (conv_lin[tokens_per_worker - taps :], docs_low[tokens_per_worker - taps :]), CTX, 1
    )
    widened = jnp.concatenate([rim_rows, conv_lin], axis=0).astype(single_float)
    widened_docs = jnp.concatenate([rim_docs.astype(jnp.int32), documents])
    prior_doc = widened_docs[taps - 1]
    conv_act, conv_back = jax.vjp(
        partial(conv_part, widened_docs=widened_docs, documents=documents),
        widened,
        conv_full.astype(single_float),
        conv_bias_full.astype(single_float),
    )
    conv_vals = conv_act.astype(brain_float_half).astype(single_float)
    mixer_in = conv_vals[:, :dssm].reshape(tokens_per_worker, HS, HP)
    write_proj = conv_vals[:, dssm : dssm + STATE]
    read_proj = conv_vals[:, dssm + STATE :]
    (step_size, decay_rate), step_back = jax.vjp(step_part, step_lin, step_bias, log_decay)
    (state_loc, carry_decay), stats_back = jax.vjp(
        partial(block_stats, documents=documents, prior_doc=prior_doc),
        mixer_in,
        write_proj,
        step_size,
        decay_rate,
    )
    chain_identity = (jnp.ones_like(carry_decay), jnp.zeros_like(state_loc))
    _, state_in = prefix((carry_decay, state_loc), CTX, chain_combine, chain_identity)
    mixed, mix_back = jax.vjp(
        partial(block_mix, documents=documents, prior_doc=prior_doc),
        mixer_in,
        write_proj,
        read_proj,
        step_size,
        decay_rate,
        skip_gain,
        state_in,
    )
    ymix_vals, gate_back = jax.vjp(
        gated_norm,
        mixed.reshape(tokens_per_worker, dssm),
        mixer_gate,
        mixer_gain_full.astype(single_float),
    )
    ymix_low = ymix_vals.astype(brain_float_half)
    mamba_out = jnp.dot(ymix_low, mamba_out_full, preferred_element_type=single_float)
    ffn_gain_full, gate_full, up_full, down_full = (
        lax.all_gather(ffn_gain, (CTX, FSDP), axis=0, tiled=True),
        lax.all_gather(gate_weight, (CTX, FSDP), axis=0, tiled=True),
        lax.all_gather(up_weight, (CTX, FSDP), axis=0, tiled=True),
        lax.all_gather(down_weight, (CTX, FSDP), axis=0, tiled=True),
    )
    mid = resid + attn_out + mamba_out
    norm_two, norm_two_back = jax.vjp(rms_scale, mid, ffn_gain_full.astype(single_float))
    normed_two = norm_two.astype(brain_float_half)
    gate_lin = jnp.dot(normed_two, gate_full, preferred_element_type=single_float)
    up_lin = jnp.dot(normed_two, up_full, preferred_element_type=single_float)
    sigmoid_gate = jax.nn.sigmoid(gate_lin)
    silu_gate = gate_lin * sigmoid_gate
    hidden = (silu_gate * up_lin).astype(brain_float_half)
    block_out = (mid + jnp.dot(hidden, down_full, preferred_element_type=single_float)).astype(
        brain_float_half
    )
    grad_out = out_grad[0]
    down_grad_w = jnp.einsum("tf,td->fd", hidden, grad_out, preferred_element_type=single_float)
    grad_hidden = jnp.einsum("td,fd->tf", grad_out, down_full, preferred_element_type=single_float)
    grad_gate = (grad_hidden * up_lin * (sigmoid_gate + silu_gate * (1.0 - sigmoid_gate))).astype(
        brain_float_half
    )
    grad_up = (grad_hidden * silu_gate).astype(brain_float_half)
    gate_grad_w = jnp.einsum(
        "td,tf->df", normed_two, grad_gate, preferred_element_type=single_float
    )
    up_grad_w = jnp.einsum("td,tf->df", normed_two, grad_up, preferred_element_type=single_float)
    grad_normed_two = jnp.einsum(
        "tf,df->td", grad_gate, gate_full, preferred_element_type=single_float
    ) + jnp.einsum("tf,df->td", grad_up, up_full, preferred_element_type=single_float)
    grad_mid_norm, ffn_gain_grad = norm_two_back(grad_normed_two)
    grad_mid = grad_out.astype(single_float) + grad_mid_norm
    ffn_sums = (
        lax.psum_scatter(ffn_gain_grad, (CTX, FSDP), scatter_dimension=0, tiled=True),
        lax.psum_scatter(gate_grad_w, (CTX, FSDP), scatter_dimension=0, tiled=True),
        lax.psum_scatter(up_grad_w, (CTX, FSDP), scatter_dimension=0, tiled=True),
        lax.psum_scatter(down_grad_w, (CTX, FSDP), scatter_dimension=0, tiled=True),
    )
    branch_grad = grad_mid.astype(brain_float_half)
    attn_out_grad_w = jnp.einsum(
        "ti,td->id", attn_low, branch_grad, preferred_element_type=single_float
    )
    attention_gradient = jnp.einsum(
        "td,id->ti", branch_grad, attn_out_full, preferred_element_type=single_float
    ).astype(brain_float_half)
    grad_group = (
        attention_gradient.reshape(tokens_per_worker, KEY_VALUE_HEADS, head_cluster, HEAD_SIZE)
        .transpose(1, 2, 0, 3)
        .reshape(KEY_VALUE_HEADS, rows_of_query, HEAD_SIZE)
    )
    row_delta = jnp.sum(grad_group.astype(single_float) * attention_cluster, axis=-1)

    def attend_back(carry, piece, start):
        query_acc, kv_grad = carry
        heads_of_key, heads_of_value, visible, scores = piece_scores(
            piece, start, query_group, query_docs, query_places
        )
        segment_rows = heads_of_key.shape[1]
        probs = jnp.where(visible[None], jnp.exp(scores - log_total[:, :, None]), 0.0)
        prob_grad = jnp.einsum(
            "gqd,gkd->gqk", grad_group, heads_of_value, preferred_element_type=single_float
        )
        score_grad = (probs * (prob_grad - row_delta[:, :, None])).astype(brain_float_half)
        query_acc = query_acc + jnp.einsum(
            "gqk,gkd->gqd", score_grad, heads_of_key, preferred_element_type=single_float
        )
        key_portion = jnp.einsum(
            "gqk,gqd->kgd", score_grad, query_group, preferred_element_type=single_float
        ) * HEAD_SIZE ** (-0.5)
        value_portion = jnp.einsum(
            "gqk,gqd->kgd",
            probs.astype(brain_float_half),
            grad_group,
            preferred_element_type=single_float,
        )
        term = jnp.concatenate(
            [
                key_portion.reshape(segment_rows, KEY_VALUE_HEADS * HEAD_SIZE),
                value_portion.reshape(segment_rows, KEY_VALUE_HEADS * HEAD_SIZE),
            ],
            axis=1,
        )
        current = lax.dynamic_slice_in_dim(kv_grad, start, segment_rows, 0)
        kv_grad = lax.dynamic_update_slice_in_dim(kv_grad, current + term, start, 0)
        return (query_acc, kv_grad)

    start_back = (
        jnp.zeros((KEY_VALUE_HEADS, rows_of_query, HEAD_SIZE), single_float),
        jnp.zeros(
            (tokens_per_worker * lax.axis_size(CTX), 2 * KEY_VALUE_HEADS * HEAD_SIZE),
            single_float,
        ),
    )
    query_acc, kv_grad = fold_local(attend_back, kv_whole, start_back)
    local_key_value = lax.psum_scatter(
        kv_grad.astype(jnp.bfloat16), CTX, scatter_dimension=0, tiled=True
    ).astype(jnp.float32)
    query_turn_grad = (
        (query_acc * HEAD_SIZE ** (-0.5))
        .reshape(KEY_VALUE_HEADS, head_cluster, tokens_per_worker, HEAD_SIZE)
        .transpose(2, 0, 1, 3)
        .reshape(tokens_per_worker, QUERY_HEADS, HEAD_SIZE)
    )
    query_lin_grad = (
        unturn_query(query_turn_grad)[0]
        .reshape(tokens_per_worker, QUERY_HEADS * HEAD_SIZE)
        .astype(brain_float_half)
    )
    key_lin_grad = (
        unrotate_key(
            local_key_value[:, : KEY_VALUE_HEADS * HEAD_SIZE].reshape(
                tokens_per_worker, KEY_VALUE_HEADS, HEAD_SIZE
            )
        )[0]
        .reshape(tokens_per_worker, KEY_VALUE_HEADS * HEAD_SIZE)
        .astype(brain_float_half)
    )
    value_linear_gradient = local_key_value[:, KEY_VALUE_HEADS * HEAD_SIZE :].astype(
        brain_float_half
    )
    mamba_grad_w = jnp.einsum(
        "ti,td->id", ymix_low, branch_grad, preferred_element_type=single_float
    )
    grad_ymix = jnp.einsum(
        "td,id->ti", branch_grad, mamba_out_full, preferred_element_type=single_float
    )
    grad_mixed, grad_zgate, mixer_gain_grad = gate_back(grad_ymix)
    zgate_low = grad_zgate.astype(brain_float_half)
    (
        grad_in_mix,
        grad_write_mix,
        grad_read,
        grad_step_mix,
        grad_rate_mix,
        skip_grad,
        grad_state_in,
    ) = mix_back(grad_mixed.reshape(tokens_per_worker, HS, HP))
    _, state_later = carried_in((carry_decay, grad_state_in), CTX, chain_combine, chain_identity)
    decay_grad = jnp.sum(state_in * state_later, axis=(1, 2))
    grad_in_stats, grad_write_stats, grad_step_stats, grad_rate_stats = stats_back(
        (state_later, decay_grad)
    )
    grad_conv = jnp.concatenate(
        [
            (grad_in_mix + grad_in_stats).reshape(tokens_per_worker, dssm),
            grad_write_mix + grad_write_stats,
            grad_read,
        ],
        axis=1,
    )
    grad_widened, conv_weight_grad, conv_bias_grad = conv_back(grad_conv)
    rim_grad = shifted(grad_widened[:taps].astype(jnp.bfloat16), CTX, -1).astype(jnp.float32)
    conv_lin_grad = (
        grad_widened[taps:].at[tokens_per_worker - taps :].add(rim_grad).astype(brain_float_half)
    )
    step_lin_grad, step_bias_grad, log_decay_grad = step_back(
        (grad_step_mix + grad_step_stats, grad_rate_mix + grad_rate_stats)
    )
    step_lin_low = step_lin_grad.astype(brain_float_half)
    query_grad_w = jnp.einsum(
        "td,ti->di", normalized_input, query_lin_grad, preferred_element_type=single_float
    )
    key_grad_w = jnp.einsum(
        "td,ti->di", normalized_input, key_lin_grad, preferred_element_type=single_float
    )
    value_grad_w = jnp.einsum(
        "td,ti->di", normalized_input, value_linear_gradient, preferred_element_type=single_float
    )
    zgate_grad_w = jnp.einsum(
        "td,ti->di", normalized_input, zgate_low, preferred_element_type=single_float
    )
    conv_in_grad_w = jnp.einsum(
        "td,ti->di", normalized_input, conv_lin_grad, preferred_element_type=single_float
    )
    step_grad_w = jnp.einsum(
        "td,ti->di", normalized_input, step_lin_low, preferred_element_type=single_float
    )
    grad_normed = (
        jnp.einsum("ti,di->td", query_lin_grad, query_full, preferred_element_type=single_float)
        + jnp.einsum("ti,di->td", key_lin_grad, complete_key, preferred_element_type=single_float)
        + jnp.einsum(
            "ti,di->td", value_linear_gradient, value_full, preferred_element_type=single_float
        )
        + jnp.einsum("ti,di->td", zgate_low, mixer_gate_full, preferred_element_type=single_float)
        + jnp.einsum("ti,di->td", conv_lin_grad, conv_in_full, preferred_element_type=single_float)
        + jnp.einsum("ti,di->td", step_lin_low, step_full, preferred_element_type=single_float)
    )
    grad_resid_norm, norm_gain_grad = norm_one_back(grad_normed)
    input_grad = (grad_mid + grad_resid_norm).astype(brain_float_half)
    mixer_sums = (
        lax.psum_scatter(norm_gain_grad, (CTX, FSDP), scatter_dimension=0, tiled=True),
        lax.psum_scatter(query_grad_w, (CTX, FSDP), scatter_dimension=0, tiled=True),
        lax.psum_scatter(key_grad_w, (CTX, FSDP), scatter_dimension=0, tiled=True),
        lax.psum_scatter(value_grad_w, (CTX, FSDP), scatter_dimension=0, tiled=True),
        lax.psum_scatter(attn_out_grad_w, (CTX, FSDP), scatter_dimension=0, tiled=True),
        lax.psum_scatter(zgate_grad_w, (CTX, FSDP), scatter_dimension=0, tiled=True),
        lax.psum_scatter(conv_in_grad_w, (CTX, FSDP), scatter_dimension=0, tiled=True),
        lax.psum_scatter(step_grad_w, (CTX, FSDP), scatter_dimension=0, tiled=True),
        lax.psum_scatter(conv_weight_grad, (CTX, FSDP), scatter_dimension=1, tiled=True),
        lax.psum_scatter(conv_bias_grad, (CTX, FSDP), scatter_dimension=0, tiled=True),
        lax.psum_scatter(mixer_gain_grad, (CTX, FSDP), scatter_dimension=0, tiled=True),
        lax.psum_scatter(mamba_grad_w, (CTX, FSDP), scatter_dimension=0, tiled=True),
    )
    summed_grads = tuple(mixer_sums) + tuple(ffn_sums)
    step_bias_sum, log_decay_sum, skip_sum = lax.psum(
        (step_bias_grad, log_decay_grad, skip_grad), (CTX, FSDP)
    )
    return (
        block_out[None],
        input_grad[None],
        summed_grads[0],
        summed_grads[1],
        summed_grads[2],
        summed_grads[3],
        summed_grads[4],
        summed_grads[5],
        summed_grads[6],
        summed_grads[7],
        summed_grads[8],
        summed_grads[9],
        step_bias_sum,
        log_decay_sum,
        skip_sum,
        summed_grads[10],
        summed_grads[11],
        summed_grads[12],
        summed_grads[13],
        summed_grads[14],
        summed_grads[15],
    )


BF = jnp.bfloat16
F32 = jnp.float32


def dotf(left, right, dims):
    return lax.dot_general(left, right, (dims, ((), ())), preferred_element_type=F32)


def mm(left, right):
    return dotf(left, right, ((left.ndim - 1,), (0,)))


def mm_nt(left, right):
    return dotf(left, right, ((1,), (1,)))


def mm_tn(left, right):
    return dotf(left, right, ((0,), (0,)))


def gather_tokens(block):
    return lax.all_gather(block, CTX, axis=0, tiled=True)


def scatter_tokens(partial_sum):
    return lax.psum_scatter(
        partial_sum.astype(BF), CTX, scatter_dimension=0, tiled=True
    ).astype(F32)


def gather_rows(shard):
    return lax.all_gather(shard, FSDP, axis=0, tiled=False)


def scatter_rows(partial_sum):
    return lax.psum_scatter(partial_sum.astype(BF), FSDP, scatter_dimension=0, tiled=False)


def swap_columns(packed):
    return lax.all_to_all(packed, CTX, split_axis=0, concat_axis=0, tiled=True)


def same_document(documents):
    places = jnp.arange(documents.shape[0])
    return (documents[:, None] == documents[None, :]) & (places[:, None] >= places[None, :])


def ssm_terms(step, rate, documents, chunks):
    length, heads = step.shape
    rows = length // chunks
    step_c = step.reshape(chunks, rows, heads).transpose(0, 2, 1)
    docs_c = documents.reshape(chunks, rows)
    prior = jnp.concatenate([jnp.full((1,), -1, docs_c.dtype), docs_c[:-1, -1]])
    last = docs_c[:, -1]
    level = jnp.cumsum(step_c * rate[None, :, None], axis=2)
    visible = jax.vmap(same_document)(docs_c)[:, None]
    spread = level[:, :, :, None] - level[:, :, None, :]
    pair = jnp.where(visible, jnp.exp(jnp.where(visible, spread, 0.0)), 0.0)
    entry = jnp.where((docs_c == prior[:, None])[:, None], jnp.exp(level), 0.0)
    tail = jnp.where((docs_c == last[:, None])[:, None], jnp.exp(level[:, :, -1:] - level), 0.0)
    carry = jnp.exp(level[:, :, -1]) * (last == prior).astype(F32)[:, None]
    return step_c, pair, entry, tail, carry


def ssm_forward(xin, write, read, terms, skip):
    step_c, pair, entry, tail, carry = terms
    chunks, heads, rows = step_c.shape
    x_c = xin.reshape(chunks, rows, heads, HP)
    write_c = write.reshape(chunks, rows, STATE)
    read_c = read.reshape(chunks, rows, STATE)
    gram = jnp.einsum("ktn,kun->ktu", read_c, write_c, preferred_element_type=F32)
    mixing = (pair * gram[:, None] * step_c[:, :, None, :]).astype(BF)
    inner = jnp.einsum("khtu,kuhp->kthp", mixing, x_c, preferred_element_type=F32)
    weight = (tail * step_c).transpose(0, 2, 1)
    weighted = (x_c.astype(F32) * weight[..., None]).astype(BF)
    local = jnp.einsum("kthp,ktn->khpn", weighted, write_c, preferred_element_type=F32)
    state = jnp.zeros_like(local[0])
    entering = []
    for k in range(chunks):
        entering.append(state)
        state = carry[k][:, None, None] * state + local[k]
    entering = jnp.stack(entering)
    reached = jnp.einsum(
        "ktn,khpn->kthp", read_c, entering.astype(BF), preferred_element_type=F32
    )
    y = (
        inner
        + reached * entry.transpose(0, 2, 1)[..., None]
        + skip[None, None, :, None] * x_c.astype(F32)
    )
    return y.reshape(chunks * rows, heads * HP), (gram, mixing, entering, reached)


def ssm_backward(grad, xin, write, read, terms, skip, rate, saved):
    step_c, pair, entry, tail, carry = terms
    gram, mixing, entering, reached = saved
    chunks, heads, rows = step_c.shape
    x_c = xin.reshape(chunks, rows, heads, HP)
    x_f = x_c.astype(F32)
    write_c = write.reshape(chunks, rows, STATE)
    read_c = read.reshape(chunks, rows, STATE)
    g = grad.reshape(chunks, rows, heads, HP)
    g_low = g.astype(BF)
    skip_grad = jnp.sum(g * x_f, axis=(0, 1, 3))
    gx = skip[None, None, :, None] * g
    gx = gx + jnp.einsum("khtu,kthp->kuhp", mixing, g_low, preferred_element_type=F32)
    g_mixing = jnp.einsum("kthp,kuhp->khtu", g_low, x_c, preferred_element_type=F32)
    masked = g_mixing * pair
    g_gram = jnp.sum(masked * step_c[:, :, None, :], axis=1).astype(BF)
    both = masked * gram[:, None]
    column = jnp.sum(both, axis=2)
    row = jnp.sum(both * step_c[:, :, None, :], axis=3)
    g_level = row - step_c * column
    g_step = column
    entry_t = entry.transpose(0, 2, 1)[..., None]
    g_entry = jnp.sum(g * reached, axis=3).transpose(0, 2, 1)
    g_level = g_level + g_entry * entry
    g_reached = (g * entry_t).astype(BF)
    g_read = jnp.einsum("ktu,kun->ktn", g_gram, write_c, preferred_element_type=F32)
    g_write = jnp.einsum("ktu,ktn->kun", g_gram, read_c, preferred_element_type=F32)
    g_read = g_read + jnp.einsum(
        "kthp,khpn->ktn", g_reached, entering.astype(BF), preferred_element_type=F32
    )
    g_enter = jnp.einsum("kthp,ktn->khpn", g_reached, read_c, preferred_element_type=F32)
    state = jnp.zeros_like(g_enter[0])
    leaving = [None] * chunks
    for k in reversed(range(chunks)):
        leaving[k] = state
        state = carry[k][:, None, None] * state + g_enter[k]
    leaving = jnp.stack(leaving)
    g_carry = jnp.sum(entering * leaving, axis=(2, 3))
    leaving_low = leaving.astype(BF)
    weight = tail * step_c
    weight_t = weight.transpose(0, 2, 1)[..., None]
    seen = jnp.einsum("ktn,khpn->kthp", write_c, leaving_low, preferred_element_type=F32)
    gx = gx + weight_t * seen
    g_weight = jnp.sum(x_f * seen, axis=3).transpose(0, 2, 1)
    weighted = (x_f * weight_t).astype(BF)
    g_write = g_write + jnp.einsum(
        "kthp,khpn->ktn", weighted, leaving_low, preferred_element_type=F32
    )
    moved = g_weight * weight
    g_step = g_step + g_weight * tail
    g_level = g_level - moved
    end = jnp.sum(moved, axis=2) + g_carry * carry
    g_level = g_level.at[:, :, -1].add(end)
    g_la = jnp.flip(jnp.cumsum(jnp.flip(g_level, 2), axis=2), 2)
    g_step = g_step + g_la * rate[None, :, None]
    rate_grad = jnp.sum(g_la * step_c, axis=(0, 2))
    length = chunks * rows
    return (
        gx.reshape(length, heads * HP),
        g_write.reshape(length, STATE),
        g_read.reshape(length, STATE),
        g_step.transpose(0, 2, 1).reshape(length, heads),
        rate_grad,
        skip_grad,
    )


def head_parallel(
    hidden_in,
    out_grad,
    doc_ids,
    norm_gain,
    query_weight,
    key_matrix,
    value_matrix,
    attn_out_weight,
    mixer_gate_weight,
    conv_in_weight,
    step_weight,
    conv_weight,
    conv_bias,
    step_bias,
    log_decay,
    skip_gain,
    mixer_gain,
    mamba_out_weight,
    ffn_gain,
    gate_weight,
    up_weight,
    down_weight,
):
    ctx = lax.axis_size(CTX)
    seqs = lax.axis_size(FSDP)
    me = lax.axis_index(CTX)
    mine = lax.axis_index(FSDP)
    tokens, width = hidden_in.shape[1:]
    length = ctx * tokens
    krows = query_weight.shape[0]
    dssm = HS * HP
    heads = HS // ctx
    inner = heads * HP
    bc = 2 * STATE // ctx
    ff = gate_weight.shape[1] // ctx
    head = HEAD_SIZE * QUERY_HEADS // ctx
    taps = CONV - 1
    step_pad = 128 - bc % 128

    small = jnp.concatenate(
        [
            norm_gain,
            ffn_gain,
            mixer_gain,
            conv_bias,
            conv_weight.reshape(-1),
            doc_ids[0].astype(BF),
        ]
    )
    small = lax.all_gather(small, (CTX, FSDP), axis=0, tiled=False)
    cuts = []
    at = 0
    for n in (norm_gain.size, ffn_gain.size, mixer_gain.size, conv_bias.size, conv_weight.size, tokens):
        cuts.append(small[:, at : at + n])
        at += n
    gain_one = cuts[0].reshape(-1).astype(F32)
    gain_two = cuts[1].reshape(-1).astype(F32)
    gain_mix = lax.dynamic_slice_in_dim(cuts[2].reshape(-1), me * inner, inner).astype(F32)
    bias_all = cuts[3].reshape(-1)
    taps_all = cuts[4].reshape(ctx * seqs, CONV, -1).transpose(1, 0, 2).reshape(CONV, -1)
    documents = lax.dynamic_index_in_dim(
        cuts[5].reshape(ctx, seqs, tokens), mine, 1, False
    ).reshape(length).astype(jnp.int32)

    def own_channels(full):
        return jnp.concatenate(
            [
                lax.dynamic_slice_in_dim(full, me * inner, inner, full.ndim - 1),
                lax.dynamic_slice_in_dim(full, dssm + me * bc, bc, full.ndim - 1),
            ],
            axis=-1,
        )

    conv_taps = own_channels(taps_all).astype(F32)
    conv_shift = own_channels(bias_all).astype(F32)
    bias_own = lax.dynamic_slice_in_dim(step_bias, me * heads, heads)
    decay_own = lax.dynamic_slice_in_dim(log_decay, me * heads, heads)
    skip_own = lax.dynamic_slice_in_dim(skip_gain, me * heads, heads)

    def by_column(weight, n):
        return weight.reshape(krows, ctx, n).transpose(1, 0, 2)

    kv_repeat = ctx // KEY_VALUE_HEADS
    conv_pack = jnp.concatenate(
        [
            by_column(conv_in_weight[:, :dssm], inner),
            by_column(conv_in_weight[:, dssm:], bc),
            jnp.pad(by_column(step_weight, heads), ((0, 0), (0, 0), (0, step_pad - heads))),
        ],
        axis=2,
    )
    rest_pack = jnp.concatenate(
        [
            by_column(query_weight, head),
            jnp.repeat(
                key_matrix.reshape(krows, KEY_VALUE_HEADS, HEAD_SIZE).transpose(1, 0, 2),
                kv_repeat,
                axis=0,
            ),
            jnp.repeat(
                value_matrix.reshape(krows, KEY_VALUE_HEADS, HEAD_SIZE).transpose(1, 0, 2),
                kv_repeat,
                axis=0,
            ),
            by_column(mixer_gate_weight, inner),
        ],
        axis=2,
    )
    ffn_pack = jnp.concatenate([by_column(gate_weight, ff), by_column(up_weight, ff)], axis=2)
    conv_cols = conv_pack.shape[2]
    rest_cols = rest_pack.shape[2]
    mixer_pack = swap_columns(jnp.concatenate([conv_pack, rest_pack], axis=2))
    conv_in_own = gather_rows(mixer_pack[:, :, :conv_cols]).reshape(width, conv_cols)
    rest_own = gather_rows(mixer_pack[:, :, conv_cols:]).reshape(width, rest_cols)
    attn_out_own = gather_rows(attn_out_weight).reshape(head, width)
    mamba_out_own = gather_rows(mamba_out_weight).reshape(inner, width)
    ffn_own = gather_rows(swap_columns(ffn_pack)).reshape(width, 2 * ff)
    down_own = gather_rows(down_weight).reshape(ff, width)

    def to_shards(x):
        return x.reshape(-1, ctx, seqs, krows).transpose(0, 2, 1, 3).reshape(-1, width)

    def from_shards(x):
        return x.reshape(-1, seqs, ctx, krows).transpose(0, 2, 1, 3).reshape(-1, width)

    resid = hidden_in[0].astype(F32)
    scale_one = lax.rsqrt(jnp.mean(resid * resid, axis=-1, keepdims=True) + EPSILON)
    normed = gather_tokens(to_shards((resid * scale_one * gain_one).astype(BF)))
    conv_all = mm(normed, conv_in_own)
    rest_all = mm(normed, rest_own)
    conv_lin = conv_all[:, : inner + bc].astype(BF).astype(F32)
    step_lin = conv_all[:, inner + bc : inner + bc + heads]
    q_lin = rest_all[:, :head]
    k_lin = rest_all[:, head : head + HEAD_SIZE]
    value = rest_all[:, head + HEAD_SIZE : head + 2 * HEAD_SIZE].astype(BF)
    zgate = rest_all[:, head + 2 * HEAD_SIZE :]

    widened = jnp.concatenate([jnp.zeros((taps, inner + bc), F32), conv_lin], axis=0)
    widened_docs = jnp.concatenate([jnp.full((taps,), -1, jnp.int32), documents])
    conv_act, conv_back = jax.vjp(
        partial(conv_part, widened_docs=widened_docs, documents=documents),
        widened,
        conv_taps,
        conv_shift,
    )
    conv_act = conv_act.astype(BF)
    shared = lax.all_gather(conv_act[:, inner:], CTX, axis=0, tiled=False)
    shared = shared.transpose(1, 0, 2).reshape(length, 2 * STATE)
    write, read = shared[:, :STATE], shared[:, STATE:]
    xin = conv_act[:, :inner]

    places = jnp.arange(length).astype(F32)
    query_turned, unturn = jax.vjp(
        partial(rotate, places=places), q_lin.reshape(length, head // HEAD_SIZE, HEAD_SIZE)
    )
    key_turned, unturn_key = jax.vjp(
        partial(rotate, places=places), k_lin.reshape(length, 1, HEAD_SIZE)
    )
    query = query_turned.astype(BF)
    key = key_turned.astype(BF)[:, 0]
    visible = same_document(documents)
    scores = jnp.einsum("thd,ud->htu", query, key, preferred_element_type=F32) * HEAD_SIZE**-0.5
    scores = jnp.where(visible[None], scores, NEGATIVE_FLOOR)
    weights = jnp.where(
        visible[None], jnp.exp(scores - jnp.max(scores, axis=-1, keepdims=True)), 0.0
    )
    probs = weights / jnp.sum(weights, axis=-1, keepdims=True)
    probs_low = probs.astype(BF)
    attn_mix = jnp.einsum("htu,ud->thd", probs_low, value, preferred_element_type=F32)
    attn_low = attn_mix.reshape(length, head).astype(BF)

    step_size, step_back = jax.vjp(
        lambda lin, bias: jax.nn.softplus(lin + bias[None, :]), step_lin, bias_own
    )
    rate = -jnp.exp(decay_own)
    terms = ssm_terms(step_size, rate, documents, ctx)
    y, saved = ssm_forward(xin, write, read, terms, skip_own)
    gated, gated_back = jax.vjp(lambda a, z: a * jax.nn.silu(z), y, zgate)
    mean_square = lax.psum(jnp.sum(gated * gated, axis=-1), CTX) / dssm
    scale_mix = lax.rsqrt(mean_square + EPSILON)[:, None]
    ymix = (gated * scale_mix * gain_mix).astype(BF)

    branch = scatter_tokens(mm(attn_low, attn_out_own) + mm(ymix, mamba_out_own))
    mid = resid + branch
    scale_two = lax.rsqrt(jnp.mean(mid * mid, axis=-1, keepdims=True) + EPSILON)
    normed_two = gather_tokens(to_shards((mid * scale_two * gain_two).astype(BF)))
    grad_all = gather_tokens(out_grad[0])

    gate_up = mm(normed_two, ffn_own)
    gate_lin, up_lin = gate_up[:, :ff], gate_up[:, ff:]
    sigmoid_gate = jax.nn.sigmoid(gate_lin)
    silu_gate = gate_lin * sigmoid_gate
    hidden = (silu_gate * up_lin).astype(BF)
    grad_hidden = mm_nt(grad_all, down_own)
    grad_gate = (
        grad_hidden * up_lin * (sigmoid_gate + silu_gate * (1.0 - sigmoid_gate))
    ).astype(BF)
    grad_up = (grad_hidden * silu_gate).astype(BF)
    grad_gu = jnp.concatenate([grad_gate, grad_up], axis=1)
    grad_n2 = from_shards(scatter_tokens(mm_nt(grad_gu, ffn_own)))
    block_out = (mid + scatter_tokens(mm(hidden, down_own))).astype(BF)
    down_grad = scatter_rows(mm_tn(hidden, grad_all).reshape(seqs, ff // seqs, width)).astype(F32)
    ffn_grad = scatter_rows(mm_tn(normed_two, grad_gu).reshape(seqs, ctx, krows, 2 * ff))
    ffn_grad = swap_columns(ffn_grad).astype(F32)

    turned = grad_n2 * gain_two
    hat_two = mid * scale_two
    ffn_gain_grad = jnp.sum(grad_n2 * hat_two, axis=0)
    grad_mid = out_grad[0].astype(F32) + scale_two * (
        turned - hat_two * jnp.mean(turned * hat_two, axis=-1, keepdims=True)
    )
    branch_grad = gather_tokens(grad_mid.astype(BF))

    attn_out_grad = scatter_rows(mm_tn(attn_low, branch_grad).reshape(seqs, -1, width)).astype(F32)
    mamba_out_grad = scatter_rows(mm_tn(ymix, branch_grad).reshape(seqs, -1, width)).astype(F32)
    grad_attn = mm_nt(branch_grad, attn_out_own).astype(BF).reshape(length, -1, HEAD_SIZE)
    grad_ymix = mm_nt(branch_grad, mamba_out_own)

    grad_prob = jnp.einsum("thd,ud->htu", grad_attn, value, preferred_element_type=F32)
    delta = jnp.sum(probs * grad_prob, axis=-1, keepdims=True)
    grad_score = (probs * (grad_prob - delta)).astype(BF)
    grad_query = (
        jnp.einsum("htu,ud->thd", grad_score, key, preferred_element_type=F32) * HEAD_SIZE**-0.5
    )
    grad_key = (
        jnp.einsum("htu,thd->ud", grad_score, query, preferred_element_type=F32) * HEAD_SIZE**-0.5
    )
    grad_value = jnp.einsum("htu,thd->ud", probs_low, grad_attn, preferred_element_type=F32)
    grad_q_lin = unturn(grad_query)[0].reshape(length, head).astype(BF)
    grad_k_lin = unturn_key(grad_key[:, None])[0].reshape(length, HEAD_SIZE).astype(BF)

    hat = gated * scale_mix
    turned_mix = grad_ymix * gain_mix
    mixer_gain_grad = jnp.sum(grad_ymix * hat, axis=0)
    along = lax.psum(jnp.sum(turned_mix * hat, axis=-1), CTX)[:, None] / dssm
    grad_gated = scale_mix * (turned_mix - hat * along)
    grad_y, grad_zgate = gated_back(grad_gated)

    grad_xin, grad_write, grad_read, grad_step, grad_rate, skip_grad = ssm_backward(
        grad_y, xin, write, read, terms, skip_own, rate, saved
    )
    grad_shared = jnp.concatenate([grad_write, grad_read], axis=1).astype(BF)
    grad_shared = lax.psum_scatter(
        grad_shared.reshape(length, ctx, bc).transpose(1, 0, 2), CTX, scatter_dimension=0
    ).astype(F32)
    grad_widened, taps_grad, shift_grad = conv_back(
        jnp.concatenate([grad_xin, grad_shared], axis=1)
    )
    grad_step_lin, step_bias_grad = step_back(grad_step)
    log_decay_grad = grad_rate * rate
    grad_conv = jnp.concatenate(
        [
            grad_widened[taps:].astype(BF),
            jnp.pad(grad_step_lin.astype(BF), ((0, 0), (0, step_pad - heads))),
        ],
        axis=1,
    )
    grad_rest = jnp.concatenate(
        [grad_q_lin, grad_k_lin, grad_value.astype(BF), grad_zgate.astype(BF)], axis=1
    )

    grad_normed = from_shards(
        scatter_tokens(mm_nt(grad_conv, conv_in_own) + mm_nt(grad_rest, rest_own))
    )
    conv_grad = scatter_rows(mm_tn(normed, grad_conv).reshape(seqs, ctx, krows, conv_cols))
    rest_grad = scatter_rows(mm_tn(normed, grad_rest).reshape(seqs, ctx, krows, rest_cols))
    mixer_grad = swap_columns(jnp.concatenate([conv_grad, rest_grad], axis=2)).astype(F32)
    turned_one = grad_normed * gain_one
    hat_one = resid * scale_one
    norm_gain_grad = jnp.sum(grad_normed * hat_one, axis=0)
    input_grad = (
        grad_mid
        + scale_one
        * (turned_one - hat_one * jnp.mean(turned_one * hat_one, axis=-1, keepdims=True))
    ).astype(BF)

    def spread_out(own, at, total):
        return lax.dynamic_update_slice_in_dim(
            jnp.zeros(own.shape[:-1] + (total,), F32), own, at, own.ndim - 1
        )

    def spread_channels(own):
        full = spread_out(own[..., :inner], me * inner, dssm + 2 * STATE)
        return lax.dynamic_update_slice_in_dim(full, own[..., inner:], dssm + me * bc, own.ndim - 1)

    parts = (
        norm_gain_grad,
        ffn_gain_grad,
        spread_out(mixer_gain_grad, me * inner, dssm),
        spread_channels(shift_grad),
        spread_channels(taps_grad).reshape(-1),
        spread_out(step_bias_grad, me * heads, HS),
        spread_out(log_decay_grad, me * heads, HS),
        spread_out(skip_grad, me * heads, HS),
    )
    sums = lax.psum(jnp.concatenate(parts), (CTX, FSDP))
    pieces = []
    at = 0
    for part in parts:
        pieces.append(sums[at : at + part.size])
        at += part.size
    place = me * seqs + mine

    def own_piece(full):
        n = full.shape[-1] // (ctx * seqs)
        return lax.dynamic_slice_in_dim(full, place * n, n, full.ndim - 1)

    def by_row(packed, start, n):
        return packed[:, :, start : start + n].transpose(1, 0, 2).reshape(krows, -1)

    base = conv_cols
    key_grad = mixer_grad[:, :, base + head : base + head + HEAD_SIZE]
    value_grad = mixer_grad[:, :, base + head + HEAD_SIZE : base + head + 2 * HEAD_SIZE]

    def over_queries(packed):
        return (
            packed.reshape(KEY_VALUE_HEADS, kv_repeat, krows, HEAD_SIZE)
            .sum(axis=1)
            .transpose(1, 0, 2)
            .reshape(krows, -1)
        )

    return (
        block_out[None],
        input_grad[None],
        own_piece(pieces[0]),
        by_row(mixer_grad, base, head),
        over_queries(key_grad),
        over_queries(value_grad),
        attn_out_grad,
        by_row(mixer_grad, base + head + 2 * HEAD_SIZE, inner),
        jnp.concatenate(
            [by_row(mixer_grad, 0, inner), by_row(mixer_grad, inner, bc)], axis=1
        ),
        by_row(mixer_grad, inner + bc, heads),
        own_piece(pieces[4].reshape(CONV, -1)),
        own_piece(pieces[3]),
        pieces[5],
        pieces[6],
        pieces[7],
        own_piece(pieces[2]),
        mamba_out_grad,
        own_piece(pieces[1]),
        by_row(ffn_grad, 0, ff),
        by_row(ffn_grad, ff, ff),
        down_grad,
    )


def solution(mesh):
    placed = (
        P(FSDP, CTX, None),
        P(FSDP, CTX, None),
        P(FSDP, CTX),
        P((CTX, FSDP)),
        P((CTX, FSDP), None),
        P((CTX, FSDP), None),
        P((CTX, FSDP), None),
        P((CTX, FSDP), None),
        P((CTX, FSDP), None),
        P((CTX, FSDP), None),
        P((CTX, FSDP), None),
        P(None, (CTX, FSDP)),
        P((CTX, FSDP)),
        P(),
        P(),
        P(),
        P((CTX, FSDP)),
        P((CTX, FSDP), None),
        P((CTX, FSDP)),
        P((CTX, FSDP), None),
        P((CTX, FSDP), None),
        P((CTX, FSDP), None),
    )
    ctx = mesh.shape[CTX]
    whole_heads = QUERY_HEADS % ctx == 0 and HS % ctx == 0 and ctx % KEY_VALUE_HEADS == 0
    return jax.shard_map(
        head_parallel if whole_heads else on_device,
        mesh=mesh,
        in_specs=placed,
        out_specs=(
            P(FSDP, CTX, None),
            P(FSDP, CTX, None),
            P((CTX, FSDP)),
            P((CTX, FSDP), None),
            P((CTX, FSDP), None),
            P((CTX, FSDP), None),
            P((CTX, FSDP), None),
            P((CTX, FSDP), None),
            P((CTX, FSDP), None),
            P((CTX, FSDP), None),
            P(None, (CTX, FSDP)),
            P((CTX, FSDP)),
            P(),
            P(),
            P(),
            P((CTX, FSDP)),
            P((CTX, FSDP), None),
            P((CTX, FSDP)),
            P((CTX, FSDP), None),
            P((CTX, FSDP), None),
            P((CTX, FSDP), None),
        ),
        check_vma=False,
    )
```

```python
from functools import partial
import itertools
import math

import jax
import jax.numpy as jnp
from jax import lax
from jax.experimental import pallas as pl
from jax.experimental.pallas import tpu as pltpu
from jax.sharding import PartitionSpec as P

CTX = "ctx"
FSDP = "fsdp"
QUERY_HEADS = 8
KEY_VALUE_HEADS = 2
HEAD_SIZE = 128
HS = 48
HP = 64
STATE = 256
CONV = 4


EPSILON = 1e-05
ROPE_BASE = 100000000000.0
NEGATIVE_FLOOR = -1e30
HIGHEST = lax.Precision.HIGHEST


def shifted(value, axis, steps):
    count = lax.axis_size(axis)
    leading, last = (max(0, -steps), min(count, count - steps))
    return lax.ppermute(value, axis, [(source, source + steps) for source in range(leading, last)])


def prefix(shard, axis, combine, identity):
    devices, position = (lax.axis_size(axis), lax.axis_index(axis))
    everything = jax.tree.map(
        lambda part, kind: lax.all_gather(part.astype(kind), axis),
        shard,
        (jnp.bfloat16, jnp.bfloat16),
    )
    start = jax.tree.map(
        lambda part, zero: jnp.broadcast_to(jnp.asarray(zero, part.dtype), part.shape),
        shard,
        identity,
    )

    def step(k, before):
        reached = k < position
        new = combine(
            before, jax.tree.map(lambda part, own: part[k].astype(own.dtype), everything, shard)
        )
        return jax.tree.map(lambda a, b: jnp.where(reached, a, b), new, before)

    return lax.fori_loop(0, devices, step, start)


def carried_in(shard, axis, join, neutral):
    count = lax.axis_size(axis)
    place = lax.axis_index(axis)
    ahead = count - 1 - place
    gathered = jax.tree.map(
        lambda a, kind: lax.all_gather(a.astype(kind), axis),
        shard,
        jax.tree.map(lambda a: jnp.bfloat16 if a.dtype == jnp.float32 else a.dtype, shard),
    )
    state = jax.tree.map(lambda a, e: jnp.zeros_like(a) + jnp.asarray(e, a.dtype), shard, neutral)

    def one(step, state):
        source = count - 1 - step
        return join(
            state,
            jax.tree.map(
                lambda a, own: lax.dynamic_index_in_dim(a, source, 0, False).astype(own.dtype),
                gathered,
                shard,
            ),
        )

    return lax.fori_loop(0, ahead, one, state)


def rms_scale(values, gain):
    return values * lax.rsqrt(jnp.mean(values * values, axis=-1, keepdims=True) + EPSILON) * gain


def rotate(values, places):
    half_size = values.shape[-1] // 2
    freqs = ROPE_BASE ** (-jnp.arange(half_size).astype(jnp.float32) / half_size)
    angles = places[:, None] * freqs[None, :]
    cosine = jnp.cos(angles)[:, None, :]
    sine = jnp.sin(angles)[:, None, :]
    first = values[..., :half_size]
    second = values[..., half_size:]
    return jnp.concatenate(
        [first * cosine - second * sine, second * cosine + first * sine], axis=-1
    )


def conv_part(widened, taps_weight, bias, widened_docs, documents):
    row_length_total = documents.shape[0]
    total = bias[None, :]
    for tap_index in range(taps_weight.shape[0]):
        same_doc = (widened_docs[tap_index : tap_index + row_length_total] == documents)[:, None]
        total = total + jnp.where(
            same_doc,
            widened[tap_index : tap_index + row_length_total] * taps_weight[tap_index][None, :],
            0.0,
        )
    return jax.nn.silu(total)


def step_part(step_lin, step_bias, log_decay):
    return (jax.nn.softplus(step_lin + step_bias), -jnp.exp(log_decay))


def block_stats(mixer_in, write_proj, step_size, decay_rate, documents, prior_doc):
    decay_log = jnp.cumsum(step_size * decay_rate[None, :], axis=0)
    last_doc = documents[-1]
    tail_weight = (
        jnp.where(
            (documents == last_doc)[:, None], jnp.exp(decay_log[-1][None, :] - decay_log), 0.0
        )
        * step_size
    )
    state_loc = jnp.einsum(
        "thp,tn->hpn", mixer_in * tail_weight[:, :, None], write_proj, precision=HIGHEST
    )
    carry_decay = jnp.exp(decay_log[-1]) * (last_doc == prior_doc).astype(jnp.float32)
    return (state_loc, carry_decay)


def block_mix(
    mixer_in,
    write_proj,
    read_proj,
    step_size,
    decay_rate,
    skip_gain,
    state_in,
    documents,
    prior_doc,
):
    decay_log = jnp.cumsum(step_size * decay_rate[None, :], axis=0)
    positions = jnp.arange(documents.shape[0])
    visible = (documents[:, None] == documents[None, :]) & (
        positions[:, None] >= positions[None, :]
    )
    spread = decay_log.T[:, :, None] - decay_log.T[:, None, :]
    decay_pair = jnp.where(visible[None], jnp.exp(jnp.where(visible[None], spread, 0.0)), 0.0)
    gram = jnp.dot(read_proj, write_proj.T, precision=HIGHEST)
    mixing = decay_pair * gram[None] * step_size.T[:, None, :]
    inner = jnp.einsum("htu,uhp->thp", mixing, mixer_in, precision=HIGHEST)
    entry = jnp.where((documents == prior_doc)[:, None], jnp.exp(decay_log), 0.0)
    carried = jnp.einsum("tn,hpn->thp", read_proj, state_in, precision=HIGHEST) * entry[:, :, None]
    return inner + carried + skip_gain[None, :, None] * mixer_in


def gated_norm(flat_mixed, mixer_gate, gain):
    return rms_scale(flat_mixed * jax.nn.silu(mixer_gate), gain)


def chain_combine(earlier, later):
    decay_early, state_early = earlier
    decay_late, state_late = later
    return (decay_early * decay_late, decay_late[:, None, None] * state_early + state_late)


def piece_scores(piece, start, query_group, query_docs, query_places):
    key_segment, value_segment, docs_piece = piece
    segment_rows = key_segment.shape[0]
    heads_of_key = key_segment.reshape(segment_rows, KEY_VALUE_HEADS, HEAD_SIZE).transpose(1, 0, 2)
    heads_of_value = value_segment.reshape(segment_rows, KEY_VALUE_HEADS, HEAD_SIZE).transpose(
        1, 0, 2
    )
    key_places = (start + jnp.arange(segment_rows)).astype(jnp.float32)
    visible = (docs_piece.astype(jnp.float32)[None, :] == query_docs[:, None]) & (
        key_places[None, :] <= query_places[:, None]
    )
    scores = jnp.einsum(
        "gqd,gkd->gqk", query_group, heads_of_key, preferred_element_type=jnp.float32
    ) * HEAD_SIZE ** (-0.5)
    return (heads_of_key, heads_of_value, visible, jnp.where(visible[None], scores, NEGATIVE_FLOOR))


def fold_local(step_fn, whole, start_carry):
    row_length_total = whole[0].shape[0]
    tile_block = math.gcd(row_length_total, 512)

    def advance(block_index, carry):
        start = block_index * tile_block
        piece = tuple((lax.dynamic_slice_in_dim(member, start, tile_block, 0) for member in whole))
        return step_fn(carry, piece, start)

    return lax.fori_loop(0, row_length_total // tile_block, advance, start_carry)


def on_device(
    hidden_in,
    out_grad,
    doc_ids,
    norm_gain,
    query_weight,
    key_matrix,
    value_matrix,
    attn_out_weight,
    mixer_gate_weight,
    conv_in_weight,
    step_weight,
    conv_weight,
    conv_bias,
    step_bias,
    log_decay,
    skip_gain,
    mixer_gain,
    mamba_out_weight,
    ffn_gain,
    gate_weight,
    up_weight,
    down_weight,
):
    single_float = jnp.float32
    brain_float_half = jnp.bfloat16
    (
        norm_full,
        query_full,
        complete_key,
        value_full,
        attn_out_full,
        mixer_gate_full,
        conv_in_full,
        step_full,
        conv_full,
        conv_bias_full,
        mixer_gain_full,
        mamba_out_full,
    ) = (
        lax.all_gather(norm_gain, (CTX, FSDP), axis=0, tiled=True),
        lax.all_gather(query_weight, (CTX, FSDP), axis=0, tiled=True),
        lax.all_gather(key_matrix, (CTX, FSDP), axis=0, tiled=True),
        lax.all_gather(value_matrix, (CTX, FSDP), axis=0, tiled=True),
        lax.all_gather(attn_out_weight, (CTX, FSDP), axis=0, tiled=True),
        lax.all_gather(mixer_gate_weight, (CTX, FSDP), axis=0, tiled=True),
        lax.all_gather(conv_in_weight, (CTX, FSDP), axis=0, tiled=True),
        lax.all_gather(step_weight, (CTX, FSDP), axis=0, tiled=True),
        lax.all_gather(conv_weight, (CTX, FSDP), axis=1, tiled=True),
        lax.all_gather(conv_bias, (CTX, FSDP), axis=0, tiled=True),
        lax.all_gather(mixer_gain, (CTX, FSDP), axis=0, tiled=True),
        lax.all_gather(mamba_out_weight, (CTX, FSDP), axis=0, tiled=True),
    )
    tokens_per_worker = hidden_in.shape[1]
    head_cluster = QUERY_HEADS // KEY_VALUE_HEADS
    dssm = HS * HP
    taps = CONV - 1
    resid = hidden_in[0].astype(single_float)
    documents = doc_ids[0]
    places = (lax.axis_index(CTX) * tokens_per_worker + jnp.arange(tokens_per_worker)).astype(
        single_float
    )
    norm_one, norm_one_back = jax.vjp(rms_scale, resid, norm_full.astype(single_float))
    normalized_input = norm_one.astype(brain_float_half)
    query_lin = jnp.dot(normalized_input, query_full, preferred_element_type=single_float).reshape(
        tokens_per_worker, QUERY_HEADS, HEAD_SIZE
    )
    key_linear = jnp.dot(
        normalized_input, complete_key, preferred_element_type=single_float
    ).reshape(tokens_per_worker, KEY_VALUE_HEADS, HEAD_SIZE)
    query_turned, unturn_query = jax.vjp(partial(rotate, places=places), query_lin)
    rotated_key, unrotate_key = jax.vjp(partial(rotate, places=places), key_linear)
    rotated_query = query_turned.astype(brain_float_half)
    flattened_key = rotated_key.astype(brain_float_half).reshape(
        tokens_per_worker, KEY_VALUE_HEADS * HEAD_SIZE
    )
    value_lowered = jnp.dot(
        normalized_input, value_full, preferred_element_type=single_float
    ).astype(brain_float_half)
    docs_low = documents.astype(brain_float_half)
    query_group = (
        rotated_query.reshape(tokens_per_worker, KEY_VALUE_HEADS, head_cluster, HEAD_SIZE)
        .transpose(1, 2, 0, 3)
        .reshape(KEY_VALUE_HEADS, head_cluster * tokens_per_worker, HEAD_SIZE)
    )
    query_places = jnp.tile(places, head_cluster)
    query_docs = jnp.tile(documents.astype(single_float), head_cluster)

    def attend_piece(carry, piece, start):
        previous_maximum, total_old, summed_old = carry
        heads_of_key, heads_of_value, visible, scores = piece_scores(
            piece, start, query_group, query_docs, query_places
        )
        peak_new = jnp.maximum(previous_maximum, jnp.max(scores, axis=-1))
        weights = jnp.where(visible[None], jnp.exp(scores - peak_new[:, :, None]), 0.0)
        factor = jnp.exp(previous_maximum - peak_new)
        total_new = total_old * factor + jnp.sum(weights, axis=-1)
        summed_new = summed_old * factor[:, :, None] + jnp.einsum(
            "gqk,gkd->gqd",
            weights.astype(brain_float_half),
            heads_of_value,
            preferred_element_type=single_float,
        )
        return (peak_new, total_new, summed_new)

    rows_of_query = head_cluster * tokens_per_worker
    start_forward = (
        jnp.full((KEY_VALUE_HEADS, rows_of_query), NEGATIVE_FLOOR, single_float),
        jnp.zeros((KEY_VALUE_HEADS, rows_of_query), single_float),
        jnp.zeros((KEY_VALUE_HEADS, rows_of_query, HEAD_SIZE), single_float),
    )
    kv_whole = (
        lax.all_gather(flattened_key, CTX, axis=0, tiled=True),
        lax.all_gather(value_lowered, CTX, axis=0, tiled=True),
        lax.all_gather(docs_low, CTX, axis=0, tiled=True),
    )
    peak, total, summed = fold_local(attend_piece, kv_whole, start_forward)
    attention_cluster = summed / total[:, :, None]
    log_total = peak + jnp.log(total)
    attn_low = (
        attention_cluster.reshape(KEY_VALUE_HEADS, head_cluster, tokens_per_worker, HEAD_SIZE)
        .transpose(2, 0, 1, 3)
        .reshape(tokens_per_worker, QUERY_HEADS * HEAD_SIZE)
        .astype(brain_float_half)
    )
    attn_out = jnp.dot(attn_low, attn_out_full, preferred_element_type=single_float)
    mixer_gate = jnp.dot(normalized_input, mixer_gate_full, preferred_element_type=single_float)
    conv_lin = jnp.dot(normalized_input, conv_in_full, preferred_element_type=single_float).astype(
        brain_float_half
    )
    step_lin = jnp.dot(normalized_input, step_full, preferred_element_type=single_float)
    rim_rows, rim_docs = shifted(
        (conv_lin[tokens_per_worker - taps :], docs_low[tokens_per_worker - taps :]), CTX, 1
    )
    widened = jnp.concatenate([rim_rows, conv_lin], axis=0).astype(single_float)
    widened_docs = jnp.concatenate([rim_docs.astype(jnp.int32), documents])
    prior_doc = widened_docs[taps - 1]
    conv_act, conv_back = jax.vjp(
        partial(conv_part, widened_docs=widened_docs, documents=documents),
        widened,
        conv_full.astype(single_float),
        conv_bias_full.astype(single_float),
    )
    conv_vals = conv_act.astype(brain_float_half).astype(single_float)
    mixer_in = conv_vals[:, :dssm].reshape(tokens_per_worker, HS, HP)
    write_proj = conv_vals[:, dssm : dssm + STATE]
    read_proj = conv_vals[:, dssm + STATE :]
    (step_size, decay_rate), step_back = jax.vjp(step_part, step_lin, step_bias, log_decay)
    (state_loc, carry_decay), stats_back = jax.vjp(
        partial(block_stats, documents=documents, prior_doc=prior_doc),
        mixer_in,
        write_proj,
        step_size,
        decay_rate,
    )
    chain_identity = (jnp.ones_like(carry_decay), jnp.zeros_like(state_loc))
    _, state_in = prefix((carry_decay, state_loc), CTX, chain_combine, chain_identity)
    mixed, mix_back = jax.vjp(
        partial(block_mix, documents=documents, prior_doc=prior_doc),
        mixer_in,
        write_proj,
        read_proj,
        step_size,
        decay_rate,
        skip_gain,
        state_in,
    )
    ymix_vals, gate_back = jax.vjp(
        gated_norm,
        mixed.reshape(tokens_per_worker, dssm),
        mixer_gate,
        mixer_gain_full.astype(single_float),
    )
    ymix_low = ymix_vals.astype(brain_float_half)
    mamba_out = jnp.dot(ymix_low, mamba_out_full, preferred_element_type=single_float)
    ffn_gain_full, gate_full, up_full, down_full = (
        lax.all_gather(ffn_gain, (CTX, FSDP), axis=0, tiled=True),
        lax.all_gather(gate_weight, (CTX, FSDP), axis=0, tiled=True),
        lax.all_gather(up_weight, (CTX, FSDP), axis=0, tiled=True),
        lax.all_gather(down_weight, (CTX, FSDP), axis=0, tiled=True),
    )
    mid = resid + attn_out + mamba_out
    norm_two, norm_two_back = jax.vjp(rms_scale, mid, ffn_gain_full.astype(single_float))
    normed_two = norm_two.astype(brain_float_half)
    gate_lin = jnp.dot(normed_two, gate_full, preferred_element_type=single_float)
    up_lin = jnp.dot(normed_two, up_full, preferred_element_type=single_float)
    sigmoid_gate = jax.nn.sigmoid(gate_lin)
    silu_gate = gate_lin * sigmoid_gate
    hidden = (silu_gate * up_lin).astype(brain_float_half)
    block_out = (mid + jnp.dot(hidden, down_full, preferred_element_type=single_float)).astype(
        brain_float_half
    )
    grad_out = out_grad[0]
    down_grad_w = jnp.einsum("tf,td->fd", hidden, grad_out, preferred_element_type=single_float)
    grad_hidden = jnp.einsum("td,fd->tf", grad_out, down_full, preferred_element_type=single_float)
    grad_gate = (grad_hidden * up_lin * (sigmoid_gate + silu_gate * (1.0 - sigmoid_gate))).astype(
        brain_float_half
    )
    grad_up = (grad_hidden * silu_gate).astype(brain_float_half)
    gate_grad_w = jnp.einsum(
        "td,tf->df", normed_two, grad_gate, preferred_element_type=single_float
    )
    up_grad_w = jnp.einsum("td,tf->df", normed_two, grad_up, preferred_element_type=single_float)
    grad_normed_two = jnp.einsum(
        "tf,df->td", grad_gate, gate_full, preferred_element_type=single_float
    ) + jnp.einsum("tf,df->td", grad_up, up_full, preferred_element_type=single_float)
    grad_mid_norm, ffn_gain_grad = norm_two_back(grad_normed_two)
    grad_mid = grad_out.astype(single_float) + grad_mid_norm
    ffn_sums = (
        lax.psum_scatter(ffn_gain_grad, (CTX, FSDP), scatter_dimension=0, tiled=True),
        lax.psum_scatter(gate_grad_w, (CTX, FSDP), scatter_dimension=0, tiled=True),
        lax.psum_scatter(up_grad_w, (CTX, FSDP), scatter_dimension=0, tiled=True),
        lax.psum_scatter(down_grad_w, (CTX, FSDP), scatter_dimension=0, tiled=True),
    )
    branch_grad = grad_mid.astype(brain_float_half)
    attn_out_grad_w = jnp.einsum(
        "ti,td->id", attn_low, branch_grad, preferred_element_type=single_float
    )
    attention_gradient = jnp.einsum(
        "td,id->ti", branch_grad, attn_out_full, preferred_element_type=single_float
    ).astype(brain_float_half)
    grad_group = (
        attention_gradient.reshape(tokens_per_worker, KEY_VALUE_HEADS, head_cluster, HEAD_SIZE)
        .transpose(1, 2, 0, 3)
        .reshape(KEY_VALUE_HEADS, rows_of_query, HEAD_SIZE)
    )
    row_delta = jnp.sum(grad_group.astype(single_float) * attention_cluster, axis=-1)

    def attend_back(carry, piece, start):
        query_acc, kv_grad = carry
        heads_of_key, heads_of_value, visible, scores = piece_scores(
            piece, start, query_group, query_docs, query_places
        )
        segment_rows = heads_of_key.shape[1]
        probs = jnp.where(visible[None], jnp.exp(scores - log_total[:, :, None]), 0.0)
        prob_grad = jnp.einsum(
            "gqd,gkd->gqk", grad_group, heads_of_value, preferred_element_type=single_float
        )
        score_grad = (probs * (prob_grad - row_delta[:, :, None])).astype(brain_float_half)
        query_acc = query_acc + jnp.einsum(
            "gqk,gkd->gqd", score_grad, heads_of_key, preferred_element_type=single_float
        )
        key_portion = jnp.einsum(
            "gqk,gqd->kgd", score_grad, query_group, preferred_element_type=single_float
        ) * HEAD_SIZE ** (-0.5)
        value_portion = jnp.einsum(
            "gqk,gqd->kgd",
            probs.astype(brain_float_half),
            grad_group,
            preferred_element_type=single_float,
        )
        term = jnp.concatenate(
            [
                key_portion.reshape(segment_rows, KEY_VALUE_HEADS * HEAD_SIZE),
                value_portion.reshape(segment_rows, KEY_VALUE_HEADS * HEAD_SIZE),
            ],
            axis=1,
        )
        current = lax.dynamic_slice_in_dim(kv_grad, start, segment_rows, 0)
        kv_grad = lax.dynamic_update_slice_in_dim(kv_grad, current + term, start, 0)
        return (query_acc, kv_grad)

    start_back = (
        jnp.zeros((KEY_VALUE_HEADS, rows_of_query, HEAD_SIZE), single_float),
        jnp.zeros(
            (tokens_per_worker * lax.axis_size(CTX), 2 * KEY_VALUE_HEADS * HEAD_SIZE),
            single_float,
        ),
    )
    query_acc, kv_grad = fold_local(attend_back, kv_whole, start_back)
    local_key_value = lax.psum_scatter(
        kv_grad.astype(jnp.bfloat16), CTX, scatter_dimension=0, tiled=True
    ).astype(jnp.float32)
    query_turn_grad = (
        (query_acc * HEAD_SIZE ** (-0.5))
        .reshape(KEY_VALUE_HEADS, head_cluster, tokens_per_worker, HEAD_SIZE)
        .transpose(2, 0, 1, 3)
        .reshape(tokens_per_worker, QUERY_HEADS, HEAD_SIZE)
    )
    query_lin_grad = (
        unturn_query(query_turn_grad)[0]
        .reshape(tokens_per_worker, QUERY_HEADS * HEAD_SIZE)
        .astype(brain_float_half)
    )
    key_lin_grad = (
        unrotate_key(
            local_key_value[:, : KEY_VALUE_HEADS * HEAD_SIZE].reshape(
                tokens_per_worker, KEY_VALUE_HEADS, HEAD_SIZE
            )
        )[0]
        .reshape(tokens_per_worker, KEY_VALUE_HEADS * HEAD_SIZE)
        .astype(brain_float_half)
    )
    value_linear_gradient = local_key_value[:, KEY_VALUE_HEADS * HEAD_SIZE :].astype(
        brain_float_half
    )
    mamba_grad_w = jnp.einsum(
        "ti,td->id", ymix_low, branch_grad, preferred_element_type=single_float
    )
    grad_ymix = jnp.einsum(
        "td,id->ti", branch_grad, mamba_out_full, preferred_element_type=single_float
    )
    grad_mixed, grad_zgate, mixer_gain_grad = gate_back(grad_ymix)
    zgate_low = grad_zgate.astype(brain_float_half)
    (
        grad_in_mix,
        grad_write_mix,
        grad_read,
        grad_step_mix,
        grad_rate_mix,
        skip_grad,
        grad_state_in,
    ) = mix_back(grad_mixed.reshape(tokens_per_worker, HS, HP))
    _, state_later = carried_in((carry_decay, grad_state_in), CTX, chain_combine, chain_identity)
    decay_grad = jnp.sum(state_in * state_later, axis=(1, 2))
    grad_in_stats, grad_write_stats, grad_step_stats, grad_rate_stats = stats_back(
        (state_later, decay_grad)
    )
    grad_conv = jnp.concatenate(
        [
            (grad_in_mix + grad_in_stats).reshape(tokens_per_worker, dssm),
            grad_write_mix + grad_write_stats,
            grad_read,
        ],
        axis=1,
    )
    grad_widened, conv_weight_grad, conv_bias_grad = conv_back(grad_conv)
    rim_grad = shifted(grad_widened[:taps].astype(jnp.bfloat16), CTX, -1).astype(jnp.float32)
    conv_lin_grad = (
        grad_widened[taps:].at[tokens_per_worker - taps :].add(rim_grad).astype(brain_float_half)
    )
    step_lin_grad, step_bias_grad, log_decay_grad = step_back(
        (grad_step_mix + grad_step_stats, grad_rate_mix + grad_rate_stats)
    )
    step_lin_low = step_lin_grad.astype(brain_float_half)
    query_grad_w = jnp.einsum(
        "td,ti->di", normalized_input, query_lin_grad, preferred_element_type=single_float
    )
    key_grad_w = jnp.einsum(
        "td,ti->di", normalized_input, key_lin_grad, preferred_element_type=single_float
    )
    value_grad_w = jnp.einsum(
        "td,ti->di", normalized_input, value_linear_gradient, preferred_element_type=single_float
    )
    zgate_grad_w = jnp.einsum(
        "td,ti->di", normalized_input, zgate_low, preferred_element_type=single_float
    )
    conv_in_grad_w = jnp.einsum(
        "td,ti->di", normalized_input, conv_lin_grad, preferred_element_type=single_float
    )
    step_grad_w = jnp.einsum(
        "td,ti->di", normalized_input, step_lin_low, preferred_element_type=single_float
    )
    grad_normed = (
        jnp.einsum("ti,di->td", query_lin_grad, query_full, preferred_element_type=single_float)
        + jnp.einsum("ti,di->td", key_lin_grad, complete_key, preferred_element_type=single_float)
        + jnp.einsum(
            "ti,di->td", value_linear_gradient, value_full, preferred_element_type=single_float
        )
        + jnp.einsum("ti,di->td", zgate_low, mixer_gate_full, preferred_element_type=single_float)
        + jnp.einsum("ti,di->td", conv_lin_grad, conv_in_full, preferred_element_type=single_float)
        + jnp.einsum("ti,di->td", step_lin_low, step_full, preferred_element_type=single_float)
    )
    grad_resid_norm, norm_gain_grad = norm_one_back(grad_normed)
    input_grad = (grad_mid + grad_resid_norm).astype(brain_float_half)
    mixer_sums = (
        lax.psum_scatter(norm_gain_grad, (CTX, FSDP), scatter_dimension=0, tiled=True),
        lax.psum_scatter(query_grad_w, (CTX, FSDP), scatter_dimension=0, tiled=True),
        lax.psum_scatter(key_grad_w, (CTX, FSDP), scatter_dimension=0, tiled=True),
        lax.psum_scatter(value_grad_w, (CTX, FSDP), scatter_dimension=0, tiled=True),
        lax.psum_scatter(attn_out_grad_w, (CTX, FSDP), scatter_dimension=0, tiled=True),
        lax.psum_scatter(zgate_grad_w, (CTX, FSDP), scatter_dimension=0, tiled=True),
        lax.psum_scatter(conv_in_grad_w, (CTX, FSDP), scatter_dimension=0, tiled=True),
        lax.psum_scatter(step_grad_w, (CTX, FSDP), scatter_dimension=0, tiled=True),
        lax.psum_scatter(conv_weight_grad, (CTX, FSDP), scatter_dimension=1, tiled=True),
        lax.psum_scatter(conv_bias_grad, (CTX, FSDP), scatter_dimension=0, tiled=True),
        lax.psum_scatter(mixer_gain_grad, (CTX, FSDP), scatter_dimension=0, tiled=True),
        lax.psum_scatter(mamba_grad_w, (CTX, FSDP), scatter_dimension=0, tiled=True),
    )
    summed_grads = tuple(mixer_sums) + tuple(ffn_sums)
    step_bias_sum, log_decay_sum, skip_sum = lax.psum(
        (step_bias_grad, log_decay_grad, skip_grad), (CTX, FSDP)
    )
    return (
        block_out[None],
        input_grad[None],
        summed_grads[0],
        summed_grads[1],
        summed_grads[2],
        summed_grads[3],
        summed_grads[4],
        summed_grads[5],
        summed_grads[6],
        summed_grads[7],
        summed_grads[8],
        summed_grads[9],
        step_bias_sum,
        log_decay_sum,
        skip_sum,
        summed_grads[10],
        summed_grads[11],
        summed_grads[12],
        summed_grads[13],
        summed_grads[14],
        summed_grads[15],
    )


BF = jnp.bfloat16
F32 = jnp.float32


def dotf(left, right, dims):
    return lax.dot_general(left, right, (dims, ((), ())), preferred_element_type=F32)


def mm(left, right):
    return dotf(left, right, ((left.ndim - 1,), (0,)))


def mm_nt(left, right):
    return dotf(left, right, ((1,), (1,)))


def mm_tn(left, right):
    return dotf(left, right, ((0,), (0,)))


MESH = pl.DeviceIdType.MESH
PLANE = 8


def plane():
    me = lax.axis_index(CTX)
    sibling = me + 1 - 2 * (me % 2)
    by_x = me + 2 - 4 * ((me // 2) % 2)
    by_y = me + 4 - 8 * (me // 4)
    return me, sibling, by_x, by_y


def greet(peers):
    barrier = pltpu.get_barrier_semaphore()
    for axis, other in peers:
        pl.semaphore_signal(barrier, inc=1, device_id={axis: other}, device_id_type=MESH)
    pl.semaphore_wait(barrier, len(peers))


def remote(src, dst, send_sem, recv_sem, axis, to):
    return pltpu.make_async_remote_copy(
        src_ref=src,
        dst_ref=dst,
        send_sem=send_sem,
        recv_sem=recv_sem,
        device_id={axis: to},
        device_id_type=MESH,
    )


def gather_kernel(pieces, x_ref, o_ref, own_sem, send_sem, recv_sem):
    rows = x_ref.shape[0]
    n = rows // pieces
    half = pieces // 2
    me, sibling, by_x, by_y = plane()
    across = by_x + by_y - me
    greet([(CTX, sibling), (CTX, by_x), (CTX, by_y)])
    keep = pltpu.make_async_copy(x_ref, o_ref.at[pl.ds(me * rows, rows)], own_sem)
    keep.start()
    started = []

    def at(block, piece):
        return o_ref.at[pl.ds(block * rows + piece * n, n)]

    def go(src, block, piece, kind, to, slot):
        copy = remote(
            src, at(block, piece), send_sem.at[slot, piece], recv_sem.at[kind, piece], CTX, to
        )
        copy.start()
        started.append(copy)

    def arrived(block, piece, kind):
        here = at(block, piece)
        remote(here, here, send_sem.at[0, piece], recv_sem.at[kind, piece], CTX, sibling).wait_recv()

    for i in range(pieces):
        a, b = i, pieces - 1 - i
        go(x_ref.at[pl.ds(a * n, n)], me, a, 1, by_x, 1)
        go(x_ref.at[pl.ds(b * n, n)], me, b, 2, by_y, 2)
    for i in range(pieces):
        go(x_ref.at[pl.ds(i * n, n)], me, i, 0, sibling, 0)
    for i in range(pieces):
        a, b = i, pieces - 1 - i
        arrived(by_x, a, 1)
        if i < half:
            go(at(by_x, a), by_x, a, 5, by_y, 5)
        go(at(by_x, a), by_x, a, 3, sibling, 3)
        arrived(by_y, b, 2)
        if i < half:
            go(at(by_y, b), by_y, b, 5, by_x, 5)
        go(at(by_y, b), by_y, b, 4, sibling, 4)
    for i in range(half):
        for p in (i, pieces - 1 - i):
            arrived(across, p, 5)
            go(at(across, p), across, p, 6, sibling, 6)
    shift = sibling - me
    for p in range(pieces):
        arrived(sibling, p, 0)
        arrived(by_x + shift, p, 3)
        arrived(by_y + shift, p, 4)
        arrived(across + shift, p, 6)
    for copy in started:
        copy.wait_send()
    keep.wait()


def gather_tokens(block, ids, pieces=4):
    rows, cols = block.shape
    return pl.pallas_call(
        partial(gather_kernel, pieces),
        out_shape=jax.ShapeDtypeStruct((PLANE * rows, cols), block.dtype),
        in_specs=[pl.BlockSpec(memory_space=pl.ANY)],
        out_specs=pl.BlockSpec(memory_space=pl.ANY),
        scratch_shapes=[
            pltpu.SemaphoreType.DMA,
            pltpu.SemaphoreType.DMA((7, pieces)),
            pltpu.SemaphoreType.DMA((7, pieces)),
        ],
        cost_estimate=lasting(22 if cols > 1024 else 8),
        compiler_params=pltpu.CompilerParams(collective_id=next(ids), has_side_effects=True),
    )(block)


def scatter_kernel(p_ref, o_ref, own, got, out, rx, ry, dx, dy, own_sem, send_sem, recv_sem):
    rows = o_ref.shape[0]
    h = rows // 2
    me, sibling, by_x, by_y = plane()
    across = by_x + by_y - me
    shift = sibling - me
    greet([(CTX, sibling), (CTX, by_x), (CTX, by_y)])
    top, low = pl.ds(0, h), pl.ds(h, h)
    loads, sends = [], []
    for k, block in enumerate((across, by_x, by_y, me)):
        for j in range(2):
            copy = remote(
                p_ref.at[pl.ds((block + shift) * rows + j * h, h)],
                got.at[k, pl.ds(j * h, h)],
                send_sem.at[k * 2 + j],
                recv_sem.at[k * 2 + j],
                CTX,
                sibling,
            )
            copy.start()
            sends.append(copy)
            load = pltpu.make_async_copy(
                p_ref.at[pl.ds(block * rows + j * h, h)],
                own.at[k, pl.ds(j * h, h)],
                own_sem.at[k * 2 + j],
            )
            load.start()
            loads.append(load)

    def pair(k, j):
        sends[k * 2 + j].wait_recv()
        loads[k * 2 + j].wait()
        part = pl.ds(j * h, h)
        return own[k, part].astype(F32) + got[k, part].astype(F32)

    def go(src, dst, slot, to):
        copy = remote(src, dst, send_sem.at[slot], recv_sem.at[slot], CTX, to)
        copy.start()
        sends.append(copy)
        return copy

    out[0, top] = pair(0, 0).astype(out.dtype)
    across_x = go(out.at[0, top], dx, 8, by_x)
    out[0, low] = pair(0, 1).astype(out.dtype)
    across_y = go(out.at[0, low], dy, 9, by_y)
    out[1, top] = pair(1, 0).astype(out.dtype)
    x_top = go(out.at[1, top], rx.at[top], 10, by_x)
    out[2, low] = pair(2, 1).astype(out.dtype)
    y_low = go(out.at[2, low], ry.at[low], 11, by_y)
    across_y.wait_recv()
    out[1, low] = (pair(1, 1) + dy[...].astype(F32)).astype(out.dtype)
    x_low = go(out.at[1, low], rx.at[low], 12, by_x)
    across_x.wait_recv()
    out[2, top] = (pair(2, 0) + dx[...].astype(F32)).astype(out.dtype)
    y_top = go(out.at[2, top], ry.at[top], 13, by_y)
    first, second = pair(3, 0), pair(3, 1)
    x_top.wait_recv()
    y_top.wait_recv()
    o_ref[top] = first + rx[top].astype(F32) + ry[top].astype(F32)
    x_low.wait_recv()
    y_low.wait_recv()
    o_ref[low] = second + rx[low].astype(F32) + ry[low].astype(F32)
    for copy in sends:
        copy.wait_send()


def scatter_tokens(partial_sum, ids):
    rows, cols = partial_sum.shape[0] // PLANE, partial_sum.shape[1]

    def room(*shape):
        return pltpu.VMEM(shape, BF)

    return pl.pallas_call(
        scatter_kernel,
        out_shape=jax.ShapeDtypeStruct((rows, cols), F32),
        in_specs=[pl.BlockSpec(memory_space=pl.ANY)],
        out_specs=pl.BlockSpec(memory_space=pltpu.VMEM),
        scratch_shapes=[
            room(4, rows, cols),
            room(4, rows, cols),
            room(3, rows, cols),
            room(rows, cols),
            room(rows, cols),
            room(rows // 2, cols),
            room(rows // 2, cols),
            pltpu.SemaphoreType.DMA((8,)),
            pltpu.SemaphoreType.DMA((14,)),
            pltpu.SemaphoreType.DMA((14,)),
        ],
        cost_estimate=lasting(22 if cols > 1024 else 8),
        compiler_params=pltpu.CompilerParams(
            collective_id=next(ids), has_side_effects=True, vmem_limit_bytes=40 * 2**20
        ),
    )(partial_sum.astype(BF))


def row_sum_kernel(x_ref, o_ref, got, send_sem, recv_sem):
    me = lax.axis_index(CTX)
    greet([(CTX, (me + j) % PLANE) for j in range(1, PLANE)])
    copies = []
    for j in range(1, PLANE):
        copy = remote(
            x_ref, got.at[j - 1], send_sem.at[j - 1], recv_sem.at[j - 1], CTX, (me + j) % PLANE
        )
        copy.start()
        copies.append(copy)
    total = x_ref[...]
    for j, copy in enumerate(copies):
        copy.wait_recv()
        total = total + got[j]
    o_ref[...] = total
    for copy in copies:
        copy.wait_send()


def row_sum(rows, ids):
    tile = rows.reshape(8, -1)
    total = pl.pallas_call(
        row_sum_kernel,
        out_shape=jax.ShapeDtypeStruct(tile.shape, F32),
        in_specs=[pl.BlockSpec(memory_space=pltpu.VMEM)],
        out_specs=pl.BlockSpec(memory_space=pltpu.VMEM),
        scratch_shapes=[
            pltpu.VMEM((PLANE - 1,) + tile.shape, F32),
            pltpu.SemaphoreType.DMA((PLANE - 1,)),
            pltpu.SemaphoreType.DMA((PLANE - 1,)),
        ],
        cost_estimate=lasting(5),
        compiler_params=pltpu.CompilerParams(collective_id=next(ids), has_side_effects=True),
    )(tile)
    return total.reshape(rows.shape)


def small_gather_kernel(seqs, x_ref, o_ref, own_sem, send_sem, recv_sem):
    me, mine = lax.axis_index(CTX), lax.axis_index(FSDP)
    others = [(FSDP, (mine + j) % seqs) for j in range(1, seqs)]
    greet(others + [(CTX, (me + j) % PLANE) for j in range(1, PLANE)])
    keep = pltpu.make_async_copy(x_ref, o_ref.at[me, mine], own_sem)
    keep.start()
    copies = []
    for j, (_, other) in enumerate(others):
        copy = remote(x_ref, o_ref.at[me, mine], send_sem.at[j], recv_sem.at[j], FSDP, other)
        copy.start()
        copies.append(copy)
    keep.wait()
    for copy in copies:
        copy.wait_recv()
    for j in range(1, PLANE):
        k = seqs + j
        copy = remote(
            o_ref.at[me], o_ref.at[me], send_sem.at[k], recv_sem.at[k], CTX, (me + j) % PLANE
        )
        copy.start()
        copies.append(copy)
    for copy in copies[seqs - 1 :]:
        copy.wait_recv()
    for copy in copies:
        copy.wait_send()


def small_gather(tile, seqs, ids):
    return pl.pallas_call(
        partial(small_gather_kernel, seqs),
        out_shape=jax.ShapeDtypeStruct((PLANE, seqs) + tile.shape, tile.dtype),
        in_specs=[pl.BlockSpec(memory_space=pltpu.VMEM)],
        out_specs=pl.BlockSpec(memory_space=pltpu.VMEM),
        scratch_shapes=[
            pltpu.SemaphoreType.DMA,
            pltpu.SemaphoreType.DMA((PLANE + seqs,)),
            pltpu.SemaphoreType.DMA((PLANE + seqs,)),
        ],
        cost_estimate=lasting(8),
        compiler_params=pltpu.CompilerParams(collective_id=next(ids), has_side_effects=True),
    )(tile)


def small_scatter_kernel(seqs, x_ref, o_ref, got, total, late, send_sem, recv_sem):
    me, mine = lax.axis_index(CTX), lax.axis_index(FSDP)
    others = [(FSDP, (mine + j) % seqs) for j in range(1, seqs)]
    greet(others + [(CTX, (me + j) % PLANE) for j in range(1, PLANE)])
    copies = []
    for j in range(1, PLANE):
        to = (me + j) % PLANE
        copy = remote(x_ref.at[to], got.at[j - 1], send_sem.at[j], recv_sem.at[j], CTX, to)
        copy.start()
        copies.append(copy)
    acc = x_ref[me]
    for j, copy in enumerate(copies):
        copy.wait_recv()
        acc = acc + got[j]
    total[...] = acc
    first = len(copies)
    for j, (_, other) in enumerate(others):
        k = PLANE + j
        copy = remote(total.at[other], late.at[j], send_sem.at[k], recv_sem.at[k], FSDP, other)
        copy.start()
        copies.append(copy)
    out = total[mine]
    for j, copy in enumerate(copies[first:]):
        copy.wait_recv()
        out = out + late[j]
    o_ref[...] = out
    for copy in copies:
        copy.wait_send()


def small_scatter(tiles, ids):
    seqs = tiles.shape[1]
    tile = tiles.shape[2:]
    return pl.pallas_call(
        partial(small_scatter_kernel, seqs),
        out_shape=jax.ShapeDtypeStruct(tile, F32),
        in_specs=[pl.BlockSpec(memory_space=pltpu.VMEM)],
        out_specs=pl.BlockSpec(memory_space=pltpu.VMEM),
        scratch_shapes=[
            pltpu.VMEM((PLANE - 1,) + tiles.shape[1:], F32),
            pltpu.VMEM(tiles.shape[1:], F32),
            pltpu.VMEM((seqs - 1,) + tile, F32),
            pltpu.SemaphoreType.DMA((PLANE + seqs,)),
            pltpu.SemaphoreType.DMA((PLANE + seqs,)),
        ],
        cost_estimate=lasting(8),
        compiler_params=pltpu.CompilerParams(collective_id=next(ids), has_side_effects=True),
    )(tiles)


def gather_rows(shard):
    return lax.all_gather(shard, FSDP, axis=0, tiled=False)


def scatter_rows(partial_sum):
    return lax.psum_scatter(partial_sum.astype(BF), FSDP, scatter_dimension=0, tiled=False)


def after(value, *earlier):
    return lax.optimization_barrier((value, *earlier))[0]


def lasting(us):
    return pl.CostEstimate(flops=int(us * 1e9), bytes_accessed=int(us * 3e6), transcendentals=0)


def swap_columns(packed):
    return lax.all_to_all(packed, CTX, split_axis=0, concat_axis=0, tiled=True)


def same_document(documents):
    places = jnp.arange(documents.shape[0])
    return (documents[:, None] == documents[None, :]) & (places[:, None] >= places[None, :])


def ssm_terms(step, rate, documents, chunks):
    length, heads = step.shape
    rows = length // chunks
    step_c = step.reshape(chunks, rows, heads).transpose(0, 2, 1)
    docs_c = documents.reshape(chunks, rows)
    prior = jnp.concatenate([jnp.full((1,), -1, docs_c.dtype), docs_c[:-1, -1]])
    last = docs_c[:, -1]
    level = jnp.cumsum(step_c * rate[None, :, None], axis=2)
    visible = jax.vmap(same_document)(docs_c)[:, None]
    spread = level[:, :, :, None] - level[:, :, None, :]
    pair = jnp.where(visible, jnp.exp(jnp.where(visible, spread, 0.0)), 0.0)
    entry = jnp.where((docs_c == prior[:, None])[:, None], jnp.exp(level), 0.0)
    tail = jnp.where((docs_c == last[:, None])[:, None], jnp.exp(level[:, :, -1:] - level), 0.0)
    carry = jnp.exp(level[:, :, -1]) * (last == prior).astype(F32)[:, None]
    return step_c, pair, entry, tail, carry


def ssm_forward(xin, write, read, terms, skip):
    step_c, pair, entry, tail, carry = terms
    chunks, heads, rows = step_c.shape
    x_c = xin.reshape(chunks, rows, heads, HP)
    write_c = write.reshape(chunks, rows, STATE)
    read_c = read.reshape(chunks, rows, STATE)
    gram = jnp.einsum("ktn,kun->ktu", read_c, write_c, preferred_element_type=F32)
    mixing = (pair * gram[:, None] * step_c[:, :, None, :]).astype(BF)
    inner = jnp.einsum("khtu,kuhp->kthp", mixing, x_c, preferred_element_type=F32)
    weight = (tail * step_c).transpose(0, 2, 1)
    weighted = (x_c.astype(F32) * weight[..., None]).astype(BF)
    local = jnp.einsum("kthp,ktn->khpn", weighted, write_c, preferred_element_type=F32)
    state = jnp.zeros_like(local[0])
    entering = []
    for k in range(chunks):
        entering.append(state)
        state = carry[k][:, None, None] * state + local[k]
    entering = jnp.stack(entering)
    reached = jnp.einsum(
        "ktn,khpn->kthp", read_c, entering.astype(BF), preferred_element_type=F32
    )
    y = (
        inner
        + reached * entry.transpose(0, 2, 1)[..., None]
        + skip[None, None, :, None] * x_c.astype(F32)
    )
    return y.reshape(chunks * rows, heads * HP), (gram, mixing, entering, reached)


def ssm_backward(grad, xin, write, read, terms, skip, rate, saved):
    step_c, pair, entry, tail, carry = terms
    gram, mixing, entering, reached = saved
    chunks, heads, rows = step_c.shape
    x_c = xin.reshape(chunks, rows, heads, HP)
    x_f = x_c.astype(F32)
    write_c = write.reshape(chunks, rows, STATE)
    read_c = read.reshape(chunks, rows, STATE)
    g = grad.reshape(chunks, rows, heads, HP)
    g_low = g.astype(BF)
    skip_grad = jnp.sum(g * x_f, axis=(0, 1, 3))
    gx = skip[None, None, :, None] * g
    gx = gx + jnp.einsum("khtu,kthp->kuhp", mixing, g_low, preferred_element_type=F32)
    g_mixing = jnp.einsum("kthp,kuhp->khtu", g_low, x_c, preferred_element_type=F32)
    masked = g_mixing * pair
    g_gram = jnp.sum(masked * step_c[:, :, None, :], axis=1).astype(BF)
    both = masked * gram[:, None]
    column = jnp.sum(both, axis=2)
    row = jnp.sum(both * step_c[:, :, None, :], axis=3)
    g_level = row - step_c * column
    g_step = column
    entry_t = entry.transpose(0, 2, 1)[..., None]
    g_entry = jnp.sum(g * reached, axis=3).transpose(0, 2, 1)
    g_level = g_level + g_entry * entry
    g_reached = (g * entry_t).astype(BF)
    g_read = jnp.einsum("ktu,kun->ktn", g_gram, write_c, preferred_element_type=F32)
    g_write = jnp.einsum("ktu,ktn->kun", g_gram, read_c, preferred_element_type=F32)
    g_read = g_read + jnp.einsum(
        "kthp,khpn->ktn", g_reached, entering.astype(BF), preferred_element_type=F32
    )
    g_enter = jnp.einsum("kthp,ktn->khpn", g_reached, read_c, preferred_element_type=F32)
    state = jnp.zeros_like(g_enter[0])
    leaving = [None] * chunks
    for k in reversed(range(chunks)):
        leaving[k] = state
        state = carry[k][:, None, None] * state + g_enter[k]
    leaving = jnp.stack(leaving)
    g_carry = jnp.sum(entering * leaving, axis=(2, 3))
    leaving_low = leaving.astype(BF)
    weight = tail * step_c
    weight_t = weight.transpose(0, 2, 1)[..., None]
    seen = jnp.einsum("ktn,khpn->kthp", write_c, leaving_low, preferred_element_type=F32)
    gx = gx + weight_t * seen
    g_weight = jnp.sum(x_f * seen, axis=3).transpose(0, 2, 1)
    weighted = (x_f * weight_t).astype(BF)
    g_write = g_write + jnp.einsum(
        "kthp,khpn->ktn", weighted, leaving_low, preferred_element_type=F32
    )
    moved = g_weight * weight
    g_step = g_step + g_weight * tail
    g_level = g_level - moved
    end = jnp.sum(moved, axis=2) + g_carry * carry
    g_level = g_level.at[:, :, -1].add(end)
    g_la = jnp.flip(jnp.cumsum(jnp.flip(g_level, 2), axis=2), 2)
    g_step = g_step + g_la * rate[None, :, None]
    rate_grad = jnp.sum(g_la * step_c, axis=(0, 2))
    length = chunks * rows
    return (
        gx.reshape(length, heads * HP),
        g_write.reshape(length, STATE),
        g_read.reshape(length, STATE),
        g_step.transpose(0, 2, 1).reshape(length, heads),
        rate_grad,
        skip_grad,
    )


def head_parallel(
    hidden_in,
    out_grad,
    doc_ids,
    norm_gain,
    query_weight,
    key_matrix,
    value_matrix,
    attn_out_weight,
    mixer_gate_weight,
    conv_in_weight,
    step_weight,
    conv_weight,
    conv_bias,
    step_bias,
    log_decay,
    skip_gain,
    mixer_gain,
    mamba_out_weight,
    ffn_gain,
    gate_weight,
    up_weight,
    down_weight,
):
    ctx = lax.axis_size(CTX)
    seqs = lax.axis_size(FSDP)
    me = lax.axis_index(CTX)
    mine = lax.axis_index(FSDP)
    tokens, width = hidden_in.shape[1:]
    length = ctx * tokens
    krows = query_weight.shape[0]
    dssm = HS * HP
    heads = HS // ctx
    inner = heads * HP
    bc = 2 * STATE // ctx
    ff = gate_weight.shape[1] // ctx
    head = HEAD_SIZE * QUERY_HEADS // ctx
    taps = CONV - 1
    step_pad = 128 - bc % 128

    ids = itertools.count(1)

    small = jnp.concatenate(
        [
            norm_gain,
            ffn_gain,
            mixer_gain,
            conv_bias,
            conv_weight.reshape(-1),
            doc_ids[0].astype(BF),
        ]
    )
    small_size = small.size
    tile_rows = -(-small_size // 2048) * 16
    small = jnp.pad(small, (0, tile_rows * 128 - small_size)).reshape(tile_rows, 128)
    small = small_gather(small, seqs, ids).reshape(ctx * seqs, -1)
    cuts = []
    at = 0
    for n in (norm_gain.size, ffn_gain.size, mixer_gain.size, conv_bias.size, conv_weight.size, tokens):
        cuts.append(small[:, at : at + n])
        at += n
    gain_one = cuts[0].reshape(-1).astype(F32)
    gain_two = cuts[1].reshape(-1).astype(F32)
    gain_mix = lax.dynamic_slice_in_dim(cuts[2].reshape(-1), me * inner, inner).astype(F32)
    bias_all = cuts[3].reshape(-1)
    taps_all = cuts[4].reshape(ctx * seqs, CONV, -1).transpose(1, 0, 2).reshape(CONV, -1)
    documents = lax.dynamic_index_in_dim(
        cuts[5].reshape(ctx, seqs, tokens), mine, 1, False
    ).reshape(length).astype(jnp.int32)

    def own_channels(full):
        return jnp.concatenate(
            [
                lax.dynamic_slice_in_dim(full, me * inner, inner, full.ndim - 1),
                lax.dynamic_slice_in_dim(full, dssm + me * bc, bc, full.ndim - 1),
            ],
            axis=-1,
        )

    conv_taps = own_channels(taps_all).astype(F32)
    conv_shift = own_channels(bias_all).astype(F32)
    bias_own = lax.dynamic_slice_in_dim(step_bias, me * heads, heads)
    decay_own = lax.dynamic_slice_in_dim(log_decay, me * heads, heads)
    skip_own = lax.dynamic_slice_in_dim(skip_gain, me * heads, heads)

    def by_column(weight, n):
        return weight.reshape(krows, ctx, n).transpose(1, 0, 2)

    kv_repeat = ctx // KEY_VALUE_HEADS
    conv_pack = jnp.concatenate(
        [
            by_column(conv_in_weight[:, :dssm], inner),
            by_column(conv_in_weight[:, dssm:], bc),
            jnp.pad(by_column(step_weight, heads), ((0, 0), (0, 0), (0, step_pad - heads))),
        ],
        axis=2,
    )
    rest_pack = jnp.concatenate(
        [
            by_column(query_weight, head),
            jnp.repeat(
                key_matrix.reshape(krows, KEY_VALUE_HEADS, HEAD_SIZE).transpose(1, 0, 2),
                kv_repeat,
                axis=0,
            ),
            jnp.repeat(
                value_matrix.reshape(krows, KEY_VALUE_HEADS, HEAD_SIZE).transpose(1, 0, 2),
                kv_repeat,
                axis=0,
            ),
            by_column(mixer_gate_weight, inner),
        ],
        axis=2,
    )
    ffn_pack = jnp.concatenate([by_column(gate_weight, ff), by_column(up_weight, ff)], axis=2)
    conv_cols = conv_pack.shape[2]
    rest_cols = rest_pack.shape[2]
    mixer_pack = swap_columns(jnp.concatenate([conv_pack, rest_pack], axis=2))
    ffn_pack = swap_columns(after(ffn_pack, mixer_pack))
    conv_in_own = gather_rows(mixer_pack[:, :, :conv_cols])
    rest_own = gather_rows(after(mixer_pack[:, :, conv_cols:], conv_in_own))
    out_own = gather_rows(after(jnp.concatenate([attn_out_weight, mamba_out_weight]), rest_own))
    ffn_own = gather_rows(after(ffn_pack, out_own))
    down_own = gather_rows(after(down_weight, ffn_own)).reshape(ff, width)
    conv_in_own = conv_in_own.reshape(width, conv_cols)
    rest_own = rest_own.reshape(width, rest_cols)
    out_rows = attn_out_weight.shape[0]
    attn_out_own = out_own[:, :out_rows].reshape(head, width)
    mamba_out_own = out_own[:, out_rows:].reshape(inner, width)
    ffn_own = ffn_own.reshape(width, 2 * ff)

    def to_shards(x):
        return x.reshape(-1, ctx, seqs, krows).transpose(0, 2, 1, 3).reshape(-1, width)

    def from_shards(x):
        return x.reshape(-1, seqs, ctx, krows).transpose(0, 2, 1, 3).reshape(-1, width)

    resid = hidden_in[0].astype(F32)
    scale_one = lax.rsqrt(jnp.mean(resid * resid, axis=-1, keepdims=True) + EPSILON)
    normed = gather_tokens(to_shards((resid * scale_one * gain_one).astype(BF)), ids)
    conv_all = mm(normed, conv_in_own)
    rest_all = mm(normed, rest_own)
    conv_lin = conv_all[:, : inner + bc].astype(BF).astype(F32)
    step_lin = conv_all[:, inner + bc : inner + bc + heads]
    q_lin = rest_all[:, :head]
    k_lin = rest_all[:, head : head + HEAD_SIZE]
    value = rest_all[:, head + HEAD_SIZE : head + 2 * HEAD_SIZE].astype(BF)
    zgate = rest_all[:, head + 2 * HEAD_SIZE :]

    widened = jnp.concatenate([jnp.zeros((taps, inner + bc), F32), conv_lin], axis=0)
    widened_docs = jnp.concatenate([jnp.full((taps,), -1, jnp.int32), documents])
    conv_act, conv_back = jax.vjp(
        partial(conv_part, widened_docs=widened_docs, documents=documents),
        widened,
        conv_taps,
        conv_shift,
    )
    conv_act = conv_act.astype(BF)
    shared = gather_tokens(conv_act[:, inner:].T, ids, 2).T
    write, read = shared[:, :STATE], shared[:, STATE:]
    xin = conv_act[:, :inner]

    places = jnp.arange(length).astype(F32)
    query_turned, unturn = jax.vjp(
        partial(rotate, places=places), q_lin.reshape(length, head // HEAD_SIZE, HEAD_SIZE)
    )
    key_turned, unturn_key = jax.vjp(
        partial(rotate, places=places), k_lin.reshape(length, 1, HEAD_SIZE)
    )
    query = query_turned.astype(BF)
    key = key_turned.astype(BF)[:, 0]
    visible = same_document(documents)
    scores = jnp.einsum("thd,ud->htu", query, key, preferred_element_type=F32) * HEAD_SIZE**-0.5
    scores = jnp.where(visible[None], scores, NEGATIVE_FLOOR)
    weights = jnp.where(
        visible[None], jnp.exp(scores - jnp.max(scores, axis=-1, keepdims=True)), 0.0
    )
    probs = weights / jnp.sum(weights, axis=-1, keepdims=True)
    probs_low = probs.astype(BF)
    attn_mix = jnp.einsum("htu,ud->thd", probs_low, value, preferred_element_type=F32)
    attn_low = attn_mix.reshape(length, head).astype(BF)

    step_size, step_back = jax.vjp(
        lambda lin, bias: jax.nn.softplus(lin + bias[None, :]), step_lin, bias_own
    )
    rate = -jnp.exp(decay_own)
    terms = ssm_terms(step_size, rate, documents, ctx)
    y, saved = ssm_forward(xin, write, read, terms, skip_own)
    gated, gated_back = jax.vjp(lambda a, z: a * jax.nn.silu(z), y, zgate)
    mean_square = row_sum(jnp.sum(gated * gated, axis=-1), ids) / dssm
    scale_mix = lax.rsqrt(mean_square + EPSILON)[:, None]
    ymix = (gated * scale_mix * gain_mix).astype(BF)

    branch = scatter_tokens(mm(attn_low, attn_out_own) + mm(ymix, mamba_out_own), ids)
    mid = resid + branch
    scale_two = lax.rsqrt(jnp.mean(mid * mid, axis=-1, keepdims=True) + EPSILON)
    normed_two = gather_tokens(to_shards((mid * scale_two * gain_two).astype(BF)), ids)
    grad_all = gather_tokens(out_grad[0], ids)

    gate_up = mm(normed_two, ffn_own)
    gate_lin, up_lin = gate_up[:, :ff], gate_up[:, ff:]
    sigmoid_gate = jax.nn.sigmoid(gate_lin)
    silu_gate = gate_lin * sigmoid_gate
    hidden = (silu_gate * up_lin).astype(BF)
    grad_hidden = mm_nt(grad_all, down_own)
    grad_gate = (
        grad_hidden * up_lin * (sigmoid_gate + silu_gate * (1.0 - sigmoid_gate))
    ).astype(BF)
    grad_up = (grad_hidden * silu_gate).astype(BF)
    grad_gu = jnp.concatenate([grad_gate, grad_up], axis=1)
    grad_n2 = from_shards(scatter_tokens(mm_nt(grad_gu, ffn_own), ids))
    block_out = (mid + scatter_tokens(mm(hidden, down_own), ids)).astype(BF)
    down_grad = scatter_rows(mm_tn(hidden, grad_all).reshape(seqs, ff // seqs, width))
    ffn_grad = mm_tn(normed_two, grad_gu).reshape(seqs, ctx, krows, 2 * ff).astype(BF)
    ffn_grad = scatter_rows(after(ffn_grad, down_grad))

    turned = grad_n2 * gain_two
    hat_two = mid * scale_two
    ffn_gain_grad = jnp.sum(grad_n2 * hat_two, axis=0)
    grad_mid = out_grad[0].astype(F32) + scale_two * (
        turned - hat_two * jnp.mean(turned * hat_two, axis=-1, keepdims=True)
    )
    branch_grad = gather_tokens(grad_mid.astype(BF), ids)

    out_grad_own = jnp.concatenate(
        [
            mm_tn(attn_low, branch_grad).reshape(seqs, -1, width),
            mm_tn(ymix, branch_grad).reshape(seqs, -1, width),
        ],
        axis=1,
    ).astype(BF)
    out_grad_own = scatter_rows(after(out_grad_own, ffn_grad)).astype(F32)
    attn_out_grad, mamba_out_grad = out_grad_own[:out_rows], out_grad_own[out_rows:]
    grad_attn = mm_nt(branch_grad, attn_out_own).astype(BF).reshape(length, -1, HEAD_SIZE)
    grad_ymix = mm_nt(branch_grad, mamba_out_own)

    grad_prob = jnp.einsum("thd,ud->htu", grad_attn, value, preferred_element_type=F32)
    delta = jnp.sum(probs * grad_prob, axis=-1, keepdims=True)
    grad_score = (probs * (grad_prob - delta)).astype(BF)
    grad_query = (
        jnp.einsum("htu,ud->thd", grad_score, key, preferred_element_type=F32) * HEAD_SIZE**-0.5
    )
    grad_key = (
        jnp.einsum("htu,thd->ud", grad_score, query, preferred_element_type=F32) * HEAD_SIZE**-0.5
    )
    grad_value = jnp.einsum("htu,thd->ud", probs_low, grad_attn, preferred_element_type=F32)
    grad_q_lin = unturn(grad_query)[0].reshape(length, head).astype(BF)
    grad_k_lin = unturn_key(grad_key[:, None])[0].reshape(length, HEAD_SIZE).astype(BF)

    hat = gated * scale_mix
    turned_mix = grad_ymix * gain_mix
    mixer_gain_grad = jnp.sum(grad_ymix * hat, axis=0)
    along = row_sum(jnp.sum(turned_mix * hat, axis=-1), ids)[:, None] / dssm
    grad_gated = scale_mix * (turned_mix - hat * along)
    grad_y, grad_zgate = gated_back(grad_gated)

    grad_xin, grad_write, grad_read, grad_step, grad_rate, skip_grad = ssm_backward(
        grad_y, xin, write, read, terms, skip_own, rate, saved
    )
    grad_shared = jnp.concatenate([grad_write, grad_read], axis=1).astype(BF)
    grad_shared = scatter_tokens(grad_shared.T, ids).T
    grad_widened, taps_grad, shift_grad = conv_back(
        jnp.concatenate([grad_xin, grad_shared], axis=1)
    )
    grad_step_lin, step_bias_grad = step_back(grad_step)
    log_decay_grad = grad_rate * rate
    grad_conv = jnp.concatenate(
        [
            grad_widened[taps:].astype(BF),
            jnp.pad(grad_step_lin.astype(BF), ((0, 0), (0, step_pad - heads))),
        ],
        axis=1,
    )
    grad_rest = jnp.concatenate(
        [grad_q_lin, grad_k_lin, grad_value.astype(BF), grad_zgate.astype(BF)], axis=1
    )

    grad_normed = from_shards(
        scatter_tokens(mm_nt(grad_conv, conv_in_own) + mm_nt(grad_rest, rest_own), ids)
    )
    rest_grad = mm_tn(normed, grad_rest).reshape(seqs, ctx, krows, rest_cols).astype(BF)
    rest_grad = scatter_rows(after(rest_grad, out_grad_own))
    conv_grad = mm_tn(normed, grad_conv).reshape(seqs, ctx, krows, conv_cols).astype(BF)
    conv_grad = scatter_rows(after(conv_grad, rest_grad))
    ffn_grad = swap_columns(ffn_grad).astype(F32)
    mixer_grad = swap_columns(jnp.concatenate([conv_grad, rest_grad], axis=2)).astype(F32)
    turned_one = grad_normed * gain_one
    hat_one = resid * scale_one
    norm_gain_grad = jnp.sum(grad_normed * hat_one, axis=0)
    input_grad = (
        grad_mid
        + scale_one
        * (turned_one - hat_one * jnp.mean(turned_one * hat_one, axis=-1, keepdims=True))
    ).astype(BF)

    def spread_out(own, at, total):
        return lax.dynamic_update_slice_in_dim(
            jnp.zeros(own.shape[:-1] + (total,), F32), own, at, own.ndim - 1
        )

    def spread_channels(own):
        full = spread_out(own[..., :inner], me * inner, dssm + 2 * STATE)
        return lax.dynamic_update_slice_in_dim(full, own[..., inner:], dssm + me * bc, own.ndim - 1)

    parts = (
        norm_gain_grad,
        ffn_gain_grad,
        spread_out(mixer_gain_grad, me * inner, dssm),
        spread_channels(shift_grad),
        spread_channels(taps_grad).reshape(-1),
        spread_out(step_bias_grad, me * heads, HS),
        spread_out(log_decay_grad, me * heads, HS),
        spread_out(skip_grad, me * heads, HS),
    )
    place = (ctx, seqs)
    tiles = [part.reshape(place + (-1,)) for part in parts[:4]]
    tiles.append(parts[4].reshape((CONV,) + place + (-1,)).transpose(1, 2, 0, 3).reshape(place + (-1,)))
    tiles.append(
        jnp.broadcast_to(jnp.concatenate(parts[5:]), place + (3 * HS,))
    )
    sizes = [tile.shape[-1] for tile in tiles]
    tile_rows = -(-sum(sizes) // 1024) * 8
    tiles = jnp.concatenate(tiles, axis=-1)
    tiles = jnp.pad(tiles, ((0, 0), (0, 0), (0, tile_rows * 128 - sum(sizes))))
    sums = small_scatter(tiles.reshape(place + (tile_rows, 128)), ids).reshape(-1)
    pieces = []
    at = 0
    for size in sizes:
        pieces.append(sums[at : at + size])
        at += size
    per_head = pieces[5].reshape(3, HS)

    def by_row(packed, start, n):
        return packed[:, :, start : start + n].transpose(1, 0, 2).reshape(krows, -1)

    base = conv_cols
    key_grad = mixer_grad[:, :, base + head : base + head + HEAD_SIZE]
    value_grad = mixer_grad[:, :, base + head + HEAD_SIZE : base + head + 2 * HEAD_SIZE]

    def over_queries(packed):
        return (
            packed.reshape(KEY_VALUE_HEADS, kv_repeat, krows, HEAD_SIZE)
            .sum(axis=1)
            .transpose(1, 0, 2)
            .reshape(krows, -1)
        )

    return (
        block_out[None],
        input_grad[None],
        pieces[0],
        by_row(mixer_grad, base, head),
        over_queries(key_grad),
        over_queries(value_grad),
        attn_out_grad,
        by_row(mixer_grad, base + head + 2 * HEAD_SIZE, inner),
        jnp.concatenate(
            [by_row(mixer_grad, 0, inner), by_row(mixer_grad, inner, bc)], axis=1
        ),
        by_row(mixer_grad, inner + bc, heads),
        pieces[4].reshape(CONV, -1),
        pieces[3],
        per_head[0],
        per_head[1],
        per_head[2],
        pieces[2],
        mamba_out_grad,
        pieces[1],
        by_row(ffn_grad, 0, ff),
        by_row(ffn_grad, ff, ff),
        down_grad.astype(F32),
    )


def solution(mesh):
    placed = (
        P(FSDP, CTX, None),
        P(FSDP, CTX, None),
        P(FSDP, CTX),
        P((CTX, FSDP)),
        P((CTX, FSDP), None),
        P((CTX, FSDP), None),
        P((CTX, FSDP), None),
        P((CTX, FSDP), None),
        P((CTX, FSDP), None),
        P((CTX, FSDP), None),
        P((CTX, FSDP), None),
        P(None, (CTX, FSDP)),
        P((CTX, FSDP)),
        P(),
        P(),
        P(),
        P((CTX, FSDP)),
        P((CTX, FSDP), None),
        P((CTX, FSDP)),
        P((CTX, FSDP), None),
        P((CTX, FSDP), None),
        P((CTX, FSDP), None),
    )
    ctx = mesh.shape[CTX]
    whole_heads = ctx == PLANE and QUERY_HEADS % ctx == 0 and HS % ctx == 0
    return jax.shard_map(
        head_parallel if whole_heads else on_device,
        mesh=mesh,
        in_specs=placed,
        out_specs=(
            P(FSDP, CTX, None),
            P(FSDP, CTX, None),
            P((CTX, FSDP)),
            P((CTX, FSDP), None),
            P((CTX, FSDP), None),
            P((CTX, FSDP), None),
            P((CTX, FSDP), None),
            P((CTX, FSDP), None),
            P((CTX, FSDP), None),
            P((CTX, FSDP), None),
            P(None, (CTX, FSDP)),
            P((CTX, FSDP)),
            P(),
            P(),
            P(),
            P((CTX, FSDP)),
            P((CTX, FSDP), None),
            P((CTX, FSDP)),
            P((CTX, FSDP), None),
            P((CTX, FSDP), None),
            P((CTX, FSDP), None),
        ),
        check_vma=False,
    )
```

```python
from functools import partial
import itertools
import math

import jax
import jax.numpy as jnp
from jax import lax
from jax.experimental import pallas as pl
from jax.experimental.pallas import tpu as pltpu
from jax.sharding import PartitionSpec as P

CTX = "ctx"
FSDP = "fsdp"
QUERY_HEADS = 8
KEY_VALUE_HEADS = 2
HEAD_SIZE = 128
HS = 48
HP = 64
STATE = 256
CONV = 4


EPSILON = 1e-05
ROPE_BASE = 100000000000.0
NEGATIVE_FLOOR = -1e30
HIGHEST = lax.Precision.HIGHEST


def shifted(value, axis, steps):
    count = lax.axis_size(axis)
    leading, last = (max(0, -steps), min(count, count - steps))
    return lax.ppermute(value, axis, [(source, source + steps) for source in range(leading, last)])


def prefix(shard, axis, combine, identity):
    devices, position = (lax.axis_size(axis), lax.axis_index(axis))
    everything = jax.tree.map(
        lambda part, kind: lax.all_gather(part.astype(kind), axis),
        shard,
        (jnp.bfloat16, jnp.bfloat16),
    )
    start = jax.tree.map(
        lambda part, zero: jnp.broadcast_to(jnp.asarray(zero, part.dtype), part.shape),
        shard,
        identity,
    )

    def step(k, before):
        reached = k < position
        new = combine(
            before, jax.tree.map(lambda part, own: part[k].astype(own.dtype), everything, shard)
        )
        return jax.tree.map(lambda a, b: jnp.where(reached, a, b), new, before)

    return lax.fori_loop(0, devices, step, start)


def carried_in(shard, axis, join, neutral):
    count = lax.axis_size(axis)
    place = lax.axis_index(axis)
    ahead = count - 1 - place
    gathered = jax.tree.map(
        lambda a, kind: lax.all_gather(a.astype(kind), axis),
        shard,
        jax.tree.map(lambda a: jnp.bfloat16 if a.dtype == jnp.float32 else a.dtype, shard),
    )
    state = jax.tree.map(lambda a, e: jnp.zeros_like(a) + jnp.asarray(e, a.dtype), shard, neutral)

    def one(step, state):
        source = count - 1 - step
        return join(
            state,
            jax.tree.map(
                lambda a, own: lax.dynamic_index_in_dim(a, source, 0, False).astype(own.dtype),
                gathered,
                shard,
            ),
        )

    return lax.fori_loop(0, ahead, one, state)


def rms_scale(values, gain):
    return values * lax.rsqrt(jnp.mean(values * values, axis=-1, keepdims=True) + EPSILON) * gain


def rotate(values, places):
    half_size = values.shape[-1] // 2
    freqs = ROPE_BASE ** (-jnp.arange(half_size).astype(jnp.float32) / half_size)
    angles = places[:, None] * freqs[None, :]
    cosine = jnp.cos(angles)[:, None, :]
    sine = jnp.sin(angles)[:, None, :]
    first = values[..., :half_size]
    second = values[..., half_size:]
    return jnp.concatenate(
        [first * cosine - second * sine, second * cosine + first * sine], axis=-1
    )


def conv_part(widened, taps_weight, bias, widened_docs, documents):
    row_length_total = documents.shape[0]
    total = bias[None, :]
    for tap_index in range(taps_weight.shape[0]):
        same_doc = (widened_docs[tap_index : tap_index + row_length_total] == documents)[:, None]
        total = total + jnp.where(
            same_doc,
            widened[tap_index : tap_index + row_length_total] * taps_weight[tap_index][None, :],
            0.0,
        )
    return jax.nn.silu(total)


def step_part(step_lin, step_bias, log_decay):
    return (jax.nn.softplus(step_lin + step_bias), -jnp.exp(log_decay))


def block_stats(mixer_in, write_proj, step_size, decay_rate, documents, prior_doc):
    decay_log = jnp.cumsum(step_size * decay_rate[None, :], axis=0)
    last_doc = documents[-1]
    tail_weight = (
        jnp.where(
            (documents == last_doc)[:, None], jnp.exp(decay_log[-1][None, :] - decay_log), 0.0
        )
        * step_size
    )
    state_loc = jnp.einsum(
        "thp,tn->hpn", mixer_in * tail_weight[:, :, None], write_proj, precision=HIGHEST
    )
    carry_decay = jnp.exp(decay_log[-1]) * (last_doc == prior_doc).astype(jnp.float32)
    return (state_loc, carry_decay)


def block_mix(
    mixer_in,
    write_proj,
    read_proj,
    step_size,
    decay_rate,
    skip_gain,
    state_in,
    documents,
    prior_doc,
):
    decay_log = jnp.cumsum(step_size * decay_rate[None, :], axis=0)
    positions = jnp.arange(documents.shape[0])
    visible = (documents[:, None] == documents[None, :]) & (
        positions[:, None] >= positions[None, :]
    )
    spread = decay_log.T[:, :, None] - decay_log.T[:, None, :]
    decay_pair = jnp.where(visible[None], jnp.exp(jnp.where(visible[None], spread, 0.0)), 0.0)
    gram = jnp.dot(read_proj, write_proj.T, precision=HIGHEST)
    mixing = decay_pair * gram[None] * step_size.T[:, None, :]
    inner = jnp.einsum("htu,uhp->thp", mixing, mixer_in, precision=HIGHEST)
    entry = jnp.where((documents == prior_doc)[:, None], jnp.exp(decay_log), 0.0)
    carried = jnp.einsum("tn,hpn->thp", read_proj, state_in, precision=HIGHEST) * entry[:, :, None]
    return inner + carried + skip_gain[None, :, None] * mixer_in


def gated_norm(flat_mixed, mixer_gate, gain):
    return rms_scale(flat_mixed * jax.nn.silu(mixer_gate), gain)


def chain_combine(earlier, later):
    decay_early, state_early = earlier
    decay_late, state_late = later
    return (decay_early * decay_late, decay_late[:, None, None] * state_early + state_late)


def piece_scores(piece, start, query_group, query_docs, query_places):
    key_segment, value_segment, docs_piece = piece
    segment_rows = key_segment.shape[0]
    heads_of_key = key_segment.reshape(segment_rows, KEY_VALUE_HEADS, HEAD_SIZE).transpose(1, 0, 2)
    heads_of_value = value_segment.reshape(segment_rows, KEY_VALUE_HEADS, HEAD_SIZE).transpose(
        1, 0, 2
    )
    key_places = (start + jnp.arange(segment_rows)).astype(jnp.float32)
    visible = (docs_piece.astype(jnp.float32)[None, :] == query_docs[:, None]) & (
        key_places[None, :] <= query_places[:, None]
    )
    scores = jnp.einsum(
        "gqd,gkd->gqk", query_group, heads_of_key, preferred_element_type=jnp.float32
    ) * HEAD_SIZE ** (-0.5)
    return (heads_of_key, heads_of_value, visible, jnp.where(visible[None], scores, NEGATIVE_FLOOR))


def fold_local(step_fn, whole, start_carry):
    row_length_total = whole[0].shape[0]
    tile_block = math.gcd(row_length_total, 512)

    def advance(block_index, carry):
        start = block_index * tile_block
        piece = tuple((lax.dynamic_slice_in_dim(member, start, tile_block, 0) for member in whole))
        return step_fn(carry, piece, start)

    return lax.fori_loop(0, row_length_total // tile_block, advance, start_carry)


def on_device(
    hidden_in,
    out_grad,
    doc_ids,
    norm_gain,
    query_weight,
    key_matrix,
    value_matrix,
    attn_out_weight,
    mixer_gate_weight,
    conv_in_weight,
    step_weight,
    conv_weight,
    conv_bias,
    step_bias,
    log_decay,
    skip_gain,
    mixer_gain,
    mamba_out_weight,
    ffn_gain,
    gate_weight,
    up_weight,
    down_weight,
):
    single_float = jnp.float32
    brain_float_half = jnp.bfloat16
    (
        norm_full,
        query_full,
        complete_key,
        value_full,
        attn_out_full,
        mixer_gate_full,
        conv_in_full,
        step_full,
        conv_full,
        conv_bias_full,
        mixer_gain_full,
        mamba_out_full,
    ) = (
        lax.all_gather(norm_gain, (CTX, FSDP), axis=0, tiled=True),
        lax.all_gather(query_weight, (CTX, FSDP), axis=0, tiled=True),
        lax.all_gather(key_matrix, (CTX, FSDP), axis=0, tiled=True),
        lax.all_gather(value_matrix, (CTX, FSDP), axis=0, tiled=True),
        lax.all_gather(attn_out_weight, (CTX, FSDP), axis=0, tiled=True),
        lax.all_gather(mixer_gate_weight, (CTX, FSDP), axis=0, tiled=True),
        lax.all_gather(conv_in_weight, (CTX, FSDP), axis=0, tiled=True),
        lax.all_gather(step_weight, (CTX, FSDP), axis=0, tiled=True),
        lax.all_gather(conv_weight, (CTX, FSDP), axis=1, tiled=True),
        lax.all_gather(conv_bias, (CTX, FSDP), axis=0, tiled=True),
        lax.all_gather(mixer_gain, (CTX, FSDP), axis=0, tiled=True),
        lax.all_gather(mamba_out_weight, (CTX, FSDP), axis=0, tiled=True),
    )
    tokens_per_worker = hidden_in.shape[1]
    head_cluster = QUERY_HEADS // KEY_VALUE_HEADS
    dssm = HS * HP
    taps = CONV - 1
    resid = hidden_in[0].astype(single_float)
    documents = doc_ids[0]
    places = (lax.axis_index(CTX) * tokens_per_worker + jnp.arange(tokens_per_worker)).astype(
        single_float
    )
    norm_one, norm_one_back = jax.vjp(rms_scale, resid, norm_full.astype(single_float))
    normalized_input = norm_one.astype(brain_float_half)
    query_lin = jnp.dot(normalized_input, query_full, preferred_element_type=single_float).reshape(
        tokens_per_worker, QUERY_HEADS, HEAD_SIZE
    )
    key_linear = jnp.dot(
        normalized_input, complete_key, preferred_element_type=single_float
    ).reshape(tokens_per_worker, KEY_VALUE_HEADS, HEAD_SIZE)
    query_turned, unturn_query = jax.vjp(partial(rotate, places=places), query_lin)
    rotated_key, unrotate_key = jax.vjp(partial(rotate, places=places), key_linear)
    rotated_query = query_turned.astype(brain_float_half)
    flattened_key = rotated_key.astype(brain_float_half).reshape(
        tokens_per_worker, KEY_VALUE_HEADS * HEAD_SIZE
    )
    value_lowered = jnp.dot(
        normalized_input, value_full, preferred_element_type=single_float
    ).astype(brain_float_half)
    docs_low = documents.astype(brain_float_half)
    query_group = (
        rotated_query.reshape(tokens_per_worker, KEY_VALUE_HEADS, head_cluster, HEAD_SIZE)
        .transpose(1, 2, 0, 3)
        .reshape(KEY_VALUE_HEADS, head_cluster * tokens_per_worker, HEAD_SIZE)
    )
    query_places = jnp.tile(places, head_cluster)
    query_docs = jnp.tile(documents.astype(single_float), head_cluster)

    def attend_piece(carry, piece, start):
        previous_maximum, total_old, summed_old = carry
        heads_of_key, heads_of_value, visible, scores = piece_scores(
            piece, start, query_group, query_docs, query_places
        )
        peak_new = jnp.maximum(previous_maximum, jnp.max(scores, axis=-1))
        weights = jnp.where(visible[None], jnp.exp(scores - peak_new[:, :, None]), 0.0)
        factor = jnp.exp(previous_maximum - peak_new)
        total_new = total_old * factor + jnp.sum(weights, axis=-1)
        summed_new = summed_old * factor[:, :, None] + jnp.einsum(
            "gqk,gkd->gqd",
            weights.astype(brain_float_half),
            heads_of_value,
            preferred_element_type=single_float,
        )
        return (peak_new, total_new, summed_new)

    rows_of_query = head_cluster * tokens_per_worker
    start_forward = (
        jnp.full((KEY_VALUE_HEADS, rows_of_query), NEGATIVE_FLOOR, single_float),
        jnp.zeros((KEY_VALUE_HEADS, rows_of_query), single_float),
        jnp.zeros((KEY_VALUE_HEADS, rows_of_query, HEAD_SIZE), single_float),
    )
    kv_whole = (
        lax.all_gather(flattened_key, CTX, axis=0, tiled=True),
        lax.all_gather(value_lowered, CTX, axis=0, tiled=True),
        lax.all_gather(docs_low, CTX, axis=0, tiled=True),
    )
    peak, total, summed = fold_local(attend_piece, kv_whole, start_forward)
    attention_cluster = summed / total[:, :, None]
    log_total = peak + jnp.log(total)
    attn_low = (
        attention_cluster.reshape(KEY_VALUE_HEADS, head_cluster, tokens_per_worker, HEAD_SIZE)
        .transpose(2, 0, 1, 3)
        .reshape(tokens_per_worker, QUERY_HEADS * HEAD_SIZE)
        .astype(brain_float_half)
    )
    attn_out = jnp.dot(attn_low, attn_out_full, preferred_element_type=single_float)
    mixer_gate = jnp.dot(normalized_input, mixer_gate_full, preferred_element_type=single_float)
    conv_lin = jnp.dot(normalized_input, conv_in_full, preferred_element_type=single_float).astype(
        brain_float_half
    )
    step_lin = jnp.dot(normalized_input, step_full, preferred_element_type=single_float)
    rim_rows, rim_docs = shifted(
        (conv_lin[tokens_per_worker - taps :], docs_low[tokens_per_worker - taps :]), CTX, 1
    )
    widened = jnp.concatenate([rim_rows, conv_lin], axis=0).astype(single_float)
    widened_docs = jnp.concatenate([rim_docs.astype(jnp.int32), documents])
    prior_doc = widened_docs[taps - 1]
    conv_act, conv_back = jax.vjp(
        partial(conv_part, widened_docs=widened_docs, documents=documents),
        widened,
        conv_full.astype(single_float),
        conv_bias_full.astype(single_float),
    )
    conv_vals = conv_act.astype(brain_float_half).astype(single_float)
    mixer_in = conv_vals[:, :dssm].reshape(tokens_per_worker, HS, HP)
    write_proj = conv_vals[:, dssm : dssm + STATE]
    read_proj = conv_vals[:, dssm + STATE :]
    (step_size, decay_rate), step_back = jax.vjp(step_part, step_lin, step_bias, log_decay)
    (state_loc, carry_decay), stats_back = jax.vjp(
        partial(block_stats, documents=documents, prior_doc=prior_doc),
        mixer_in,
        write_proj,
        step_size,
        decay_rate,
    )
    chain_identity = (jnp.ones_like(carry_decay), jnp.zeros_like(state_loc))
    _, state_in = prefix((carry_decay, state_loc), CTX, chain_combine, chain_identity)
    mixed, mix_back = jax.vjp(
        partial(block_mix, documents=documents, prior_doc=prior_doc),
        mixer_in,
        write_proj,
        read_proj,
        step_size,
        decay_rate,
        skip_gain,
        state_in,
    )
    ymix_vals, gate_back = jax.vjp(
        gated_norm,
        mixed.reshape(tokens_per_worker, dssm),
        mixer_gate,
        mixer_gain_full.astype(single_float),
    )
    ymix_low = ymix_vals.astype(brain_float_half)
    mamba_out = jnp.dot(ymix_low, mamba_out_full, preferred_element_type=single_float)
    ffn_gain_full, gate_full, up_full, down_full = (
        lax.all_gather(ffn_gain, (CTX, FSDP), axis=0, tiled=True),
        lax.all_gather(gate_weight, (CTX, FSDP), axis=0, tiled=True),
        lax.all_gather(up_weight, (CTX, FSDP), axis=0, tiled=True),
        lax.all_gather(down_weight, (CTX, FSDP), axis=0, tiled=True),
    )
    mid = resid + attn_out + mamba_out
    norm_two, norm_two_back = jax.vjp(rms_scale, mid, ffn_gain_full.astype(single_float))
    normed_two = norm_two.astype(brain_float_half)
    gate_lin = jnp.dot(normed_two, gate_full, preferred_element_type=single_float)
    up_lin = jnp.dot(normed_two, up_full, preferred_element_type=single_float)
    sigmoid_gate = jax.nn.sigmoid(gate_lin)
    silu_gate = gate_lin * sigmoid_gate
    hidden = (silu_gate * up_lin).astype(brain_float_half)
    block_out = (mid + jnp.dot(hidden, down_full, preferred_element_type=single_float)).astype(
        brain_float_half
    )
    grad_out = out_grad[0]
    down_grad_w = jnp.einsum("tf,td->fd", hidden, grad_out, preferred_element_type=single_float)
    grad_hidden = jnp.einsum("td,fd->tf", grad_out, down_full, preferred_element_type=single_float)
    grad_gate = (grad_hidden * up_lin * (sigmoid_gate + silu_gate * (1.0 - sigmoid_gate))).astype(
        brain_float_half
    )
    grad_up = (grad_hidden * silu_gate).astype(brain_float_half)
    gate_grad_w = jnp.einsum(
        "td,tf->df", normed_two, grad_gate, preferred_element_type=single_float
    )
    up_grad_w = jnp.einsum("td,tf->df", normed_two, grad_up, preferred_element_type=single_float)
    grad_normed_two = jnp.einsum(
        "tf,df->td", grad_gate, gate_full, preferred_element_type=single_float
    ) + jnp.einsum("tf,df->td", grad_up, up_full, preferred_element_type=single_float)
    grad_mid_norm, ffn_gain_grad = norm_two_back(grad_normed_two)
    grad_mid = grad_out.astype(single_float) + grad_mid_norm
    ffn_sums = (
        lax.psum_scatter(ffn_gain_grad, (CTX, FSDP), scatter_dimension=0, tiled=True),
        lax.psum_scatter(gate_grad_w, (CTX, FSDP), scatter_dimension=0, tiled=True),
        lax.psum_scatter(up_grad_w, (CTX, FSDP), scatter_dimension=0, tiled=True),
        lax.psum_scatter(down_grad_w, (CTX, FSDP), scatter_dimension=0, tiled=True),
    )
    branch_grad = grad_mid.astype(brain_float_half)
    attn_out_grad_w = jnp.einsum(
        "ti,td->id", attn_low, branch_grad, preferred_element_type=single_float
    )
    attention_gradient = jnp.einsum(
        "td,id->ti", branch_grad, attn_out_full, preferred_element_type=single_float
    ).astype(brain_float_half)
    grad_group = (
        attention_gradient.reshape(tokens_per_worker, KEY_VALUE_HEADS, head_cluster, HEAD_SIZE)
        .transpose(1, 2, 0, 3)
        .reshape(KEY_VALUE_HEADS, rows_of_query, HEAD_SIZE)
    )
    row_delta = jnp.sum(grad_group.astype(single_float) * attention_cluster, axis=-1)

    def attend_back(carry, piece, start):
        query_acc, kv_grad = carry
        heads_of_key, heads_of_value, visible, scores = piece_scores(
            piece, start, query_group, query_docs, query_places
        )
        segment_rows = heads_of_key.shape[1]
        probs = jnp.where(visible[None], jnp.exp(scores - log_total[:, :, None]), 0.0)
        prob_grad = jnp.einsum(
            "gqd,gkd->gqk", grad_group, heads_of_value, preferred_element_type=single_float
        )
        score_grad = (probs * (prob_grad - row_delta[:, :, None])).astype(brain_float_half)
        query_acc = query_acc + jnp.einsum(
            "gqk,gkd->gqd", score_grad, heads_of_key, preferred_element_type=single_float
        )
        key_portion = jnp.einsum(
            "gqk,gqd->kgd", score_grad, query_group, preferred_element_type=single_float
        ) * HEAD_SIZE ** (-0.5)
        value_portion = jnp.einsum(
            "gqk,gqd->kgd",
            probs.astype(brain_float_half),
            grad_group,
            preferred_element_type=single_float,
        )
        term = jnp.concatenate(
            [
                key_portion.reshape(segment_rows, KEY_VALUE_HEADS * HEAD_SIZE),
                value_portion.reshape(segment_rows, KEY_VALUE_HEADS * HEAD_SIZE),
            ],
            axis=1,
        )
        current = lax.dynamic_slice_in_dim(kv_grad, start, segment_rows, 0)
        kv_grad = lax.dynamic_update_slice_in_dim(kv_grad, current + term, start, 0)
        return (query_acc, kv_grad)

    start_back = (
        jnp.zeros((KEY_VALUE_HEADS, rows_of_query, HEAD_SIZE), single_float),
        jnp.zeros(
            (tokens_per_worker * lax.axis_size(CTX), 2 * KEY_VALUE_HEADS * HEAD_SIZE),
            single_float,
        ),
    )
    query_acc, kv_grad = fold_local(attend_back, kv_whole, start_back)
    local_key_value = lax.psum_scatter(
        kv_grad.astype(jnp.bfloat16), CTX, scatter_dimension=0, tiled=True
    ).astype(jnp.float32)
    query_turn_grad = (
        (query_acc * HEAD_SIZE ** (-0.5))
        .reshape(KEY_VALUE_HEADS, head_cluster, tokens_per_worker, HEAD_SIZE)
        .transpose(2, 0, 1, 3)
        .reshape(tokens_per_worker, QUERY_HEADS, HEAD_SIZE)
    )
    query_lin_grad = (
        unturn_query(query_turn_grad)[0]
        .reshape(tokens_per_worker, QUERY_HEADS * HEAD_SIZE)
        .astype(brain_float_half)
    )
    key_lin_grad = (
        unrotate_key(
            local_key_value[:, : KEY_VALUE_HEADS * HEAD_SIZE].reshape(
                tokens_per_worker, KEY_VALUE_HEADS, HEAD_SIZE
            )
        )[0]
        .reshape(tokens_per_worker, KEY_VALUE_HEADS * HEAD_SIZE)
        .astype(brain_float_half)
    )
    value_linear_gradient = local_key_value[:, KEY_VALUE_HEADS * HEAD_SIZE :].astype(
        brain_float_half
    )
    mamba_grad_w = jnp.einsum(
        "ti,td->id", ymix_low, branch_grad, preferred_element_type=single_float
    )
    grad_ymix = jnp.einsum(
        "td,id->ti", branch_grad, mamba_out_full, preferred_element_type=single_float
    )
    grad_mixed, grad_zgate, mixer_gain_grad = gate_back(grad_ymix)
    zgate_low = grad_zgate.astype(brain_float_half)
    (
        grad_in_mix,
        grad_write_mix,
        grad_read,
        grad_step_mix,
        grad_rate_mix,
        skip_grad,
        grad_state_in,
    ) = mix_back(grad_mixed.reshape(tokens_per_worker, HS, HP))
    _, state_later = carried_in((carry_decay, grad_state_in), CTX, chain_combine, chain_identity)
    decay_grad = jnp.sum(state_in * state_later, axis=(1, 2))
    grad_in_stats, grad_write_stats, grad_step_stats, grad_rate_stats = stats_back(
        (state_later, decay_grad)
    )
    grad_conv = jnp.concatenate(
        [
            (grad_in_mix + grad_in_stats).reshape(tokens_per_worker, dssm),
            grad_write_mix + grad_write_stats,
            grad_read,
        ],
        axis=1,
    )
    grad_widened, conv_weight_grad, conv_bias_grad = conv_back(grad_conv)
    rim_grad = shifted(grad_widened[:taps].astype(jnp.bfloat16), CTX, -1).astype(jnp.float32)
    conv_lin_grad = (
        grad_widened[taps:].at[tokens_per_worker - taps :].add(rim_grad).astype(brain_float_half)
    )
    step_lin_grad, step_bias_grad, log_decay_grad = step_back(
        (grad_step_mix + grad_step_stats, grad_rate_mix + grad_rate_stats)
    )
    step_lin_low = step_lin_grad.astype(brain_float_half)
    query_grad_w = jnp.einsum(
        "td,ti->di", normalized_input, query_lin_grad, preferred_element_type=single_float
    )
    key_grad_w = jnp.einsum(
        "td,ti->di", normalized_input, key_lin_grad, preferred_element_type=single_float
    )
    value_grad_w = jnp.einsum(
        "td,ti->di", normalized_input, value_linear_gradient, preferred_element_type=single_float
    )
    zgate_grad_w = jnp.einsum(
        "td,ti->di", normalized_input, zgate_low, preferred_element_type=single_float
    )
    conv_in_grad_w = jnp.einsum(
        "td,ti->di", normalized_input, conv_lin_grad, preferred_element_type=single_float
    )
    step_grad_w = jnp.einsum(
        "td,ti->di", normalized_input, step_lin_low, preferred_element_type=single_float
    )
    grad_normed = (
        jnp.einsum("ti,di->td", query_lin_grad, query_full, preferred_element_type=single_float)
        + jnp.einsum("ti,di->td", key_lin_grad, complete_key, preferred_element_type=single_float)
        + jnp.einsum(
            "ti,di->td", value_linear_gradient, value_full, preferred_element_type=single_float
        )
        + jnp.einsum("ti,di->td", zgate_low, mixer_gate_full, preferred_element_type=single_float)
        + jnp.einsum("ti,di->td", conv_lin_grad, conv_in_full, preferred_element_type=single_float)
        + jnp.einsum("ti,di->td", step_lin_low, step_full, preferred_element_type=single_float)
    )
    grad_resid_norm, norm_gain_grad = norm_one_back(grad_normed)
    input_grad = (grad_mid + grad_resid_norm).astype(brain_float_half)
    mixer_sums = (
        lax.psum_scatter(norm_gain_grad, (CTX, FSDP), scatter_dimension=0, tiled=True),
        lax.psum_scatter(query_grad_w, (CTX, FSDP), scatter_dimension=0, tiled=True),
        lax.psum_scatter(key_grad_w, (CTX, FSDP), scatter_dimension=0, tiled=True),
        lax.psum_scatter(value_grad_w, (CTX, FSDP), scatter_dimension=0, tiled=True),
        lax.psum_scatter(attn_out_grad_w, (CTX, FSDP), scatter_dimension=0, tiled=True),
        lax.psum_scatter(zgate_grad_w, (CTX, FSDP), scatter_dimension=0, tiled=True),
        lax.psum_scatter(conv_in_grad_w, (CTX, FSDP), scatter_dimension=0, tiled=True),
        lax.psum_scatter(step_grad_w, (CTX, FSDP), scatter_dimension=0, tiled=True),
        lax.psum_scatter(conv_weight_grad, (CTX, FSDP), scatter_dimension=1, tiled=True),
        lax.psum_scatter(conv_bias_grad, (CTX, FSDP), scatter_dimension=0, tiled=True),
        lax.psum_scatter(mixer_gain_grad, (CTX, FSDP), scatter_dimension=0, tiled=True),
        lax.psum_scatter(mamba_grad_w, (CTX, FSDP), scatter_dimension=0, tiled=True),
    )
    summed_grads = tuple(mixer_sums) + tuple(ffn_sums)
    step_bias_sum, log_decay_sum, skip_sum = lax.psum(
        (step_bias_grad, log_decay_grad, skip_grad), (CTX, FSDP)
    )
    return (
        block_out[None],
        input_grad[None],
        summed_grads[0],
        summed_grads[1],
        summed_grads[2],
        summed_grads[3],
        summed_grads[4],
        summed_grads[5],
        summed_grads[6],
        summed_grads[7],
        summed_grads[8],
        summed_grads[9],
        step_bias_sum,
        log_decay_sum,
        skip_sum,
        summed_grads[10],
        summed_grads[11],
        summed_grads[12],
        summed_grads[13],
        summed_grads[14],
        summed_grads[15],
    )


BF = jnp.bfloat16
F32 = jnp.float32


def dotf(left, right, dims):
    return lax.dot_general(left, right, (dims, ((), ())), preferred_element_type=F32)


def mm(left, right):
    return dotf(left, right, ((left.ndim - 1,), (0,)))


def mm_nt(left, right):
    return dotf(left, right, ((1,), (1,)))


def mm_tn(left, right):
    return dotf(left, right, ((0,), (0,)))


MESH = pl.DeviceIdType.MESH
PLANE = 8


def plane():
    me = lax.axis_index(CTX)
    sibling = me + 1 - 2 * (me % 2)
    by_x = me + 2 - 4 * ((me // 2) % 2)
    by_y = me + 4 - 8 * (me // 4)
    return me, sibling, by_x, by_y


def unused(kernel, used, extra):
    def call(*refs):
        return kernel(*refs[:used], *refs[used + extra :])

    return call


def greet(peers):
    barrier = pltpu.get_barrier_semaphore()
    for axis, other in peers:
        pl.semaphore_signal(barrier, inc=1, device_id={axis: other}, device_id_type=MESH)
    pl.semaphore_wait(barrier, len(peers))


def remote(src, dst, send_sem, recv_sem, axis, to):
    return pltpu.make_async_remote_copy(
        src_ref=src,
        dst_ref=dst,
        send_sem=send_sem,
        recv_sem=recv_sem,
        device_id={axis: to},
        device_id_type=MESH,
    )


def together(*tasks):
    tasks = list(tasks)
    while tasks:
        for task in list(tasks):
            if next(task, None) is None:
                tasks.remove(task)


def other_places(axis, count):
    place = lax.axis_index(axis)
    return [(axis, (place + j) % count) for j in range(1, count)]


def gather_steps(pieces, x_ref, o_ref, own_sem, send_sem, recv_sem):
    rows = x_ref.shape[0]
    n = rows // pieces
    half = pieces // 2
    me, sibling, by_x, by_y = plane()
    across = by_x + by_y - me
    keep = pltpu.make_async_copy(x_ref, o_ref.at[pl.ds(me * rows, rows)], own_sem)
    keep.start()
    started = []

    def at(block, piece):
        return o_ref.at[pl.ds(block * rows + piece * n, n)]

    def go(src, block, piece, kind, to, slot):
        copy = remote(
            src, at(block, piece), send_sem.at[slot, piece], recv_sem.at[kind, piece], CTX, to
        )
        copy.start()
        started.append(copy)

    def arrived(block, piece, kind):
        here = at(block, piece)
        remote(here, here, send_sem.at[0, piece], recv_sem.at[kind, piece], CTX, sibling).wait_recv()

    for i in range(pieces):
        a, b = i, pieces - 1 - i
        go(x_ref.at[pl.ds(a * n, n)], me, a, 1, by_x, 1)
        go(x_ref.at[pl.ds(b * n, n)], me, b, 2, by_y, 2)
    for i in range(pieces):
        go(x_ref.at[pl.ds(i * n, n)], me, i, 0, sibling, 0)
    yield True
    for i in range(pieces):
        a, b = i, pieces - 1 - i
        arrived(by_x, a, 1)
        if i < half:
            go(at(by_x, a), by_x, a, 5, by_y, 5)
        go(at(by_x, a), by_x, a, 3, sibling, 3)
        arrived(by_y, b, 2)
        if i < half:
            go(at(by_y, b), by_y, b, 5, by_x, 5)
        go(at(by_y, b), by_y, b, 4, sibling, 4)
        yield True
    for i in range(half):
        for p in (i, pieces - 1 - i):
            arrived(across, p, 5)
            go(at(across, p), across, p, 6, sibling, 6)
        yield True
    shift = sibling - me
    for p in range(pieces):
        arrived(sibling, p, 0)
        arrived(by_x + shift, p, 3)
        arrived(by_y + shift, p, 4)
        arrived(across + shift, p, 6)
    for copy in started:
        copy.wait_send()
    keep.wait()


def chain_steps(pieces, count, x_ref, o_ref, own_sem, send_sem, recv_sem):
    mine = lax.axis_index(FSDP)
    n = x_ref.shape[0] // pieces
    up, down = mine + 1, mine - 1
    has_up, has_down = mine < count - 1, mine > 0
    keep = pltpu.make_async_copy(x_ref, o_ref.at[mine], own_sem)
    keep.start()

    def copy(src, block, piece, way, hop, to):
        return remote(
            src,
            o_ref.at[block, pl.ds(piece * n, n)],
            send_sem.at[way, hop, piece],
            recv_sem.at[way, hop, piece],
            FSDP,
            to,
        )

    def own(piece):
        return x_ref.at[pl.ds(piece * n, n)]

    for p in range(pieces):

        @pl.when(has_up)
        def _(p=p):
            copy(own(p), mine, p, 0, 0, up).start()

        @pl.when(has_down)
        def _(p=p):
            copy(own(p), mine, p, 1, 0, down).start()

    yield True
    for d in range(1, count):
        for p in range(pieces):

            @pl.when(mine >= d)
            def _(d=d, p=p):
                here = o_ref.at[mine - d, pl.ds(p * n, n)]
                copy(here, mine - d, p, 0, d - 1, down).wait_recv()

                @pl.when(has_up)
                def _():
                    copy(here, mine - d, p, 0, d, up).start()

            @pl.when(mine + d < count)
            def _(d=d, p=p):
                here = o_ref.at[mine + d, pl.ds(p * n, n)]
                copy(here, mine + d, p, 1, d - 1, up).wait_recv()

                @pl.when(has_down)
                def _():
                    copy(here, mine + d, p, 1, d, down).start()

            yield True
    for d in range(count - 1):
        for p in range(pieces):

            @pl.when((mine >= d) & has_up)
            def _(d=d, p=p):
                copy(own(p), mine - d, p, 0, d, up).wait_send()

            @pl.when((mine + d < count) & has_down)
            def _(d=d, p=p):
                copy(own(p), mine + d, p, 1, d, down).wait_send()

    keep.wait()


def chain_scratch(pieces, count):
    return [
        pltpu.SemaphoreType.DMA,
        pltpu.SemaphoreType.DMA((2, count - 1, pieces)),
        pltpu.SemaphoreType.DMA((2, count - 1, pieces)),
    ]


def gather_kernel(pieces, *refs):
    me, sibling, by_x, by_y = plane()
    greet([(CTX, sibling), (CTX, by_x), (CTX, by_y)])
    together(gather_steps(pieces, *refs))


def gather_tokens(block, ids, pieces=4, waits=()):
    rows, cols = block.shape
    return pl.pallas_call(
        unused(partial(gather_kernel, pieces), 1, len(waits)),
        out_shape=jax.ShapeDtypeStruct((PLANE * rows, cols), block.dtype),
        in_specs=[pl.BlockSpec(memory_space=pl.ANY)] * (1 + len(waits)),
        out_specs=pl.BlockSpec(memory_space=pl.ANY),
        scratch_shapes=[
            pltpu.SemaphoreType.DMA,
            pltpu.SemaphoreType.DMA((7, pieces)),
            pltpu.SemaphoreType.DMA((7, pieces)),
        ],
        cost_estimate=lasting(22 if cols > 1024 else 8),
        compiler_params=pltpu.CompilerParams(collective_id=next(ids), has_side_effects=True),
    )(block, *waits)


def scatter_steps(
    seqs, p_ref, o_ref, own, got, out, rx, ry, dx, dy, own_sem, send_sem, recv_sem, make=None
):
    rows = o_ref.shape[0]
    h = rows // 2
    me, sibling, by_x, by_y = plane()
    across = by_x + by_y - me
    shift = sibling - me
    top, low = pl.ds(0, h), pl.ds(h, h)
    loads, sends = [], []
    for k, block in enumerate((across, by_x, by_y, me)):
        if make is not None:
            make(block // 2)
        for j in range(2):
            copy = remote(
                p_ref.at[pl.ds((block + shift) * rows + j * h, h)],
                got.at[k, pl.ds(j * h, h)],
                send_sem.at[k * 2 + j],
                recv_sem.at[k * 2 + j],
                CTX,
                sibling,
            )
            copy.start()
            sends.append(copy)
            load = pltpu.make_async_copy(
                p_ref.at[pl.ds(block * rows + j * h, h)],
                own.at[k, pl.ds(j * h, h)],
                own_sem.at[k * 2 + j],
            )
            load.start()
            loads.append(load)

    def pair(k, j):
        sends[k * 2 + j].wait_recv()
        loads[k * 2 + j].wait()
        part = pl.ds(j * h, h)
        return own[k, part].astype(F32) + got[k, part].astype(F32)

    def put(part, total):
        if not seqs:
            o_ref[part] = total
            return
        chunk = total.shape[1] // (PLANE * seqs)
        per = 128 // chunk
        for k in range(total.shape[1] // 128):
            blocks = [(n % seqs) * PLANE + n // seqs for n in range(k * per, (k + 1) * per)]
            o_ref[part, k * 128 : (k + 1) * 128] = jnp.concatenate(
                [total[:, b * chunk : (b + 1) * chunk] for b in blocks], axis=1
            )

    def go(src, dst, slot, to):
        copy = remote(src, dst, send_sem.at[slot], recv_sem.at[slot], CTX, to)
        copy.start()
        sends.append(copy)
        return copy

    yield True
    out[0, top] = pair(0, 0).astype(out.dtype)
    across_x = go(out.at[0, top], dx, 8, by_x)
    out[0, low] = pair(0, 1).astype(out.dtype)
    across_y = go(out.at[0, low], dy, 9, by_y)
    out[1, top] = pair(1, 0).astype(out.dtype)
    x_top = go(out.at[1, top], rx.at[top], 10, by_x)
    out[2, low] = pair(2, 1).astype(out.dtype)
    y_low = go(out.at[2, low], ry.at[low], 11, by_y)
    yield True
    across_y.wait_recv()
    out[1, low] = (pair(1, 1) + dy[...].astype(F32)).astype(out.dtype)
    x_low = go(out.at[1, low], rx.at[low], 12, by_x)
    across_x.wait_recv()
    out[2, top] = (pair(2, 0) + dx[...].astype(F32)).astype(out.dtype)
    y_top = go(out.at[2, top], ry.at[top], 13, by_y)
    yield True
    first, second = pair(3, 0), pair(3, 1)
    x_top.wait_recv()
    y_top.wait_recv()
    put(top, first + rx[top].astype(F32) + ry[top].astype(F32))
    x_low.wait_recv()
    y_low.wait_recv()
    put(low, second + rx[low].astype(F32) + ry[low].astype(F32))
    for copy in sends:
        copy.wait_send()


def scatter_kernel(seqs, *refs):
    me, sibling, by_x, by_y = plane()
    greet([(CTX, sibling), (CTX, by_x), (CTX, by_y)])
    together(scatter_steps(seqs, *refs))


def scatter_scratch(rows, cols):
    def room(*shape):
        return pltpu.VMEM(shape, BF)

    return [
        room(4, rows, cols),
        room(4, rows, cols),
        room(3, rows, cols),
        room(rows, cols),
        room(rows, cols),
        room(rows // 2, cols),
        room(rows // 2, cols),
        pltpu.SemaphoreType.DMA((8,)),
        pltpu.SemaphoreType.DMA((14,)),
        pltpu.SemaphoreType.DMA((14,)),
    ]


def scatter_tokens(partial_sum, ids, waits=(), seqs=0):
    rows, cols = partial_sum.shape[0] // PLANE, partial_sum.shape[1]

    return pl.pallas_call(
        unused(partial(scatter_kernel, seqs), 1, len(waits)),
        out_shape=jax.ShapeDtypeStruct((rows, cols), F32),
        in_specs=[pl.BlockSpec(memory_space=pl.ANY)] * (1 + len(waits)),
        out_specs=pl.BlockSpec(memory_space=pltpu.VMEM),
        scratch_shapes=scatter_scratch(rows, cols),
        cost_estimate=lasting(22 if cols > 1024 else 8),
        compiler_params=pltpu.CompilerParams(
            collective_id=next(ids), has_side_effects=True, vmem_limit_bytes=40 * 2**20
        ),
    )(partial_sum.astype(BF), *waits)


def row_sum_kernel(x_ref, o_ref, got, send_sem, recv_sem):
    me = lax.axis_index(CTX)
    greet([(CTX, (me + j) % PLANE) for j in range(1, PLANE)])
    copies = []
    for j in range(1, PLANE):
        copy = remote(
            x_ref, got.at[j - 1], send_sem.at[j - 1], recv_sem.at[j - 1], CTX, (me + j) % PLANE
        )
        copy.start()
        copies.append(copy)
    total = x_ref[...]
    for j, copy in enumerate(copies):
        copy.wait_recv()
        total = total + got[j]
    o_ref[...] = total
    for copy in copies:
        copy.wait_send()


def row_sum(rows, ids, waits=()):
    tile = rows.reshape(8, -1)
    total = pl.pallas_call(
        unused(row_sum_kernel, 1, len(waits)),
        out_shape=jax.ShapeDtypeStruct(tile.shape, F32),
        in_specs=[pl.BlockSpec(memory_space=pltpu.VMEM)]
        + [pl.BlockSpec(memory_space=pl.ANY)] * len(waits),
        out_specs=pl.BlockSpec(memory_space=pltpu.VMEM),
        scratch_shapes=[
            pltpu.VMEM((PLANE - 1,) + tile.shape, F32),
            pltpu.SemaphoreType.DMA((PLANE - 1,)),
            pltpu.SemaphoreType.DMA((PLANE - 1,)),
        ],
        cost_estimate=lasting(5),
        compiler_params=pltpu.CompilerParams(collective_id=next(ids), has_side_effects=True),
    )(tile, *waits)
    return total.reshape(rows.shape)


def small_gather_steps(seqs, x_ref, o_ref, own_sem, send_sem, recv_sem):
    me, mine = lax.axis_index(CTX), lax.axis_index(FSDP)
    keep = pltpu.make_async_copy(x_ref, o_ref.at[me, mine], own_sem)
    keep.start()
    copies = []
    for j, (axis, other) in enumerate(other_places(FSDP, seqs)):
        copy = remote(x_ref, o_ref.at[me, mine], send_sem.at[j], recv_sem.at[j], axis, other)
        copy.start()
        copies.append(copy)
    yield True
    keep.wait()
    for copy in copies:
        copy.wait_recv()
    for j, (axis, other) in enumerate(other_places(CTX, PLANE)):
        k = seqs + j
        copy = remote(o_ref.at[me], o_ref.at[me], send_sem.at[k], recv_sem.at[k], axis, other)
        copy.start()
        copies.append(copy)
    for _ in range(8):
        yield True
    for copy in copies[seqs - 1 :]:
        copy.wait_recv()
    for copy in copies:
        copy.wait_send()


def columns(ref, place, count):
    return ref.at[:, pl.ds(pl.multiple_of(place * count, 128), count)]


def swap_steps(delay, patience, routes, own_sem, send_sem, recv_sem):
    me = lax.axis_index(CTX)
    for _ in range(delay):
        yield True
    keeps, copies = [], []
    for k, (part, land) in enumerate(routes):
        keep = pltpu.make_async_copy(part(me), land(me), own_sem.at[k])
        keep.start()
        keeps.append(keep)
    for j in (4, 2, 6, 3, 5, 7, 1):
        to = (me + j) % PLANE
        for k, (part, land) in enumerate(routes):
            copy = remote(part(to), land(me), send_sem.at[j, k], recv_sem.at[j, k], CTX, to)
            copy.start()
            copies.append(copy)
    for _ in range(patience):
        yield True
    for copy in copies:
        copy.wait_recv()
    for copy in copies:
        copy.wait_send()
    for keep in keeps:
        keep.wait()


def swap_scratch(routes):
    return [
        pltpu.SemaphoreType.DMA((routes,)),
        pltpu.SemaphoreType.DMA((PLANE, routes)),
        pltpu.SemaphoreType.DMA((PLANE, routes)),
    ]


def one_after(*tasks):
    for task in tasks:
        yield from task


def opening_kernel(seqs, pieces, *refs):
    tile, shard, hat, rows, query, zgate, channels, mixed, gate, up = refs[:10]
    o_tile, o_shard, o_hat, o_rows, conv, rest, ffn, o_conv = refs[10:18]
    sems = refs[18:]
    sems = [sems[k : k + 3] for k in range(0, len(sems), 3)]
    head = query.shape[1] // PLANE
    inner = zgate.shape[1] // PLANE
    half = gate.shape[1] // PLANE
    greet(other_places(FSDP, seqs) + other_places(CTX, PLANE))
    to_conv = [
        (lambda to: columns(channels, to, inner), lambda at: conv.at[at, :, :inner]),
        (lambda to: mixed.at[to], lambda at: conv.at[at, :, inner:]),
    ]
    to_rest = [
        (lambda to: columns(query, to, head), lambda at: rest.at[at, :, :head]),
        (lambda to: columns(zgate, to, inner), lambda at: rest.at[at, :, head:]),
    ]
    to_ffn = [
        (lambda to: columns(gate, to, half), lambda at: ffn.at[at, :, :half]),
        (lambda to: columns(up, to, half), lambda at: ffn.at[at, :, half:]),
    ]
    together(
        one_after(
            swap_steps(0, 1, to_conv, *sems[0]), chain_steps(4, seqs, conv, o_conv, *sems[1])
        ),
        chain_steps(4, seqs, shard, o_shard, *sems[2]),
        small_gather_steps(seqs, tile, o_tile, *sems[3]),
        gather_steps(pieces, hat, o_hat, *sems[4]),
        swap_steps(1, 8, to_rest, *sems[5]),
        swap_steps(3, 8, to_ffn, *sems[6]),
        one_after(delay_steps(5), gather_steps(pieces, rows, o_rows, *sems[7])),
    )


def delay_steps(turns):
    for _ in range(turns):
        yield True


def opening(tile, shard, hat, rows, query, zgate, channels, mixed, gate, up, seqs, ids, pieces=2):
    anywhere = pl.BlockSpec(memory_space=pl.ANY)
    krows = query.shape[0]
    inner = zgate.shape[1] // PLANE
    conv_cols = inner + mixed.shape[2]
    rest_cols = query.shape[1] // PLANE + inner
    ffn_cols = (gate.shape[1] + up.shape[1]) // PLANE

    def shape(*dims):
        return jax.ShapeDtypeStruct(dims, BF)

    def three(*dims):
        return [
            pltpu.SemaphoreType.DMA,
            pltpu.SemaphoreType.DMA(dims),
            pltpu.SemaphoreType.DMA(dims),
        ]

    return pl.pallas_call(
        partial(opening_kernel, seqs, pieces),
        out_shape=(
            shape(PLANE, seqs, *tile.shape),
            shape(seqs, *shard.shape),
            shape(PLANE * hat.shape[0], hat.shape[1]),
            shape(PLANE * rows.shape[0], rows.shape[1]),
            shape(PLANE, krows, conv_cols),
            shape(PLANE, krows, rest_cols),
            shape(PLANE, krows, ffn_cols),
            shape(seqs, PLANE, krows, conv_cols),
        ),
        in_specs=[anywhere] * 10,
        out_specs=(anywhere,) * 8,
        scratch_shapes=swap_scratch(2)
        + chain_scratch(4, seqs)
        + chain_scratch(4, seqs)
        + three(PLANE + seqs)
        + three(7, pieces)
        + swap_scratch(2)
        + swap_scratch(2)
        + three(7, pieces),
        cost_estimate=lasting(70),
        compiler_params=pltpu.CompilerParams(collective_id=next(ids), has_side_effects=True),
    )(tile, shard, hat, rows, query, zgate, channels, mixed, gate, up)


def small_scatter_steps(seqs, x_ref, o_ref, mine_ref, got, total, late, own_sem, send_sem, recv_sem):
    me, mine = lax.axis_index(CTX), lax.axis_index(FSDP)
    load = pltpu.make_async_copy(x_ref.at[me], mine_ref, own_sem)
    load.start()
    copies = []
    for j, (axis, to) in enumerate(other_places(CTX, PLANE)):
        copy = remote(x_ref.at[to], got.at[j], send_sem.at[j], recv_sem.at[j], axis, to)
        copy.start()
        copies.append(copy)
    yield True
    load.wait()
    acc = mine_ref[...]
    for j, copy in enumerate(copies):
        copy.wait_recv()
        acc = acc + got[j]
    total[...] = acc
    first = len(copies)
    for j, (axis, other) in enumerate(other_places(FSDP, seqs)):
        k = PLANE + j
        copy = remote(total.at[other], late.at[j], send_sem.at[k], recv_sem.at[k], axis, other)
        copy.start()
        copies.append(copy)
    yield True
    out = total[mine]
    for j, copy in enumerate(copies[first:]):
        copy.wait_recv()
        out = out + late[j]
    o_ref[...] = out
    for copy in copies:
        copy.wait_send()


def scatter_two_kernel(p_ref, q_ref, o_ref, oq_ref, *scratch):
    me, sibling, by_x, by_y = plane()
    greet([(CTX, sibling), (CTX, by_x), (CTX, by_y)])
    together(
        scatter_steps(0, p_ref, o_ref, *scratch[:10]),
        scatter_steps(0, q_ref, oq_ref, *scratch[10:]),
    )


def scatter_two(first, second, ids, waits=()):
    near = pl.BlockSpec(memory_space=pltpu.VMEM)
    shapes = [(x.shape[0] // PLANE, x.shape[1]) for x in (first, second)]
    return pl.pallas_call(
        unused(scatter_two_kernel, 2, len(waits)),
        out_shape=tuple(jax.ShapeDtypeStruct(shape, F32) for shape in shapes),
        in_specs=[pl.BlockSpec(memory_space=pl.ANY)] * (2 + len(waits)),
        out_specs=(near, near),
        scratch_shapes=scatter_scratch(*shapes[0]) + scatter_scratch(*shapes[1]),
        cost_estimate=lasting(28),
        compiler_params=pltpu.CompilerParams(
            collective_id=next(ids), has_side_effects=True, vmem_limit_bytes=40 * 2**20
        ),
    )(first, second, *waits)


def closing_kernel(
    seqs, g1, g2, g3, w1, w2, w3, rest, ffn, hat, o_ref, norm_ref, query, zgate, gate, up, p_ref, *scratch
):
    factors, own, sems = (g1, g2, g3, w1, w2, w3), scratch[:6], scratch[6]
    scratch = scratch[7:]
    loads = [
        pltpu.make_async_copy(factors[k], own[k], sems.at[k]) for k in range(len(factors))
    ]
    for load in loads:
        load.start()
    greet(other_places(CTX, PLANE))
    head = query.shape[1] // PLANE
    inner = zgate.shape[1] // PLANE
    half = gate.shape[1] // PLANE
    pair = 2 * o_ref.shape[0]

    def make(chip):
        rows = pl.ds(pl.multiple_of(chip * pair, pair), pair)
        total = 0.0
        for g, w in zip(own[:3], own[3:]):
            total = total + lax.dot_general(
                g[rows, :], w[...], (((1,), (1,)), ((), ())), preferred_element_type=F32
            )
        p_ref[rows, :] = total.astype(BF)

    from_rest = [
        (lambda to: rest.at[to, :, :head], lambda at: columns(query, at, head)),
        (lambda to: rest.at[to, :, head:], lambda at: columns(zgate, at, inner)),
    ]
    from_ffn = [
        (lambda to: ffn.at[to, :, :half], lambda at: columns(gate, at, half)),
        (lambda to: ffn.at[to, :, half:], lambda at: columns(up, at, half)),
    ]
    for load in loads:
        load.wait()
    together(
        swap_steps(0, 8, from_rest, *scratch[10:13]),
        swap_steps(0, 8, from_ffn, *scratch[13:]),
        scatter_steps(seqs, p_ref, o_ref, *scratch[:10], make=make),
    )
    total = jnp.sum(o_ref[...] * hat[...], axis=0, keepdims=True)
    norm_ref[...] = jnp.zeros_like(norm_ref)
    part = total.shape[1] // (PLANE * seqs)
    for k in range(PLANE * seqs):
        norm_ref[k // seqs, k % seqs, 0:1, 0:part] = total[:, k * part : (k + 1) * part]


def closing(grads, weights, rest, ffn, hat, head, seqs, ids, waits=()):
    anywhere = pl.BlockSpec(memory_space=pl.ANY)
    near = pl.BlockSpec(memory_space=pltpu.VMEM)
    length, cols = grads[0].shape[0], weights[0].shape[0]
    rows = length // PLANE
    _, krows, rest_cols = rest.shape
    half = ffn.shape[2] // 2

    def wide(count):
        return jax.ShapeDtypeStruct((krows, PLANE * count), BF)

    return pl.pallas_call(
        unused(partial(closing_kernel, seqs), 9, len(waits)),
        out_shape=(
            jax.ShapeDtypeStruct((rows, cols), F32),
            jax.ShapeDtypeStruct((PLANE, seqs, 8, 128), F32),
            wide(head),
            wide(rest_cols - head),
            wide(half),
            wide(half),
        ),
        in_specs=[anywhere] * 8 + [near] + [anywhere] * len(waits),
        out_specs=(near, near) + (anywhere,) * 4,
        scratch_shapes=[pltpu.VMEM((length, cols), BF)]
        + [pltpu.VMEM(x.shape, BF) for x in (*grads, *weights)]
        + [pltpu.SemaphoreType.DMA((6,))]
        + scatter_scratch(rows, cols)
        + swap_scratch(2)
        + swap_scratch(2),
        cost_estimate=lasting(35),
        compiler_params=pltpu.CompilerParams(
            collective_id=next(ids), has_side_effects=True, vmem_limit_bytes=60 * 2**20
        ),
    )(*grads, *weights, rest, ffn, hat, *waits)


def step_sum_steps(seqs, x_ref, o_ref, land, got, own_sem, send_sem, recv_sem):
    me, mine = lax.axis_index(CTX), lax.axis_index(FSDP)
    keep = pltpu.make_async_copy(x_ref.at[me], land.at[me], own_sem)
    keep.start()
    copies = []
    for j, (axis, to) in enumerate(other_places(CTX, PLANE)):
        copy = remote(x_ref.at[to], land.at[me], send_sem.at[j], recv_sem.at[j], axis, to)
        copy.start()
        copies.append(copy)
    yield True
    keep.wait()
    for copy in copies:
        copy.wait_recv()
    first = len(copies)
    for j, (axis, other) in enumerate(other_places(FSDP, seqs)):
        k = PLANE + j
        copy = remote(land.at[:, other], got.at[j], send_sem.at[k], recv_sem.at[k], axis, other)
        copy.start()
        copies.append(copy)
    yield True
    total = land[:, mine]
    for j, copy in enumerate(copies[first:]):
        copy.wait_recv()
        total = total + got[j]
    o_ref[...] = total
    for copy in copies:
        copy.wait_send()


def last_kernel(
    seqs, norm, ffn_gain, mixer_gain, channel, by_head, step, conv,
    small_ref, step_ref, channels, key, value,
    mixed, x_ref, st_ref, full, *scratch
):
    me = lax.axis_index(CTX)
    given = (norm, ffn_gain, mixer_gain, channel, by_head, step)
    near, sems, scratch = scratch[:6], scratch[6], scratch[7:]
    loads = [pltpu.make_async_copy(given[k], near[k], sems.at[k]) for k in range(len(given))]
    for load in loads:
        load.start()
    norm, ffn_gain, mixer_gain, channel, by_head, step = near
    devices = PLANE * seqs
    krows = conv.shape[1]
    bc = 2 * STATE // PLANE
    total = channels.shape[1] - 2 * STATE
    inner = total // PLANE
    kv = value.shape[1] // PLANE
    from_conv = [
        (lambda to: conv.at[to, :, :inner], lambda at: columns(channels, at, inner)),
        (lambda to: conv.at[to, :, inner:], lambda at: mixed.at[at]),
    ]
    x_ref[...] = jnp.zeros_like(x_ref)
    full[...] = jnp.zeros_like(full)
    st_ref[...] = jnp.zeros_like(st_ref)
    for load in loads:
        load.wait()
    kinds = channel.shape[0]
    full[0:kinds, pl.ds(pl.multiple_of(me * inner, 128), inner)] = channel[:, :inner]
    for k in range(PLANE):
        full[0:kinds, total + k * bc : total + (k + 1) * bc] = jnp.where(
            me == k, channel[:, inner:], 0.0
        )
    heads = by_head.shape[1]
    mine_only = [jnp.where(me == k, by_head[...], 0.0) for k in range(PLANE)]
    spread = jnp.concatenate(mine_only, axis=1)
    part, wide = ffn_gain.shape[1] // devices, full.shape[1] // devices
    for n in range(devices):
        c, f = n // seqs, n % seqs
        x_ref[c, f, 0:1, 0:part] = ffn_gain[:, n * part : (n + 1) * part]
        x_ref[c, f, 1:2, :] = norm[c, f, 0:1, :]
        x_ref[c, f, 3 : 3 + kinds, 0:wide] = full[0:kinds, n * wide : (n + 1) * wide]
        x_ref[c, f, 8:11, 0 : PLANE * heads] = spread
        at = (f * PLANE + c) * krows
        st_ref[c, f, 0:heads, 0:krows] = step[:, at : at + krows]
    part = inner // seqs
    for f in range(seqs):
        x_ref[me, f, 2:3, 0:part] = mixer_gain[:, f * part : (f + 1) * part]
    greet(other_places(FSDP, seqs) + other_places(CTX, PLANE))
    together(
        small_scatter_steps(seqs, x_ref, small_ref, *scratch[:7]),
        step_sum_steps(seqs, st_ref, step_ref, *scratch[7:12]),
        swap_steps(0, 2, from_conv, *scratch[12:]),
    )
    blocks = [mixed[k].astype(F32) for k in range(PLANE)]
    channels[:, total:] = jnp.concatenate([b[:, :bc] for b in blocks], axis=1).astype(BF)
    value[...] = jnp.concatenate([b[:, bc + kv :] for b in blocks], axis=1)
    half = kv // 2
    group = PLANE // KEY_VALUE_HEADS
    turned = []
    for k in range(0, PLANE, group):
        for at in (bc, bc + half):
            turned += [b[:, at : at + half] for b in blocks[k : k + group]]
    key[...] = jnp.concatenate(turned, axis=1)


def last_exchange(small, conv, inner, kv, seqs, ids):
    anywhere = pl.BlockSpec(memory_space=pl.ANY)
    near = pl.BlockSpec(memory_space=pltpu.VMEM)
    _, krows, cols = conv.shape

    def room(*shape):
        return pltpu.VMEM(shape, F32)

    two = [pltpu.SemaphoreType.DMA((PLANE + seqs,)), pltpu.SemaphoreType.DMA((PLANE + seqs,))]
    return pl.pallas_call(
        partial(last_kernel, seqs),
        out_shape=(
            jax.ShapeDtypeStruct((16, 128), F32),
            jax.ShapeDtypeStruct((PLANE, 8, 128), F32),
            jax.ShapeDtypeStruct((krows, PLANE * inner + 2 * STATE), BF),
            jax.ShapeDtypeStruct((krows, PLANE * kv), F32),
            jax.ShapeDtypeStruct((krows, PLANE * kv), F32),
        ),
        in_specs=[anywhere] * 7,
        out_specs=(near,) * 5,
        scratch_shapes=[
            pltpu.VMEM((PLANE, krows, cols - inner), BF),
            room(PLANE, seqs, 16, 128),
            room(PLANE, seqs, 8, 128),
            room(8, PLANE * inner + 2 * STATE),
            *[room(*x.shape) for x in small],
            pltpu.SemaphoreType.DMA((6,)),
            room(seqs, 16, 128),
            room(PLANE - 1, seqs, 16, 128),
            room(seqs, 16, 128),
            room(seqs - 1, 16, 128),
            pltpu.SemaphoreType.DMA,
            *two,
            room(PLANE, seqs, 8, 128),
            room(seqs - 1, PLANE, 8, 128),
            pltpu.SemaphoreType.DMA,
            *two,
        ]
        + swap_scratch(2),
        cost_estimate=lasting(15),
        compiler_params=pltpu.CompilerParams(
            collective_id=next(ids), has_side_effects=True, vmem_limit_bytes=40 * 2**20
        ),
    )(*small, conv)


def gather_rows(shard):
    return lax.all_gather(shard, FSDP, axis=0, tiled=False)


def scatter_rows(partial_sum):
    return lax.psum_scatter(partial_sum.astype(BF), FSDP, scatter_dimension=0, tiled=False)


def hold_kernel(*refs):
    pass


def hold(value, *earlier):
    anywhere = pl.BlockSpec(memory_space=pl.ANY)
    return pl.pallas_call(
        hold_kernel,
        out_shape=jax.ShapeDtypeStruct(value.shape, value.dtype),
        in_specs=[anywhere] * (1 + len(earlier)),
        out_specs=anywhere,
        input_output_aliases={0: 0},
    )(value, *earlier)


def lasting(us):
    return pl.CostEstimate(flops=int(us * 0.3e9), bytes_accessed=int(us * 0.3e6), transcendentals=0)


def same_document(documents):
    places = jnp.arange(documents.shape[0])
    return (documents[:, None] == documents[None, :]) & (places[:, None] >= places[None, :])


def rotate_some(values, places, first_pair, pairs):
    half = values.shape[-1] // 2
    freqs = ROPE_BASE ** (-(first_pair + jnp.arange(half)).astype(F32) / pairs)
    angles = places[:, None] * freqs[None, :]
    cosine, sine = jnp.cos(angles), jnp.sin(angles)
    first, second = values[:, :half], values[:, half:]
    return jnp.concatenate(
        [first * cosine - second * sine, second * cosine + first * sine], axis=-1
    )


def ssm_terms(step, rate, documents, chunks):
    length, heads = step.shape
    rows = length // chunks
    step_c = step.reshape(chunks, rows, heads).transpose(0, 2, 1)
    docs_c = documents.reshape(chunks, rows)
    prior = jnp.concatenate([jnp.full((1,), -1, docs_c.dtype), docs_c[:-1, -1]])
    last = docs_c[:, -1]
    level = jnp.cumsum(step_c * rate[None, :, None], axis=2)
    visible = jax.vmap(same_document)(docs_c)[:, None]
    spread = level[:, :, :, None] - level[:, :, None, :]
    pair = jnp.where(visible, jnp.exp(jnp.where(visible, spread, 0.0)), 0.0)
    entry = jnp.where((docs_c == prior[:, None])[:, None], jnp.exp(level), 0.0)
    tail = jnp.where((docs_c == last[:, None])[:, None], jnp.exp(level[:, :, -1:] - level), 0.0)
    carry = jnp.exp(level[:, :, -1]) * (last == prior).astype(F32)[:, None]
    k, j, i = (jnp.arange(chunks).reshape(shape) for shape in ((-1, 1, 1), (1, -1, 1), (1, 1, -1)))
    between = ((j < i) & (i < k))[..., None]
    reach = jnp.prod(jnp.where(between, carry[None, None], 1.0), axis=2)
    reach = jnp.where((j < k), reach, 0.0)
    return step_c, pair, entry, tail, carry, reach


def ssm_forward(xin, write, read, terms, skip):
    step_c, pair, entry, tail, carry, reach = terms
    chunks, heads, rows = step_c.shape
    x_c = xin.reshape(chunks, rows, heads, HP)
    write_c = write.reshape(chunks, rows, STATE)
    read_c = read.reshape(chunks, rows, STATE)
    gram = jnp.einsum("ktn,kun->ktu", read_c, write_c, preferred_element_type=F32)
    mixing = (pair * gram[:, None] * step_c[:, :, None, :]).astype(BF)
    inner = jnp.einsum("khtu,kuhp->kthp", mixing, x_c, preferred_element_type=F32)
    weight = (tail * step_c).transpose(0, 2, 1)
    weighted = (x_c.astype(F32) * weight[..., None]).astype(BF)
    local = jnp.einsum("kthp,ktn->khpn", weighted, write_c, preferred_element_type=F32)
    entering = jnp.sum(reach[:, :, :, None, None] * local[None], axis=1)
    reached = jnp.einsum(
        "ktn,khpn->kthp", read_c, entering.astype(BF), preferred_element_type=F32
    )
    y = (
        inner
        + reached * entry.transpose(0, 2, 1)[..., None]
        + skip[None, None, :, None] * x_c.astype(F32)
    )
    return y.reshape(chunks * rows, heads * HP), (gram, mixing, entering, reached)


def ssm_backward(grad, xin, write, read, terms, skip, rate, saved):
    step_c, pair, entry, tail, carry, reach = terms
    gram, mixing, entering, reached = saved
    chunks, heads, rows = step_c.shape
    x_c = xin.reshape(chunks, rows, heads, HP)
    x_f = x_c.astype(F32)
    write_c = write.reshape(chunks, rows, STATE)
    read_c = read.reshape(chunks, rows, STATE)
    g = grad.reshape(chunks, rows, heads, HP)
    g_low = g.astype(BF)
    skip_grad = jnp.sum(g * x_f, axis=(0, 1, 3))
    gx = skip[None, None, :, None] * g
    gx = gx + jnp.einsum("khtu,kthp->kuhp", mixing, g_low, preferred_element_type=F32)
    g_mixing = jnp.einsum("kthp,kuhp->khtu", g_low, x_c, preferred_element_type=F32)
    masked = g_mixing * pair
    g_gram = jnp.sum(masked * step_c[:, :, None, :], axis=1).astype(BF)
    both = masked * gram[:, None]
    column = jnp.sum(both, axis=2)
    row = jnp.sum(both * step_c[:, :, None, :], axis=3)
    g_level = row - step_c * column
    g_step = column
    entry_t = entry.transpose(0, 2, 1)[..., None]
    g_entry = jnp.sum(g * reached, axis=3).transpose(0, 2, 1)
    g_level = g_level + g_entry * entry
    g_reached = (g * entry_t).astype(BF)
    g_read = jnp.einsum("ktu,kun->ktn", g_gram, write_c, preferred_element_type=F32)
    g_write = jnp.einsum("ktu,ktn->kun", g_gram, read_c, preferred_element_type=F32)
    g_read = g_read + jnp.einsum(
        "kthp,khpn->ktn", g_reached, entering.astype(BF), preferred_element_type=F32
    )
    g_enter = jnp.einsum("kthp,ktn->khpn", g_reached, read_c, preferred_element_type=F32)
    leaving = jnp.sum(reach.transpose(1, 0, 2)[:, :, :, None, None] * g_enter[None], axis=1)
    g_carry = jnp.sum(entering * leaving, axis=(2, 3))
    leaving_low = leaving.astype(BF)
    weight = tail * step_c
    weight_t = weight.transpose(0, 2, 1)[..., None]
    seen = jnp.einsum("ktn,khpn->kthp", write_c, leaving_low, preferred_element_type=F32)
    gx = gx + weight_t * seen
    g_weight = jnp.sum(x_f * seen, axis=3).transpose(0, 2, 1)
    weighted = (x_f * weight_t).astype(BF)
    g_write = g_write + jnp.einsum(
        "kthp,khpn->ktn", weighted, leaving_low, preferred_element_type=F32
    )
    moved = g_weight * weight
    g_step = g_step + g_weight * tail
    g_level = g_level - moved
    end = jnp.sum(moved, axis=2) + g_carry * carry
    g_level = g_level.at[:, :, -1].add(end)
    g_la = jnp.flip(jnp.cumsum(jnp.flip(g_level, 2), axis=2), 2)
    g_step = g_step + g_la * rate[None, :, None]
    rate_grad = jnp.sum(g_la * step_c, axis=(0, 2))
    length = chunks * rows
    return (
        gx.reshape(length, heads * HP),
        g_write.reshape(length, STATE),
        g_read.reshape(length, STATE),
        g_step.transpose(0, 2, 1).reshape(length, heads),
        rate_grad,
        skip_grad,
    )


def head_parallel(
    hidden_in,
    out_grad,
    doc_ids,
    norm_gain,
    query_weight,
    key_matrix,
    value_matrix,
    attn_out_weight,
    mixer_gate_weight,
    conv_in_weight,
    step_weight,
    conv_weight,
    conv_bias,
    step_bias,
    log_decay,
    skip_gain,
    mixer_gain,
    mamba_out_weight,
    ffn_gain,
    gate_weight,
    up_weight,
    down_weight,
):
    ctx = lax.axis_size(CTX)
    seqs = lax.axis_size(FSDP)
    me = lax.axis_index(CTX)
    mine = lax.axis_index(FSDP)
    tokens, width = hidden_in.shape[1:]
    length = ctx * tokens
    krows = query_weight.shape[0]
    dssm = HS * HP
    heads = HS // ctx
    inner = heads * HP
    bc = 2 * STATE // ctx
    ff = gate_weight.shape[1] // ctx
    head = HEAD_SIZE * QUERY_HEADS // ctx
    taps = CONV - 1

    ids = itertools.count(1)

    def to_shards(x):
        return x.reshape(-1, ctx, seqs, krows).transpose(0, 2, 1, 3).reshape(-1, width)

    def from_shards(x):
        return x.reshape(-1, seqs, ctx, krows).transpose(0, 2, 1, 3).reshape(-1, width)

    small = jnp.concatenate(
        [
            norm_gain,
            ffn_gain,
            mixer_gain,
            conv_bias,
            conv_weight.reshape(-1),
            doc_ids[0].astype(BF),
            step_weight.reshape(-1),
        ]
    )
    small_size = small.size
    tile_rows = -(-small_size // 2048) * 16
    small = jnp.pad(small, (0, tile_rows * 128 - small_size)).reshape(tile_rows, 128)

    def by_column(weight, n):
        return weight.reshape(krows, ctx, n).transpose(1, 0, 2)

    kv_repeat = ctx // KEY_VALUE_HEADS
    kv = HEAD_SIZE // kv_repeat
    half = kv // 2
    key_pack = (
        key_matrix.reshape(krows, KEY_VALUE_HEADS, 2, kv_repeat, half)
        .transpose(1, 3, 0, 2, 4)
        .reshape(ctx, krows, kv)
    )
    mixed_pack = jnp.concatenate(
        [by_column(conv_in_weight[:, dssm:], bc), key_pack, by_column(value_matrix, kv)], axis=2
    )
    conv_cols = inner + bc + 2 * kv
    rest_cols = head + inner
    resid = hidden_in[0].astype(F32)
    scale_one = lax.rsqrt(jnp.mean(resid * resid, axis=-1, keepdims=True) + EPSILON)
    hat_one = resid * scale_one
    small, out_own, normed, grad_all, _, rest_pack, ffn_pack, conv_in_own = opening(
        small,
        jnp.concatenate([attn_out_weight, mamba_out_weight]),
        to_shards(hat_one.astype(BF)),
        out_grad[0],
        query_weight,
        mixer_gate_weight,
        conv_in_weight,
        mixed_pack,
        gate_weight,
        up_weight,
        seqs,
        ids,
    )
    conv_in_own = conv_in_own.reshape(width, conv_cols)
    small = small.reshape(ctx * seqs, -1)
    cuts = []
    at = 0
    for n in (norm_gain.size, ffn_gain.size, mixer_gain.size, conv_bias.size, conv_weight.size, tokens, step_weight.size):
        cuts.append(small[:, at : at + n])
        at += n
    gain_one = cuts[0].reshape(-1).astype(F32)
    gain_two = cuts[1].reshape(-1).astype(F32)
    gain_mix = lax.dynamic_slice_in_dim(cuts[2].reshape(-1), me * inner, inner).astype(F32)
    bias_all = cuts[3].reshape(-1)
    taps_all = cuts[4].reshape(ctx * seqs, CONV, -1).transpose(1, 0, 2).reshape(CONV, -1)
    documents = lax.dynamic_index_in_dim(
        cuts[5].reshape(ctx, seqs, tokens), mine, 1, False
    ).reshape(length).astype(jnp.int32)

    def own_channels(full):
        return jnp.concatenate(
            [
                lax.dynamic_slice_in_dim(full, me * inner, inner, full.ndim - 1),
                lax.dynamic_slice_in_dim(full, dssm + me * bc, bc, full.ndim - 1),
            ],
            axis=-1,
        )

    conv_taps = own_channels(taps_all).astype(F32)
    conv_shift = own_channels(bias_all).astype(F32)
    bias_own = lax.dynamic_slice_in_dim(step_bias, me * heads, heads)
    decay_own = lax.dynamic_slice_in_dim(log_decay, me * heads, heads)
    skip_own = lax.dynamic_slice_in_dim(skip_gain, me * heads, heads)

    rest_own = gather_rows(rest_pack).reshape(width, rest_cols)
    out_rows = attn_out_weight.shape[0]
    out_own = jnp.concatenate(
        [out_own[:, :out_rows].reshape(head, width), out_own[:, out_rows:].reshape(inner, width)]
    )
    ffn_own = gather_rows(ffn_pack).reshape(width, 2 * ff)
    down_own = gather_rows(down_weight).reshape(ff, width)
    step_own = lax.dynamic_slice_in_dim(
        cuts[6].reshape(ctx, seqs, krows, HS).transpose(1, 0, 2, 3).reshape(width, HS),
        me * heads,
        heads,
        1,
    )
    step_room = ((0, 0), (0, 128 - heads))
    step_wide = jnp.pad(step_own, step_room)

    normed = (normed.astype(F32) * to_shards(gain_one[None])).astype(BF)
    conv_all = mm(normed, conv_in_own)
    rest_all = mm(normed, rest_own)
    conv_lin = conv_all[:, : inner + bc].astype(BF).astype(F32)
    k_lin = conv_all[:, inner + bc : inner + bc + kv]
    v_lin = conv_all[:, inner + bc + kv :]
    step_lin = mm(normed, step_own)
    q_lin = rest_all[:, :head]
    zgate = rest_all[:, head:]

    widened = jnp.concatenate([jnp.zeros((taps, inner + bc), F32), conv_lin], axis=0)
    widened_docs = jnp.concatenate([jnp.full((taps,), -1, jnp.int32), documents])
    conv_act, conv_back = jax.vjp(
        partial(conv_part, widened_docs=widened_docs, documents=documents),
        widened,
        conv_taps,
        conv_shift,
    )
    conv_act = conv_act.astype(BF)
    places = jnp.arange(length).astype(F32)
    first_pair = (me % kv_repeat) * half
    key_turned, unturn_key = jax.vjp(
        lambda lin: rotate_some(lin, places, first_pair, HEAD_SIZE // 2), k_lin
    )
    shared = jnp.concatenate(
        [conv_act[:, inner:], key_turned.astype(BF), v_lin.astype(BF)], axis=1
    ).T
    shared = gather_tokens(shared, ids, 2).reshape(ctx, bc + 2 * kv, length)
    write_read = shared[:, :bc].reshape(2 * STATE, length).T
    write, read = write_read[:, :STATE], write_read[:, STATE:]
    group = me // kv_repeat * kv_repeat
    own_kv = lax.dynamic_slice_in_dim(shared[:, bc:], group, kv_repeat, 0)
    key = (
        own_kv[:, :kv]
        .reshape(kv_repeat, 2, half, length)
        .transpose(1, 0, 2, 3)
        .reshape(HEAD_SIZE, length)
        .T
    )
    value = own_kv[:, kv:].reshape(HEAD_SIZE, length).T
    xin = conv_act[:, :inner]

    query_turned, unturn = jax.vjp(
        partial(rotate, places=places), q_lin.reshape(length, head // HEAD_SIZE, HEAD_SIZE)
    )
    query = query_turned.astype(BF)
    visible = same_document(documents)
    scores = jnp.einsum("thd,ud->htu", query, key, preferred_element_type=F32) * HEAD_SIZE**-0.5
    scores = jnp.where(visible[None], scores, NEGATIVE_FLOOR)
    weights = jnp.where(
        visible[None], jnp.exp(scores - jnp.max(scores, axis=-1, keepdims=True)), 0.0
    )
    probs = weights / jnp.sum(weights, axis=-1, keepdims=True)
    probs_low = probs.astype(BF)
    attn_mix = jnp.einsum("htu,ud->thd", probs_low, value, preferred_element_type=F32)
    attn_low = attn_mix.reshape(length, head).astype(BF)

    step_size, step_back = jax.vjp(
        lambda lin, bias: jax.nn.softplus(lin + bias[None, :]), step_lin, bias_own
    )
    rate = -jnp.exp(decay_own)
    terms = ssm_terms(step_size, rate, documents, ctx)
    y, saved = ssm_forward(xin, write, read, terms, skip_own)
    gated, gated_back = jax.vjp(lambda a, z: a * jax.nn.silu(z), y, zgate)
    mean_square = row_sum(jnp.sum(gated * gated, axis=-1), ids) / dssm
    scale_mix = lax.rsqrt(mean_square + EPSILON)[:, None]
    ymix = (gated * scale_mix * gain_mix).astype(BF)

    mixed = jnp.concatenate([attn_low, ymix], axis=1)
    branch = scatter_tokens(mm(mixed, out_own), ids)
    mid = resid + branch
    scale_two = lax.rsqrt(jnp.mean(mid * mid, axis=-1, keepdims=True) + EPSILON)
    normed_two = gather_tokens(to_shards((mid * scale_two * gain_two).astype(BF)), ids)

    gate_up = mm(normed_two, ffn_own)
    gate_lin, up_lin = gate_up[:, :ff], gate_up[:, ff:]
    sigmoid_gate = jax.nn.sigmoid(gate_lin)
    silu_gate = gate_lin * sigmoid_gate
    hidden = (silu_gate * up_lin).astype(BF)
    grad_hidden = mm_nt(grad_all, down_own)
    grad_gate = (
        grad_hidden * up_lin * (sigmoid_gate + silu_gate * (1.0 - sigmoid_gate))
    ).astype(BF)
    grad_up = (grad_hidden * silu_gate).astype(BF)
    grad_gu = jnp.concatenate([grad_gate, grad_up], axis=1)
    down_grad = scatter_rows(mm_tn(hidden, grad_all).reshape(seqs, ff // seqs, width))
    ffn_grad = mm_tn(normed_two, grad_gu).reshape(seqs, ctx, krows, 2 * ff).astype(BF)
    grad_n2 = scatter_tokens(mm_nt(grad_gu, ffn_own), ids, (ffn_grad,), seqs=seqs)
    ffn_grad = scatter_rows(ffn_grad)

    turned = grad_n2 * gain_two
    hat_two = mid * scale_two
    ffn_gain_grad = jnp.sum(grad_n2 * hat_two, axis=0, keepdims=True)
    grad_mid = out_grad[0].astype(F32) + scale_two * (
        turned - hat_two * jnp.mean(turned * hat_two, axis=-1, keepdims=True)
    )
    branch_grad = hold(gather_tokens(grad_mid.astype(BF), ids), down_grad)

    out_grad_own = mm_tn(mixed, branch_grad).astype(BF)
    out_part = jnp.concatenate(
        [
            out_grad_own[:head].reshape(seqs, -1, width),
            out_grad_own[head:].reshape(seqs, -1, width),
        ],
        axis=1,
    )
    out_grad_own = scatter_rows(hold(out_part, ffn_grad))
    grad_mixed = mm_nt(branch_grad, out_own)
    grad_attn = grad_mixed[:, :head].astype(BF).reshape(length, -1, HEAD_SIZE)
    grad_ymix = grad_mixed[:, head:]

    grad_prob = jnp.einsum("thd,ud->htu", grad_attn, value, preferred_element_type=F32)
    delta = jnp.sum(probs * grad_prob, axis=-1, keepdims=True)
    grad_score = (probs * (grad_prob - delta)).astype(BF)
    grad_query = (
        jnp.einsum("htu,ud->thd", grad_score, key, preferred_element_type=F32) * HEAD_SIZE**-0.5
    )
    grad_key = (
        jnp.einsum("htu,thd->ud", grad_score, query, preferred_element_type=F32) * HEAD_SIZE**-0.5
    )
    grad_value = jnp.einsum("htu,thd->ud", probs_low, grad_attn, preferred_element_type=F32)
    grad_q_lin = unturn(grad_query)[0].reshape(length, head).astype(BF)

    hat = gated * scale_mix
    turned_mix = grad_ymix * gain_mix
    mixer_gain_grad = jnp.sum(grad_ymix * hat, axis=0, keepdims=True)
    along = row_sum(jnp.sum(turned_mix * hat, axis=-1), ids, (down_grad,))[:, None] / dssm
    grad_gated = scale_mix * (turned_mix - hat * along)
    grad_y, grad_zgate = gated_back(grad_gated)

    grad_rest = jnp.concatenate([grad_q_lin, grad_zgate.astype(BF)], axis=1)
    rest_part = mm_tn(normed, grad_rest).reshape(seqs, ctx, krows, rest_cols).astype(BF)

    grad_xin, grad_write, grad_read, grad_step, grad_rate, skip_grad = ssm_backward(
        grad_y, xin, write, read, terms, skip_own, rate, saved
    )
    grad_key = (
        grad_key.T.reshape(2, kv_repeat, half, length)
        .transpose(1, 0, 2, 3)
        .reshape(kv_repeat, kv, length)
    )
    grad_kv = jnp.concatenate([grad_key, grad_value.T.reshape(kv_repeat, kv, length)], axis=1)
    grad_kv = lax.dynamic_update_slice_in_dim(
        jnp.zeros((ctx, 2 * kv, length), BF), grad_kv.astype(BF), group, 0
    )
    grad_shared = jnp.concatenate([grad_write, grad_read], axis=1).astype(BF)
    grad_shared = jnp.concatenate([grad_shared.T.reshape(ctx, bc, length), grad_kv], axis=1)
    grad_shared, last = scatter_two(
        grad_shared.reshape(ctx * (bc + 2 * kv), length),
        mm(hidden, down_own).astype(BF),
        ids,
        (ffn_grad, rest_part),
    )
    block_out = (mid + last).astype(BF)
    grad_shared = grad_shared.T
    grad_k_lin = unturn_key(grad_shared[:, bc : bc + kv])[0].astype(BF)
    grad_v_lin = grad_shared[:, bc + kv :].astype(BF)
    grad_shared = grad_shared[:, :bc]
    grad_widened, taps_grad, shift_grad = conv_back(
        jnp.concatenate([grad_xin, grad_shared], axis=1)
    )
    grad_step_lin, step_bias_grad = step_back(grad_step)
    log_decay_grad = grad_rate * rate
    grad_conv = jnp.concatenate(
        [grad_widened[taps:].astype(BF), grad_k_lin, grad_v_lin], axis=1
    )
    grad_step_low = grad_step_lin.astype(BF)
    step_grad = mm_tn(grad_step_low, normed)
    rest_grad = scatter_rows(rest_part)
    conv_grad = mm_tn(normed, grad_conv).reshape(seqs, ctx, krows, conv_cols)
    conv_grad = scatter_rows(conv_grad)
    grad_normed, norm_rows, query_grad, zgate_grad, gate_grad, up_grad = closing(
        (grad_conv, grad_rest, jnp.pad(grad_step_low, step_room)),
        (conv_in_own, rest_own, step_wide),
        rest_grad,
        ffn_grad,
        hat_one,
        head,
        seqs,
        ids,
        (out_grad_own,),
    )

    sums, step_sums, channels_grad, key_grad, value_grad = last_exchange(
        (
            norm_rows,
            ffn_gain_grad,
            mixer_gain_grad,
            jnp.concatenate([shift_grad[None], taps_grad]),
            jnp.stack([step_bias_grad, log_decay_grad, skip_grad]),
            step_grad,
        ),
        conv_grad,
        inner,
        kv,
        seqs,
        ids,
    )
    step_grad = step_sums[:, :heads, :krows].reshape(HS, krows).T

    turned_one = grad_normed * gain_one
    input_grad = (
        grad_mid
        + scale_one
        * (turned_one - hat_one * jnp.mean(turned_one * hat_one, axis=-1, keepdims=True))
    ).astype(BF)

    return (
        block_out[None],
        input_grad[None],
        sums[1, :krows],
        query_grad.astype(F32),
        key_grad,
        value_grad,
        out_grad_own[:out_rows].astype(F32),
        zgate_grad.astype(F32),
        channels_grad.astype(F32),
        step_grad,
        sums[4 : 4 + CONV, : conv_weight.shape[1]],
        sums[3, : conv_bias.size],
        sums[8, :HS],
        sums[9, :HS],
        sums[10, :HS],
        sums[2, : mixer_gain.size],
        out_grad_own[out_rows:].astype(F32),
        sums[0, :krows],
        gate_grad.astype(F32),
        up_grad.astype(F32),
        down_grad.astype(F32),
    )


def solution(mesh):
    placed = (
        P(FSDP, CTX, None),
        P(FSDP, CTX, None),
        P(FSDP, CTX),
        P((CTX, FSDP)),
        P((CTX, FSDP), None),
        P((CTX, FSDP), None),
        P((CTX, FSDP), None),
        P((CTX, FSDP), None),
        P((CTX, FSDP), None),
        P((CTX, FSDP), None),
        P((CTX, FSDP), None),
        P(None, (CTX, FSDP)),
        P((CTX, FSDP)),
        P(),
        P(),
        P(),
        P((CTX, FSDP)),
        P((CTX, FSDP), None),
        P((CTX, FSDP)),
        P((CTX, FSDP), None),
        P((CTX, FSDP), None),
        P((CTX, FSDP), None),
    )
    ctx = mesh.shape[CTX]
    whole_heads = ctx == PLANE and QUERY_HEADS % ctx == 0 and HS % ctx == 0
    return jax.shard_map(
        head_parallel if whole_heads else on_device,
        mesh=mesh,
        in_specs=placed,
        out_specs=(
            P(FSDP, CTX, None),
            P(FSDP, CTX, None),
            P((CTX, FSDP)),
            P((CTX, FSDP), None),
            P((CTX, FSDP), None),
            P((CTX, FSDP), None),
            P((CTX, FSDP), None),
            P((CTX, FSDP), None),
            P((CTX, FSDP), None),
            P((CTX, FSDP), None),
            P(None, (CTX, FSDP)),
            P((CTX, FSDP)),
            P(),
            P(),
            P(),
            P((CTX, FSDP)),
            P((CTX, FSDP), None),
            P((CTX, FSDP)),
            P((CTX, FSDP), None),
            P((CTX, FSDP), None),
            P((CTX, FSDP), None),
        ),
        check_vma=False,
    )
```

```python
from functools import partial
import itertools
import math

import jax
import jax.numpy as jnp
from jax import lax
from jax.experimental import pallas as pl
from jax.experimental.pallas import tpu as pltpu
from jax.sharding import PartitionSpec as P

CTX = "ctx"
FSDP = "fsdp"
QUERY_HEADS = 8
KEY_VALUE_HEADS = 2
HEAD_SIZE = 128
HS = 48
HP = 64
STATE = 256
CONV = 4


EPSILON = 1e-05
ROPE_BASE = 100000000000.0
NEGATIVE_FLOOR = -1e30
HIGHEST = lax.Precision.HIGHEST


def shifted(value, axis, steps):
    count = lax.axis_size(axis)
    leading, last = (max(0, -steps), min(count, count - steps))
    return lax.ppermute(value, axis, [(source, source + steps) for source in range(leading, last)])


def prefix(shard, axis, combine, identity):
    devices, position = (lax.axis_size(axis), lax.axis_index(axis))
    everything = jax.tree.map(
        lambda part, kind: lax.all_gather(part.astype(kind), axis),
        shard,
        (jnp.bfloat16, jnp.bfloat16),
    )
    start = jax.tree.map(
        lambda part, zero: jnp.broadcast_to(jnp.asarray(zero, part.dtype), part.shape),
        shard,
        identity,
    )

    def step(k, before):
        reached = k < position
        new = combine(
            before, jax.tree.map(lambda part, own: part[k].astype(own.dtype), everything, shard)
        )
        return jax.tree.map(lambda a, b: jnp.where(reached, a, b), new, before)

    return lax.fori_loop(0, devices, step, start)


def carried_in(shard, axis, join, neutral):
    count = lax.axis_size(axis)
    place = lax.axis_index(axis)
    ahead = count - 1 - place
    gathered = jax.tree.map(
        lambda a, kind: lax.all_gather(a.astype(kind), axis),
        shard,
        jax.tree.map(lambda a: jnp.bfloat16 if a.dtype == jnp.float32 else a.dtype, shard),
    )
    state = jax.tree.map(lambda a, e: jnp.zeros_like(a) + jnp.asarray(e, a.dtype), shard, neutral)

    def one(step, state):
        source = count - 1 - step
        return join(
            state,
            jax.tree.map(
                lambda a, own: lax.dynamic_index_in_dim(a, source, 0, False).astype(own.dtype),
                gathered,
                shard,
            ),
        )

    return lax.fori_loop(0, ahead, one, state)


def rms_scale(values, gain):
    return values * lax.rsqrt(jnp.mean(values * values, axis=-1, keepdims=True) + EPSILON) * gain


def rotate(values, places):
    half_size = values.shape[-1] // 2
    freqs = ROPE_BASE ** (-jnp.arange(half_size).astype(jnp.float32) / half_size)
    angles = places[:, None] * freqs[None, :]
    cosine = jnp.cos(angles)[:, None, :]
    sine = jnp.sin(angles)[:, None, :]
    first = values[..., :half_size]
    second = values[..., half_size:]
    return jnp.concatenate(
        [first * cosine - second * sine, second * cosine + first * sine], axis=-1
    )


def conv_part(widened, taps_weight, bias, widened_docs, documents):
    row_length_total = documents.shape[0]
    total = bias[None, :]
    for tap_index in range(taps_weight.shape[0]):
        same_doc = (widened_docs[tap_index : tap_index + row_length_total] == documents)[:, None]
        total = total + jnp.where(
            same_doc,
            widened[tap_index : tap_index + row_length_total] * taps_weight[tap_index][None, :],
            0.0,
        )
    return jax.nn.silu(total)


def step_part(step_lin, step_bias, log_decay):
    return (jax.nn.softplus(step_lin + step_bias), -jnp.exp(log_decay))


def block_stats(mixer_in, write_proj, step_size, decay_rate, documents, prior_doc):
    decay_log = jnp.cumsum(step_size * decay_rate[None, :], axis=0)
    last_doc = documents[-1]
    tail_weight = (
        jnp.where(
            (documents == last_doc)[:, None], jnp.exp(decay_log[-1][None, :] - decay_log), 0.0
        )
        * step_size
    )
    state_loc = jnp.einsum(
        "thp,tn->hpn", mixer_in * tail_weight[:, :, None], write_proj, precision=HIGHEST
    )
    carry_decay = jnp.exp(decay_log[-1]) * (last_doc == prior_doc).astype(jnp.float32)
    return (state_loc, carry_decay)


def block_mix(
    mixer_in,
    write_proj,
    read_proj,
    step_size,
    decay_rate,
    skip_gain,
    state_in,
    documents,
    prior_doc,
):
    decay_log = jnp.cumsum(step_size * decay_rate[None, :], axis=0)
    positions = jnp.arange(documents.shape[0])
    visible = (documents[:, None] == documents[None, :]) & (
        positions[:, None] >= positions[None, :]
    )
    spread = decay_log.T[:, :, None] - decay_log.T[:, None, :]
    decay_pair = jnp.where(visible[None], jnp.exp(jnp.where(visible[None], spread, 0.0)), 0.0)
    gram = jnp.dot(read_proj, write_proj.T, precision=HIGHEST)
    mixing = decay_pair * gram[None] * step_size.T[:, None, :]
    inner = jnp.einsum("htu,uhp->thp", mixing, mixer_in, precision=HIGHEST)
    entry = jnp.where((documents == prior_doc)[:, None], jnp.exp(decay_log), 0.0)
    carried = jnp.einsum("tn,hpn->thp", read_proj, state_in, precision=HIGHEST) * entry[:, :, None]
    return inner + carried + skip_gain[None, :, None] * mixer_in


def gated_norm(flat_mixed, mixer_gate, gain):
    return rms_scale(flat_mixed * jax.nn.silu(mixer_gate), gain)


def chain_combine(earlier, later):
    decay_early, state_early = earlier
    decay_late, state_late = later
    return (decay_early * decay_late, decay_late[:, None, None] * state_early + state_late)


def piece_scores(piece, start, query_group, query_docs, query_places):
    key_segment, value_segment, docs_piece = piece
    segment_rows = key_segment.shape[0]
    heads_of_key = key_segment.reshape(segment_rows, KEY_VALUE_HEADS, HEAD_SIZE).transpose(1, 0, 2)
    heads_of_value = value_segment.reshape(segment_rows, KEY_VALUE_HEADS, HEAD_SIZE).transpose(
        1, 0, 2
    )
    key_places = (start + jnp.arange(segment_rows)).astype(jnp.float32)
    visible = (docs_piece.astype(jnp.float32)[None, :] == query_docs[:, None]) & (
        key_places[None, :] <= query_places[:, None]
    )
    scores = jnp.einsum(
        "gqd,gkd->gqk", query_group, heads_of_key, preferred_element_type=jnp.float32
    ) * HEAD_SIZE ** (-0.5)
    return (heads_of_key, heads_of_value, visible, jnp.where(visible[None], scores, NEGATIVE_FLOOR))


def fold_local(step_fn, whole, start_carry):
    row_length_total = whole[0].shape[0]
    tile_block = math.gcd(row_length_total, 512)

    def advance(block_index, carry):
        start = block_index * tile_block
        piece = tuple((lax.dynamic_slice_in_dim(member, start, tile_block, 0) for member in whole))
        return step_fn(carry, piece, start)

    return lax.fori_loop(0, row_length_total // tile_block, advance, start_carry)


def on_device(
    hidden_in,
    out_grad,
    doc_ids,
    norm_gain,
    query_weight,
    key_matrix,
    value_matrix,
    attn_out_weight,
    mixer_gate_weight,
    conv_in_weight,
    step_weight,
    conv_weight,
    conv_bias,
    step_bias,
    log_decay,
    skip_gain,
    mixer_gain,
    mamba_out_weight,
    ffn_gain,
    gate_weight,
    up_weight,
    down_weight,
):
    single_float = jnp.float32
    brain_float_half = jnp.bfloat16
    (
        norm_full,
        query_full,
        complete_key,
        value_full,
        attn_out_full,
        mixer_gate_full,
        conv_in_full,
        step_full,
        conv_full,
        conv_bias_full,
        mixer_gain_full,
        mamba_out_full,
    ) = (
        lax.all_gather(norm_gain, (CTX, FSDP), axis=0, tiled=True),
        lax.all_gather(query_weight, (CTX, FSDP), axis=0, tiled=True),
        lax.all_gather(key_matrix, (CTX, FSDP), axis=0, tiled=True),
        lax.all_gather(value_matrix, (CTX, FSDP), axis=0, tiled=True),
        lax.all_gather(attn_out_weight, (CTX, FSDP), axis=0, tiled=True),
        lax.all_gather(mixer_gate_weight, (CTX, FSDP), axis=0, tiled=True),
        lax.all_gather(conv_in_weight, (CTX, FSDP), axis=0, tiled=True),
        lax.all_gather(step_weight, (CTX, FSDP), axis=0, tiled=True),
        lax.all_gather(conv_weight, (CTX, FSDP), axis=1, tiled=True),
        lax.all_gather(conv_bias, (CTX, FSDP), axis=0, tiled=True),
        lax.all_gather(mixer_gain, (CTX, FSDP), axis=0, tiled=True),
        lax.all_gather(mamba_out_weight, (CTX, FSDP), axis=0, tiled=True),
    )
    tokens_per_worker = hidden_in.shape[1]
    head_cluster = QUERY_HEADS // KEY_VALUE_HEADS
    dssm = HS * HP
    taps = CONV - 1
    resid = hidden_in[0].astype(single_float)
    documents = doc_ids[0]
    places = (lax.axis_index(CTX) * tokens_per_worker + jnp.arange(tokens_per_worker)).astype(
        single_float
    )
    norm_one, norm_one_back = jax.vjp(rms_scale, resid, norm_full.astype(single_float))
    normalized_input = norm_one.astype(brain_float_half)
    query_lin = jnp.dot(normalized_input, query_full, preferred_element_type=single_float).reshape(
        tokens_per_worker, QUERY_HEADS, HEAD_SIZE
    )
    key_linear = jnp.dot(
        normalized_input, complete_key, preferred_element_type=single_float
    ).reshape(tokens_per_worker, KEY_VALUE_HEADS, HEAD_SIZE)
    query_turned, unturn_query = jax.vjp(partial(rotate, places=places), query_lin)
    rotated_key, unrotate_key = jax.vjp(partial(rotate, places=places), key_linear)
    rotated_query = query_turned.astype(brain_float_half)
    flattened_key = rotated_key.astype(brain_float_half).reshape(
        tokens_per_worker, KEY_VALUE_HEADS * HEAD_SIZE
    )
    value_lowered = jnp.dot(
        normalized_input, value_full, preferred_element_type=single_float
    ).astype(brain_float_half)
    docs_low = documents.astype(brain_float_half)
    query_group = (
        rotated_query.reshape(tokens_per_worker, KEY_VALUE_HEADS, head_cluster, HEAD_SIZE)
        .transpose(1, 2, 0, 3)
        .reshape(KEY_VALUE_HEADS, head_cluster * tokens_per_worker, HEAD_SIZE)
    )
    query_places = jnp.tile(places, head_cluster)
    query_docs = jnp.tile(documents.astype(single_float), head_cluster)

    def attend_piece(carry, piece, start):
        previous_maximum, total_old, summed_old = carry
        heads_of_key, heads_of_value, visible, scores = piece_scores(
            piece, start, query_group, query_docs, query_places
        )
        peak_new = jnp.maximum(previous_maximum, jnp.max(scores, axis=-1))
        weights = jnp.where(visible[None], jnp.exp(scores - peak_new[:, :, None]), 0.0)
        factor = jnp.exp(previous_maximum - peak_new)
        total_new = total_old * factor + jnp.sum(weights, axis=-1)
        summed_new = summed_old * factor[:, :, None] + jnp.einsum(
            "gqk,gkd->gqd",
            weights.astype(brain_float_half),
            heads_of_value,
            preferred_element_type=single_float,
        )
        return (peak_new, total_new, summed_new)

    rows_of_query = head_cluster * tokens_per_worker
    start_forward = (
        jnp.full((KEY_VALUE_HEADS, rows_of_query), NEGATIVE_FLOOR, single_float),
        jnp.zeros((KEY_VALUE_HEADS, rows_of_query), single_float),
        jnp.zeros((KEY_VALUE_HEADS, rows_of_query, HEAD_SIZE), single_float),
    )
    kv_whole = (
        lax.all_gather(flattened_key, CTX, axis=0, tiled=True),
        lax.all_gather(value_lowered, CTX, axis=0, tiled=True),
        lax.all_gather(docs_low, CTX, axis=0, tiled=True),
    )
    peak, total, summed = fold_local(attend_piece, kv_whole, start_forward)
    attention_cluster = summed / total[:, :, None]
    log_total = peak + jnp.log(total)
    attn_low = (
        attention_cluster.reshape(KEY_VALUE_HEADS, head_cluster, tokens_per_worker, HEAD_SIZE)
        .transpose(2, 0, 1, 3)
        .reshape(tokens_per_worker, QUERY_HEADS * HEAD_SIZE)
        .astype(brain_float_half)
    )
    attn_out = jnp.dot(attn_low, attn_out_full, preferred_element_type=single_float)
    mixer_gate = jnp.dot(normalized_input, mixer_gate_full, preferred_element_type=single_float)
    conv_lin = jnp.dot(normalized_input, conv_in_full, preferred_element_type=single_float).astype(
        brain_float_half
    )
    step_lin = jnp.dot(normalized_input, step_full, preferred_element_type=single_float)
    rim_rows, rim_docs = shifted(
        (conv_lin[tokens_per_worker - taps :], docs_low[tokens_per_worker - taps :]), CTX, 1
    )
    widened = jnp.concatenate([rim_rows, conv_lin], axis=0).astype(single_float)
    widened_docs = jnp.concatenate([rim_docs.astype(jnp.int32), documents])
    prior_doc = widened_docs[taps - 1]
    conv_act, conv_back = jax.vjp(
        partial(conv_part, widened_docs=widened_docs, documents=documents),
        widened,
        conv_full.astype(single_float),
        conv_bias_full.astype(single_float),
    )
    conv_vals = conv_act.astype(brain_float_half).astype(single_float)
    mixer_in = conv_vals[:, :dssm].reshape(tokens_per_worker, HS, HP)
    write_proj = conv_vals[:, dssm : dssm + STATE]
    read_proj = conv_vals[:, dssm + STATE :]
    (step_size, decay_rate), step_back = jax.vjp(step_part, step_lin, step_bias, log_decay)
    (state_loc, carry_decay), stats_back = jax.vjp(
        partial(block_stats, documents=documents, prior_doc=prior_doc),
        mixer_in,
        write_proj,
        step_size,
        decay_rate,
    )
    chain_identity = (jnp.ones_like(carry_decay), jnp.zeros_like(state_loc))
    _, state_in = prefix((carry_decay, state_loc), CTX, chain_combine, chain_identity)
    mixed, mix_back = jax.vjp(
        partial(block_mix, documents=documents, prior_doc=prior_doc),
        mixer_in,
        write_proj,
        read_proj,
        step_size,
        decay_rate,
        skip_gain,
        state_in,
    )
    ymix_vals, gate_back = jax.vjp(
        gated_norm,
        mixed.reshape(tokens_per_worker, dssm),
        mixer_gate,
        mixer_gain_full.astype(single_float),
    )
    ymix_low = ymix_vals.astype(brain_float_half)
    mamba_out = jnp.dot(ymix_low, mamba_out_full, preferred_element_type=single_float)
    ffn_gain_full, gate_full, up_full, down_full = (
        lax.all_gather(ffn_gain, (CTX, FSDP), axis=0, tiled=True),
        lax.all_gather(gate_weight, (CTX, FSDP), axis=0, tiled=True),
        lax.all_gather(up_weight, (CTX, FSDP), axis=0, tiled=True),
        lax.all_gather(down_weight, (CTX, FSDP), axis=0, tiled=True),
    )
    mid = resid + attn_out + mamba_out
    norm_two, norm_two_back = jax.vjp(rms_scale, mid, ffn_gain_full.astype(single_float))
    normed_two = norm_two.astype(brain_float_half)
    gate_lin = jnp.dot(normed_two, gate_full, preferred_element_type=single_float)
    up_lin = jnp.dot(normed_two, up_full, preferred_element_type=single_float)
    sigmoid_gate = jax.nn.sigmoid(gate_lin)
    silu_gate = gate_lin * sigmoid_gate
    hidden = (silu_gate * up_lin).astype(brain_float_half)
    block_out = (mid + jnp.dot(hidden, down_full, preferred_element_type=single_float)).astype(
        brain_float_half
    )
    grad_out = out_grad[0]
    down_grad_w = jnp.einsum("tf,td->fd", hidden, grad_out, preferred_element_type=single_float)
    grad_hidden = jnp.einsum("td,fd->tf", grad_out, down_full, preferred_element_type=single_float)
    grad_gate = (grad_hidden * up_lin * (sigmoid_gate + silu_gate * (1.0 - sigmoid_gate))).astype(
        brain_float_half
    )
    grad_up = (grad_hidden * silu_gate).astype(brain_float_half)
    gate_grad_w = jnp.einsum(
        "td,tf->df", normed_two, grad_gate, preferred_element_type=single_float
    )
    up_grad_w = jnp.einsum("td,tf->df", normed_two, grad_up, preferred_element_type=single_float)
    grad_normed_two = jnp.einsum(
        "tf,df->td", grad_gate, gate_full, preferred_element_type=single_float
    ) + jnp.einsum("tf,df->td", grad_up, up_full, preferred_element_type=single_float)
    grad_mid_norm, ffn_gain_grad = norm_two_back(grad_normed_two)
    grad_mid = grad_out.astype(single_float) + grad_mid_norm
    ffn_sums = (
        lax.psum_scatter(ffn_gain_grad, (CTX, FSDP), scatter_dimension=0, tiled=True),
        lax.psum_scatter(gate_grad_w, (CTX, FSDP), scatter_dimension=0, tiled=True),
        lax.psum_scatter(up_grad_w, (CTX, FSDP), scatter_dimension=0, tiled=True),
        lax.psum_scatter(down_grad_w, (CTX, FSDP), scatter_dimension=0, tiled=True),
    )
    branch_grad = grad_mid.astype(brain_float_half)
    attn_out_grad_w = jnp.einsum(
        "ti,td->id", attn_low, branch_grad, preferred_element_type=single_float
    )
    attention_gradient = jnp.einsum(
        "td,id->ti", branch_grad, attn_out_full, preferred_element_type=single_float
    ).astype(brain_float_half)
    grad_group = (
        attention_gradient.reshape(tokens_per_worker, KEY_VALUE_HEADS, head_cluster, HEAD_SIZE)
        .transpose(1, 2, 0, 3)
        .reshape(KEY_VALUE_HEADS, rows_of_query, HEAD_SIZE)
    )
    row_delta = jnp.sum(grad_group.astype(single_float) * attention_cluster, axis=-1)

    def attend_back(carry, piece, start):
        query_acc, kv_grad = carry
        heads_of_key, heads_of_value, visible, scores = piece_scores(
            piece, start, query_group, query_docs, query_places
        )
        segment_rows = heads_of_key.shape[1]
        probs = jnp.where(visible[None], jnp.exp(scores - log_total[:, :, None]), 0.0)
        prob_grad = jnp.einsum(
            "gqd,gkd->gqk", grad_group, heads_of_value, preferred_element_type=single_float
        )
        score_grad = (probs * (prob_grad - row_delta[:, :, None])).astype(brain_float_half)
        query_acc = query_acc + jnp.einsum(
            "gqk,gkd->gqd", score_grad, heads_of_key, preferred_element_type=single_float
        )
        key_portion = jnp.einsum(
            "gqk,gqd->kgd", score_grad, query_group, preferred_element_type=single_float
        ) * HEAD_SIZE ** (-0.5)
        value_portion = jnp.einsum(
            "gqk,gqd->kgd",
            probs.astype(brain_float_half),
            grad_group,
            preferred_element_type=single_float,
        )
        term = jnp.concatenate(
            [
                key_portion.reshape(segment_rows, KEY_VALUE_HEADS * HEAD_SIZE),
                value_portion.reshape(segment_rows, KEY_VALUE_HEADS * HEAD_SIZE),
            ],
            axis=1,
        )
        current = lax.dynamic_slice_in_dim(kv_grad, start, segment_rows, 0)
        kv_grad = lax.dynamic_update_slice_in_dim(kv_grad, current + term, start, 0)
        return (query_acc, kv_grad)

    start_back = (
        jnp.zeros((KEY_VALUE_HEADS, rows_of_query, HEAD_SIZE), single_float),
        jnp.zeros(
            (tokens_per_worker * lax.axis_size(CTX), 2 * KEY_VALUE_HEADS * HEAD_SIZE),
            single_float,
        ),
    )
    query_acc, kv_grad = fold_local(attend_back, kv_whole, start_back)
    local_key_value = lax.psum_scatter(
        kv_grad.astype(jnp.bfloat16), CTX, scatter_dimension=0, tiled=True
    ).astype(jnp.float32)
    query_turn_grad = (
        (query_acc * HEAD_SIZE ** (-0.5))
        .reshape(KEY_VALUE_HEADS, head_cluster, tokens_per_worker, HEAD_SIZE)
        .transpose(2, 0, 1, 3)
        .reshape(tokens_per_worker, QUERY_HEADS, HEAD_SIZE)
    )
    query_lin_grad = (
        unturn_query(query_turn_grad)[0]
        .reshape(tokens_per_worker, QUERY_HEADS * HEAD_SIZE)
        .astype(brain_float_half)
    )
    key_lin_grad = (
        unrotate_key(
            local_key_value[:, : KEY_VALUE_HEADS * HEAD_SIZE].reshape(
                tokens_per_worker, KEY_VALUE_HEADS, HEAD_SIZE
            )
        )[0]
        .reshape(tokens_per_worker, KEY_VALUE_HEADS * HEAD_SIZE)
        .astype(brain_float_half)
    )
    value_linear_gradient = local_key_value[:, KEY_VALUE_HEADS * HEAD_SIZE :].astype(
        brain_float_half
    )
    mamba_grad_w = jnp.einsum(
        "ti,td->id", ymix_low, branch_grad, preferred_element_type=single_float
    )
    grad_ymix = jnp.einsum(
        "td,id->ti", branch_grad, mamba_out_full, preferred_element_type=single_float
    )
    grad_mixed, grad_zgate, mixer_gain_grad = gate_back(grad_ymix)
    zgate_low = grad_zgate.astype(brain_float_half)
    (
        grad_in_mix,
        grad_write_mix,
        grad_read,
        grad_step_mix,
        grad_rate_mix,
        skip_grad,
        grad_state_in,
    ) = mix_back(grad_mixed.reshape(tokens_per_worker, HS, HP))
    _, state_later = carried_in((carry_decay, grad_state_in), CTX, chain_combine, chain_identity)
    decay_grad = jnp.sum(state_in * state_later, axis=(1, 2))
    grad_in_stats, grad_write_stats, grad_step_stats, grad_rate_stats = stats_back(
        (state_later, decay_grad)
    )
    grad_conv = jnp.concatenate(
        [
            (grad_in_mix + grad_in_stats).reshape(tokens_per_worker, dssm),
            grad_write_mix + grad_write_stats,
            grad_read,
        ],
        axis=1,
    )
    grad_widened, conv_weight_grad, conv_bias_grad = conv_back(grad_conv)
    rim_grad = shifted(grad_widened[:taps].astype(jnp.bfloat16), CTX, -1).astype(jnp.float32)
    conv_lin_grad = (
        grad_widened[taps:].at[tokens_per_worker - taps :].add(rim_grad).astype(brain_float_half)
    )
    step_lin_grad, step_bias_grad, log_decay_grad = step_back(
        (grad_step_mix + grad_step_stats, grad_rate_mix + grad_rate_stats)
    )
    step_lin_low = step_lin_grad.astype(brain_float_half)
    query_grad_w = jnp.einsum(
        "td,ti->di", normalized_input, query_lin_grad, preferred_element_type=single_float
    )
    key_grad_w = jnp.einsum(
        "td,ti->di", normalized_input, key_lin_grad, preferred_element_type=single_float
    )
    value_grad_w = jnp.einsum(
        "td,ti->di", normalized_input, value_linear_gradient, preferred_element_type=single_float
    )
    zgate_grad_w = jnp.einsum(
        "td,ti->di", normalized_input, zgate_low, preferred_element_type=single_float
    )
    conv_in_grad_w = jnp.einsum(
        "td,ti->di", normalized_input, conv_lin_grad, preferred_element_type=single_float
    )
    step_grad_w = jnp.einsum(
        "td,ti->di", normalized_input, step_lin_low, preferred_element_type=single_float
    )
    grad_normed = (
        jnp.einsum("ti,di->td", query_lin_grad, query_full, preferred_element_type=single_float)
        + jnp.einsum("ti,di->td", key_lin_grad, complete_key, preferred_element_type=single_float)
        + jnp.einsum(
            "ti,di->td", value_linear_gradient, value_full, preferred_element_type=single_float
        )
        + jnp.einsum("ti,di->td", zgate_low, mixer_gate_full, preferred_element_type=single_float)
        + jnp.einsum("ti,di->td", conv_lin_grad, conv_in_full, preferred_element_type=single_float)
        + jnp.einsum("ti,di->td", step_lin_low, step_full, preferred_element_type=single_float)
    )
    grad_resid_norm, norm_gain_grad = norm_one_back(grad_normed)
    input_grad = (grad_mid + grad_resid_norm).astype(brain_float_half)
    mixer_sums = (
        lax.psum_scatter(norm_gain_grad, (CTX, FSDP), scatter_dimension=0, tiled=True),
        lax.psum_scatter(query_grad_w, (CTX, FSDP), scatter_dimension=0, tiled=True),
        lax.psum_scatter(key_grad_w, (CTX, FSDP), scatter_dimension=0, tiled=True),
        lax.psum_scatter(value_grad_w, (CTX, FSDP), scatter_dimension=0, tiled=True),
        lax.psum_scatter(attn_out_grad_w, (CTX, FSDP), scatter_dimension=0, tiled=True),
        lax.psum_scatter(zgate_grad_w, (CTX, FSDP), scatter_dimension=0, tiled=True),
        lax.psum_scatter(conv_in_grad_w, (CTX, FSDP), scatter_dimension=0, tiled=True),
        lax.psum_scatter(step_grad_w, (CTX, FSDP), scatter_dimension=0, tiled=True),
        lax.psum_scatter(conv_weight_grad, (CTX, FSDP), scatter_dimension=1, tiled=True),
        lax.psum_scatter(conv_bias_grad, (CTX, FSDP), scatter_dimension=0, tiled=True),
        lax.psum_scatter(mixer_gain_grad, (CTX, FSDP), scatter_dimension=0, tiled=True),
        lax.psum_scatter(mamba_grad_w, (CTX, FSDP), scatter_dimension=0, tiled=True),
    )
    summed_grads = tuple(mixer_sums) + tuple(ffn_sums)
    step_bias_sum, log_decay_sum, skip_sum = lax.psum(
        (step_bias_grad, log_decay_grad, skip_grad), (CTX, FSDP)
    )
    return (
        block_out[None],
        input_grad[None],
        summed_grads[0],
        summed_grads[1],
        summed_grads[2],
        summed_grads[3],
        summed_grads[4],
        summed_grads[5],
        summed_grads[6],
        summed_grads[7],
        summed_grads[8],
        summed_grads[9],
        step_bias_sum,
        log_decay_sum,
        skip_sum,
        summed_grads[10],
        summed_grads[11],
        summed_grads[12],
        summed_grads[13],
        summed_grads[14],
        summed_grads[15],
    )


BF = jnp.bfloat16
F32 = jnp.float32


def dotf(left, right, dims):
    return lax.dot_general(left, right, (dims, ((), ())), preferred_element_type=F32)


def mm(left, right):
    return dotf(left, right, ((left.ndim - 1,), (0,)))


def mm_nt(left, right):
    return dotf(left, right, ((1,), (1,)))


def mm_tn(left, right):
    return dotf(left, right, ((0,), (0,)))


MESH = pl.DeviceIdType.MESH
PLANE = 8


def plane():
    me = lax.axis_index(CTX)
    sibling = me + 1 - 2 * (me % 2)
    by_x = me + 2 - 4 * ((me // 2) % 2)
    by_y = me + 4 - 8 * (me // 4)
    return me, sibling, by_x, by_y


def unused(kernel, used, extra):
    def call(*refs):
        return kernel(*refs[:used], *refs[used + extra :])

    return call


def greet(peers):
    barrier = pltpu.get_barrier_semaphore()
    for axis, other in peers:
        pl.semaphore_signal(barrier, inc=1, device_id={axis: other}, device_id_type=MESH)
    pl.semaphore_wait(barrier, len(peers))


def remote(src, dst, send_sem, recv_sem, axis, to):
    return pltpu.make_async_remote_copy(
        src_ref=src,
        dst_ref=dst,
        send_sem=send_sem,
        recv_sem=recv_sem,
        device_id={axis: to},
        device_id_type=MESH,
    )


def together(*tasks):
    tasks = list(tasks)
    while tasks:
        for task in list(tasks):
            if next(task, None) is None:
                tasks.remove(task)


def other_places(axis, count):
    place = lax.axis_index(axis)
    return [(axis, (place + j) % count) for j in range(1, count)]


def gather_steps(pieces, x_ref, o_ref, own_sem, send_sem, recv_sem):
    rows = x_ref.shape[0]
    n = rows // pieces
    half = pieces // 2
    me, sibling, by_x, by_y = plane()
    across = by_x + by_y - me
    keep = pltpu.make_async_copy(x_ref, o_ref.at[pl.ds(me * rows, rows)], own_sem)
    keep.start()
    started = []

    def at(block, piece):
        return o_ref.at[pl.ds(block * rows + piece * n, n)]

    def go(src, block, piece, kind, to, slot):
        copy = remote(
            src, at(block, piece), send_sem.at[slot, piece], recv_sem.at[kind, piece], CTX, to
        )
        copy.start()
        started.append(copy)

    def arrived(block, piece, kind):
        here = at(block, piece)
        remote(here, here, send_sem.at[0, piece], recv_sem.at[kind, piece], CTX, sibling).wait_recv()

    for i in range(pieces):
        a, b = i, pieces - 1 - i
        go(x_ref.at[pl.ds(a * n, n)], me, a, 1, by_x, 1)
        go(x_ref.at[pl.ds(b * n, n)], me, b, 2, by_y, 2)
    for i in range(pieces):
        go(x_ref.at[pl.ds(i * n, n)], me, i, 0, sibling, 0)
    yield True
    for i in range(pieces):
        a, b = i, pieces - 1 - i
        arrived(by_x, a, 1)
        if i < half:
            go(at(by_x, a), by_x, a, 5, by_y, 5)
        go(at(by_x, a), by_x, a, 3, sibling, 3)
        arrived(by_y, b, 2)
        if i < half:
            go(at(by_y, b), by_y, b, 5, by_x, 5)
        go(at(by_y, b), by_y, b, 4, sibling, 4)
        yield True
    for i in range(half):
        for p in (i, pieces - 1 - i):
            arrived(across, p, 5)
            go(at(across, p), across, p, 6, sibling, 6)
        yield True
    shift = sibling - me
    for p in range(pieces):
        arrived(sibling, p, 0)
        arrived(by_x + shift, p, 3)
        arrived(by_y + shift, p, 4)
        arrived(across + shift, p, 6)
    for copy in started:
        copy.wait_send()
    keep.wait()


def chain_steps(pieces, count, x_ref, o_ref, own_sem, send_sem, recv_sem):
    mine = lax.axis_index(FSDP)
    n = x_ref.shape[0] // pieces
    up, down = mine + 1, mine - 1
    has_up, has_down = mine < count - 1, mine > 0
    keep = pltpu.make_async_copy(x_ref, o_ref.at[mine], own_sem)
    keep.start()

    def copy(src, block, piece, way, hop, to):
        return remote(
            src,
            o_ref.at[block, pl.ds(piece * n, n)],
            send_sem.at[way, hop, piece],
            recv_sem.at[way, hop, piece],
            FSDP,
            to,
        )

    def own(piece):
        return x_ref.at[pl.ds(piece * n, n)]

    for p in range(pieces):

        @pl.when(has_up)
        def _(p=p):
            copy(own(p), mine, p, 0, 0, up).start()

        @pl.when(has_down)
        def _(p=p):
            copy(own(p), mine, p, 1, 0, down).start()

    yield True
    for d in range(1, count):
        for p in range(pieces):

            @pl.when(mine >= d)
            def _(d=d, p=p):
                here = o_ref.at[mine - d, pl.ds(p * n, n)]
                copy(here, mine - d, p, 0, d - 1, down).wait_recv()

                @pl.when(has_up)
                def _():
                    copy(here, mine - d, p, 0, d, up).start()

            @pl.when(mine + d < count)
            def _(d=d, p=p):
                here = o_ref.at[mine + d, pl.ds(p * n, n)]
                copy(here, mine + d, p, 1, d - 1, up).wait_recv()

                @pl.when(has_down)
                def _():
                    copy(here, mine + d, p, 1, d, down).start()

            yield True
    for d in range(count - 1):
        for p in range(pieces):

            @pl.when((mine >= d) & has_up)
            def _(d=d, p=p):
                copy(own(p), mine - d, p, 0, d, up).wait_send()

            @pl.when((mine + d < count) & has_down)
            def _(d=d, p=p):
                copy(own(p), mine + d, p, 1, d, down).wait_send()

    keep.wait()


def chain_scratch(pieces, count):
    return [
        pltpu.SemaphoreType.DMA,
        pltpu.SemaphoreType.DMA((2, count - 1, pieces)),
        pltpu.SemaphoreType.DMA((2, count - 1, pieces)),
    ]


def gather_kernel(pieces, *refs):
    me, sibling, by_x, by_y = plane()
    greet([(CTX, sibling), (CTX, by_x), (CTX, by_y)])
    together(gather_steps(pieces, *refs))


def gather_tokens(block, ids, pieces=4, waits=()):
    rows, cols = block.shape
    return pl.pallas_call(
        unused(partial(gather_kernel, pieces), 1, len(waits)),
        out_shape=jax.ShapeDtypeStruct((PLANE * rows, cols), block.dtype),
        in_specs=[pl.BlockSpec(memory_space=pl.ANY)] * (1 + len(waits)),
        out_specs=pl.BlockSpec(memory_space=pl.ANY),
        scratch_shapes=[
            pltpu.SemaphoreType.DMA,
            pltpu.SemaphoreType.DMA((7, pieces)),
            pltpu.SemaphoreType.DMA((7, pieces)),
        ],
        cost_estimate=lasting(22 if cols > 1024 else 8),
        compiler_params=pltpu.CompilerParams(collective_id=next(ids), has_side_effects=True),
    )(block, *waits)


def scatter_steps(
    seqs, p_ref, o_ref, own, got, out, rx, ry, dx, dy, own_sem, send_sem, recv_sem, make=None
):
    rows = o_ref.shape[0]
    h = rows // 2
    me, sibling, by_x, by_y = plane()
    across = by_x + by_y - me
    shift = sibling - me
    top, low = pl.ds(0, h), pl.ds(h, h)
    loads, sends = [], []
    for k, block in enumerate((across, by_x, by_y, me)):
        if make is not None:
            make(block // 2)
        for j in range(2):
            copy = remote(
                p_ref.at[pl.ds((block + shift) * rows + j * h, h)],
                got.at[k, pl.ds(j * h, h)],
                send_sem.at[k * 2 + j],
                recv_sem.at[k * 2 + j],
                CTX,
                sibling,
            )
            copy.start()
            sends.append(copy)
            load = pltpu.make_async_copy(
                p_ref.at[pl.ds(block * rows + j * h, h)],
                own.at[k, pl.ds(j * h, h)],
                own_sem.at[k * 2 + j],
            )
            load.start()
            loads.append(load)

    def pair(k, j):
        sends[k * 2 + j].wait_recv()
        loads[k * 2 + j].wait()
        part = pl.ds(j * h, h)
        return own[k, part].astype(F32) + got[k, part].astype(F32)

    def put(part, total):
        if not seqs:
            o_ref[part] = total
            return
        chunk = total.shape[1] // (PLANE * seqs)
        per = 128 // chunk
        for k in range(total.shape[1] // 128):
            blocks = [(n % seqs) * PLANE + n // seqs for n in range(k * per, (k + 1) * per)]
            o_ref[part, k * 128 : (k + 1) * 128] = jnp.concatenate(
                [total[:, b * chunk : (b + 1) * chunk] for b in blocks], axis=1
            )

    def go(src, dst, slot, to):
        copy = remote(src, dst, send_sem.at[slot], recv_sem.at[slot], CTX, to)
        copy.start()
        sends.append(copy)
        return copy

    yield True
    out[0, top] = pair(0, 0).astype(out.dtype)
    across_x = go(out.at[0, top], dx, 8, by_x)
    out[0, low] = pair(0, 1).astype(out.dtype)
    across_y = go(out.at[0, low], dy, 9, by_y)
    out[1, top] = pair(1, 0).astype(out.dtype)
    x_top = go(out.at[1, top], rx.at[top], 10, by_x)
    out[2, low] = pair(2, 1).astype(out.dtype)
    y_low = go(out.at[2, low], ry.at[low], 11, by_y)
    yield True
    across_y.wait_recv()
    out[1, low] = (pair(1, 1) + dy[...].astype(F32)).astype(out.dtype)
    x_low = go(out.at[1, low], rx.at[low], 12, by_x)
    across_x.wait_recv()
    out[2, top] = (pair(2, 0) + dx[...].astype(F32)).astype(out.dtype)
    y_top = go(out.at[2, top], ry.at[top], 13, by_y)
    yield True
    first, second = pair(3, 0), pair(3, 1)
    x_top.wait_recv()
    y_top.wait_recv()
    put(top, first + rx[top].astype(F32) + ry[top].astype(F32))
    x_low.wait_recv()
    y_low.wait_recv()
    put(low, second + rx[low].astype(F32) + ry[low].astype(F32))
    for copy in sends:
        copy.wait_send()


def scatter_kernel(seqs, *refs):
    me, sibling, by_x, by_y = plane()
    greet([(CTX, sibling), (CTX, by_x), (CTX, by_y)])
    together(scatter_steps(seqs, *refs))


def scatter_scratch(rows, cols):
    def room(*shape):
        return pltpu.VMEM(shape, BF)

    return [
        room(4, rows, cols),
        room(4, rows, cols),
        room(3, rows, cols),
        room(rows, cols),
        room(rows, cols),
        room(rows // 2, cols),
        room(rows // 2, cols),
        pltpu.SemaphoreType.DMA((8,)),
        pltpu.SemaphoreType.DMA((14,)),
        pltpu.SemaphoreType.DMA((14,)),
    ]


def scatter_tokens(partial_sum, ids, waits=(), seqs=0):
    rows, cols = partial_sum.shape[0] // PLANE, partial_sum.shape[1]

    return pl.pallas_call(
        unused(partial(scatter_kernel, seqs), 1, len(waits)),
        out_shape=jax.ShapeDtypeStruct((rows, cols), F32),
        in_specs=[pl.BlockSpec(memory_space=pl.ANY)] * (1 + len(waits)),
        out_specs=pl.BlockSpec(memory_space=pltpu.VMEM),
        scratch_shapes=scatter_scratch(rows, cols),
        cost_estimate=lasting(22 if cols > 1024 else 8),
        compiler_params=pltpu.CompilerParams(
            collective_id=next(ids), has_side_effects=True, vmem_limit_bytes=40 * 2**20
        ),
    )(partial_sum.astype(BF), *waits)


def row_sum_kernel(x_ref, o_ref, got, send_sem, recv_sem):
    me = lax.axis_index(CTX)
    greet([(CTX, (me + j) % PLANE) for j in range(1, PLANE)])
    copies = []
    for j in range(1, PLANE):
        copy = remote(
            x_ref, got.at[j - 1], send_sem.at[j - 1], recv_sem.at[j - 1], CTX, (me + j) % PLANE
        )
        copy.start()
        copies.append(copy)
    total = x_ref[...]
    for j, copy in enumerate(copies):
        copy.wait_recv()
        total = total + got[j]
    o_ref[...] = total
    for copy in copies:
        copy.wait_send()


def row_sum(rows, ids, waits=()):
    tile = rows.reshape(8, -1)
    total = pl.pallas_call(
        unused(row_sum_kernel, 1, len(waits)),
        out_shape=jax.ShapeDtypeStruct(tile.shape, F32),
        in_specs=[pl.BlockSpec(memory_space=pltpu.VMEM)]
        + [pl.BlockSpec(memory_space=pl.ANY)] * len(waits),
        out_specs=pl.BlockSpec(memory_space=pltpu.VMEM),
        scratch_shapes=[
            pltpu.VMEM((PLANE - 1,) + tile.shape, F32),
            pltpu.SemaphoreType.DMA((PLANE - 1,)),
            pltpu.SemaphoreType.DMA((PLANE - 1,)),
        ],
        cost_estimate=lasting(5),
        compiler_params=pltpu.CompilerParams(collective_id=next(ids), has_side_effects=True),
    )(tile, *waits)
    return total.reshape(rows.shape)


def small_gather_steps(seqs, x_ref, o_ref, own_sem, send_sem, recv_sem):
    me, mine = lax.axis_index(CTX), lax.axis_index(FSDP)
    keep = pltpu.make_async_copy(x_ref, o_ref.at[me, mine], own_sem)
    keep.start()
    copies = []
    for j, (axis, other) in enumerate(other_places(FSDP, seqs)):
        copy = remote(x_ref, o_ref.at[me, mine], send_sem.at[j], recv_sem.at[j], axis, other)
        copy.start()
        copies.append(copy)
    yield True
    keep.wait()
    for copy in copies:
        copy.wait_recv()
    for j, (axis, other) in enumerate(other_places(CTX, PLANE)):
        k = seqs + j
        copy = remote(o_ref.at[me], o_ref.at[me], send_sem.at[k], recv_sem.at[k], axis, other)
        copy.start()
        copies.append(copy)
    for _ in range(8):
        yield True
    for copy in copies[seqs - 1 :]:
        copy.wait_recv()
    for copy in copies:
        copy.wait_send()


def columns(ref, place, count):
    return ref.at[:, pl.ds(pl.multiple_of(place * count, 128), count)]


def swap_steps(delay, patience, routes, own_sem, send_sem, recv_sem):
    me = lax.axis_index(CTX)
    for _ in range(delay):
        yield True
    keeps, copies = [], []
    for k, (part, land) in enumerate(routes):
        keep = pltpu.make_async_copy(part(me), land(me), own_sem.at[k])
        keep.start()
        keeps.append(keep)
    for j in (4, 2, 6, 3, 5, 7, 1):
        to = (me + j) % PLANE
        for k, (part, land) in enumerate(routes):
            copy = remote(part(to), land(me), send_sem.at[j, k], recv_sem.at[j, k], CTX, to)
            copy.start()
            copies.append(copy)
    for _ in range(patience):
        yield True
    for copy in copies:
        copy.wait_recv()
    for copy in copies:
        copy.wait_send()
    for keep in keeps:
        keep.wait()


def swap_scratch(routes):
    return [
        pltpu.SemaphoreType.DMA((routes,)),
        pltpu.SemaphoreType.DMA((PLANE, routes)),
        pltpu.SemaphoreType.DMA((PLANE, routes)),
    ]


def one_after(*tasks):
    for task in tasks:
        yield from task


def opening_kernel(seqs, pieces, *refs):
    tile, shard, hat, rows, query, zgate, channels, mixed, gate, up = refs[:10]
    o_tile, o_shard, o_hat, o_rows, conv, rest, ffn, o_conv = refs[10:18]
    sems = refs[18:]
    sems = [sems[k : k + 3] for k in range(0, len(sems), 3)]
    head = query.shape[1] // PLANE
    inner = zgate.shape[1] // PLANE
    half = gate.shape[1] // PLANE
    greet(other_places(FSDP, seqs) + other_places(CTX, PLANE))
    to_conv = [
        (lambda to: columns(channels, to, inner), lambda at: conv.at[at, :, :inner]),
        (lambda to: mixed.at[to], lambda at: conv.at[at, :, inner:]),
    ]
    to_rest = [
        (lambda to: columns(query, to, head), lambda at: rest.at[at, :, :head]),
        (lambda to: columns(zgate, to, inner), lambda at: rest.at[at, :, head:]),
    ]
    to_ffn = [
        (lambda to: columns(gate, to, half), lambda at: ffn.at[at, :, :half]),
        (lambda to: columns(up, to, half), lambda at: ffn.at[at, :, half:]),
    ]
    together(
        one_after(
            swap_steps(0, 1, to_conv, *sems[0]), chain_steps(4, seqs, conv, o_conv, *sems[1])
        ),
        chain_steps(4, seqs, shard, o_shard, *sems[2]),
        small_gather_steps(seqs, tile, o_tile, *sems[3]),
        gather_steps(pieces, hat, o_hat, *sems[4]),
        swap_steps(1, 8, to_rest, *sems[5]),
        swap_steps(3, 8, to_ffn, *sems[6]),
        one_after(delay_steps(5), gather_steps(pieces, rows, o_rows, *sems[7])),
    )


def delay_steps(turns):
    for _ in range(turns):
        yield True


def opening(tile, shard, hat, rows, query, zgate, channels, mixed, gate, up, seqs, ids, pieces=2):
    anywhere = pl.BlockSpec(memory_space=pl.ANY)
    krows = query.shape[0]
    inner = zgate.shape[1] // PLANE
    conv_cols = inner + mixed.shape[2]
    rest_cols = query.shape[1] // PLANE + inner
    ffn_cols = (gate.shape[1] + up.shape[1]) // PLANE

    def shape(*dims):
        return jax.ShapeDtypeStruct(dims, BF)

    def three(*dims):
        return [
            pltpu.SemaphoreType.DMA,
            pltpu.SemaphoreType.DMA(dims),
            pltpu.SemaphoreType.DMA(dims),
        ]

    return pl.pallas_call(
        partial(opening_kernel, seqs, pieces),
        out_shape=(
            shape(PLANE, seqs, *tile.shape),
            shape(seqs, *shard.shape),
            shape(PLANE * hat.shape[0], hat.shape[1]),
            shape(PLANE * rows.shape[0], rows.shape[1]),
            shape(PLANE, krows, conv_cols),
            shape(PLANE, krows, rest_cols),
            shape(PLANE, krows, ffn_cols),
            shape(seqs, PLANE, krows, conv_cols),
        ),
        in_specs=[anywhere] * 10,
        out_specs=(anywhere,) * 8,
        scratch_shapes=swap_scratch(2)
        + chain_scratch(4, seqs)
        + chain_scratch(4, seqs)
        + three(PLANE + seqs)
        + three(7, pieces)
        + swap_scratch(2)
        + swap_scratch(2)
        + three(7, pieces),
        cost_estimate=lasting(70),
        compiler_params=pltpu.CompilerParams(collective_id=next(ids), has_side_effects=True),
    )(tile, shard, hat, rows, query, zgate, channels, mixed, gate, up)


def small_scatter_steps(seqs, x_ref, o_ref, mine_ref, got, total, late, own_sem, send_sem, recv_sem):
    me, mine = lax.axis_index(CTX), lax.axis_index(FSDP)
    load = pltpu.make_async_copy(x_ref.at[me], mine_ref, own_sem)
    load.start()
    copies = []
    for j, (axis, to) in enumerate(other_places(CTX, PLANE)):
        copy = remote(x_ref.at[to], got.at[j], send_sem.at[j], recv_sem.at[j], axis, to)
        copy.start()
        copies.append(copy)
    yield True
    load.wait()
    acc = mine_ref[...]
    for j, copy in enumerate(copies):
        copy.wait_recv()
        acc = acc + got[j]
    total[...] = acc
    first = len(copies)
    for j, (axis, other) in enumerate(other_places(FSDP, seqs)):
        k = PLANE + j
        copy = remote(total.at[other], late.at[j], send_sem.at[k], recv_sem.at[k], axis, other)
        copy.start()
        copies.append(copy)
    yield True
    out = total[mine]
    for j, copy in enumerate(copies[first:]):
        copy.wait_recv()
        out = out + late[j]
    o_ref[...] = out
    for copy in copies:
        copy.wait_send()


def product_steps(kind, block, rounds, a_any, b_any, o_any, a, b, o, sems):
    loads = [
        pltpu.make_async_copy(src, dst, sems.at[k])
        for k, (src, dst) in enumerate(((a_any, a), (b_any, b)))
    ]
    for load in loads:
        load.start()
    yield True
    for load in loads:
        load.wait()
    count = o.shape[0] // block
    per = -(-count // rounds)
    for first in range(0, count, per):

        def one(k, carry):
            rows = pl.ds(pl.multiple_of(k * block, 128), block)
            if kind:
                part = lax.dot_general(
                    a[:, rows], b[...], (((0,), (0,)), ((), ())), preferred_element_type=F32
                )
            else:
                part = jnp.dot(a[rows, :], b[...], preferred_element_type=F32)
            o[rows, :] = part.astype(BF)
            return carry

        lax.fori_loop(first, min(first + per, count), one, 0)
        yield True
    store = pltpu.make_async_copy(o, o_any, sems.at[2])
    store.start()
    yield True
    store.wait()


def product_scratch(kind, a, b):
    rows = a.shape[1] if kind else a.shape[0]
    return [
        pltpu.VMEM(a.shape, BF),
        pltpu.VMEM(b.shape, BF),
        pltpu.VMEM((rows, b.shape[1]), BF),
        pltpu.SemaphoreType.DMA((3,)),
    ]


def scatter_beside_kernel(seqs, p_ref, a, b, o_ref, o, *scratch):
    me, sibling, by_x, by_y = plane()
    greet([(CTX, sibling), (CTX, by_x), (CTX, by_y)])
    together(
        scatter_steps(seqs, p_ref, o_ref, *scratch[:10]),
        product_steps(1, 256, 3, a, b, o, *scratch[10:]),
    )


def scatter_beside(partial_sum, a, b, seqs, ids, waits=()):
    anywhere = pl.BlockSpec(memory_space=pl.ANY)
    rows, cols = partial_sum.shape[0] // PLANE, partial_sum.shape[1]
    return pl.pallas_call(
        unused(partial(scatter_beside_kernel, seqs), 3, len(waits)),
        out_shape=(
            jax.ShapeDtypeStruct((rows, cols), F32),
            jax.ShapeDtypeStruct((a.shape[1], b.shape[1]), BF),
        ),
        in_specs=[anywhere] * (3 + len(waits)),
        out_specs=(pl.BlockSpec(memory_space=pltpu.VMEM), anywhere),
        scratch_shapes=scatter_scratch(rows, cols) + product_scratch(1, a, b),
        cost_estimate=lasting(25),
        compiler_params=pltpu.CompilerParams(
            collective_id=next(ids), has_side_effects=True, vmem_limit_bytes=40 * 2**20
        ),
    )(partial_sum.astype(BF), a, b, *waits)


def gather_beside_kernel(pieces, x_ref, a, b, o_ref, o, *scratch):
    me, sibling, by_x, by_y = plane()
    greet([(CTX, sibling), (CTX, by_x), (CTX, by_y)])
    together(
        gather_steps(pieces, x_ref, o_ref, *scratch[:3]),
        product_steps(0, 256, 4, a, b, o, *scratch[3:]),
    )


def gather_beside(block, a, b, ids, pieces=4):
    anywhere = pl.BlockSpec(memory_space=pl.ANY)
    rows, cols = block.shape
    return pl.pallas_call(
        partial(gather_beside_kernel, pieces),
        out_shape=(
            jax.ShapeDtypeStruct((PLANE * rows, cols), BF),
            jax.ShapeDtypeStruct((a.shape[0], b.shape[1]), BF),
        ),
        in_specs=[anywhere] * 3,
        out_specs=(anywhere, anywhere),
        scratch_shapes=[
            pltpu.SemaphoreType.DMA,
            pltpu.SemaphoreType.DMA((7, pieces)),
            pltpu.SemaphoreType.DMA((7, pieces)),
        ]
        + product_scratch(0, a, b),
        cost_estimate=lasting(22),
        compiler_params=pltpu.CompilerParams(
            collective_id=next(ids), has_side_effects=True, vmem_limit_bytes=40 * 2**20
        ),
    )(block, a, b)


def scatter_two_kernel(p_ref, q_ref, o_ref, oq_ref, *scratch):
    me, sibling, by_x, by_y = plane()
    greet([(CTX, sibling), (CTX, by_x), (CTX, by_y)])
    together(
        scatter_steps(0, p_ref, o_ref, *scratch[:10]),
        scatter_steps(0, q_ref, oq_ref, *scratch[10:]),
    )


def scatter_two(first, second, ids, waits=()):
    near = pl.BlockSpec(memory_space=pltpu.VMEM)
    shapes = [(x.shape[0] // PLANE, x.shape[1]) for x in (first, second)]
    return pl.pallas_call(
        unused(scatter_two_kernel, 2, len(waits)),
        out_shape=tuple(jax.ShapeDtypeStruct(shape, F32) for shape in shapes),
        in_specs=[pl.BlockSpec(memory_space=pl.ANY)] * (2 + len(waits)),
        out_specs=(near, near),
        scratch_shapes=scatter_scratch(*shapes[0]) + scatter_scratch(*shapes[1]),
        cost_estimate=lasting(28),
        compiler_params=pltpu.CompilerParams(
            collective_id=next(ids), has_side_effects=True, vmem_limit_bytes=40 * 2**20
        ),
    )(first, second, *waits)


def closing_kernel(
    seqs, g1, g2, g3, w1, w2, w3, rest, ffn, hat, o_ref, norm_ref, query, zgate, gate, up, p_ref, *scratch
):
    factors, own, sems = (g1, g2, g3, w1, w2, w3), scratch[:6], scratch[6]
    scratch = scratch[7:]
    loads = [
        pltpu.make_async_copy(factors[k], own[k], sems.at[k]) for k in range(len(factors))
    ]
    for load in loads:
        load.start()
    greet(other_places(CTX, PLANE))
    head = query.shape[1] // PLANE
    inner = zgate.shape[1] // PLANE
    half = gate.shape[1] // PLANE
    pair = 2 * o_ref.shape[0]

    def make(chip):
        rows = pl.ds(pl.multiple_of(chip * pair, pair), pair)
        total = 0.0
        for g, w in zip(own[:3], own[3:]):
            total = total + lax.dot_general(
                g[rows, :], w[...], (((1,), (1,)), ((), ())), preferred_element_type=F32
            )
        p_ref[rows, :] = total.astype(BF)

    from_rest = [
        (lambda to: rest.at[to, :, :head], lambda at: columns(query, at, head)),
        (lambda to: rest.at[to, :, head:], lambda at: columns(zgate, at, inner)),
    ]
    from_ffn = [
        (lambda to: ffn.at[to, :, :half], lambda at: columns(gate, at, half)),
        (lambda to: ffn.at[to, :, half:], lambda at: columns(up, at, half)),
    ]
    for load in loads:
        load.wait()
    together(
        swap_steps(0, 8, from_rest, *scratch[10:13]),
        swap_steps(0, 8, from_ffn, *scratch[13:]),
        scatter_steps(seqs, p_ref, o_ref, *scratch[:10], make=make),
    )
    total = jnp.sum(o_ref[...] * hat[...], axis=0, keepdims=True)
    norm_ref[...] = jnp.zeros_like(norm_ref)
    part = total.shape[1] // (PLANE * seqs)
    for k in range(PLANE * seqs):
        norm_ref[k // seqs, k % seqs, 0:1, 0:part] = total[:, k * part : (k + 1) * part]


def closing(grads, weights, rest, ffn, hat, head, seqs, ids, waits=()):
    anywhere = pl.BlockSpec(memory_space=pl.ANY)
    near = pl.BlockSpec(memory_space=pltpu.VMEM)
    length, cols = grads[0].shape[0], weights[0].shape[0]
    rows = length // PLANE
    _, krows, rest_cols = rest.shape
    half = ffn.shape[2] // 2

    def wide(count):
        return jax.ShapeDtypeStruct((krows, PLANE * count), BF)

    return pl.pallas_call(
        unused(partial(closing_kernel, seqs), 9, len(waits)),
        out_shape=(
            jax.ShapeDtypeStruct((rows, cols), F32),
            jax.ShapeDtypeStruct((PLANE, seqs, 8, 128), F32),
            wide(head),
            wide(rest_cols - head),
            wide(half),
            wide(half),
        ),
        in_specs=[anywhere] * 8 + [near] + [anywhere] * len(waits),
        out_specs=(near, near) + (anywhere,) * 4,
        scratch_shapes=[pltpu.VMEM((length, cols), BF)]
        + [pltpu.VMEM(x.shape, BF) for x in (*grads, *weights)]
        + [pltpu.SemaphoreType.DMA((6,))]
        + scatter_scratch(rows, cols)
        + swap_scratch(2)
        + swap_scratch(2),
        cost_estimate=lasting(35),
        compiler_params=pltpu.CompilerParams(
            collective_id=next(ids), has_side_effects=True, vmem_limit_bytes=60 * 2**20
        ),
    )(*grads, *weights, rest, ffn, hat, *waits)


def step_sum_steps(seqs, x_ref, o_ref, land, got, own_sem, send_sem, recv_sem):
    me, mine = lax.axis_index(CTX), lax.axis_index(FSDP)
    keep = pltpu.make_async_copy(x_ref.at[me], land.at[me], own_sem)
    keep.start()
    copies = []
    for j, (axis, to) in enumerate(other_places(CTX, PLANE)):
        copy = remote(x_ref.at[to], land.at[me], send_sem.at[j], recv_sem.at[j], axis, to)
        copy.start()
        copies.append(copy)
    yield True
    keep.wait()
    for copy in copies:
        copy.wait_recv()
    first = len(copies)
    for j, (axis, other) in enumerate(other_places(FSDP, seqs)):
        k = PLANE + j
        copy = remote(land.at[:, other], got.at[j], send_sem.at[k], recv_sem.at[k], axis, other)
        copy.start()
        copies.append(copy)
    yield True
    total = land[:, mine]
    for j, copy in enumerate(copies[first:]):
        copy.wait_recv()
        total = total + got[j]
    o_ref[...] = total
    for copy in copies:
        copy.wait_send()


def last_kernel(
    seqs, norm, ffn_gain, mixer_gain, channel, by_head, step, conv,
    small_ref, step_ref, channels, key, value,
    mixed, x_ref, st_ref, full, *scratch
):
    me = lax.axis_index(CTX)
    given = (norm, ffn_gain, mixer_gain, channel, by_head, step)
    near, sems, scratch = scratch[:6], scratch[6], scratch[7:]
    loads = [pltpu.make_async_copy(given[k], near[k], sems.at[k]) for k in range(len(given))]
    for load in loads:
        load.start()
    norm, ffn_gain, mixer_gain, channel, by_head, step = near
    devices = PLANE * seqs
    krows = conv.shape[1]
    bc = 2 * STATE // PLANE
    total = channels.shape[1] - 2 * STATE
    inner = total // PLANE
    kv = value.shape[1] // PLANE
    from_conv = [
        (lambda to: conv.at[to, :, :inner], lambda at: columns(channels, at, inner)),
        (lambda to: conv.at[to, :, inner:], lambda at: mixed.at[at]),
    ]
    x_ref[...] = jnp.zeros_like(x_ref)
    full[...] = jnp.zeros_like(full)
    st_ref[...] = jnp.zeros_like(st_ref)
    for load in loads:
        load.wait()
    kinds = channel.shape[0]
    full[0:kinds, pl.ds(pl.multiple_of(me * inner, 128), inner)] = channel[:, :inner]
    for k in range(PLANE):
        full[0:kinds, total + k * bc : total + (k + 1) * bc] = jnp.where(
            me == k, channel[:, inner:], 0.0
        )
    heads = by_head.shape[1]
    mine_only = [jnp.where(me == k, by_head[...], 0.0) for k in range(PLANE)]
    spread = jnp.concatenate(mine_only, axis=1)
    part, wide = ffn_gain.shape[1] // devices, full.shape[1] // devices
    for n in range(devices):
        c, f = n // seqs, n % seqs
        x_ref[c, f, 0:1, 0:part] = ffn_gain[:, n * part : (n + 1) * part]
        x_ref[c, f, 1:2, :] = norm[c, f, 0:1, :]
        x_ref[c, f, 3 : 3 + kinds, 0:wide] = full[0:kinds, n * wide : (n + 1) * wide]
        x_ref[c, f, 8:11, 0 : PLANE * heads] = spread
        at = (f * PLANE + c) * krows
        st_ref[c, f, 0:heads, 0:krows] = step[:, at : at + krows]
    part = inner // seqs
    for f in range(seqs):
        x_ref[me, f, 2:3, 0:part] = mixer_gain[:, f * part : (f + 1) * part]
    greet(other_places(FSDP, seqs) + other_places(CTX, PLANE))
    together(
        small_scatter_steps(seqs, x_ref, small_ref, *scratch[:7]),
        step_sum_steps(seqs, st_ref, step_ref, *scratch[7:12]),
        swap_steps(0, 2, from_conv, *scratch[12:]),
    )
    blocks = [mixed[k].astype(F32) for k in range(PLANE)]
    channels[:, total:] = jnp.concatenate([b[:, :bc] for b in blocks], axis=1).astype(BF)
    value[...] = jnp.concatenate([b[:, bc + kv :] for b in blocks], axis=1)
    half = kv // 2
    group = PLANE // KEY_VALUE_HEADS
    turned = []
    for k in range(0, PLANE, group):
        for at in (bc, bc + half):
            turned += [b[:, at : at + half] for b in blocks[k : k + group]]
    key[...] = jnp.concatenate(turned, axis=1)


def last_exchange(small, conv, inner, kv, seqs, ids):
    anywhere = pl.BlockSpec(memory_space=pl.ANY)
    near = pl.BlockSpec(memory_space=pltpu.VMEM)
    _, krows, cols = conv.shape

    def room(*shape):
        return pltpu.VMEM(shape, F32)

    two = [pltpu.SemaphoreType.DMA((PLANE + seqs,)), pltpu.SemaphoreType.DMA((PLANE + seqs,))]
    return pl.pallas_call(
        partial(last_kernel, seqs),
        out_shape=(
            jax.ShapeDtypeStruct((16, 128), F32),
            jax.ShapeDtypeStruct((PLANE, 8, 128), F32),
            jax.ShapeDtypeStruct((krows, PLANE * inner + 2 * STATE), BF),
            jax.ShapeDtypeStruct((krows, PLANE * kv), F32),
            jax.ShapeDtypeStruct((krows, PLANE * kv), F32),
        ),
        in_specs=[anywhere] * 7,
        out_specs=(near,) * 5,
        scratch_shapes=[
            pltpu.VMEM((PLANE, krows, cols - inner), BF),
            room(PLANE, seqs, 16, 128),
            room(PLANE, seqs, 8, 128),
            room(8, PLANE * inner + 2 * STATE),
            *[room(*x.shape) for x in small],
            pltpu.SemaphoreType.DMA((6,)),
            room(seqs, 16, 128),
            room(PLANE - 1, seqs, 16, 128),
            room(seqs, 16, 128),
            room(seqs - 1, 16, 128),
            pltpu.SemaphoreType.DMA,
            *two,
            room(PLANE, seqs, 8, 128),
            room(seqs - 1, PLANE, 8, 128),
            pltpu.SemaphoreType.DMA,
            *two,
        ]
        + swap_scratch(2),
        cost_estimate=lasting(15),
        compiler_params=pltpu.CompilerParams(
            collective_id=next(ids), has_side_effects=True, vmem_limit_bytes=40 * 2**20
        ),
    )(*small, conv)


def gather_rows(shard):
    return lax.all_gather(shard, FSDP, axis=0, tiled=False)


def scatter_rows(partial_sum):
    return lax.psum_scatter(partial_sum.astype(BF), FSDP, scatter_dimension=0, tiled=False)


def hold_kernel(*refs):
    pass


def hold(value, *earlier):
    anywhere = pl.BlockSpec(memory_space=pl.ANY)
    return pl.pallas_call(
        hold_kernel,
        out_shape=jax.ShapeDtypeStruct(value.shape, value.dtype),
        in_specs=[anywhere] * (1 + len(earlier)),
        out_specs=anywhere,
        input_output_aliases={0: 0},
    )(value, *earlier)


def lasting(us):
    return pl.CostEstimate(flops=int(us * 0.3e9), bytes_accessed=int(us * 0.3e6), transcendentals=0)


def same_document(documents):
    places = jnp.arange(documents.shape[0])
    return (documents[:, None] == documents[None, :]) & (places[:, None] >= places[None, :])


def rotate_some(values, places, first_pair, pairs):
    half = values.shape[-1] // 2
    freqs = ROPE_BASE ** (-(first_pair + jnp.arange(half)).astype(F32) / pairs)
    angles = places[:, None] * freqs[None, :]
    cosine, sine = jnp.cos(angles), jnp.sin(angles)
    first, second = values[:, :half], values[:, half:]
    return jnp.concatenate(
        [first * cosine - second * sine, second * cosine + first * sine], axis=-1
    )


def ssm_terms(step, rate, documents, chunks):
    length, heads = step.shape
    rows = length // chunks
    step_c = step.reshape(chunks, rows, heads).transpose(0, 2, 1)
    docs_c = documents.reshape(chunks, rows)
    prior = jnp.concatenate([jnp.full((1,), -1, docs_c.dtype), docs_c[:-1, -1]])
    last = docs_c[:, -1]
    level = jnp.cumsum(step_c * rate[None, :, None], axis=2)
    visible = jax.vmap(same_document)(docs_c)[:, None]
    spread = level[:, :, :, None] - level[:, :, None, :]
    pair = jnp.where(visible, jnp.exp(jnp.where(visible, spread, 0.0)), 0.0)
    entry = jnp.where((docs_c == prior[:, None])[:, None], jnp.exp(level), 0.0)
    tail = jnp.where((docs_c == last[:, None])[:, None], jnp.exp(level[:, :, -1:] - level), 0.0)
    carry = jnp.exp(level[:, :, -1]) * (last == prior).astype(F32)[:, None]
    k, j, i = (jnp.arange(chunks).reshape(shape) for shape in ((-1, 1, 1), (1, -1, 1), (1, 1, -1)))
    between = ((j < i) & (i < k))[..., None]
    reach = jnp.prod(jnp.where(between, carry[None, None], 1.0), axis=2)
    reach = jnp.where((j < k), reach, 0.0)
    return step_c, pair, entry, tail, carry, reach


def ssm_forward(xin, write, read, terms, skip):
    step_c, pair, entry, tail, carry, reach = terms
    chunks, heads, rows = step_c.shape
    x_c = xin.reshape(chunks, rows, heads, HP)
    write_c = write.reshape(chunks, rows, STATE)
    read_c = read.reshape(chunks, rows, STATE)
    gram = jnp.einsum("ktn,kun->ktu", read_c, write_c, preferred_element_type=F32)
    mixing = (pair * gram[:, None] * step_c[:, :, None, :]).astype(BF)
    inner = jnp.einsum("khtu,kuhp->kthp", mixing, x_c, preferred_element_type=F32)
    weight = (tail * step_c).transpose(0, 2, 1)
    weighted = (x_c.astype(F32) * weight[..., None]).astype(BF)
    local = jnp.einsum("kthp,ktn->khpn", weighted, write_c, preferred_element_type=F32)
    entering = jnp.sum(reach[:, :, :, None, None] * local[None], axis=1)
    reached = jnp.einsum(
        "ktn,khpn->kthp", read_c, entering.astype(BF), preferred_element_type=F32
    )
    y = (
        inner
        + reached * entry.transpose(0, 2, 1)[..., None]
        + skip[None, None, :, None] * x_c.astype(F32)
    )
    return y.reshape(chunks * rows, heads * HP), (gram, mixing, entering, reached)


def ssm_backward(grad, xin, write, read, terms, skip, rate, saved):
    step_c, pair, entry, tail, carry, reach = terms
    gram, mixing, entering, reached = saved
    chunks, heads, rows = step_c.shape
    x_c = xin.reshape(chunks, rows, heads, HP)
    x_f = x_c.astype(F32)
    write_c = write.reshape(chunks, rows, STATE)
    read_c = read.reshape(chunks, rows, STATE)
    g = grad.reshape(chunks, rows, heads, HP)
    g_low = g.astype(BF)
    skip_grad = jnp.sum(g * x_f, axis=(0, 1, 3))
    gx = skip[None, None, :, None] * g
    gx = gx + jnp.einsum("khtu,kthp->kuhp", mixing, g_low, preferred_element_type=F32)
    g_mixing = jnp.einsum("kthp,kuhp->khtu", g_low, x_c, preferred_element_type=F32)
    masked = g_mixing * pair
    g_gram = jnp.sum(masked * step_c[:, :, None, :], axis=1).astype(BF)
    both = masked * gram[:, None]
    column = jnp.sum(both, axis=2)
    row = jnp.sum(both * step_c[:, :, None, :], axis=3)
    g_level = row - step_c * column
    g_step = column
    entry_t = entry.transpose(0, 2, 1)[..., None]
    g_entry = jnp.sum(g * reached, axis=3).transpose(0, 2, 1)
    g_level = g_level + g_entry * entry
    g_reached = (g * entry_t).astype(BF)
    g_read = jnp.einsum("ktu,kun->ktn", g_gram, write_c, preferred_element_type=F32)
    g_write = jnp.einsum("ktu,ktn->kun", g_gram, read_c, preferred_element_type=F32)
    g_read = g_read + jnp.einsum(
        "kthp,khpn->ktn", g_reached, entering.astype(BF), preferred_element_type=F32
    )
    g_enter = jnp.einsum("kthp,ktn->khpn", g_reached, read_c, preferred_element_type=F32)
    leaving = jnp.sum(reach.transpose(1, 0, 2)[:, :, :, None, None] * g_enter[None], axis=1)
    g_carry = jnp.sum(entering * leaving, axis=(2, 3))
    leaving_low = leaving.astype(BF)
    weight = tail * step_c
    weight_t = weight.transpose(0, 2, 1)[..., None]
    seen = jnp.einsum("ktn,khpn->kthp", write_c, leaving_low, preferred_element_type=F32)
    gx = gx + weight_t * seen
    g_weight = jnp.sum(x_f * seen, axis=3).transpose(0, 2, 1)
    weighted = (x_f * weight_t).astype(BF)
    g_write = g_write + jnp.einsum(
        "kthp,khpn->ktn", weighted, leaving_low, preferred_element_type=F32
    )
    moved = g_weight * weight
    g_step = g_step + g_weight * tail
    g_level = g_level - moved
    end = jnp.sum(moved, axis=2) + g_carry * carry
    g_level = g_level.at[:, :, -1].add(end)
    g_la = jnp.flip(jnp.cumsum(jnp.flip(g_level, 2), axis=2), 2)
    g_step = g_step + g_la * rate[None, :, None]
    rate_grad = jnp.sum(g_la * step_c, axis=(0, 2))
    length = chunks * rows
    return (
        gx.reshape(length, heads * HP),
        g_write.reshape(length, STATE),
        g_read.reshape(length, STATE),
        g_step.transpose(0, 2, 1).reshape(length, heads),
        rate_grad,
        skip_grad,
    )


def head_parallel(
    hidden_in,
    out_grad,
    doc_ids,
    norm_gain,
    query_weight,
    key_matrix,
    value_matrix,
    attn_out_weight,
    mixer_gate_weight,
    conv_in_weight,
    step_weight,
    conv_weight,
    conv_bias,
    step_bias,
    log_decay,
    skip_gain,
    mixer_gain,
    mamba_out_weight,
    ffn_gain,
    gate_weight,
    up_weight,
    down_weight,
):
    ctx = lax.axis_size(CTX)
    seqs = lax.axis_size(FSDP)
    me = lax.axis_index(CTX)
    mine = lax.axis_index(FSDP)
    tokens, width = hidden_in.shape[1:]
    length = ctx * tokens
    krows = query_weight.shape[0]
    dssm = HS * HP
    heads = HS // ctx
    inner = heads * HP
    bc = 2 * STATE // ctx
    ff = gate_weight.shape[1] // ctx
    head = HEAD_SIZE * QUERY_HEADS // ctx
    taps = CONV - 1

    ids = itertools.count(1)

    def to_shards(x):
        return x.reshape(-1, ctx, seqs, krows).transpose(0, 2, 1, 3).reshape(-1, width)

    def from_shards(x):
        return x.reshape(-1, seqs, ctx, krows).transpose(0, 2, 1, 3).reshape(-1, width)

    small = jnp.concatenate(
        [
            norm_gain,
            ffn_gain,
            mixer_gain,
            conv_bias,
            conv_weight.reshape(-1),
            doc_ids[0].astype(BF),
            step_weight.reshape(-1),
        ]
    )
    small_size = small.size
    tile_rows = -(-small_size // 2048) * 16
    small = jnp.pad(small, (0, tile_rows * 128 - small_size)).reshape(tile_rows, 128)

    def by_column(weight, n):
        return weight.reshape(krows, ctx, n).transpose(1, 0, 2)

    kv_repeat = ctx // KEY_VALUE_HEADS
    kv = HEAD_SIZE // kv_repeat
    half = kv // 2
    key_pack = (
        key_matrix.reshape(krows, KEY_VALUE_HEADS, 2, kv_repeat, half)
        .transpose(1, 3, 0, 2, 4)
        .reshape(ctx, krows, kv)
    )
    mixed_pack = jnp.concatenate(
        [by_column(conv_in_weight[:, dssm:], bc), key_pack, by_column(value_matrix, kv)], axis=2
    )
    conv_cols = inner + bc + 2 * kv
    rest_cols = head + inner
    resid = hidden_in[0].astype(F32)
    scale_one = lax.rsqrt(jnp.mean(resid * resid, axis=-1, keepdims=True) + EPSILON)
    hat_one = resid * scale_one
    small, out_own, normed, grad_all, _, rest_pack, ffn_pack, conv_in_own = opening(
        small,
        jnp.concatenate([attn_out_weight, mamba_out_weight]),
        to_shards(hat_one.astype(BF)),
        out_grad[0],
        query_weight,
        mixer_gate_weight,
        conv_in_weight,
        mixed_pack,
        gate_weight,
        up_weight,
        seqs,
        ids,
    )
    conv_in_own = conv_in_own.reshape(width, conv_cols)
    small = small.reshape(ctx * seqs, -1)
    cuts = []
    at = 0
    for n in (norm_gain.size, ffn_gain.size, mixer_gain.size, conv_bias.size, conv_weight.size, tokens, step_weight.size):
        cuts.append(small[:, at : at + n])
        at += n
    gain_one = cuts[0].reshape(-1).astype(F32)
    gain_two = cuts[1].reshape(-1).astype(F32)
    gain_mix = lax.dynamic_slice_in_dim(cuts[2].reshape(-1), me * inner, inner).astype(F32)
    bias_all = cuts[3].reshape(-1)
    taps_all = cuts[4].reshape(ctx * seqs, CONV, -1).transpose(1, 0, 2).reshape(CONV, -1)
    documents = lax.dynamic_index_in_dim(
        cuts[5].reshape(ctx, seqs, tokens), mine, 1, False
    ).reshape(length).astype(jnp.int32)

    def own_channels(full):
        return jnp.concatenate(
            [
                lax.dynamic_slice_in_dim(full, me * inner, inner, full.ndim - 1),
                lax.dynamic_slice_in_dim(full, dssm + me * bc, bc, full.ndim - 1),
            ],
            axis=-1,
        )

    conv_taps = own_channels(taps_all).astype(F32)
    conv_shift = own_channels(bias_all).astype(F32)
    bias_own = lax.dynamic_slice_in_dim(step_bias, me * heads, heads)
    decay_own = lax.dynamic_slice_in_dim(log_decay, me * heads, heads)
    skip_own = lax.dynamic_slice_in_dim(skip_gain, me * heads, heads)

    rest_own = gather_rows(rest_pack).reshape(width, rest_cols)
    out_rows = attn_out_weight.shape[0]
    out_own = jnp.concatenate(
        [out_own[:, :out_rows].reshape(head, width), out_own[:, out_rows:].reshape(inner, width)]
    )
    ffn_own = gather_rows(ffn_pack).reshape(width, 2 * ff)
    down_own = gather_rows(down_weight).reshape(ff, width)
    step_own = lax.dynamic_slice_in_dim(
        cuts[6].reshape(ctx, seqs, krows, HS).transpose(1, 0, 2, 3).reshape(width, HS),
        me * heads,
        heads,
        1,
    )
    step_room = ((0, 0), (0, 128 - heads))
    step_wide = jnp.pad(step_own, step_room)

    normed = (normed.astype(F32) * to_shards(gain_one[None])).astype(BF)
    conv_all = mm(normed, conv_in_own)
    rest_all = mm(normed, rest_own)
    conv_lin = conv_all[:, : inner + bc].astype(BF).astype(F32)
    k_lin = conv_all[:, inner + bc : inner + bc + kv]
    v_lin = conv_all[:, inner + bc + kv :]
    step_lin = mm(normed, step_own)
    q_lin = rest_all[:, :head]
    zgate = rest_all[:, head:]

    widened = jnp.concatenate([jnp.zeros((taps, inner + bc), F32), conv_lin], axis=0)
    widened_docs = jnp.concatenate([jnp.full((taps,), -1, jnp.int32), documents])
    conv_act, conv_back = jax.vjp(
        partial(conv_part, widened_docs=widened_docs, documents=documents),
        widened,
        conv_taps,
        conv_shift,
    )
    conv_act = conv_act.astype(BF)
    places = jnp.arange(length).astype(F32)
    first_pair = (me % kv_repeat) * half
    key_turned, unturn_key = jax.vjp(
        lambda lin: rotate_some(lin, places, first_pair, HEAD_SIZE // 2), k_lin
    )
    shared = jnp.concatenate(
        [conv_act[:, inner:], key_turned.astype(BF), v_lin.astype(BF)], axis=1
    ).T
    shared = gather_tokens(shared, ids, 2).reshape(ctx, bc + 2 * kv, length)
    write_read = shared[:, :bc].reshape(2 * STATE, length).T
    write, read = write_read[:, :STATE], write_read[:, STATE:]
    group = me // kv_repeat * kv_repeat
    own_kv = lax.dynamic_slice_in_dim(shared[:, bc:], group, kv_repeat, 0)
    key = (
        own_kv[:, :kv]
        .reshape(kv_repeat, 2, half, length)
        .transpose(1, 0, 2, 3)
        .reshape(HEAD_SIZE, length)
        .T
    )
    value = own_kv[:, kv:].reshape(HEAD_SIZE, length).T
    xin = conv_act[:, :inner]

    query_turned, unturn = jax.vjp(
        partial(rotate, places=places), q_lin.reshape(length, head // HEAD_SIZE, HEAD_SIZE)
    )
    query = query_turned.astype(BF)
    visible = same_document(documents)
    scores = jnp.einsum("thd,ud->htu", query, key, preferred_element_type=F32) * HEAD_SIZE**-0.5
    scores = jnp.where(visible[None], scores, NEGATIVE_FLOOR)
    weights = jnp.where(
        visible[None], jnp.exp(scores - jnp.max(scores, axis=-1, keepdims=True)), 0.0
    )
    probs = weights / jnp.sum(weights, axis=-1, keepdims=True)
    probs_low = probs.astype(BF)
    attn_mix = jnp.einsum("htu,ud->thd", probs_low, value, preferred_element_type=F32)
    attn_low = attn_mix.reshape(length, head).astype(BF)

    step_size, step_back = jax.vjp(
        lambda lin, bias: jax.nn.softplus(lin + bias[None, :]), step_lin, bias_own
    )
    rate = -jnp.exp(decay_own)
    terms = ssm_terms(step_size, rate, documents, ctx)
    y, saved = ssm_forward(xin, write, read, terms, skip_own)
    gated, gated_back = jax.vjp(lambda a, z: a * jax.nn.silu(z), y, zgate)
    mean_square = row_sum(jnp.sum(gated * gated, axis=-1), ids) / dssm
    scale_mix = lax.rsqrt(mean_square + EPSILON)[:, None]
    ymix = (gated * scale_mix * gain_mix).astype(BF)

    mixed = jnp.concatenate([attn_low, ymix], axis=1)
    branch = scatter_tokens(mm(mixed, out_own), ids)
    mid = resid + branch
    scale_two = lax.rsqrt(jnp.mean(mid * mid, axis=-1, keepdims=True) + EPSILON)
    normed_two = gather_tokens(to_shards((mid * scale_two * gain_two).astype(BF)), ids)

    gate_up = mm(normed_two, ffn_own)
    gate_lin, up_lin = gate_up[:, :ff], gate_up[:, ff:]
    sigmoid_gate = jax.nn.sigmoid(gate_lin)
    silu_gate = gate_lin * sigmoid_gate
    hidden = (silu_gate * up_lin).astype(BF)
    down_part = mm_tn(hidden, grad_all).astype(BF).reshape(seqs, ff // seqs, width)
    down_own = hold(down_own, down_part)
    grad_hidden = mm_nt(grad_all, down_own)
    grad_gate = (
        grad_hidden * up_lin * (sigmoid_gate + silu_gate * (1.0 - sigmoid_gate))
    ).astype(BF)
    grad_up = (grad_hidden * silu_gate).astype(BF)
    grad_gu = jnp.concatenate([grad_gate, grad_up], axis=1)
    down_grad = scatter_rows(down_part)
    grad_n2, ffn_grad = scatter_beside(mm_nt(grad_gu, ffn_own), normed_two, grad_gu, seqs, ids)
    ffn_grad = scatter_rows(ffn_grad.reshape(seqs, ctx, krows, 2 * ff))

    turned = grad_n2 * gain_two
    hat_two = mid * scale_two
    ffn_gain_grad = jnp.sum(grad_n2 * hat_two, axis=0, keepdims=True)
    grad_mid = out_grad[0].astype(F32) + scale_two * (
        turned - hat_two * jnp.mean(turned * hat_two, axis=-1, keepdims=True)
    )
    branch_grad, last = gather_beside(grad_mid.astype(BF), hidden, down_own, ids)
    branch_grad = hold(branch_grad, down_grad)

    out_grad_own = mm_tn(mixed, branch_grad).astype(BF)
    out_part = jnp.concatenate(
        [
            out_grad_own[:head].reshape(seqs, -1, width),
            out_grad_own[head:].reshape(seqs, -1, width),
        ],
        axis=1,
    )
    out_grad_own = scatter_rows(hold(out_part, ffn_grad))
    grad_attn = mm_nt(branch_grad, out_own[:head]).astype(BF).reshape(length, -1, HEAD_SIZE)
    grad_ymix = mm_nt(branch_grad, out_own[head:])

    grad_prob = jnp.einsum("thd,ud->htu", grad_attn, value, preferred_element_type=F32)
    delta = jnp.sum(probs * grad_prob, axis=-1, keepdims=True)
    grad_score = (probs * (grad_prob - delta)).astype(BF)
    grad_query = (
        jnp.einsum("htu,ud->thd", grad_score, key, preferred_element_type=F32) * HEAD_SIZE**-0.5
    )
    grad_key = (
        jnp.einsum("htu,thd->ud", grad_score, query, preferred_element_type=F32) * HEAD_SIZE**-0.5
    )
    grad_value = jnp.einsum("htu,thd->ud", probs_low, grad_attn, preferred_element_type=F32)
    grad_q_lin = unturn(grad_query)[0].reshape(length, head).astype(BF)

    hat = gated * scale_mix
    turned_mix = grad_ymix * gain_mix
    mixer_gain_grad = jnp.sum(grad_ymix * hat, axis=0, keepdims=True)
    along = row_sum(jnp.sum(turned_mix * hat, axis=-1), ids, (down_grad,))[:, None] / dssm
    grad_gated = scale_mix * (turned_mix - hat * along)
    grad_y, grad_zgate = gated_back(grad_gated)

    grad_rest = jnp.concatenate([grad_q_lin, grad_zgate.astype(BF)], axis=1)
    rest_part = mm_tn(normed, grad_rest).reshape(seqs, ctx, krows, rest_cols).astype(BF)

    grad_xin, grad_write, grad_read, grad_step, grad_rate, skip_grad = ssm_backward(
        grad_y, xin, write, read, terms, skip_own, rate, saved
    )
    grad_key = (
        grad_key.T.reshape(2, kv_repeat, half, length)
        .transpose(1, 0, 2, 3)
        .reshape(kv_repeat, kv, length)
    )
    grad_kv = jnp.concatenate([grad_key, grad_value.T.reshape(kv_repeat, kv, length)], axis=1)
    grad_kv = lax.dynamic_update_slice_in_dim(
        jnp.zeros((ctx, 2 * kv, length), BF), grad_kv.astype(BF), group, 0
    )
    grad_shared = jnp.concatenate([grad_write, grad_read], axis=1).astype(BF)
    grad_shared = jnp.concatenate([grad_shared.T.reshape(ctx, bc, length), grad_kv], axis=1)
    grad_shared, last = scatter_two(
        grad_shared.reshape(ctx * (bc + 2 * kv), length),
        last,
        ids,
        (ffn_grad, rest_part),
    )
    block_out = (mid + last).astype(BF)
    grad_shared = grad_shared.T
    grad_k_lin = unturn_key(grad_shared[:, bc : bc + kv])[0].astype(BF)
    grad_v_lin = grad_shared[:, bc + kv :].astype(BF)
    grad_shared = grad_shared[:, :bc]
    grad_widened, taps_grad, shift_grad = conv_back(
        jnp.concatenate([grad_xin, grad_shared], axis=1)
    )
    grad_step_lin, step_bias_grad = step_back(grad_step)
    log_decay_grad = grad_rate * rate
    grad_conv = jnp.concatenate(
        [grad_widened[taps:].astype(BF), grad_k_lin, grad_v_lin], axis=1
    )
    grad_step_low = grad_step_lin.astype(BF)
    step_grad = mm_tn(grad_step_low, normed)
    rest_grad = scatter_rows(rest_part)
    conv_grad = mm_tn(normed, grad_conv).reshape(seqs, ctx, krows, conv_cols)
    conv_grad = scatter_rows(conv_grad)
    grad_normed, norm_rows, query_grad, zgate_grad, gate_grad, up_grad = closing(
        (grad_conv, grad_rest, jnp.pad(grad_step_low, step_room)),
        (conv_in_own, rest_own, step_wide),
        rest_grad,
        ffn_grad,
        hat_one,
        head,
        seqs,
        ids,
        (out_grad_own,),
    )

    sums, step_sums, channels_grad, key_grad, value_grad = last_exchange(
        (
            norm_rows,
            ffn_gain_grad,
            mixer_gain_grad,
            jnp.concatenate([shift_grad[None], taps_grad]),
            jnp.stack([step_bias_grad, log_decay_grad, skip_grad]),
            step_grad,
        ),
        conv_grad,
        inner,
        kv,
        seqs,
        ids,
    )
    step_grad = step_sums[:, :heads, :krows].reshape(HS, krows).T

    turned_one = grad_normed * gain_one
    input_grad = (
        grad_mid
        + scale_one
        * (turned_one - hat_one * jnp.mean(turned_one * hat_one, axis=-1, keepdims=True))
    ).astype(BF)

    return (
        block_out[None],
        input_grad[None],
        sums[1, :krows],
        query_grad.astype(F32),
        key_grad,
        value_grad,
        out_grad_own[:out_rows].astype(F32),
        zgate_grad.astype(F32),
        channels_grad.astype(F32),
        step_grad,
        sums[4 : 4 + CONV, : conv_weight.shape[1]],
        sums[3, : conv_bias.size],
        sums[8, :HS],
        sums[9, :HS],
        sums[10, :HS],
        sums[2, : mixer_gain.size],
        out_grad_own[out_rows:].astype(F32),
        sums[0, :krows],
        gate_grad.astype(F32),
        up_grad.astype(F32),
        down_grad.astype(F32),
    )


def solution(mesh):
    placed = (
        P(FSDP, CTX, None),
        P(FSDP, CTX, None),
        P(FSDP, CTX),
        P((CTX, FSDP)),
        P((CTX, FSDP), None),
        P((CTX, FSDP), None),
        P((CTX, FSDP), None),
        P((CTX, FSDP), None),
        P((CTX, FSDP), None),
        P((CTX, FSDP), None),
        P((CTX, FSDP), None),
        P(None, (CTX, FSDP)),
        P((CTX, FSDP)),
        P(),
        P(),
        P(),
        P((CTX, FSDP)),
        P((CTX, FSDP), None),
        P((CTX, FSDP)),
        P((CTX, FSDP), None),
        P((CTX, FSDP), None),
        P((CTX, FSDP), None),
    )
    ctx = mesh.shape[CTX]
    whole_heads = ctx == PLANE and QUERY_HEADS % ctx == 0 and HS % ctx == 0
    return jax.shard_map(
        head_parallel if whole_heads else on_device,
        mesh=mesh,
        in_specs=placed,
        out_specs=(
            P(FSDP, CTX, None),
            P(FSDP, CTX, None),
            P((CTX, FSDP)),
            P((CTX, FSDP), None),
            P((CTX, FSDP), None),
            P((CTX, FSDP), None),
            P((CTX, FSDP), None),
            P((CTX, FSDP), None),
            P((CTX, FSDP), None),
            P((CTX, FSDP), None),
            P(None, (CTX, FSDP)),
            P((CTX, FSDP)),
            P(),
            P(),
            P(),
            P((CTX, FSDP)),
            P((CTX, FSDP), None),
            P((CTX, FSDP)),
            P((CTX, FSDP), None),
            P((CTX, FSDP), None),
            P((CTX, FSDP), None),
        ),
        check_vma=False,
    )
```

```python
from functools import partial
import itertools
import math

import jax
import jax.numpy as jnp
from jax import lax
from jax.experimental import pallas as pl
from jax.experimental.pallas import tpu as pltpu
from jax.sharding import PartitionSpec as P

CTX = "ctx"
FSDP = "fsdp"
QUERY_HEADS = 8
KEY_VALUE_HEADS = 2
HEAD_SIZE = 128
HS = 48
HP = 64
STATE = 256
CONV = 4


EPSILON = 1e-05
ROPE_BASE = 100000000000.0
NEGATIVE_FLOOR = -1e30
HIGHEST = lax.Precision.HIGHEST


def shifted(value, axis, steps):
    count = lax.axis_size(axis)
    leading, last = (max(0, -steps), min(count, count - steps))
    return lax.ppermute(value, axis, [(source, source + steps) for source in range(leading, last)])


def prefix(shard, axis, combine, identity):
    devices, position = (lax.axis_size(axis), lax.axis_index(axis))
    everything = jax.tree.map(
        lambda part, kind: lax.all_gather(part.astype(kind), axis),
        shard,
        (jnp.bfloat16, jnp.bfloat16),
    )
    start = jax.tree.map(
        lambda part, zero: jnp.broadcast_to(jnp.asarray(zero, part.dtype), part.shape),
        shard,
        identity,
    )

    def step(k, before):
        reached = k < position
        new = combine(
            before, jax.tree.map(lambda part, own: part[k].astype(own.dtype), everything, shard)
        )
        return jax.tree.map(lambda a, b: jnp.where(reached, a, b), new, before)

    return lax.fori_loop(0, devices, step, start)


def carried_in(shard, axis, join, neutral):
    count = lax.axis_size(axis)
    place = lax.axis_index(axis)
    ahead = count - 1 - place
    gathered = jax.tree.map(
        lambda a, kind: lax.all_gather(a.astype(kind), axis),
        shard,
        jax.tree.map(lambda a: jnp.bfloat16 if a.dtype == jnp.float32 else a.dtype, shard),
    )
    state = jax.tree.map(lambda a, e: jnp.zeros_like(a) + jnp.asarray(e, a.dtype), shard, neutral)

    def one(step, state):
        source = count - 1 - step
        return join(
            state,
            jax.tree.map(
                lambda a, own: lax.dynamic_index_in_dim(a, source, 0, False).astype(own.dtype),
                gathered,
                shard,
            ),
        )

    return lax.fori_loop(0, ahead, one, state)


def rms_scale(values, gain):
    return values * lax.rsqrt(jnp.mean(values * values, axis=-1, keepdims=True) + EPSILON) * gain


def rotate(values, places):
    half_size = values.shape[-1] // 2
    freqs = ROPE_BASE ** (-jnp.arange(half_size).astype(jnp.float32) / half_size)
    angles = places[:, None] * freqs[None, :]
    cosine = jnp.cos(angles)[:, None, :]
    sine = jnp.sin(angles)[:, None, :]
    first = values[..., :half_size]
    second = values[..., half_size:]
    return jnp.concatenate(
        [first * cosine - second * sine, second * cosine + first * sine], axis=-1
    )


def conv_part(widened, taps_weight, bias, widened_docs, documents):
    row_length_total = documents.shape[0]
    total = bias[None, :]
    for tap_index in range(taps_weight.shape[0]):
        same_doc = (widened_docs[tap_index : tap_index + row_length_total] == documents)[:, None]
        total = total + jnp.where(
            same_doc,
            widened[tap_index : tap_index + row_length_total] * taps_weight[tap_index][None, :],
            0.0,
        )
    return jax.nn.silu(total)


def step_part(step_lin, step_bias, log_decay):
    return (jax.nn.softplus(step_lin + step_bias), -jnp.exp(log_decay))


def block_stats(mixer_in, write_proj, step_size, decay_rate, documents, prior_doc):
    decay_log = jnp.cumsum(step_size * decay_rate[None, :], axis=0)
    last_doc = documents[-1]
    tail_weight = (
        jnp.where(
            (documents == last_doc)[:, None], jnp.exp(decay_log[-1][None, :] - decay_log), 0.0
        )
        * step_size
    )
    state_loc = jnp.einsum(
        "thp,tn->hpn", mixer_in * tail_weight[:, :, None], write_proj, precision=HIGHEST
    )
    carry_decay = jnp.exp(decay_log[-1]) * (last_doc == prior_doc).astype(jnp.float32)
    return (state_loc, carry_decay)


def block_mix(
    mixer_in,
    write_proj,
    read_proj,
    step_size,
    decay_rate,
    skip_gain,
    state_in,
    documents,
    prior_doc,
):
    decay_log = jnp.cumsum(step_size * decay_rate[None, :], axis=0)
    positions = jnp.arange(documents.shape[0])
    visible = (documents[:, None] == documents[None, :]) & (
        positions[:, None] >= positions[None, :]
    )
    spread = decay_log.T[:, :, None] - decay_log.T[:, None, :]
    decay_pair = jnp.where(visible[None], jnp.exp(jnp.where(visible[None], spread, 0.0)), 0.0)
    gram = jnp.dot(read_proj, write_proj.T, precision=HIGHEST)
    mixing = decay_pair * gram[None] * step_size.T[:, None, :]
    inner = jnp.einsum("htu,uhp->thp", mixing, mixer_in, precision=HIGHEST)
    entry = jnp.where((documents == prior_doc)[:, None], jnp.exp(decay_log), 0.0)
    carried = jnp.einsum("tn,hpn->thp", read_proj, state_in, precision=HIGHEST) * entry[:, :, None]
    return inner + carried + skip_gain[None, :, None] * mixer_in


def gated_norm(flat_mixed, mixer_gate, gain):
    return rms_scale(flat_mixed * jax.nn.silu(mixer_gate), gain)


def chain_combine(earlier, later):
    decay_early, state_early = earlier
    decay_late, state_late = later
    return (decay_early * decay_late, decay_late[:, None, None] * state_early + state_late)


def piece_scores(piece, start, query_group, query_docs, query_places):
    key_segment, value_segment, docs_piece = piece
    segment_rows = key_segment.shape[0]
    heads_of_key = key_segment.reshape(segment_rows, KEY_VALUE_HEADS, HEAD_SIZE).transpose(1, 0, 2)
    heads_of_value = value_segment.reshape(segment_rows, KEY_VALUE_HEADS, HEAD_SIZE).transpose(
        1, 0, 2
    )
    key_places = (start + jnp.arange(segment_rows)).astype(jnp.float32)
    visible = (docs_piece.astype(jnp.float32)[None, :] == query_docs[:, None]) & (
        key_places[None, :] <= query_places[:, None]
    )
    scores = jnp.einsum(
        "gqd,gkd->gqk", query_group, heads_of_key, preferred_element_type=jnp.float32
    ) * HEAD_SIZE ** (-0.5)
    return (heads_of_key, heads_of_value, visible, jnp.where(visible[None], scores, NEGATIVE_FLOOR))


def fold_local(step_fn, whole, start_carry):
    row_length_total = whole[0].shape[0]
    tile_block = math.gcd(row_length_total, 512)

    def advance(block_index, carry):
        start = block_index * tile_block
        piece = tuple((lax.dynamic_slice_in_dim(member, start, tile_block, 0) for member in whole))
        return step_fn(carry, piece, start)

    return lax.fori_loop(0, row_length_total // tile_block, advance, start_carry)


def on_device(
    hidden_in,
    out_grad,
    doc_ids,
    norm_gain,
    query_weight,
    key_matrix,
    value_matrix,
    attn_out_weight,
    mixer_gate_weight,
    conv_in_weight,
    step_weight,
    conv_weight,
    conv_bias,
    step_bias,
    log_decay,
    skip_gain,
    mixer_gain,
    mamba_out_weight,
    ffn_gain,
    gate_weight,
    up_weight,
    down_weight,
):
    single_float = jnp.float32
    brain_float_half = jnp.bfloat16
    (
        norm_full,
        query_full,
        complete_key,
        value_full,
        attn_out_full,
        mixer_gate_full,
        conv_in_full,
        step_full,
        conv_full,
        conv_bias_full,
        mixer_gain_full,
        mamba_out_full,
    ) = (
        lax.all_gather(norm_gain, (CTX, FSDP), axis=0, tiled=True),
        lax.all_gather(query_weight, (CTX, FSDP), axis=0, tiled=True),
        lax.all_gather(key_matrix, (CTX, FSDP), axis=0, tiled=True),
        lax.all_gather(value_matrix, (CTX, FSDP), axis=0, tiled=True),
        lax.all_gather(attn_out_weight, (CTX, FSDP), axis=0, tiled=True),
        lax.all_gather(mixer_gate_weight, (CTX, FSDP), axis=0, tiled=True),
        lax.all_gather(conv_in_weight, (CTX, FSDP), axis=0, tiled=True),
        lax.all_gather(step_weight, (CTX, FSDP), axis=0, tiled=True),
        lax.all_gather(conv_weight, (CTX, FSDP), axis=1, tiled=True),
        lax.all_gather(conv_bias, (CTX, FSDP), axis=0, tiled=True),
        lax.all_gather(mixer_gain, (CTX, FSDP), axis=0, tiled=True),
        lax.all_gather(mamba_out_weight, (CTX, FSDP), axis=0, tiled=True),
    )
    tokens_per_worker = hidden_in.shape[1]
    head_cluster = QUERY_HEADS // KEY_VALUE_HEADS
    dssm = HS * HP
    taps = CONV - 1
    resid = hidden_in[0].astype(single_float)
    documents = doc_ids[0]
    places = (lax.axis_index(CTX) * tokens_per_worker + jnp.arange(tokens_per_worker)).astype(
        single_float
    )
    norm_one, norm_one_back = jax.vjp(rms_scale, resid, norm_full.astype(single_float))
    normalized_input = norm_one.astype(brain_float_half)
    query_lin = jnp.dot(normalized_input, query_full, preferred_element_type=single_float).reshape(
        tokens_per_worker, QUERY_HEADS, HEAD_SIZE
    )
    key_linear = jnp.dot(
        normalized_input, complete_key, preferred_element_type=single_float
    ).reshape(tokens_per_worker, KEY_VALUE_HEADS, HEAD_SIZE)
    query_turned, unturn_query = jax.vjp(partial(rotate, places=places), query_lin)
    rotated_key, unrotate_key = jax.vjp(partial(rotate, places=places), key_linear)
    rotated_query = query_turned.astype(brain_float_half)
    flattened_key = rotated_key.astype(brain_float_half).reshape(
        tokens_per_worker, KEY_VALUE_HEADS * HEAD_SIZE
    )
    value_lowered = jnp.dot(
        normalized_input, value_full, preferred_element_type=single_float
    ).astype(brain_float_half)
    docs_low = documents.astype(brain_float_half)
    query_group = (
        rotated_query.reshape(tokens_per_worker, KEY_VALUE_HEADS, head_cluster, HEAD_SIZE)
        .transpose(1, 2, 0, 3)
        .reshape(KEY_VALUE_HEADS, head_cluster * tokens_per_worker, HEAD_SIZE)
    )
    query_places = jnp.tile(places, head_cluster)
    query_docs = jnp.tile(documents.astype(single_float), head_cluster)

    def attend_piece(carry, piece, start):
        previous_maximum, total_old, summed_old = carry
        heads_of_key, heads_of_value, visible, scores = piece_scores(
            piece, start, query_group, query_docs, query_places
        )
        peak_new = jnp.maximum(previous_maximum, jnp.max(scores, axis=-1))
        weights = jnp.where(visible[None], jnp.exp(scores - peak_new[:, :, None]), 0.0)
        factor = jnp.exp(previous_maximum - peak_new)
        total_new = total_old * factor + jnp.sum(weights, axis=-1)
        summed_new = summed_old * factor[:, :, None] + jnp.einsum(
            "gqk,gkd->gqd",
            weights.astype(brain_float_half),
            heads_of_value,
            preferred_element_type=single_float,
        )
        return (peak_new, total_new, summed_new)

    rows_of_query = head_cluster * tokens_per_worker
    start_forward = (
        jnp.full((KEY_VALUE_HEADS, rows_of_query), NEGATIVE_FLOOR, single_float),
        jnp.zeros((KEY_VALUE_HEADS, rows_of_query), single_float),
        jnp.zeros((KEY_VALUE_HEADS, rows_of_query, HEAD_SIZE), single_float),
    )
    kv_whole = (
        lax.all_gather(flattened_key, CTX, axis=0, tiled=True),
        lax.all_gather(value_lowered, CTX, axis=0, tiled=True),
        lax.all_gather(docs_low, CTX, axis=0, tiled=True),
    )
    peak, total, summed = fold_local(attend_piece, kv_whole, start_forward)
    attention_cluster = summed / total[:, :, None]
    log_total = peak + jnp.log(total)
    attn_low = (
        attention_cluster.reshape(KEY_VALUE_HEADS, head_cluster, tokens_per_worker, HEAD_SIZE)
        .transpose(2, 0, 1, 3)
        .reshape(tokens_per_worker, QUERY_HEADS * HEAD_SIZE)
        .astype(brain_float_half)
    )
    attn_out = jnp.dot(attn_low, attn_out_full, preferred_element_type=single_float)
    mixer_gate = jnp.dot(normalized_input, mixer_gate_full, preferred_element_type=single_float)
    conv_lin = jnp.dot(normalized_input, conv_in_full, preferred_element_type=single_float).astype(
        brain_float_half
    )
    step_lin = jnp.dot(normalized_input, step_full, preferred_element_type=single_float)
    rim_rows, rim_docs = shifted(
        (conv_lin[tokens_per_worker - taps :], docs_low[tokens_per_worker - taps :]), CTX, 1
    )
    widened = jnp.concatenate([rim_rows, conv_lin], axis=0).astype(single_float)
    widened_docs = jnp.concatenate([rim_docs.astype(jnp.int32), documents])
    prior_doc = widened_docs[taps - 1]
    conv_act, conv_back = jax.vjp(
        partial(conv_part, widened_docs=widened_docs, documents=documents),
        widened,
        conv_full.astype(single_float),
        conv_bias_full.astype(single_float),
    )
    conv_vals = conv_act.astype(brain_float_half).astype(single_float)
    mixer_in = conv_vals[:, :dssm].reshape(tokens_per_worker, HS, HP)
    write_proj = conv_vals[:, dssm : dssm + STATE]
    read_proj = conv_vals[:, dssm + STATE :]
    (step_size, decay_rate), step_back = jax.vjp(step_part, step_lin, step_bias, log_decay)
    (state_loc, carry_decay), stats_back = jax.vjp(
        partial(block_stats, documents=documents, prior_doc=prior_doc),
        mixer_in,
        write_proj,
        step_size,
        decay_rate,
    )
    chain_identity = (jnp.ones_like(carry_decay), jnp.zeros_like(state_loc))
    _, state_in = prefix((carry_decay, state_loc), CTX, chain_combine, chain_identity)
    mixed, mix_back = jax.vjp(
        partial(block_mix, documents=documents, prior_doc=prior_doc),
        mixer_in,
        write_proj,
        read_proj,
        step_size,
        decay_rate,
        skip_gain,
        state_in,
    )
    ymix_vals, gate_back = jax.vjp(
        gated_norm,
        mixed.reshape(tokens_per_worker, dssm),
        mixer_gate,
        mixer_gain_full.astype(single_float),
    )
    ymix_low = ymix_vals.astype(brain_float_half)
    mamba_out = jnp.dot(ymix_low, mamba_out_full, preferred_element_type=single_float)
    ffn_gain_full, gate_full, up_full, down_full = (
        lax.all_gather(ffn_gain, (CTX, FSDP), axis=0, tiled=True),
        lax.all_gather(gate_weight, (CTX, FSDP), axis=0, tiled=True),
        lax.all_gather(up_weight, (CTX, FSDP), axis=0, tiled=True),
        lax.all_gather(down_weight, (CTX, FSDP), axis=0, tiled=True),
    )
    mid = resid + attn_out + mamba_out
    norm_two, norm_two_back = jax.vjp(rms_scale, mid, ffn_gain_full.astype(single_float))
    normed_two = norm_two.astype(brain_float_half)
    gate_lin = jnp.dot(normed_two, gate_full, preferred_element_type=single_float)
    up_lin = jnp.dot(normed_two, up_full, preferred_element_type=single_float)
    sigmoid_gate = jax.nn.sigmoid(gate_lin)
    silu_gate = gate_lin * sigmoid_gate
    hidden = (silu_gate * up_lin).astype(brain_float_half)
    block_out = (mid + jnp.dot(hidden, down_full, preferred_element_type=single_float)).astype(
        brain_float_half
    )
    grad_out = out_grad[0]
    down_grad_w = jnp.einsum("tf,td->fd", hidden, grad_out, preferred_element_type=single_float)
    grad_hidden = jnp.einsum("td,fd->tf", grad_out, down_full, preferred_element_type=single_float)
    grad_gate = (grad_hidden * up_lin * (sigmoid_gate + silu_gate * (1.0 - sigmoid_gate))).astype(
        brain_float_half
    )
    grad_up = (grad_hidden * silu_gate).astype(brain_float_half)
    gate_grad_w = jnp.einsum(
        "td,tf->df", normed_two, grad_gate, preferred_element_type=single_float
    )
    up_grad_w = jnp.einsum("td,tf->df", normed_two, grad_up, preferred_element_type=single_float)
    grad_normed_two = jnp.einsum(
        "tf,df->td", grad_gate, gate_full, preferred_element_type=single_float
    ) + jnp.einsum("tf,df->td", grad_up, up_full, preferred_element_type=single_float)
    grad_mid_norm, ffn_gain_grad = norm_two_back(grad_normed_two)
    grad_mid = grad_out.astype(single_float) + grad_mid_norm
    ffn_sums = (
        lax.psum_scatter(ffn_gain_grad, (CTX, FSDP), scatter_dimension=0, tiled=True),
        lax.psum_scatter(gate_grad_w, (CTX, FSDP), scatter_dimension=0, tiled=True),
        lax.psum_scatter(up_grad_w, (CTX, FSDP), scatter_dimension=0, tiled=True),
        lax.psum_scatter(down_grad_w, (CTX, FSDP), scatter_dimension=0, tiled=True),
    )
    branch_grad = grad_mid.astype(brain_float_half)
    attn_out_grad_w = jnp.einsum(
        "ti,td->id", attn_low, branch_grad, preferred_element_type=single_float
    )
    attention_gradient = jnp.einsum(
        "td,id->ti", branch_grad, attn_out_full, preferred_element_type=single_float
    ).astype(brain_float_half)
    grad_group = (
        attention_gradient.reshape(tokens_per_worker, KEY_VALUE_HEADS, head_cluster, HEAD_SIZE)
        .transpose(1, 2, 0, 3)
        .reshape(KEY_VALUE_HEADS, rows_of_query, HEAD_SIZE)
    )
    row_delta = jnp.sum(grad_group.astype(single_float) * attention_cluster, axis=-1)

    def attend_back(carry, piece, start):
        query_acc, kv_grad = carry
        heads_of_key, heads_of_value, visible, scores = piece_scores(
            piece, start, query_group, query_docs, query_places
        )
        segment_rows = heads_of_key.shape[1]
        probs = jnp.where(visible[None], jnp.exp(scores - log_total[:, :, None]), 0.0)
        prob_grad = jnp.einsum(
            "gqd,gkd->gqk", grad_group, heads_of_value, preferred_element_type=single_float
        )
        score_grad = (probs * (prob_grad - row_delta[:, :, None])).astype(brain_float_half)
        query_acc = query_acc + jnp.einsum(
            "gqk,gkd->gqd", score_grad, heads_of_key, preferred_element_type=single_float
        )
        key_portion = jnp.einsum(
            "gqk,gqd->kgd", score_grad, query_group, preferred_element_type=single_float
        ) * HEAD_SIZE ** (-0.5)
        value_portion = jnp.einsum(
            "gqk,gqd->kgd",
            probs.astype(brain_float_half),
            grad_group,
            preferred_element_type=single_float,
        )
        term = jnp.concatenate(
            [
                key_portion.reshape(segment_rows, KEY_VALUE_HEADS * HEAD_SIZE),
                value_portion.reshape(segment_rows, KEY_VALUE_HEADS * HEAD_SIZE),
            ],
            axis=1,
        )
        current = lax.dynamic_slice_in_dim(kv_grad, start, segment_rows, 0)
        kv_grad = lax.dynamic_update_slice_in_dim(kv_grad, current + term, start, 0)
        return (query_acc, kv_grad)

    start_back = (
        jnp.zeros((KEY_VALUE_HEADS, rows_of_query, HEAD_SIZE), single_float),
        jnp.zeros(
            (tokens_per_worker * lax.axis_size(CTX), 2 * KEY_VALUE_HEADS * HEAD_SIZE),
            single_float,
        ),
    )
    query_acc, kv_grad = fold_local(attend_back, kv_whole, start_back)
    local_key_value = lax.psum_scatter(
        kv_grad.astype(jnp.bfloat16), CTX, scatter_dimension=0, tiled=True
    ).astype(jnp.float32)
    query_turn_grad = (
        (query_acc * HEAD_SIZE ** (-0.5))
        .reshape(KEY_VALUE_HEADS, head_cluster, tokens_per_worker, HEAD_SIZE)
        .transpose(2, 0, 1, 3)
        .reshape(tokens_per_worker, QUERY_HEADS, HEAD_SIZE)
    )
    query_lin_grad = (
        unturn_query(query_turn_grad)[0]
        .reshape(tokens_per_worker, QUERY_HEADS * HEAD_SIZE)
        .astype(brain_float_half)
    )
    key_lin_grad = (
        unrotate_key(
            local_key_value[:, : KEY_VALUE_HEADS * HEAD_SIZE].reshape(
                tokens_per_worker, KEY_VALUE_HEADS, HEAD_SIZE
            )
        )[0]
        .reshape(tokens_per_worker, KEY_VALUE_HEADS * HEAD_SIZE)
        .astype(brain_float_half)
    )
    value_linear_gradient = local_key_value[:, KEY_VALUE_HEADS * HEAD_SIZE :].astype(
        brain_float_half
    )
    mamba_grad_w = jnp.einsum(
        "ti,td->id", ymix_low, branch_grad, preferred_element_type=single_float
    )
    grad_ymix = jnp.einsum(
        "td,id->ti", branch_grad, mamba_out_full, preferred_element_type=single_float
    )
    grad_mixed, grad_zgate, mixer_gain_grad = gate_back(grad_ymix)
    zgate_low = grad_zgate.astype(brain_float_half)
    (
        grad_in_mix,
        grad_write_mix,
        grad_read,
        grad_step_mix,
        grad_rate_mix,
        skip_grad,
        grad_state_in,
    ) = mix_back(grad_mixed.reshape(tokens_per_worker, HS, HP))
    _, state_later = carried_in((carry_decay, grad_state_in), CTX, chain_combine, chain_identity)
    decay_grad = jnp.sum(state_in * state_later, axis=(1, 2))
    grad_in_stats, grad_write_stats, grad_step_stats, grad_rate_stats = stats_back(
        (state_later, decay_grad)
    )
    grad_conv = jnp.concatenate(
        [
            (grad_in_mix + grad_in_stats).reshape(tokens_per_worker, dssm),
            grad_write_mix + grad_write_stats,
            grad_read,
        ],
        axis=1,
    )
    grad_widened, conv_weight_grad, conv_bias_grad = conv_back(grad_conv)
    rim_grad = shifted(grad_widened[:taps].astype(jnp.bfloat16), CTX, -1).astype(jnp.float32)
    conv_lin_grad = (
        grad_widened[taps:].at[tokens_per_worker - taps :].add(rim_grad).astype(brain_float_half)
    )
    step_lin_grad, step_bias_grad, log_decay_grad = step_back(
        (grad_step_mix + grad_step_stats, grad_rate_mix + grad_rate_stats)
    )
    step_lin_low = step_lin_grad.astype(brain_float_half)
    query_grad_w = jnp.einsum(
        "td,ti->di", normalized_input, query_lin_grad, preferred_element_type=single_float
    )
    key_grad_w = jnp.einsum(
        "td,ti->di", normalized_input, key_lin_grad, preferred_element_type=single_float
    )
    value_grad_w = jnp.einsum(
        "td,ti->di", normalized_input, value_linear_gradient, preferred_element_type=single_float
    )
    zgate_grad_w = jnp.einsum(
        "td,ti->di", normalized_input, zgate_low, preferred_element_type=single_float
    )
    conv_in_grad_w = jnp.einsum(
        "td,ti->di", normalized_input, conv_lin_grad, preferred_element_type=single_float
    )
    step_grad_w = jnp.einsum(
        "td,ti->di", normalized_input, step_lin_low, preferred_element_type=single_float
    )
    grad_normed = (
        jnp.einsum("ti,di->td", query_lin_grad, query_full, preferred_element_type=single_float)
        + jnp.einsum("ti,di->td", key_lin_grad, complete_key, preferred_element_type=single_float)
        + jnp.einsum(
            "ti,di->td", value_linear_gradient, value_full, preferred_element_type=single_float
        )
        + jnp.einsum("ti,di->td", zgate_low, mixer_gate_full, preferred_element_type=single_float)
        + jnp.einsum("ti,di->td", conv_lin_grad, conv_in_full, preferred_element_type=single_float)
        + jnp.einsum("ti,di->td", step_lin_low, step_full, preferred_element_type=single_float)
    )
    grad_resid_norm, norm_gain_grad = norm_one_back(grad_normed)
    input_grad = (grad_mid + grad_resid_norm).astype(brain_float_half)
    mixer_sums = (
        lax.psum_scatter(norm_gain_grad, (CTX, FSDP), scatter_dimension=0, tiled=True),
        lax.psum_scatter(query_grad_w, (CTX, FSDP), scatter_dimension=0, tiled=True),
        lax.psum_scatter(key_grad_w, (CTX, FSDP), scatter_dimension=0, tiled=True),
        lax.psum_scatter(value_grad_w, (CTX, FSDP), scatter_dimension=0, tiled=True),
        lax.psum_scatter(attn_out_grad_w, (CTX, FSDP), scatter_dimension=0, tiled=True),
        lax.psum_scatter(zgate_grad_w, (CTX, FSDP), scatter_dimension=0, tiled=True),
        lax.psum_scatter(conv_in_grad_w, (CTX, FSDP), scatter_dimension=0, tiled=True),
        lax.psum_scatter(step_grad_w, (CTX, FSDP), scatter_dimension=0, tiled=True),
        lax.psum_scatter(conv_weight_grad, (CTX, FSDP), scatter_dimension=1, tiled=True),
        lax.psum_scatter(conv_bias_grad, (CTX, FSDP), scatter_dimension=0, tiled=True),
        lax.psum_scatter(mixer_gain_grad, (CTX, FSDP), scatter_dimension=0, tiled=True),
        lax.psum_scatter(mamba_grad_w, (CTX, FSDP), scatter_dimension=0, tiled=True),
    )
    summed_grads = tuple(mixer_sums) + tuple(ffn_sums)
    step_bias_sum, log_decay_sum, skip_sum = lax.psum(
        (step_bias_grad, log_decay_grad, skip_grad), (CTX, FSDP)
    )
    return (
        block_out[None],
        input_grad[None],
        summed_grads[0],
        summed_grads[1],
        summed_grads[2],
        summed_grads[3],
        summed_grads[4],
        summed_grads[5],
        summed_grads[6],
        summed_grads[7],
        summed_grads[8],
        summed_grads[9],
        step_bias_sum,
        log_decay_sum,
        skip_sum,
        summed_grads[10],
        summed_grads[11],
        summed_grads[12],
        summed_grads[13],
        summed_grads[14],
        summed_grads[15],
    )


BF = jnp.bfloat16
F32 = jnp.float32


def dotf(left, right, dims):
    return lax.dot_general(left, right, (dims, ((), ())), preferred_element_type=F32)


def mm(left, right):
    return dotf(left, right, ((left.ndim - 1,), (0,)))


def mm_nt(left, right):
    return dotf(left, right, ((1,), (1,)))


def mm_tn(left, right):
    return dotf(left, right, ((0,), (0,)))


MESH = pl.DeviceIdType.MESH
PLANE = 8


def plane():
    me = lax.axis_index(CTX)
    sibling = me + 1 - 2 * (me % 2)
    by_x = me + 2 - 4 * ((me // 2) % 2)
    by_y = me + 4 - 8 * (me // 4)
    return me, sibling, by_x, by_y


def unused(kernel, used, extra):
    def call(*refs):
        return kernel(*refs[:used], *refs[used + extra :])

    return call


def greet(peers):
    barrier = pltpu.get_barrier_semaphore()
    for axis, other in peers:
        pl.semaphore_signal(barrier, inc=1, device_id={axis: other}, device_id_type=MESH)
    pl.semaphore_wait(barrier, len(peers))


def remote(src, dst, send_sem, recv_sem, axis, to):
    return pltpu.make_async_remote_copy(
        src_ref=src,
        dst_ref=dst,
        send_sem=send_sem,
        recv_sem=recv_sem,
        device_id={axis: to},
        device_id_type=MESH,
    )


def together(*tasks):
    tasks = list(tasks)
    while tasks:
        for task in list(tasks):
            if next(task, None) is None:
                tasks.remove(task)


def other_places(axis, count):
    place = lax.axis_index(axis)
    return [(axis, (place + j) % count) for j in range(1, count)]


def gather_steps(pieces, x_ref, o_ref, own_sem, send_sem, recv_sem):
    rows = x_ref.shape[0]
    n = rows // pieces
    half = pieces // 2
    me, sibling, by_x, by_y = plane()
    across = by_x + by_y - me
    keep = pltpu.make_async_copy(x_ref, o_ref.at[pl.ds(me * rows, rows)], own_sem)
    keep.start()
    started = []

    def at(block, piece):
        return o_ref.at[pl.ds(block * rows + piece * n, n)]

    def go(src, block, piece, kind, to, slot):
        copy = remote(
            src, at(block, piece), send_sem.at[slot, piece], recv_sem.at[kind, piece], CTX, to
        )
        copy.start()
        started.append(copy)

    def arrived(block, piece, kind):
        here = at(block, piece)
        remote(here, here, send_sem.at[0, piece], recv_sem.at[kind, piece], CTX, sibling).wait_recv()

    for i in range(pieces):
        a, b = i, pieces - 1 - i
        go(x_ref.at[pl.ds(a * n, n)], me, a, 1, by_x, 1)
        go(x_ref.at[pl.ds(b * n, n)], me, b, 2, by_y, 2)
    for i in range(pieces):
        go(x_ref.at[pl.ds(i * n, n)], me, i, 0, sibling, 0)
    yield True
    for i in range(pieces):
        a, b = i, pieces - 1 - i
        arrived(by_x, a, 1)
        if i < half:
            go(at(by_x, a), by_x, a, 5, by_y, 5)
        go(at(by_x, a), by_x, a, 3, sibling, 3)
        arrived(by_y, b, 2)
        if i < half:
            go(at(by_y, b), by_y, b, 5, by_x, 5)
        go(at(by_y, b), by_y, b, 4, sibling, 4)
        yield True
    for i in range(half):
        for p in (i, pieces - 1 - i):
            arrived(across, p, 5)
            go(at(across, p), across, p, 6, sibling, 6)
        yield True
    shift = sibling - me
    for p in range(pieces):
        arrived(sibling, p, 0)
        arrived(by_x + shift, p, 3)
        arrived(by_y + shift, p, 4)
        arrived(across + shift, p, 6)
    for copy in started:
        copy.wait_send()
    keep.wait()


def chain_steps(pieces, count, x_ref, o_ref, own_sem, send_sem, recv_sem):
    mine = lax.axis_index(FSDP)
    n = x_ref.shape[0] // pieces
    up, down = mine + 1, mine - 1
    has_up, has_down = mine < count - 1, mine > 0
    keep = pltpu.make_async_copy(x_ref, o_ref.at[mine], own_sem)
    keep.start()

    def copy(src, block, piece, way, hop, to):
        return remote(
            src,
            o_ref.at[block, pl.ds(piece * n, n)],
            send_sem.at[way, hop, piece],
            recv_sem.at[way, hop, piece],
            FSDP,
            to,
        )

    def own(piece):
        return x_ref.at[pl.ds(piece * n, n)]

    for p in range(pieces):

        @pl.when(has_up)
        def _(p=p):
            copy(own(p), mine, p, 0, 0, up).start()

        @pl.when(has_down)
        def _(p=p):
            copy(own(p), mine, p, 1, 0, down).start()

    yield True
    for d in range(1, count):
        for p in range(pieces):

            @pl.when(mine >= d)
            def _(d=d, p=p):
                here = o_ref.at[mine - d, pl.ds(p * n, n)]
                copy(here, mine - d, p, 0, d - 1, down).wait_recv()

                @pl.when(has_up)
                def _():
                    copy(here, mine - d, p, 0, d, up).start()

            @pl.when(mine + d < count)
            def _(d=d, p=p):
                here = o_ref.at[mine + d, pl.ds(p * n, n)]
                copy(here, mine + d, p, 1, d - 1, up).wait_recv()

                @pl.when(has_down)
                def _():
                    copy(here, mine + d, p, 1, d, down).start()

            yield True
    for d in range(count - 1):
        for p in range(pieces):

            @pl.when((mine >= d) & has_up)
            def _(d=d, p=p):
                copy(own(p), mine - d, p, 0, d, up).wait_send()

            @pl.when((mine + d < count) & has_down)
            def _(d=d, p=p):
                copy(own(p), mine + d, p, 1, d, down).wait_send()

    keep.wait()


def chain_scratch(pieces, count):
    return [
        pltpu.SemaphoreType.DMA,
        pltpu.SemaphoreType.DMA((2, count - 1, pieces)),
        pltpu.SemaphoreType.DMA((2, count - 1, pieces)),
    ]


def gather_kernel(pieces, *refs):
    me, sibling, by_x, by_y = plane()
    greet([(CTX, sibling), (CTX, by_x), (CTX, by_y)])
    together(gather_steps(pieces, *refs))


def gather_tokens(block, ids, pieces=4, waits=()):
    rows, cols = block.shape
    return pl.pallas_call(
        unused(partial(gather_kernel, pieces), 1, len(waits)),
        out_shape=jax.ShapeDtypeStruct((PLANE * rows, cols), block.dtype),
        in_specs=[pl.BlockSpec(memory_space=pl.ANY)] * (1 + len(waits)),
        out_specs=pl.BlockSpec(memory_space=pl.ANY),
        scratch_shapes=[
            pltpu.SemaphoreType.DMA,
            pltpu.SemaphoreType.DMA((7, pieces)),
            pltpu.SemaphoreType.DMA((7, pieces)),
        ],
        cost_estimate=lasting(22 if cols > 1024 else 8),
        compiler_params=pltpu.CompilerParams(collective_id=next(ids), has_side_effects=True),
    )(block, *waits)


def scatter_steps(
    seqs, p_ref, o_ref, own, got, out, rx, ry, dx, dy, own_sem, send_sem, recv_sem, make=None
):
    rows = o_ref.shape[0]
    h = rows // 2
    me, sibling, by_x, by_y = plane()
    across = by_x + by_y - me
    shift = sibling - me
    top, low = pl.ds(0, h), pl.ds(h, h)
    loads, sends = [], []
    for k, block in enumerate((across, by_x, by_y, me)):
        if make is not None:
            make(block // 2)
        for j in range(2):
            copy = remote(
                p_ref.at[pl.ds((block + shift) * rows + j * h, h)],
                got.at[k, pl.ds(j * h, h)],
                send_sem.at[k * 2 + j],
                recv_sem.at[k * 2 + j],
                CTX,
                sibling,
            )
            copy.start()
            sends.append(copy)
            load = pltpu.make_async_copy(
                p_ref.at[pl.ds(block * rows + j * h, h)],
                own.at[k, pl.ds(j * h, h)],
                own_sem.at[k * 2 + j],
            )
            load.start()
            loads.append(load)

    def pair(k, j):
        sends[k * 2 + j].wait_recv()
        loads[k * 2 + j].wait()
        part = pl.ds(j * h, h)
        return own[k, part].astype(F32) + got[k, part].astype(F32)

    def put(part, total):
        if not seqs:
            o_ref[part] = total
            return
        chunk = total.shape[1] // (PLANE * seqs)
        per = 128 // chunk
        for k in range(total.shape[1] // 128):
            blocks = [(n % seqs) * PLANE + n // seqs for n in range(k * per, (k + 1) * per)]
            o_ref[part, k * 128 : (k + 1) * 128] = jnp.concatenate(
                [total[:, b * chunk : (b + 1) * chunk] for b in blocks], axis=1
            )

    def go(src, dst, slot, to):
        copy = remote(src, dst, send_sem.at[slot], recv_sem.at[slot], CTX, to)
        copy.start()
        sends.append(copy)
        return copy

    yield True
    out[0, top] = pair(0, 0).astype(out.dtype)
    across_x = go(out.at[0, top], dx, 8, by_x)
    out[0, low] = pair(0, 1).astype(out.dtype)
    across_y = go(out.at[0, low], dy, 9, by_y)
    out[1, top] = pair(1, 0).astype(out.dtype)
    x_top = go(out.at[1, top], rx.at[top], 10, by_x)
    out[2, low] = pair(2, 1).astype(out.dtype)
    y_low = go(out.at[2, low], ry.at[low], 11, by_y)
    yield True
    across_y.wait_recv()
    out[1, low] = (pair(1, 1) + dy[...].astype(F32)).astype(out.dtype)
    x_low = go(out.at[1, low], rx.at[low], 12, by_x)
    across_x.wait_recv()
    out[2, top] = (pair(2, 0) + dx[...].astype(F32)).astype(out.dtype)
    y_top = go(out.at[2, top], ry.at[top], 13, by_y)
    yield True
    first, second = pair(3, 0), pair(3, 1)
    x_top.wait_recv()
    y_top.wait_recv()
    put(top, first + rx[top].astype(F32) + ry[top].astype(F32))
    x_low.wait_recv()
    y_low.wait_recv()
    put(low, second + rx[low].astype(F32) + ry[low].astype(F32))
    for copy in sends:
        copy.wait_send()


def scatter_kernel(seqs, *refs):
    me, sibling, by_x, by_y = plane()
    greet([(CTX, sibling), (CTX, by_x), (CTX, by_y)])
    together(scatter_steps(seqs, *refs))


def scatter_scratch(rows, cols):
    def room(*shape):
        return pltpu.VMEM(shape, BF)

    return [
        room(4, rows, cols),
        room(4, rows, cols),
        room(3, rows, cols),
        room(rows, cols),
        room(rows, cols),
        room(rows // 2, cols),
        room(rows // 2, cols),
        pltpu.SemaphoreType.DMA((8,)),
        pltpu.SemaphoreType.DMA((14,)),
        pltpu.SemaphoreType.DMA((14,)),
    ]


def scatter_tokens(partial_sum, ids, waits=(), seqs=0):
    rows, cols = partial_sum.shape[0] // PLANE, partial_sum.shape[1]

    return pl.pallas_call(
        unused(partial(scatter_kernel, seqs), 1, len(waits)),
        out_shape=jax.ShapeDtypeStruct((rows, cols), F32),
        in_specs=[pl.BlockSpec(memory_space=pl.ANY)] * (1 + len(waits)),
        out_specs=pl.BlockSpec(memory_space=pltpu.VMEM),
        scratch_shapes=scatter_scratch(rows, cols),
        cost_estimate=lasting(22 if cols > 1024 else 8),
        compiler_params=pltpu.CompilerParams(
            collective_id=next(ids), has_side_effects=True, vmem_limit_bytes=40 * 2**20
        ),
    )(partial_sum.astype(BF), *waits)


def row_sum_steps(x_ref, o_ref, got, send_sem, recv_sem):
    copies = []
    for j, (axis, other) in enumerate(other_places(CTX, PLANE)):
        copy = remote(x_ref, got.at[j], send_sem.at[j], recv_sem.at[j], axis, other)
        copy.start()
        copies.append(copy)
    for _ in range(3):
        yield True
    total = x_ref[...]
    for j, copy in enumerate(copies):
        copy.wait_recv()
        total = total + got[j]
    o_ref[...] = total
    for copy in copies:
        copy.wait_send()


def row_sum_kernel(*refs):
    greet(other_places(CTX, PLANE))
    together(row_sum_steps(*refs))


def row_sum_beside_kernel(seqs, head, x_ref, a, b, o_ref, o, *scratch):
    first = head // seqs
    second = o.shape[1] - first

    def stores(made):
        return [
            (made.at[pl.ds(f * first, first)], o.at[f, pl.ds(0, first)]) for f in range(seqs)
        ] + [
            (made.at[pl.ds(head + f * second, second)], o.at[f, pl.ds(first, second)])
            for f in range(seqs)
        ]

    greet(other_places(CTX, PLANE))
    together(
        row_sum_steps(x_ref, o_ref, *scratch[:3]),
        product_steps(1, 256, 1, stores, a, b, *scratch[3:]),
    )


def row_sum_beside(rows, a, b, head, seqs, ids, waits=()):
    anywhere = pl.BlockSpec(memory_space=pl.ANY)
    near = pl.BlockSpec(memory_space=pltpu.VMEM)
    tile = rows.reshape(8, -1)
    total, product = pl.pallas_call(
        unused(partial(row_sum_beside_kernel, seqs, head), 3, len(waits)),
        out_shape=(
            jax.ShapeDtypeStruct(tile.shape, F32),
            jax.ShapeDtypeStruct((seqs, a.shape[1] // seqs, b.shape[1]), BF),
        ),
        in_specs=[near] + [anywhere] * (2 + len(waits)),
        out_specs=(near, anywhere),
        scratch_shapes=[
            pltpu.VMEM((PLANE - 1,) + tile.shape, F32),
            pltpu.SemaphoreType.DMA((PLANE - 1,)),
            pltpu.SemaphoreType.DMA((PLANE - 1,)),
        ]
        + product_scratch(1, a, b, 2 * seqs),
        cost_estimate=lasting(8),
        compiler_params=pltpu.CompilerParams(
            collective_id=next(ids), has_side_effects=True, vmem_limit_bytes=40 * 2**20
        ),
    )(tile, a, b, *waits)
    return total.reshape(rows.shape), product


def row_sum(rows, ids, waits=()):
    tile = rows.reshape(8, -1)
    total = pl.pallas_call(
        unused(row_sum_kernel, 1, len(waits)),
        out_shape=jax.ShapeDtypeStruct(tile.shape, F32),
        in_specs=[pl.BlockSpec(memory_space=pltpu.VMEM)]
        + [pl.BlockSpec(memory_space=pl.ANY)] * len(waits),
        out_specs=pl.BlockSpec(memory_space=pltpu.VMEM),
        scratch_shapes=[
            pltpu.VMEM((PLANE - 1,) + tile.shape, F32),
            pltpu.SemaphoreType.DMA((PLANE - 1,)),
            pltpu.SemaphoreType.DMA((PLANE - 1,)),
        ],
        cost_estimate=lasting(5),
        compiler_params=pltpu.CompilerParams(collective_id=next(ids), has_side_effects=True),
    )(tile, *waits)
    return total.reshape(rows.shape)


def small_gather_steps(seqs, x_ref, o_ref, own_sem, send_sem, recv_sem):
    me, mine = lax.axis_index(CTX), lax.axis_index(FSDP)
    keep = pltpu.make_async_copy(x_ref, o_ref.at[me, mine], own_sem)
    keep.start()
    copies = []
    for j, (axis, other) in enumerate(other_places(FSDP, seqs)):
        copy = remote(x_ref, o_ref.at[me, mine], send_sem.at[j], recv_sem.at[j], axis, other)
        copy.start()
        copies.append(copy)
    yield True
    keep.wait()
    for copy in copies:
        copy.wait_recv()
    for j, (axis, other) in enumerate(other_places(CTX, PLANE)):
        k = seqs + j
        copy = remote(o_ref.at[me], o_ref.at[me], send_sem.at[k], recv_sem.at[k], axis, other)
        copy.start()
        copies.append(copy)
    for _ in range(8):
        yield True
    for copy in copies[seqs - 1 :]:
        copy.wait_recv()
    for copy in copies:
        copy.wait_send()


def columns(ref, place, count):
    return ref.at[:, pl.ds(pl.multiple_of(place * count, 128), count)]


def swap_steps(delay, patience, routes, own_sem, send_sem, recv_sem):
    me = lax.axis_index(CTX)
    for _ in range(delay):
        yield True
    keeps, copies = [], []
    for k, (part, land) in enumerate(routes):
        keep = pltpu.make_async_copy(part(me), land(me), own_sem.at[k])
        keep.start()
        keeps.append(keep)
    for j in (4, 2, 6, 3, 5, 7, 1):
        to = (me + j) % PLANE
        for k, (part, land) in enumerate(routes):
            copy = remote(part(to), land(me), send_sem.at[j, k], recv_sem.at[j, k], CTX, to)
            copy.start()
            copies.append(copy)
    for _ in range(patience):
        yield True
    for copy in copies:
        copy.wait_recv()
    for copy in copies:
        copy.wait_send()
    for keep in keeps:
        keep.wait()


def swap_scratch(routes):
    return [
        pltpu.SemaphoreType.DMA((routes,)),
        pltpu.SemaphoreType.DMA((PLANE, routes)),
        pltpu.SemaphoreType.DMA((PLANE, routes)),
    ]


def one_after(*tasks):
    for task in tasks:
        yield from task


def opening_kernel(seqs, pieces, *refs):
    tile, shard, hat, rows, query, zgate, channels, mixed, gate, up = refs[:10]
    o_tile, o_shard, o_hat, o_rows, conv, rest, ffn, o_conv = refs[10:18]
    sems = refs[18:]
    sems = [sems[k : k + 3] for k in range(0, len(sems), 3)]
    head = query.shape[1] // PLANE
    inner = zgate.shape[1] // PLANE
    half = gate.shape[1] // PLANE
    greet(other_places(FSDP, seqs) + other_places(CTX, PLANE))
    to_conv = [
        (lambda to: columns(channels, to, inner), lambda at: conv.at[at, :, :inner]),
        (lambda to: mixed.at[to], lambda at: conv.at[at, :, inner:]),
    ]
    to_rest = [
        (lambda to: columns(query, to, head), lambda at: rest.at[at, :, :head]),
        (lambda to: columns(zgate, to, inner), lambda at: rest.at[at, :, head:]),
    ]
    to_ffn = [
        (lambda to: columns(gate, to, half), lambda at: ffn.at[at, :, :half]),
        (lambda to: columns(up, to, half), lambda at: ffn.at[at, :, half:]),
    ]
    together(
        one_after(
            swap_steps(0, 1, to_conv, *sems[0]), chain_steps(4, seqs, conv, o_conv, *sems[1])
        ),
        chain_steps(4, seqs, shard, o_shard, *sems[2]),
        small_gather_steps(seqs, tile, o_tile, *sems[3]),
        gather_steps(pieces, hat, o_hat, *sems[4]),
        swap_steps(1, 8, to_rest, *sems[5]),
        swap_steps(3, 8, to_ffn, *sems[6]),
        one_after(delay_steps(5), gather_steps(pieces, rows, o_rows, *sems[7])),
    )


def delay_steps(turns):
    for _ in range(turns):
        yield True


def opening(tile, shard, hat, rows, query, zgate, channels, mixed, gate, up, seqs, ids, pieces=2):
    anywhere = pl.BlockSpec(memory_space=pl.ANY)
    krows = query.shape[0]
    inner = zgate.shape[1] // PLANE
    conv_cols = inner + mixed.shape[2]
    rest_cols = query.shape[1] // PLANE + inner
    ffn_cols = (gate.shape[1] + up.shape[1]) // PLANE

    def shape(*dims):
        return jax.ShapeDtypeStruct(dims, BF)

    def three(*dims):
        return [
            pltpu.SemaphoreType.DMA,
            pltpu.SemaphoreType.DMA(dims),
            pltpu.SemaphoreType.DMA(dims),
        ]

    return pl.pallas_call(
        partial(opening_kernel, seqs, pieces),
        out_shape=(
            shape(PLANE, seqs, *tile.shape),
            shape(seqs, *shard.shape),
            shape(PLANE * hat.shape[0], hat.shape[1]),
            shape(PLANE * rows.shape[0], rows.shape[1]),
            shape(PLANE, krows, conv_cols),
            shape(PLANE, krows, rest_cols),
            shape(PLANE, krows, ffn_cols),
            shape(seqs, PLANE, krows, conv_cols),
        ),
        in_specs=[anywhere] * 10,
        out_specs=(anywhere,) * 8,
        scratch_shapes=swap_scratch(2)
        + chain_scratch(4, seqs)
        + chain_scratch(4, seqs)
        + three(PLANE + seqs)
        + three(7, pieces)
        + swap_scratch(2)
        + swap_scratch(2)
        + three(7, pieces),
        cost_estimate=lasting(70),
        compiler_params=pltpu.CompilerParams(collective_id=next(ids), has_side_effects=True),
    )(tile, shard, hat, rows, query, zgate, channels, mixed, gate, up)


def small_scatter_steps(seqs, x_ref, o_ref, mine_ref, got, total, late, own_sem, send_sem, recv_sem):
    me, mine = lax.axis_index(CTX), lax.axis_index(FSDP)
    load = pltpu.make_async_copy(x_ref.at[me], mine_ref, own_sem)
    load.start()
    copies = []
    for j, (axis, to) in enumerate(other_places(CTX, PLANE)):
        copy = remote(x_ref.at[to], got.at[j], send_sem.at[j], recv_sem.at[j], axis, to)
        copy.start()
        copies.append(copy)
    yield True
    load.wait()
    acc = mine_ref[...]
    for j, copy in enumerate(copies):
        copy.wait_recv()
        acc = acc + got[j]
    total[...] = acc
    first = len(copies)
    for j, (axis, other) in enumerate(other_places(FSDP, seqs)):
        k = PLANE + j
        copy = remote(total.at[other], late.at[j], send_sem.at[k], recv_sem.at[k], axis, other)
        copy.start()
        copies.append(copy)
    yield True
    out = total[mine]
    for j, copy in enumerate(copies[first:]):
        copy.wait_recv()
        out = out + late[j]
    o_ref[...] = out
    for copy in copies:
        copy.wait_send()


def product_steps(kind, block, rounds, stores, a_any, b_any, a, b, o, sems):
    loads = [
        pltpu.make_async_copy(src, dst, sems.at[k])
        for k, (src, dst) in enumerate(((a_any, a), (b_any, b)))
    ]
    for load in loads:
        load.start()
    yield True
    for load in loads:
        load.wait()
    count = o.shape[0] // block
    per = -(-count // rounds)
    for first in range(0, count, per):

        def one(k, carry):
            rows = pl.ds(pl.multiple_of(k * block, 128), block)
            if kind:
                part = lax.dot_general(
                    a[:, rows], b[...], (((0,), (0,)), ((), ())), preferred_element_type=F32
                )
            else:
                part = jnp.dot(a[rows, :], b[...], preferred_element_type=F32)
            o[rows, :] = part.astype(BF)
            return carry

        lax.fori_loop(first, min(first + per, count), one, 0)
        yield True
    copies = [
        pltpu.make_async_copy(src, dst, sems.at[2 + k]) for k, (src, dst) in enumerate(stores(o))
    ]
    for copy in copies:
        copy.start()
    yield True
    for copy in copies:
        copy.wait()


def product_scratch(kind, a, b, stores=1):
    rows = a.shape[1] if kind else a.shape[0]
    return [
        pltpu.VMEM(a.shape, BF),
        pltpu.VMEM(b.shape, BF),
        pltpu.VMEM((rows, b.shape[1]), BF),
        pltpu.SemaphoreType.DMA((2 + stores,)),
    ]


def scatter_beside_kernel(seqs, p_ref, a, b, o_ref, o, *scratch):
    me, sibling, by_x, by_y = plane()
    greet([(CTX, sibling), (CTX, by_x), (CTX, by_y)])
    together(
        scatter_steps(seqs, p_ref, o_ref, *scratch[:10]),
        product_steps(1, 256, 3, lambda made: [(made, o)], a, b, *scratch[10:]),
    )


def scatter_beside(partial_sum, a, b, seqs, ids, waits=()):
    anywhere = pl.BlockSpec(memory_space=pl.ANY)
    rows, cols = partial_sum.shape[0] // PLANE, partial_sum.shape[1]
    return pl.pallas_call(
        unused(partial(scatter_beside_kernel, seqs), 3, len(waits)),
        out_shape=(
            jax.ShapeDtypeStruct((rows, cols), F32),
            jax.ShapeDtypeStruct((a.shape[1], b.shape[1]), BF),
        ),
        in_specs=[anywhere] * (3 + len(waits)),
        out_specs=(pl.BlockSpec(memory_space=pltpu.VMEM), anywhere),
        scratch_shapes=scatter_scratch(rows, cols) + product_scratch(1, a, b),
        cost_estimate=lasting(25),
        compiler_params=pltpu.CompilerParams(
            collective_id=next(ids), has_side_effects=True, vmem_limit_bytes=40 * 2**20
        ),
    )(partial_sum.astype(BF), a, b, *waits)


def gather_beside_kernel(pieces, x_ref, a, b, o_ref, o, *scratch):
    me, sibling, by_x, by_y = plane()
    greet([(CTX, sibling), (CTX, by_x), (CTX, by_y)])
    together(
        gather_steps(pieces, x_ref, o_ref, *scratch[:3]),
        product_steps(0, 256, 4, lambda made: [(made, o)], a, b, *scratch[3:]),
    )


def gather_beside(block, a, b, ids, pieces=4):
    anywhere = pl.BlockSpec(memory_space=pl.ANY)
    rows, cols = block.shape
    return pl.pallas_call(
        partial(gather_beside_kernel, pieces),
        out_shape=(
            jax.ShapeDtypeStruct((PLANE * rows, cols), BF),
            jax.ShapeDtypeStruct((a.shape[0], b.shape[1]), BF),
        ),
        in_specs=[anywhere] * 3,
        out_specs=(anywhere, anywhere),
        scratch_shapes=[
            pltpu.SemaphoreType.DMA,
            pltpu.SemaphoreType.DMA((7, pieces)),
            pltpu.SemaphoreType.DMA((7, pieces)),
        ]
        + product_scratch(0, a, b),
        cost_estimate=lasting(22),
        compiler_params=pltpu.CompilerParams(
            collective_id=next(ids), has_side_effects=True, vmem_limit_bytes=40 * 2**20
        ),
    )(block, a, b)


def scatter_two_kernel(p_ref, q_ref, o_ref, oq_ref, *scratch):
    me, sibling, by_x, by_y = plane()
    greet([(CTX, sibling), (CTX, by_x), (CTX, by_y)])
    together(
        scatter_steps(0, p_ref, o_ref, *scratch[:10]),
        scatter_steps(0, q_ref, oq_ref, *scratch[10:]),
    )


def scatter_two(first, second, ids, waits=()):
    near = pl.BlockSpec(memory_space=pltpu.VMEM)
    shapes = [(x.shape[0] // PLANE, x.shape[1]) for x in (first, second)]
    return pl.pallas_call(
        unused(scatter_two_kernel, 2, len(waits)),
        out_shape=tuple(jax.ShapeDtypeStruct(shape, F32) for shape in shapes),
        in_specs=[pl.BlockSpec(memory_space=pl.ANY)] * (2 + len(waits)),
        out_specs=(near, near),
        scratch_shapes=scatter_scratch(*shapes[0]) + scatter_scratch(*shapes[1]),
        cost_estimate=lasting(28),
        compiler_params=pltpu.CompilerParams(
            collective_id=next(ids), has_side_effects=True, vmem_limit_bytes=40 * 2**20
        ),
    )(first, second, *waits)


def closing_kernel(
    seqs, g1, g2, g3, w1, w2, w3, rest, ffn, hat, o_ref, norm_ref, query, zgate, gate, up, p_ref, *scratch
):
    factors, own, sems = (g1, g2, g3, w1, w2, w3), scratch[:6], scratch[6]
    scratch = scratch[7:]
    loads = [
        pltpu.make_async_copy(factors[k], own[k], sems.at[k]) for k in range(len(factors))
    ]
    for load in loads:
        load.start()
    greet(other_places(CTX, PLANE))
    head = query.shape[1] // PLANE
    inner = zgate.shape[1] // PLANE
    half = gate.shape[1] // PLANE
    pair = 2 * o_ref.shape[0]

    def make(chip):
        rows = pl.ds(pl.multiple_of(chip * pair, pair), pair)
        total = 0.0
        for g, w in zip(own[:3], own[3:]):
            total = total + lax.dot_general(
                g[rows, :], w[...], (((1,), (1,)), ((), ())), preferred_element_type=F32
            )
        p_ref[rows, :] = total.astype(BF)

    from_rest = [
        (lambda to: rest.at[to, :, :head], lambda at: columns(query, at, head)),
        (lambda to: rest.at[to, :, head:], lambda at: columns(zgate, at, inner)),
    ]
    from_ffn = [
        (lambda to: ffn.at[to, :, :half], lambda at: columns(gate, at, half)),
        (lambda to: ffn.at[to, :, half:], lambda at: columns(up, at, half)),
    ]
    for load in loads:
        load.wait()
    together(
        swap_steps(0, 8, from_rest, *scratch[10:13]),
        swap_steps(0, 8, from_ffn, *scratch[13:]),
        scatter_steps(seqs, p_ref, o_ref, *scratch[:10], make=make),
    )
    total = jnp.sum(o_ref[...] * hat[...], axis=0, keepdims=True)
    norm_ref[...] = jnp.zeros_like(norm_ref)
    part = total.shape[1] // (PLANE * seqs)
    for k in range(PLANE * seqs):
        norm_ref[k // seqs, k % seqs, 0:1, 0:part] = total[:, k * part : (k + 1) * part]


def closing(grads, weights, rest, ffn, hat, head, seqs, ids, waits=()):
    anywhere = pl.BlockSpec(memory_space=pl.ANY)
    near = pl.BlockSpec(memory_space=pltpu.VMEM)
    length, cols = grads[0].shape[0], weights[0].shape[0]
    rows = length // PLANE
    _, krows, rest_cols = rest.shape
    half = ffn.shape[2] // 2

    def wide(count):
        return jax.ShapeDtypeStruct((krows, PLANE * count), BF)

    return pl.pallas_call(
        unused(partial(closing_kernel, seqs), 9, len(waits)),
        out_shape=(
            jax.ShapeDtypeStruct((rows, cols), F32),
            jax.ShapeDtypeStruct((PLANE, seqs, 8, 128), F32),
            wide(head),
            wide(rest_cols - head),
            wide(half),
            wide(half),
        ),
        in_specs=[anywhere] * 8 + [near] + [anywhere] * len(waits),
        out_specs=(near, near) + (anywhere,) * 4,
        scratch_shapes=[pltpu.VMEM((length, cols), BF)]
        + [pltpu.VMEM(x.shape, BF) for x in (*grads, *weights)]
        + [pltpu.SemaphoreType.DMA((6,))]
        + scatter_scratch(rows, cols)
        + swap_scratch(2)
        + swap_scratch(2),
        cost_estimate=lasting(35),
        compiler_params=pltpu.CompilerParams(
            collective_id=next(ids), has_side_effects=True, vmem_limit_bytes=60 * 2**20
        ),
    )(*grads, *weights, rest, ffn, hat, *waits)


def step_sum_steps(seqs, x_ref, o_ref, land, got, own_sem, send_sem, recv_sem):
    me, mine = lax.axis_index(CTX), lax.axis_index(FSDP)
    keep = pltpu.make_async_copy(x_ref.at[me], land.at[me], own_sem)
    keep.start()
    copies = []
    for j, (axis, to) in enumerate(other_places(CTX, PLANE)):
        copy = remote(x_ref.at[to], land.at[me], send_sem.at[j], recv_sem.at[j], axis, to)
        copy.start()
        copies.append(copy)
    yield True
    keep.wait()
    for copy in copies:
        copy.wait_recv()
    first = len(copies)
    for j, (axis, other) in enumerate(other_places(FSDP, seqs)):
        k = PLANE + j
        copy = remote(land.at[:, other], got.at[j], send_sem.at[k], recv_sem.at[k], axis, other)
        copy.start()
        copies.append(copy)
    yield True
    total = land[:, mine]
    for j, copy in enumerate(copies[first:]):
        copy.wait_recv()
        total = total + got[j]
    o_ref[...] = total
    for copy in copies:
        copy.wait_send()


def last_kernel(
    seqs, norm, ffn_gain, mixer_gain, channel, by_head, step, conv,
    small_ref, step_ref, channels, key, value,
    mixed, x_ref, st_ref, full, *scratch
):
    me = lax.axis_index(CTX)
    given = (norm, ffn_gain, mixer_gain, channel, by_head, step)
    near, sems, scratch = scratch[:6], scratch[6], scratch[7:]
    loads = [pltpu.make_async_copy(given[k], near[k], sems.at[k]) for k in range(len(given))]
    for load in loads:
        load.start()
    norm, ffn_gain, mixer_gain, channel, by_head, step = near
    devices = PLANE * seqs
    krows = conv.shape[1]
    bc = 2 * STATE // PLANE
    total = channels.shape[1] - 2 * STATE
    inner = total // PLANE
    kv = value.shape[1] // PLANE
    from_conv = [
        (lambda to: conv.at[to, :, :inner], lambda at: columns(channels, at, inner)),
        (lambda to: conv.at[to, :, inner:], lambda at: mixed.at[at]),
    ]
    x_ref[...] = jnp.zeros_like(x_ref)
    full[...] = jnp.zeros_like(full)
    st_ref[...] = jnp.zeros_like(st_ref)
    for load in loads:
        load.wait()
    kinds = channel.shape[0]
    full[0:kinds, pl.ds(pl.multiple_of(me * inner, 128), inner)] = channel[:, :inner]
    for k in range(PLANE):
        full[0:kinds, total + k * bc : total + (k + 1) * bc] = jnp.where(
            me == k, channel[:, inner:], 0.0
        )
    heads = by_head.shape[1]
    mine_only = [jnp.where(me == k, by_head[...], 0.0) for k in range(PLANE)]
    spread = jnp.concatenate(mine_only, axis=1)
    part, wide = ffn_gain.shape[1] // devices, full.shape[1] // devices
    for n in range(devices):
        c, f = n // seqs, n % seqs
        x_ref[c, f, 0:1, 0:part] = ffn_gain[:, n * part : (n + 1) * part]
        x_ref[c, f, 1:2, :] = norm[c, f, 0:1, :]
        x_ref[c, f, 3 : 3 + kinds, 0:wide] = full[0:kinds, n * wide : (n + 1) * wide]
        x_ref[c, f, 8:11, 0 : PLANE * heads] = spread
        at = (f * PLANE + c) * krows
        st_ref[c, f, 0:heads, 0:krows] = step[:, at : at + krows]
    part = inner // seqs
    for f in range(seqs):
        x_ref[me, f, 2:3, 0:part] = mixer_gain[:, f * part : (f + 1) * part]
    greet(other_places(FSDP, seqs) + other_places(CTX, PLANE))
    together(
        small_scatter_steps(seqs, x_ref, small_ref, *scratch[:7]),
        step_sum_steps(seqs, st_ref, step_ref, *scratch[7:12]),
        swap_steps(0, 2, from_conv, *scratch[12:]),
    )
    blocks = [mixed[k].astype(F32) for k in range(PLANE)]
    channels[:, total:] = jnp.concatenate([b[:, :bc] for b in blocks], axis=1).astype(BF)
    value[...] = jnp.concatenate([b[:, bc + kv :] for b in blocks], axis=1)
    half = kv // 2
    group = PLANE // KEY_VALUE_HEADS
    turned = []
    for k in range(0, PLANE, group):
        for at in (bc, bc + half):
            turned += [b[:, at : at + half] for b in blocks[k : k + group]]
    key[...] = jnp.concatenate(turned, axis=1)


def last_exchange(small, conv, inner, kv, seqs, ids, waits=()):
    anywhere = pl.BlockSpec(memory_space=pl.ANY)
    near = pl.BlockSpec(memory_space=pltpu.VMEM)
    _, krows, cols = conv.shape

    def room(*shape):
        return pltpu.VMEM(shape, F32)

    two = [pltpu.SemaphoreType.DMA((PLANE + seqs,)), pltpu.SemaphoreType.DMA((PLANE + seqs,))]
    return pl.pallas_call(
        unused(partial(last_kernel, seqs), 7, len(waits)),
        out_shape=(
            jax.ShapeDtypeStruct((16, 128), F32),
            jax.ShapeDtypeStruct((PLANE, 8, 128), F32),
            jax.ShapeDtypeStruct((krows, PLANE * inner + 2 * STATE), BF),
            jax.ShapeDtypeStruct((krows, PLANE * kv), F32),
            jax.ShapeDtypeStruct((krows, PLANE * kv), F32),
        ),
        in_specs=[anywhere] * (7 + len(waits)),
        out_specs=(near,) * 5,
        scratch_shapes=[
            pltpu.VMEM((PLANE, krows, cols - inner), BF),
            room(PLANE, seqs, 16, 128),
            room(PLANE, seqs, 8, 128),
            room(8, PLANE * inner + 2 * STATE),
            *[room(*x.shape) for x in small],
            pltpu.SemaphoreType.DMA((6,)),
            room(seqs, 16, 128),
            room(PLANE - 1, seqs, 16, 128),
            room(seqs, 16, 128),
            room(seqs - 1, 16, 128),
            pltpu.SemaphoreType.DMA,
            *two,
            room(PLANE, seqs, 8, 128),
            room(seqs - 1, PLANE, 8, 128),
            pltpu.SemaphoreType.DMA,
            *two,
        ]
        + swap_scratch(2),
        cost_estimate=lasting(15),
        compiler_params=pltpu.CompilerParams(
            collective_id=next(ids), has_side_effects=True, vmem_limit_bytes=40 * 2**20
        ),
    )(*small, conv, *waits)


def gather_rows(shard):
    return lax.all_gather(shard, FSDP, axis=0, tiled=False)


def scatter_rows(partial_sum):
    return lax.psum_scatter(partial_sum.astype(BF), FSDP, scatter_dimension=0, tiled=False)


def hold_kernel(*refs):
    pass


def hold(value, *earlier):
    anywhere = pl.BlockSpec(memory_space=pl.ANY)
    return pl.pallas_call(
        hold_kernel,
        out_shape=jax.ShapeDtypeStruct(value.shape, value.dtype),
        in_specs=[anywhere] * (1 + len(earlier)),
        out_specs=anywhere,
        input_output_aliases={0: 0},
    )(value, *earlier)


def lasting(us):
    return pl.CostEstimate(flops=int(us * 0.3e9), bytes_accessed=int(us * 0.3e6), transcendentals=0)


def same_document(documents):
    places = jnp.arange(documents.shape[0])
    return (documents[:, None] == documents[None, :]) & (places[:, None] >= places[None, :])


def rotate_some(values, places, first_pair, pairs):
    half = values.shape[-1] // 2
    freqs = ROPE_BASE ** (-(first_pair + jnp.arange(half)).astype(F32) / pairs)
    angles = places[:, None] * freqs[None, :]
    cosine, sine = jnp.cos(angles), jnp.sin(angles)
    first, second = values[:, :half], values[:, half:]
    return jnp.concatenate(
        [first * cosine - second * sine, second * cosine + first * sine], axis=-1
    )


def ssm_terms(step, rate, documents, chunks):
    length, heads = step.shape
    rows = length // chunks
    step_c = step.reshape(chunks, rows, heads).transpose(0, 2, 1)
    docs_c = documents.reshape(chunks, rows)
    prior = jnp.concatenate([jnp.full((1,), -1, docs_c.dtype), docs_c[:-1, -1]])
    last = docs_c[:, -1]
    level = jnp.cumsum(step_c * rate[None, :, None], axis=2)
    visible = jax.vmap(same_document)(docs_c)[:, None]
    spread = level[:, :, :, None] - level[:, :, None, :]
    pair = jnp.where(visible, jnp.exp(jnp.where(visible, spread, 0.0)), 0.0)
    entry = jnp.where((docs_c == prior[:, None])[:, None], jnp.exp(level), 0.0)
    tail = jnp.where((docs_c == last[:, None])[:, None], jnp.exp(level[:, :, -1:] - level), 0.0)
    carry = jnp.exp(level[:, :, -1]) * (last == prior).astype(F32)[:, None]
    k, j, i = (jnp.arange(chunks).reshape(shape) for shape in ((-1, 1, 1), (1, -1, 1), (1, 1, -1)))
    between = ((j < i) & (i < k))[..., None]
    reach = jnp.prod(jnp.where(between, carry[None, None], 1.0), axis=2)
    reach = jnp.where((j < k), reach, 0.0)
    return step_c, pair, entry, tail, carry, reach


def ssm_forward(xin, write, read, terms, skip):
    step_c, pair, entry, tail, carry, reach = terms
    chunks, heads, rows = step_c.shape
    x_c = xin.reshape(chunks, rows, heads, HP)
    write_c = write.reshape(chunks, rows, STATE)
    read_c = read.reshape(chunks, rows, STATE)
    gram = jnp.einsum("ktn,kun->ktu", read_c, write_c, preferred_element_type=F32)
    mixing = (pair * gram[:, None] * step_c[:, :, None, :]).astype(BF)
    inner = jnp.einsum("khtu,kuhp->kthp", mixing, x_c, preferred_element_type=F32)
    weight = (tail * step_c).transpose(0, 2, 1)
    weighted = (x_c.astype(F32) * weight[..., None]).astype(BF)
    local = jnp.einsum("kthp,ktn->khpn", weighted, write_c, preferred_element_type=F32)
    entering = jnp.sum(reach[:, :, :, None, None] * local[None], axis=1)
    reached = jnp.einsum(
        "ktn,khpn->kthp", read_c, entering.astype(BF), preferred_element_type=F32
    )
    y = (
        inner
        + reached * entry.transpose(0, 2, 1)[..., None]
        + skip[None, None, :, None] * x_c.astype(F32)
    )
    return y.reshape(chunks * rows, heads * HP), (gram, mixing, entering, reached)


def ssm_backward(grad, xin, write, read, terms, skip, rate, saved):
    step_c, pair, entry, tail, carry, reach = terms
    gram, mixing, entering, reached = saved
    chunks, heads, rows = step_c.shape
    x_c = xin.reshape(chunks, rows, heads, HP)
    x_f = x_c.astype(F32)
    write_c = write.reshape(chunks, rows, STATE)
    read_c = read.reshape(chunks, rows, STATE)
    g = grad.reshape(chunks, rows, heads, HP)
    g_low = g.astype(BF)
    skip_grad = jnp.sum(g * x_f, axis=(0, 1, 3))
    gx = skip[None, None, :, None] * g
    gx = gx + jnp.einsum("khtu,kthp->kuhp", mixing, g_low, preferred_element_type=F32)
    g_mixing = jnp.einsum("kthp,kuhp->khtu", g_low, x_c, preferred_element_type=F32)
    masked = g_mixing * pair
    g_gram = jnp.sum(masked * step_c[:, :, None, :], axis=1).astype(BF)
    both = masked * gram[:, None]
    column = jnp.sum(both, axis=2)
    row = jnp.sum(both * step_c[:, :, None, :], axis=3)
    g_level = row - step_c * column
    g_step = column
    entry_t = entry.transpose(0, 2, 1)[..., None]
    g_entry = jnp.sum(g * reached, axis=3).transpose(0, 2, 1)
    g_level = g_level + g_entry * entry
    g_reached = (g * entry_t).astype(BF)
    g_read = jnp.einsum("ktu,kun->ktn", g_gram, write_c, preferred_element_type=F32)
    g_write = jnp.einsum("ktu,ktn->kun", g_gram, read_c, preferred_element_type=F32)
    g_read = g_read + jnp.einsum(
        "kthp,khpn->ktn", g_reached, entering.astype(BF), preferred_element_type=F32
    )
    g_enter = jnp.einsum("kthp,ktn->khpn", g_reached, read_c, preferred_element_type=F32)
    leaving = jnp.sum(reach.transpose(1, 0, 2)[:, :, :, None, None] * g_enter[None], axis=1)
    g_carry = jnp.sum(entering * leaving, axis=(2, 3))
    leaving_low = leaving.astype(BF)
    weight = tail * step_c
    weight_t = weight.transpose(0, 2, 1)[..., None]
    seen = jnp.einsum("ktn,khpn->kthp", write_c, leaving_low, preferred_element_type=F32)
    gx = gx + weight_t * seen
    g_weight = jnp.sum(x_f * seen, axis=3).transpose(0, 2, 1)
    weighted = (x_f * weight_t).astype(BF)
    g_write = g_write + jnp.einsum(
        "kthp,khpn->ktn", weighted, leaving_low, preferred_element_type=F32
    )
    moved = g_weight * weight
    g_step = g_step + g_weight * tail
    g_level = g_level - moved
    end = jnp.sum(moved, axis=2) + g_carry * carry
    g_level = g_level.at[:, :, -1].add(end)
    g_la = jnp.flip(jnp.cumsum(jnp.flip(g_level, 2), axis=2), 2)
    g_step = g_step + g_la * rate[None, :, None]
    rate_grad = jnp.sum(g_la * step_c, axis=(0, 2))
    length = chunks * rows
    return (
        gx.reshape(length, heads * HP),
        g_write.reshape(length, STATE),
        g_read.reshape(length, STATE),
        g_step.transpose(0, 2, 1).reshape(length, heads),
        rate_grad,
        skip_grad,
    )


def head_parallel(
    hidden_in,
    out_grad,
    doc_ids,
    norm_gain,
    query_weight,
    key_matrix,
    value_matrix,
    attn_out_weight,
    mixer_gate_weight,
    conv_in_weight,
    step_weight,
    conv_weight,
    conv_bias,
    step_bias,
    log_decay,
    skip_gain,
    mixer_gain,
    mamba_out_weight,
    ffn_gain,
    gate_weight,
    up_weight,
    down_weight,
):
    ctx = lax.axis_size(CTX)
    seqs = lax.axis_size(FSDP)
    me = lax.axis_index(CTX)
    mine = lax.axis_index(FSDP)
    tokens, width = hidden_in.shape[1:]
    length = ctx * tokens
    krows = query_weight.shape[0]
    dssm = HS * HP
    heads = HS // ctx
    inner = heads * HP
    bc = 2 * STATE // ctx
    ff = gate_weight.shape[1] // ctx
    head = HEAD_SIZE * QUERY_HEADS // ctx
    taps = CONV - 1

    ids = itertools.count(1)

    def to_shards(x):
        return x.reshape(-1, ctx, seqs, krows).transpose(0, 2, 1, 3).reshape(-1, width)

    def from_shards(x):
        return x.reshape(-1, seqs, ctx, krows).transpose(0, 2, 1, 3).reshape(-1, width)

    small = jnp.concatenate(
        [
            norm_gain,
            ffn_gain,
            mixer_gain,
            conv_bias,
            conv_weight.reshape(-1),
            doc_ids[0].astype(BF),
            step_weight.reshape(-1),
        ]
    )
    small_size = small.size
    tile_rows = -(-small_size // 2048) * 16
    small = jnp.pad(small, (0, tile_rows * 128 - small_size)).reshape(tile_rows, 128)

    def by_column(weight, n):
        return weight.reshape(krows, ctx, n).transpose(1, 0, 2)

    kv_repeat = ctx // KEY_VALUE_HEADS
    kv = HEAD_SIZE // kv_repeat
    half = kv // 2
    key_pack = (
        key_matrix.reshape(krows, KEY_VALUE_HEADS, 2, kv_repeat, half)
        .transpose(1, 3, 0, 2, 4)
        .reshape(ctx, krows, kv)
    )
    mixed_pack = jnp.concatenate(
        [by_column(conv_in_weight[:, dssm:], bc), key_pack, by_column(value_matrix, kv)], axis=2
    )
    conv_cols = inner + bc + 2 * kv
    rest_cols = head + inner
    resid = hidden_in[0].astype(F32)
    scale_one = lax.rsqrt(jnp.mean(resid * resid, axis=-1, keepdims=True) + EPSILON)
    hat_one = resid * scale_one
    small, out_own, normed, grad_all, _, rest_pack, ffn_pack, conv_in_own = opening(
        small,
        jnp.concatenate([attn_out_weight, mamba_out_weight]),
        to_shards(hat_one.astype(BF)),
        out_grad[0],
        query_weight,
        mixer_gate_weight,
        conv_in_weight,
        mixed_pack,
        gate_weight,
        up_weight,
        seqs,
        ids,
    )
    conv_in_own = conv_in_own.reshape(width, conv_cols)
    small = small.reshape(ctx * seqs, -1)
    cuts = []
    at = 0
    for n in (norm_gain.size, ffn_gain.size, mixer_gain.size, conv_bias.size, conv_weight.size, tokens, step_weight.size):
        cuts.append(small[:, at : at + n])
        at += n
    gain_one = cuts[0].reshape(-1).astype(F32)
    gain_two = cuts[1].reshape(-1).astype(F32)
    gain_mix = lax.dynamic_slice_in_dim(cuts[2].reshape(-1), me * inner, inner).astype(F32)
    bias_all = cuts[3].reshape(-1)
    taps_all = cuts[4].reshape(ctx * seqs, CONV, -1).transpose(1, 0, 2).reshape(CONV, -1)
    documents = lax.dynamic_index_in_dim(
        cuts[5].reshape(ctx, seqs, tokens), mine, 1, False
    ).reshape(length).astype(jnp.int32)

    def own_channels(full):
        return jnp.concatenate(
            [
                lax.dynamic_slice_in_dim(full, me * inner, inner, full.ndim - 1),
                lax.dynamic_slice_in_dim(full, dssm + me * bc, bc, full.ndim - 1),
            ],
            axis=-1,
        )

    conv_taps = own_channels(taps_all).astype(F32)
    conv_shift = own_channels(bias_all).astype(F32)
    bias_own = lax.dynamic_slice_in_dim(step_bias, me * heads, heads)
    decay_own = lax.dynamic_slice_in_dim(log_decay, me * heads, heads)
    skip_own = lax.dynamic_slice_in_dim(skip_gain, me * heads, heads)

    rest_own = gather_rows(rest_pack).reshape(width, rest_cols)
    out_rows = attn_out_weight.shape[0]
    out_own = jnp.concatenate(
        [out_own[:, :out_rows].reshape(head, width), out_own[:, out_rows:].reshape(inner, width)]
    )
    ffn_own = gather_rows(ffn_pack).reshape(width, 2 * ff)
    down_own = gather_rows(down_weight).reshape(ff, width)
    step_own = lax.dynamic_slice_in_dim(
        cuts[6].reshape(ctx, seqs, krows, HS).transpose(1, 0, 2, 3).reshape(width, HS),
        me * heads,
        heads,
        1,
    )
    step_room = ((0, 0), (0, 128 - heads))
    step_wide = jnp.pad(step_own, step_room)

    normed = (normed.astype(F32) * to_shards(gain_one[None])).astype(BF)
    conv_all = mm(normed, conv_in_own)
    rest_all = mm(normed, rest_own)
    conv_lin = conv_all[:, : inner + bc].astype(BF).astype(F32)
    k_lin = conv_all[:, inner + bc : inner + bc + kv]
    v_lin = conv_all[:, inner + bc + kv :]
    step_lin = mm(normed, step_own)
    q_lin = rest_all[:, :head]
    zgate = rest_all[:, head:]

    widened = jnp.concatenate([jnp.zeros((taps, inner + bc), F32), conv_lin], axis=0)
    widened_docs = jnp.concatenate([jnp.full((taps,), -1, jnp.int32), documents])
    conv_act, conv_back = jax.vjp(
        partial(conv_part, widened_docs=widened_docs, documents=documents),
        widened,
        conv_taps,
        conv_shift,
    )
    conv_act = conv_act.astype(BF)
    places = jnp.arange(length).astype(F32)
    first_pair = (me % kv_repeat) * half
    key_turned, unturn_key = jax.vjp(
        lambda lin: rotate_some(lin, places, first_pair, HEAD_SIZE // 2), k_lin
    )
    shared = jnp.concatenate(
        [conv_act[:, inner:], key_turned.astype(BF), v_lin.astype(BF)], axis=1
    ).T
    shared = gather_tokens(shared, ids, 2).reshape(ctx, bc + 2 * kv, length)
    write_read = shared[:, :bc].reshape(2 * STATE, length).T
    write, read = write_read[:, :STATE], write_read[:, STATE:]
    group = me // kv_repeat * kv_repeat
    own_kv = lax.dynamic_slice_in_dim(shared[:, bc:], group, kv_repeat, 0)
    key = (
        own_kv[:, :kv]
        .reshape(kv_repeat, 2, half, length)
        .transpose(1, 0, 2, 3)
        .reshape(HEAD_SIZE, length)
        .T
    )
    value = own_kv[:, kv:].reshape(HEAD_SIZE, length).T
    xin = conv_act[:, :inner]

    query_turned, unturn = jax.vjp(
        partial(rotate, places=places), q_lin.reshape(length, head // HEAD_SIZE, HEAD_SIZE)
    )
    query = query_turned.astype(BF)
    visible = same_document(documents)
    scores = jnp.einsum("thd,ud->htu", query, key, preferred_element_type=F32) * HEAD_SIZE**-0.5
    scores = jnp.where(visible[None], scores, NEGATIVE_FLOOR)
    weights = jnp.where(
        visible[None], jnp.exp(scores - jnp.max(scores, axis=-1, keepdims=True)), 0.0
    )
    probs = weights / jnp.sum(weights, axis=-1, keepdims=True)
    probs_low = probs.astype(BF)
    attn_mix = jnp.einsum("htu,ud->thd", probs_low, value, preferred_element_type=F32)
    attn_low = attn_mix.reshape(length, head).astype(BF)

    step_size, step_back = jax.vjp(
        lambda lin, bias: jax.nn.softplus(lin + bias[None, :]), step_lin, bias_own
    )
    rate = -jnp.exp(decay_own)
    terms = ssm_terms(step_size, rate, documents, ctx)
    y, saved = ssm_forward(xin, write, read, terms, skip_own)
    gated, gated_back = jax.vjp(lambda a, z: a * jax.nn.silu(z), y, zgate)
    mean_square = row_sum(jnp.sum(gated * gated, axis=-1), ids) / dssm
    scale_mix = lax.rsqrt(mean_square + EPSILON)[:, None]
    ymix = (gated * scale_mix * gain_mix).astype(BF)

    mixed = jnp.concatenate([attn_low, ymix], axis=1)
    branch = scatter_tokens(mm(mixed, out_own), ids)
    mid = resid + branch
    scale_two = lax.rsqrt(jnp.mean(mid * mid, axis=-1, keepdims=True) + EPSILON)
    normed_two = gather_tokens(to_shards((mid * scale_two * gain_two).astype(BF)), ids)

    gate_up = mm(normed_two, ffn_own)
    gate_lin, up_lin = gate_up[:, :ff], gate_up[:, ff:]
    sigmoid_gate = jax.nn.sigmoid(gate_lin)
    silu_gate = gate_lin * sigmoid_gate
    hidden = (silu_gate * up_lin).astype(BF)
    down_part = mm_tn(hidden, grad_all).astype(BF).reshape(seqs, ff // seqs, width)
    down_own = hold(down_own, down_part)
    grad_hidden = mm_nt(grad_all, down_own)
    grad_gate = (
        grad_hidden * up_lin * (sigmoid_gate + silu_gate * (1.0 - sigmoid_gate))
    ).astype(BF)
    grad_up = (grad_hidden * silu_gate).astype(BF)
    grad_gu = jnp.concatenate([grad_gate, grad_up], axis=1)
    down_grad = scatter_rows(down_part)
    grad_n2, ffn_grad = scatter_beside(mm_nt(grad_gu, ffn_own), normed_two, grad_gu, seqs, ids)
    ffn_grad = scatter_rows(ffn_grad.reshape(seqs, ctx, krows, 2 * ff))

    turned = grad_n2 * gain_two
    hat_two = mid * scale_two
    ffn_gain_grad = jnp.sum(grad_n2 * hat_two, axis=0, keepdims=True)
    grad_mid = out_grad[0].astype(F32) + scale_two * (
        turned - hat_two * jnp.mean(turned * hat_two, axis=-1, keepdims=True)
    )
    branch_grad, last = gather_beside(grad_mid.astype(BF), hidden, down_own, ids)
    branch_grad = hold(branch_grad, down_grad)

    grad_attn = mm_nt(branch_grad, out_own[:head]).astype(BF).reshape(length, -1, HEAD_SIZE)
    grad_ymix = mm_nt(branch_grad, out_own[head:])

    grad_prob = jnp.einsum("thd,ud->htu", grad_attn, value, preferred_element_type=F32)
    delta = jnp.sum(probs * grad_prob, axis=-1, keepdims=True)
    grad_score = (probs * (grad_prob - delta)).astype(BF)
    grad_query = (
        jnp.einsum("htu,ud->thd", grad_score, key, preferred_element_type=F32) * HEAD_SIZE**-0.5
    )
    grad_key = (
        jnp.einsum("htu,thd->ud", grad_score, query, preferred_element_type=F32) * HEAD_SIZE**-0.5
    )
    grad_value = jnp.einsum("htu,thd->ud", probs_low, grad_attn, preferred_element_type=F32)
    grad_q_lin = unturn(grad_query)[0].reshape(length, head).astype(BF)

    hat = gated * scale_mix
    turned_mix = grad_ymix * gain_mix
    mixer_gain_grad = jnp.sum(grad_ymix * hat, axis=0, keepdims=True)
    along, out_part = row_sum_beside(
        jnp.sum(turned_mix * hat, axis=-1), mixed, branch_grad, head, seqs, ids, (down_grad,)
    )
    out_grad_own = scatter_rows(hold(out_part, ffn_grad))
    along = along[:, None] / dssm
    grad_gated = scale_mix * (turned_mix - hat * along)
    grad_y, grad_zgate = gated_back(grad_gated)

    grad_rest = jnp.concatenate([grad_q_lin, grad_zgate.astype(BF)], axis=1)
    rest_part = mm_tn(normed, grad_rest).reshape(seqs, ctx, krows, rest_cols).astype(BF)

    grad_xin, grad_write, grad_read, grad_step, grad_rate, skip_grad = ssm_backward(
        grad_y, xin, write, read, terms, skip_own, rate, saved
    )
    grad_key = (
        grad_key.T.reshape(2, kv_repeat, half, length)
        .transpose(1, 0, 2, 3)
        .reshape(kv_repeat, kv, length)
    )
    grad_kv = jnp.concatenate([grad_key, grad_value.T.reshape(kv_repeat, kv, length)], axis=1)
    grad_kv = lax.dynamic_update_slice_in_dim(
        jnp.zeros((ctx, 2 * kv, length), BF), grad_kv.astype(BF), group, 0
    )
    grad_shared = jnp.concatenate([grad_write, grad_read], axis=1).astype(BF)
    grad_shared = jnp.concatenate([grad_shared.T.reshape(ctx, bc, length), grad_kv], axis=1)
    grad_shared, last = scatter_two(
        grad_shared.reshape(ctx * (bc + 2 * kv), length),
        last,
        ids,
        (ffn_grad, rest_part),
    )
    block_out = (mid + last).astype(BF)
    grad_shared = grad_shared.T
    grad_k_lin = unturn_key(grad_shared[:, bc : bc + kv])[0].astype(BF)
    grad_v_lin = grad_shared[:, bc + kv :].astype(BF)
    grad_shared = grad_shared[:, :bc]
    grad_widened, taps_grad, shift_grad = conv_back(
        jnp.concatenate([grad_xin, grad_shared], axis=1)
    )
    grad_step_lin, step_bias_grad = step_back(grad_step)
    log_decay_grad = grad_rate * rate
    grad_conv = jnp.concatenate(
        [grad_widened[taps:].astype(BF), grad_k_lin, grad_v_lin], axis=1
    )
    grad_step_low = grad_step_lin.astype(BF)
    step_grad = mm_tn(grad_step_low, normed)
    rest_grad = scatter_rows(rest_part)
    conv_grad = mm_tn(normed, grad_conv).reshape(seqs, ctx, krows, conv_cols)
    conv_grad = scatter_rows(conv_grad)
    attn_out_grad = out_grad_own[:out_rows].astype(F32)
    mamba_out_grad = out_grad_own[out_rows:].astype(F32)
    down_grad = down_grad.astype(F32)
    grad_normed, norm_rows, query_grad, zgate_grad, gate_grad, up_grad = closing(
        (grad_conv, grad_rest, jnp.pad(grad_step_low, step_room)),
        (conv_in_own, rest_own, step_wide),
        rest_grad,
        ffn_grad,
        hat_one,
        head,
        seqs,
        ids,
        (attn_out_grad, mamba_out_grad, down_grad),
    )

    gate_grad, up_grad = gate_grad.astype(F32), up_grad.astype(F32)

    sums, step_sums, channels_grad, key_grad, value_grad = last_exchange(
        (
            norm_rows,
            ffn_gain_grad,
            mixer_gain_grad,
            jnp.concatenate([shift_grad[None], taps_grad]),
            jnp.stack([step_bias_grad, log_decay_grad, skip_grad]),
            step_grad,
        ),
        conv_grad,
        inner,
        kv,
        seqs,
        ids,
    )
    step_grad = step_sums[:, :heads, :krows].reshape(HS, krows).T

    turned_one = grad_normed * gain_one
    input_grad = (
        grad_mid
        + scale_one
        * (turned_one - hat_one * jnp.mean(turned_one * hat_one, axis=-1, keepdims=True))
    ).astype(BF)

    return (
        block_out[None],
        input_grad[None],
        sums[1, :krows],
        query_grad.astype(F32),
        key_grad,
        value_grad,
        attn_out_grad,
        zgate_grad.astype(F32),
        channels_grad.astype(F32),
        step_grad,
        sums[4 : 4 + CONV, : conv_weight.shape[1]],
        sums[3, : conv_bias.size],
        sums[8, :HS],
        sums[9, :HS],
        sums[10, :HS],
        sums[2, : mixer_gain.size],
        mamba_out_grad,
        sums[0, :krows],
        gate_grad,
        up_grad,
        down_grad,
    )


def solution(mesh):
    placed = (
        P(FSDP, CTX, None),
        P(FSDP, CTX, None),
        P(FSDP, CTX),
        P((CTX, FSDP)),
        P((CTX, FSDP), None),
        P((CTX, FSDP), None),
        P((CTX, FSDP), None),
        P((CTX, FSDP), None),
        P((CTX, FSDP), None),
        P((CTX, FSDP), None),
        P((CTX, FSDP), None),
        P(None, (CTX, FSDP)),
        P((CTX, FSDP)),
        P(),
        P(),
        P(),
        P((CTX, FSDP)),
        P((CTX, FSDP), None),
        P((CTX, FSDP)),
        P((CTX, FSDP), None),
        P((CTX, FSDP), None),
        P((CTX, FSDP), None),
    )
    ctx = mesh.shape[CTX]
    whole_heads = ctx == PLANE and QUERY_HEADS % ctx == 0 and HS % ctx == 0
    return jax.shard_map(
        head_parallel if whole_heads else on_device,
        mesh=mesh,
        in_specs=placed,
        out_specs=(
            P(FSDP, CTX, None),
            P(FSDP, CTX, None),
            P((CTX, FSDP)),
            P((CTX, FSDP), None),
            P((CTX, FSDP), None),
            P((CTX, FSDP), None),
            P((CTX, FSDP), None),
            P((CTX, FSDP), None),
            P((CTX, FSDP), None),
            P((CTX, FSDP), None),
            P(None, (CTX, FSDP)),
            P((CTX, FSDP)),
            P(),
            P(),
            P(),
            P((CTX, FSDP)),
            P((CTX, FSDP), None),
            P((CTX, FSDP)),
            P((CTX, FSDP), None),
            P((CTX, FSDP), None),
            P((CTX, FSDP), None),
        ),
        check_vma=False,
    )
```
